32 devices in a mesh: gx: 8 (over z, x), gy: 4 (over y, core).
Axes of the slice: x: 2, y: 2, z: 4, core: 2. Of those that a mesh axis runs over, the one named last changes fastest.
Arguments:
- velocity: float32 [256, 512, 256], P('gx', 'gy'), may hold values from -6 to 6
- threshold_table: float32 [16], replicated, may hold values from 0.05 to 1.5
- band_index: int32 [3, 7], replicated, may hold values from 0 to 15
Outputs:
- updated: float32 [256, 512, 256], P('gx', 'gy')
The draws below stay inside these ranges and needn't reach their ends.
All inputs are finite; a program needn't handle non-finite values.
Results may differ from the reference program's by a relative error of at most 0.0003.
Values sent between devices are 32-bit elements; how exact they have to be, the bound alone decides.
No kernel may reach another device: no remote copies, remote signals or barrier semaphores. Data moves between devices by JAX's collectives and lax.ppermute only.
A program may use at most 128 MiB of HBM per device.

```python
import math
import jax
import jax.numpy as jnp
from jax import lax

NZ = 256
LEVELS = 3
TABLE = 16
NX = 256
NY = 512


def set_ends(array, key, smallest, top_value):
    index_at = [jax.random.randint(jax.random.fold_in(key, axis), (), 0, length) for axis, length in enumerate(array.shape)]
    longest = array.shape.index(max(array.shape))
    neighbour = index_at[:longest] + [(index_at[longest] + 1) % array.shape[longest]] + index_at[longest + 1:]
    return array.at[tuple(index_at)].set(smallest).at[tuple(neighbour)].set(top_value)


def levels(rng, shape, pieces, least, high):
    loudness = 1.0
    for dim, parts in pieces:
        steps = jax.random.uniform(jax.random.fold_in(jax.random.fold_in(rng, 6), dim), (parts,), jnp.float32, least / len(pieces), high / len(pieces))
        loudness = loudness * jnp.repeat(jnp.exp(steps), shape[dim] // parts).reshape((-1,) + (1,) * (len(shape) - 1 - dim))
    return loudness


def scatter_about(rng, dims, scale, reach, cuts=(), kind=jnp.bfloat16):
    entries = scale * jax.random.normal(rng, dims, jnp.float32)
    if cuts:
        entries = entries * levels(rng, dims, cuts, -0.22, 0.18)
    return jnp.clip(entries, -reach, reach).astype(kind)


def setup_inputs(seed: int = 0) -> dict:
    seeds = jax.random.split(jax.random.key(seed), 4)
    velocity = scatter_about(seeds[0], (NX, NY, NZ), 1.0, 6.0, ((0, 8), (1, 4)), jnp.float32)
    threshold_table = jnp.clip(jnp.exp(jax.random.uniform(seeds[1], (TABLE,), jnp.float32, math.log(0.05), math.log(1.5))), 0.05, 1.5)
    band_index = set_ends(jax.random.randint(seeds[2], (LEVELS, 7), 0, TABLE), jax.random.fold_in(seeds[2], 1), 0, TABLE - 1).astype(jnp.int32)
    return {"velocity": velocity, "threshold_table": threshold_table, "band_index": band_index}


filt_low = [0.23037781330885523, 0.7148465705525415, 0.6308807679295904, -0.02798376941698385,
            -0.18703481171888114, 0.030841381835986965, 0.032883011666982945, -0.010597401784997278]
filt_high = [((-1.0) ** j) * filt_low[7 - j] for j in range(8)]


def wrapped(field, dim, width):
    size = field.shape[dim]
    left = lax.slice_in_dim(field, size - width, size, 1, dim)
    right = lax.slice_in_dim(field, 0, width, 1, dim)
    return jnp.concatenate([left, field, right], axis=dim)


def analyse(extended, dim):
    count = extended.shape[dim] - 6
    low = 0.0
    high = 0.0
    for j in range(8):
        taken = lax.slice_in_dim(extended, j, j + count - 1, 2, dim)
        low = low + filt_low[j] * taken
        high = high + filt_high[j] * taken
    return low, high


def synthesise(low_ext, high_ext, dim):
    half = low_ext.shape[dim] - 4
    even = 0.0
    odd = 0.0
    for j in range(8):
        if j % 2 == 1:
            start = (3 - j) // 2 + 2
        else:
            start = (4 - j) // 2 + 2
        term = filt_low[j] * lax.slice_in_dim(low_ext, start, start + half, 1, dim) + filt_high[j] * lax.slice_in_dim(high_ext, start, start + half, 1, dim)
        if j % 2 == 1:
            even = even + term
        else:
            odd = odd + term
    joined = jnp.stack([even, odd], axis=dim + 1)
    shape = list(even.shape)
    shape[dim] = 2 * half
    return joined.reshape(shape)


def depth_and_bands(ybands):
    zlow, zhigh = analyse(wrapped(ybands, 4, 3), 4)
    stacked = jnp.stack([zlow, zhigh], axis=2)
    return stacked.reshape((8,) + zlow.shape[2:])


def depth_synth(bands):
    split = bands.reshape((2, 2, 2) + bands.shape[1:])
    return synthesise(wrapped(split[:, :, 0], 4, 2), wrapped(split[:, :, 1], 4, 2), 4)


def shrink(bands, table, indices):
    match = indices[:, None] == jnp.arange(table.shape[0], dtype=jnp.int32)[None, :]
    thresh = jnp.sum(jnp.where(match, table[None, :], 0.0), axis=1)
    thresh = thresh[:, None, None, None]
    return jnp.sign(bands) * jnp.maximum(jnp.abs(bands) - thresh, 0.0)


def reference(velocity, threshold_table, band_index):
    approx = velocity
    details = []
    for level in range(LEVELS):
        low, high = analyse(wrapped(approx, 0, 3), 0)
        stacked = jnp.stack([low, high])
        ylow, yhigh = analyse(wrapped(stacked, 2, 3), 2)
        bands = depth_and_bands(jnp.stack([ylow, yhigh], axis=1))
        details.append(shrink(bands[1:], threshold_table, band_index[level]))
        approx = bands[0]
    recon = approx
    for level in range(LEVELS - 1, -1, -1):
        bands = jnp.concatenate([recon[None], details[level]], axis=0)
        yzpart = depth_synth(bands)
        extended = wrapped(yzpart, 3, 2)
        ypart = synthesise(extended[:, 0], extended[:, 1], 2)
        extended = wrapped(ypart, 1, 2)
        recon = synthesise(extended[0], extended[1], 0)
    return recon
```

```python
import functools

import jax
import jax.numpy as jnp
import ml_dtypes
import numpy as np
from jax import lax
from jax.experimental import pallas as pl
from jax.experimental.pallas import tpu as pltpu
from jax.sharding import PartitionSpec as P

H = [
    0.23037781330885523,
    0.7148465705525415,
    0.6308807679295904,
    -0.02798376941698385,
    -0.18703481171888114,
    0.030841381835986965,
    0.032883011666982945,
    -0.010597401784997278,
]
G = [(-1.0) ** j * H[7 - j] for j in range(8)]
F32 = jnp.float32
BF16 = jnp.bfloat16
NOTHING = 3.0e38
VMEM_BYTES = 56 * 1024 * 1024


def tap(filt, j):
    return filt[j] if 0 <= j < 8 else 0.0


def analysis_rows(cells, ks):
    matrix = np.zeros((2 * len(ks), len(cells)))
    for row, k in enumerate(ks):
        for col, cell in enumerate(cells):
            if k is not None and cell is not None:
                matrix[row, col] = tap(H, cell - 2 * k + 3)
                matrix[len(ks) + row, col] = tap(G, cell - 2 * k + 3)
    return matrix


def synthesis_rows(cells, ks):
    return analysis_rows(cells, ks).T


def periodic(length, padded_to):
    matrix = np.zeros((padded_to, padded_to))
    for k in range(length // 2):
        for j in range(8):
            matrix[(2 * k + j - 3) % length, k] += H[j]
            matrix[(2 * k + j - 3) % length, length // 2 + k] += G[j]
    return matrix


def fill(items, length):
    return items + [None] * (length - len(items))


def up_to(count, step):
    return -(-count // step) * step


def pieces(matrix):
    rows, cols = matrix.shape
    matrix = np.pad(matrix, ((0, up_to(rows, 16) - rows), (0, up_to(cols, 16) - cols))).astype(np.float32)
    high = matrix.astype(ml_dtypes.bfloat16)
    low = (matrix - high.astype(np.float32)).astype(ml_dtypes.bfloat16)
    return [high, low]


def halves(values):
    high = values.astype(BF16)
    return high, (values - high.astype(F32)).astype(BF16)


def dot(left, right):
    return jnp.dot(left, right, preferred_element_type=F32)


def times(values, matrix):
    high, low = halves(values)
    return dot(high, matrix[0][...]) + (dot(low, matrix[0][...]) + dot(high, matrix[1][...]))


def left_times(matrix, values):
    missing = matrix[0].shape[1] - values.shape[0]
    if missing:
        values = jnp.concatenate([values, jnp.zeros((missing, values.shape[1]), F32)], axis=0)
    high, low = halves(values)
    return dot(matrix[0][...], high) + (dot(matrix[0][...], low) + dot(matrix[1][...], high))


def added(terms):
    total = None
    for coef, value in terms:
        part = value if coef == 1.0 else coef * value
        total = part if total is None else total + part
    return total


def x_terms(k, n):
    terms = []
    for j in range(8):
        cell = 2 * k + j - 3
        if 0 <= cell < n:
            terms.append((cell, H[j], G[j]))
        elif cell == -1:
            terms.append(("l1", H[j], G[j]))
        elif cell == n:
            terms.append(("r1", H[j], G[j]))
    if k == 0:
        terms.append(("l2", 1.0, G[0] / H[0]))
    if k == n // 2 - 1:
        terms.append(("r2", 1.0, G[6] / H[6]))
    return terms


def x_low(get, k, n):
    return added([(low, get(key)) for key, low, _ in x_terms(k, n)])


def x_high(get, k, n):
    return added([(high, get(key)) for key, _, high in x_terms(k, n)])


def x_synth(m, lows, highs):
    terms = [(H[m + 3 - 2 * k], v) for k, v in lows.items() if 0 <= m + 3 - 2 * k < 8]
    terms += [(G[m + 3 - 2 * k], v) for k, v in highs.items() if 0 <= m + 3 - 2 * k < 8]
    return added(terms)


def spill_up(low, high, n):
    first = added([(H[5], low[n - 1]), (G[5], high[n - 1]), (H[7], low[n - 2]), (G[7], high[n - 2])])
    return first, added([(H[6], low[n - 1]), (G[6], high[n - 1])])


def spill_down(low, high):
    first = added([(H[2], low[0]), (G[2], high[0]), (H[0], low[1]), (G[0], high[1])])
    return first, added([(H[1], low[0]), (G[1], high[0])])


THIRD_UP = H[7] / H[6]
THIRD_DOWN = H[0] / H[1]


def shrink(values, thresh):
    return values - jnp.minimum(jnp.maximum(values, -thresh), thresh)


def call(kernel, grid, in_specs, out_specs, out_shapes, args, flops, moved, scratch=(), name=None):
    return pl.pallas_call(
        kernel,
        grid=grid,
        in_specs=in_specs,
        out_specs=out_specs,
        out_shape=out_shapes,
        scratch_shapes=list(scratch),
        name=name,
        cost_estimate=pl.CostEstimate(flops=int(flops), bytes_accessed=int(moved), transcendentals=0),
        compiler_params=pltpu.CompilerParams(vmem_limit_bytes=VMEM_BYTES),
    )(*args)


def shape(*dims):
    return jax.ShapeDtypeStruct(dims, F32)


def whole(array):
    dims = array.shape
    return pl.BlockSpec(dims, lambda *_: (0,) * len(dims))


def whole_out(*dims):
    return pl.BlockSpec(dims, lambda *_: (0,) * len(dims))


SMEM = pl.BlockSpec(memory_space=pltpu.SMEM)


def x_messages(last, first, up, down):
    up[0] = last[3]
    up[1] = H[0] * last[1] + H[1] * last[2]
    down[0] = first[0]
    down[1] = H[6] * first[1] + H[7] * first[2]


def first_messages(v):
    nx, ny, nz = v.shape

    def kernel(last, first, y_last, y_first, up, down, y_up, y_down):
        x_messages(last, first, up, down)
        y_up[...] = y_last[...]
        y_down[...] = y_first[...]

    return call(
        kernel,
        (1,),
        [
            pl.BlockSpec((4, ny, nz), lambda i: (nx // 4 - 1, 0, 0)),
            pl.BlockSpec((4, ny, nz), lambda i: (0, 0, 0)),
            pl.BlockSpec((nx, 8, nz), lambda i: (0, ny // 8 - 1, 0)),
            pl.BlockSpec((nx, 8, nz), lambda i: (0, 0, 0)),
        ],
        [whole_out(2, ny, nz)] * 2 + [whole_out(nx, 8, nz)] * 2,
        [shape(2, ny, nz)] * 2 + [shape(nx, 8, nz)] * 2,
        [v] * 4,
        1e6,
        3e6,
        name="first_messages",
    )


def corner_messages(y_left, y_right):
    nx, rows, nz = y_left.shape

    def kernel(last_l, first_l, last_r, first_r, up, down):
        for part, last, first in ((0, last_l, first_l), (1, last_r, first_r)):
            at = pl.ds(8 * part, 8)
            up[0, at] = last[3]
            up[1, at] = H[0] * last[1] + H[1] * last[2]
            down[0, at] = first[0]
            down[1, at] = H[6] * first[1] + H[7] * first[2]

    last = pl.BlockSpec((4, rows, nz), lambda i: (nx // 4 - 1, 0, 0))
    first = pl.BlockSpec((4, rows, nz), lambda i: (0, 0, 0))
    return call(
        kernel,
        (1,),
        [last, first, last, first],
        [whole_out(2, 16, nz)] * 2,
        [shape(2, 16, nz)] * 2,
        [y_left, y_left, y_right, y_right],
        1e5,
        2e5,
        name="corner_messages",
    )


def depth_analysis(v, z_matrix):
    nx, ny, nz = v.shape

    def kernel(v_ref, z0, z1, out):
        out[...] = times(v_ref[...].reshape(4 * ny, nz), (z0, z1)).reshape(4, ny, nz)

    block = pl.BlockSpec((4, ny, nz), lambda i: (i, 0, 0))
    return call(
        kernel,
        (nx // 4,),
        [block, whole(z_matrix[0]), whole(z_matrix[1])],
        block,
        shape(nx, ny, nz),
        [v, *z_matrix],
        6 * nx * ny * nz * nz,
        8 * nx * ny * nz,
        name="depth_analysis",
    )


def y_analysis(zed, y_left, y_right, z_matrix, y_matrix):
    nx, ny, nz = zed.shape
    rows = y_matrix[0].shape[0]

    def kernel(zed_ref, left, right, z0, z1, y0, y1, out):
        sides = jnp.concatenate([left[...].reshape(32, nz), right[...].reshape(32, nz)], axis=0)
        sides = times(sides, (z0, z1))
        for i in range(4):
            plane = jnp.concatenate(
                [sides[8 * i : 8 * i + 8], zed_ref[i], sides[32 + 8 * i : 40 + 8 * i]], axis=0
            )
            out[i] = left_times((y0, y1), plane)

    return call(
        kernel,
        (nx // 4,),
        [
            pl.BlockSpec((4, ny, nz), lambda i: (i, 0, 0)),
            pl.BlockSpec((4, 8, nz), lambda i: (i, 0, 0)),
            pl.BlockSpec((4, 8, nz), lambda i: (i, 0, 0)),
        ]
        + [whole(m) for m in z_matrix + y_matrix],
        pl.BlockSpec((4, rows, nz), lambda i: (i, 0, 0)),
        shape(nx, rows, nz),
        [zed, y_left, y_right, *z_matrix, *y_matrix],
        6 * nx * rows * (ny + 16) * nz,
        4 * nx * nz * (ny + rows + 16),
        name="y_analysis",
    )


def first_approx(bands, x_left, x_right, c_left, c_right, z_matrix, y_matrix, own, ghost_rows):
    nx, rows, nz = bands.shape
    ny = x_left.shape[1]
    half_rows = rows // 2
    half_z = nz // 2
    n1 = nx // 2

    def kernel(b_ref, xl, xr, cl, cr, z0, z1, y0, y1, halo, approx, up, down):
        for side, (main, corner) in enumerate(((xl, cl), (xr, cr))):
            for i in range(2):
                plane = jnp.concatenate([corner[i, :8], main[i], corner[i, 8:]], axis=0)
                halo[2 * side + i] = left_times((y0, y1), times(plane, (z0, z1)))
        place = {"l1": 0, "l2": 1, "r1": 2, "r2": 3}

        def tile(t, carry):
            at = pl.ds(pl.multiple_of(t * 8, 8), 8)

            def get(key):
                if isinstance(key, str):
                    return halo[place[key], at, :half_z]
                return b_ref[key, at]

            for k in range(n1):
                approx[k, at] = x_low(get, k, nx)
            return carry

        lax.fori_loop(0, own // 8, tile, 0)
        up[...] = approx[:, own - ghost_rows :]
        down[...] = approx[:, :ghost_rows]

    return call(
        kernel,
        (1,),
        [pl.BlockSpec((nx, half_rows, half_z), lambda i: (0, 0, 0))]
        + [whole(a) for a in (x_left, x_right, c_left, c_right, *z_matrix, *y_matrix)],
        [
            whole_out(4, rows, nz),
            whole_out(n1, own, half_z),
            whole_out(n1, ghost_rows, half_z),
            whole_out(n1, ghost_rows, half_z),
        ],
        [
            shape(4, rows, nz),
            shape(n1, own, half_z),
            shape(n1, ghost_rows, half_z),
            shape(n1, ghost_rows, half_z),
        ],
        [bands, x_left, x_right, c_left, c_right, *z_matrix, *y_matrix],
        24 * rows * (ny + 16) * nz + 24 * (ny + 16) * nz * nz,
        6e6,
        name="first_approx",
    )


def detail_bands(bands, halo, table, index):
    nx, rows, nz = bands.shape
    n1 = nx // 2
    step_rows = 24 if (rows // 2) % 24 == 0 else 8
    steps = rows // step_rows
    half_z = nz // 2

    def kernel(table_ref, index_ref, b_ref, h_ref, out):
        by = (pl.program_id(0) >= steps // 2).astype(jnp.int32)
        place = {"l1": 0, "l2": 1, "r1": 2, "r2": 3}
        limits = {}
        for bx in range(2):
            for bz in range(2):
                band = 4 * bx + 2 * by + bz
                found = table_ref[index_ref[0, jnp.maximum(band - 1, 0)]]
                limits[bx, bz] = jnp.where(band == 0, NOTHING, found)

        def tile(t, carry):
            at = pl.ds(pl.multiple_of(t * 8, 8), 8)
            for bz in range(2):
                lanes = pl.ds(bz * half_z, half_z)

                def get(key):
                    if isinstance(key, str):
                        return h_ref[place[key], at, lanes]
                    return b_ref[key, at, lanes]

                for k in range(n1):
                    out[k, at, lanes] = shrink(x_low(get, k, nx), limits[0, bz])
                    out[n1 + k, at, lanes] = shrink(x_high(get, k, nx), limits[1, bz])
            return carry

        lax.fori_loop(0, step_rows // 8, tile, 0)

    block = pl.BlockSpec((nx, step_rows, nz), lambda i: (0, i, 0))
    return call(
        kernel,
        (steps,),
        [SMEM, SMEM, block, pl.BlockSpec((4, step_rows, nz), lambda i: (0, i, 0))],
        block,
        shape(nx, rows, nz),
        [table, index, bands, halo],
        40 * nx * rows * nz,
        8 * nx * rows * nz,
        name="detail_bands",
    )


def detail_yz(coeffs, z_matrix, y_matrix):
    nx, rows, nz = coeffs.shape
    ny = y_matrix[0].shape[0]
    blocks = nx // 8

    def kernel(c_ref, z0, z1, y0, y1, out, up, down):
        step = pl.program_id(0)
        zed = times(c_ref[...].reshape(4 * rows, nz), (z0, z1))
        for i in range(4):
            out[i] = left_times((y0, y1), zed[i * rows : (i + 1) * rows])

        @pl.when(step == 0)
        def _():
            down[0] = H[2] * out[0] + H[0] * out[1]
            down[1] = H[1] * out[0]

        @pl.when(step == blocks)
        def _():
            down[0] += G[2] * out[0] + G[0] * out[1]
            down[1] += G[1] * out[0]

        @pl.when(step == blocks - 1)
        def _():
            up[0] = H[5] * out[3] + H[7] * out[2]
            up[1] = H[6] * out[3]

        @pl.when(step == 2 * blocks - 1)
        def _():
            up[0] += G[5] * out[3] + G[7] * out[2]
            up[1] += G[6] * out[3]

    return call(
        kernel,
        (2 * blocks,),
        [pl.BlockSpec((4, rows, nz), lambda i: (i, 0, 0))] + [whole(m) for m in z_matrix + y_matrix],
        [pl.BlockSpec((4, ny, nz), lambda i: (i, 0, 0)), whole_out(2, ny, nz), whole_out(2, ny, nz)],
        [shape(nx, ny, nz), shape(2, ny, nz), shape(2, ny, nz)],
        [coeffs, *z_matrix, *y_matrix],
        6 * nx * rows * nz * nz + 6 * nx * rows * ny * nz,
        4 * nx * nz * (rows + ny),
        name="detail_yz",
    )


def detail_x(parts):
    nx, ny, nz = parts.shape
    n1 = nx // 2
    step_rows = 16

    def kernel(p_ref, out):
        def tile(t, carry):
            at = pl.ds(pl.multiple_of(t * 8, 8), 8)
            for lane in range(0, nz, 128):
                lanes = pl.ds(lane, 128)
                for m in range(nx):
                    ks = [k for k in range(n1) if 0 <= m + 3 - 2 * k < 8]
                    lows = {k: p_ref[k, at, lanes] for k in ks}
                    highs = {k: p_ref[n1 + k, at, lanes] for k in ks}
                    out[m, at, lanes] = x_synth(m, lows, highs)
            return carry

        lax.fori_loop(0, step_rows // 8, tile, 0)

    block = pl.BlockSpec((nx, step_rows, nz), lambda i: (0, i, 0))
    return call(
        kernel,
        (ny // step_rows,),
        [block],
        block,
        shape(nx, ny, nz),
        [parts],
        16 * nx * ny * nz,
        8 * nx * ny * nz,
        name="detail_x",
    )


def second_bands(own, left, right, z_matrix, y_matrix, low_rows):
    n1, own_rows, nz = own.shape
    ghost_rows = left.shape[1]
    in_rows = own_rows + 2 * ghost_rows
    rows = 2 * low_rows
    lane_half = nz // 2

    def kernel(o_ref, l_ref, r_ref, z0, z1, y0, y1, out, up, down):
        for i in range(0, n1, 4):
            stack = jnp.concatenate(
                [part[j] for j in range(i, i + 4) for part in (o_ref, l_ref, r_ref)], axis=0
            )
            zed = times(stack, (z0, z1))
            for j in range(4):
                out[i + j] = left_times((y0, y1), zed[j * in_rows : (j + 1) * in_rows])
        low = lambda c: out[c, :low_rows]
        up[0:rows] = out[n1 - 1]
        up[rows : 2 * rows] = H[0] * out[n1 - 3] + H[1] * out[n1 - 2]
        first = added([(H[j], low(n1 - 5 + j)) for j in range(5)])
        second = added([(H[0] * H[j], low(n1 - 9 + j)) for j in range(8)])
        second += added([(H[1] * H[j], low(n1 - 7 + j)) for j in range(7)])
        lane = lax.broadcasted_iota(jnp.int32, first.shape, 1)
        up[2 * rows :] = jnp.where(lane < lane_half, first, pltpu.roll(second, lane_half, 1))
        down[0:rows] = out[0]
        down[rows : 2 * rows] = H[6] * out[1] + H[7] * out[2]
        first = added([(H[j], low(j - 3)) for j in range(3, 8)])
        second = added([(H[6] * H[j], low(j - 1)) for j in range(1, 8)])
        second += added([(H[7] * H[j], low(j + 1)) for j in range(8)])
        down[2 * rows :] = jnp.where(lane < lane_half, first, pltpu.roll(second, lane_half, 1))

    message = 2 * rows + low_rows
    return call(
        kernel,
        (1,),
        [whole(a) for a in (own, left, right, *z_matrix, *y_matrix)],
        [whole_out(n1, rows, nz), whole_out(message, nz), whole_out(message, nz)],
        [shape(n1, rows, nz), shape(message, nz), shape(message, nz)],
        [own, left, right, *z_matrix, *y_matrix],
        6 * n1 * in_rows * nz * (nz + rows),
        4 * n1 * nz * (in_rows + rows),
        name="second_bands",
    )


def limits_plane(table_ref, index_ref, level, bx, dims, row_split, lane_split, zeroth):
    row_high = lax.broadcasted_iota(jnp.int32, dims, 0) >= row_split
    lane_high = lax.broadcasted_iota(jnp.int32, dims, 1) >= lane_split

    def limit(by, bz):
        band = 4 * bx + 2 * by + bz
        return zeroth if band == 0 else table_ref[index_ref[level, band - 1]]

    low_y = jnp.where(lane_high, limit(0, 1), limit(0, 0))
    return jnp.where(row_high, jnp.where(lane_high, limit(1, 1), limit(1, 0)), low_y)


def coarse(bands, left, right, table, index, z1_mats, z2_mats, ya2, ys2, ys1, low_rows, z1_len):
    n1, rows, nz = bands.shape
    n2, n3 = n1 // 2, n1 // 4
    rows2 = ya2[0].shape[0]
    out_rows = up_to(ys1[0].shape[0], 8)
    out_rows = ys1[2]
    mats = [*z1_mats, *z2_mats, *ya2[:2], *ys2[:2], *ys1[:2]]
    lane_half = z1_len // 2

    def kernel(table_ref, index_ref, b_ref, l_ref, r_ref, *refs):
        z1s, z2a, z2s, a2, s2, s1 = [refs[2 * i : 2 * i + 2] for i in range(6)]
        approx, up, down, c1, p1 = refs[12:]
        sides = {
            "l1": lambda: l_ref[0:rows],
            "l2": lambda: l_ref[rows : 2 * rows],
            "r1": lambda: r_ref[0:rows],
            "r2": lambda: r_ref[rows : 2 * rows],
        }
        get = lambda key: sides[key]() if isinstance(key, str) else b_ref[key]
        lowpart = lambda c: b_ref[c, :low_rows]
        dims = (rows, nz)
        quiet = limits_plane(table_ref, index_ref, 1, 0, dims, low_rows, lane_half, NOTHING)
        loud = limits_plane(table_ref, index_ref, 1, 1, dims, low_rows, lane_half, NOTHING)
        planes = []
        for k in range(n2):
            low = x_low(get, k, n1)
            planes.append(low[:low_rows])
            c1[k] = shrink(low, quiet)
            c1[n2 + k] = shrink(x_high(get, k, n1), loud)
        packed = l_ref[2 * rows :]
        planes.append(packed + added([(H[5 + i], lowpart(i)) for i in range(3)]))
        planes.append(pltpu.roll(packed, lane_half, 1) + H[1] * H[7] * lowpart(0))
        packed = r_ref[2 * rows :]
        planes.append(packed + added([(H[i], lowpart(n1 - 3 + i)) for i in range(3)]))
        planes.append(pltpu.roll(packed, lane_half, 1) + H[6] * H[0] * lowpart(n1 - 1))
        zed = times(jnp.concatenate(planes, axis=0), z2a)
        third = [left_times(a2, zed[i * low_rows : (i + 1) * low_rows]) for i in range(len(planes))]
        keys = {"l1": n2, "l2": n2 + 1, "r1": n2 + 2, "r2": n2 + 3}
        get2 = lambda key: third[keys.get(key, key)]
        dims = (rows2, nz)
        quiet = limits_plane(table_ref, index_ref, 2, 0, dims, rows2 // 2, lane_half // 2, 0.0)
        loud = limits_plane(table_ref, index_ref, 2, 1, dims, rows2 // 2, lane_half // 2, 0.0)
        kept = [shrink(x_low(get2, k, n2), quiet) for k in range(n3)]
        kept += [shrink(x_high(get2, k, n2), loud) for k in range(n3)]
        zed = times(jnp.concatenate(kept, axis=0), z2s)
        parts = [left_times(s2, zed[i * rows2 : (i + 1) * rows2])[:low_rows] for i in range(2 * n3)]
        lows = dict(enumerate(parts[:n3]))
        highs = dict(enumerate(parts[n3:]))
        ghosts = [-3, -2, -1, n2, n2 + 1, n2 + 2]
        for k in range(n2):
            c1[k, :low_rows] += x_synth(k, lows, highs)
        stack = [x_synth(k, lows, highs) for k in ghosts]
        pad = jnp.zeros((rows - low_rows, nz), F32)
        stack_zed = times(jnp.concatenate(stack, axis=0), z1s)
        for i in range(6):
            plane = jnp.concatenate([stack_zed[i * low_rows : (i + 1) * low_rows], pad], axis=0)
            p1[2 * n2 + i] = left_times(s1, plane)[:out_rows]
        for i in range(0, 2 * n2, 4):
            zed = times(c1[i : i + 4].reshape(4 * rows, nz), z1s)
            for j in range(4):
                p1[i + j] = left_times(s1, zed[j * rows : (j + 1) * rows])[:out_rows]
        lows = {k: p1.at[k] for k in range(n2)}
        highs = {k: p1.at[n2 + k] for k in range(n2)}
        for i, k in enumerate(ghosts):
            lows[k] = p1.at[2 * n2 + i]

        def cell(m):
            near = lambda part: {k: ref[...] for k, ref in part.items() if 0 <= m + 3 - 2 * k < 8}
            return x_synth(m, near(lows), near(highs))

        for m in range(-2, n1 + 2):
            approx[m + 2] = cell(m)
        value = lambda part, ks: {k: part[k][...] for k in ks}
        ends = (n2 - 2, n2 - 1)
        up[0], up[1] = approx[n1], approx[n1 + 1]
        up[2], up[3] = spill_up(value(lows, ends), value(highs, ends), n2)
        up[4], up[5] = lows[n2][...], lows[n2 + 1][...]
        down[0], down[1] = approx[2], approx[3]
        down[2], down[3] = spill_down(value(lows, (0, 1)), value(highs, (0, 1)))
        down[4], down[5] = lows[-1][...], lows[-2][...]

    return call(
        kernel,
        (1,),
        [SMEM, SMEM] + [whole(a) for a in (bands, left, right, *mats)],
        [whole_out(n1 + 4, out_rows, nz), whole_out(6, out_rows, nz), whole_out(6, out_rows, nz)],
        [shape(n1 + 4, out_rows, nz), shape(6, out_rows, nz), shape(6, out_rows, nz)],
        [table, index, bands, left, right, *mats],
        1.5e9,
        8 * n1 * rows * nz,
        scratch=[pltpu.VMEM((2 * n2, rows, nz), F32), pltpu.VMEM((2 * n2 + 6, out_rows, nz), F32)],
        name="coarse",
    )


def final(approx, left, right, detail, e_left, e_right, z_matrix, y_matrix):
    planes, rows, half_z = approx.shape
    nx, ny, nz = detail.shape
    n1 = nx // 2
    n2 = n1 // 2
    step_rows = 16

    def kernel(a_ref, l_ref, r_ref, d_ref, el, er, z0, z1, y0, y1, out, total, parts):
        @pl.when(pl.program_id(0) == 0)
        def _():
            for m in range(n1):
                terms = [(1.0, a_ref[m + 2])]
                for k, coef, source in ((0, 1.0, 4), (1, 1.0, 5), (2, THIRD_UP, 5)):
                    if 0 <= m + 3 - 2 * k < 8:
                        terms.append((coef * H[m + 3 - 2 * k], l_ref[source]))
                for k, coef, source in ((n2 - 1, 1.0, 4), (n2 - 2, 1.0, 5), (n2 - 3, THIRD_DOWN, 5)):
                    if 0 <= m + 3 - 2 * k < 8:
                        terms.append((coef * H[m + 3 - 2 * k], r_ref[source]))
                if m < 3:
                    terms.append(((1.0, 1.0, THIRD_UP)[m], l_ref[(2, 3, 3)[m]]))
                if m >= n1 - 3:
                    terms.append(((1.0, 1.0, THIRD_DOWN)[n1 - 1 - m], r_ref[(2, 3, 3)[n1 - 1 - m]]))
                total[m + 2] = added(terms)
            total[0] = a_ref[0] + l_ref[0]
            total[1] = a_ref[1] + l_ref[1]
            total[n1 + 2] = a_ref[n1 + 2] + r_ref[0]
            total[n1 + 3] = a_ref[n1 + 3] + r_ref[1]
            for i in range(0, planes, 4):
                zed = times(total[i : i + 4].reshape(4 * rows, half_z), (z0, z1))
                for j in range(4):
                    parts[i + j] = left_times((y0, y1), zed[j * rows : (j + 1) * rows])

        start = pl.program_id(0) * step_rows

        def tile(t, carry):
            at = pl.ds(pl.multiple_of(t * 8, 8), 8)
            within = pl.ds(pl.multiple_of(start + t * 8, 8), 8)
            for lane in range(0, nz, 128):
                lanes = pl.ds(lane, 128)
                for m in range(nx):
                    ks = [k for k in range(-2, n1 + 2) if 0 <= m + 3 - 2 * k < 8]
                    value = d_ref[m, at, lanes] + x_synth(m, {k: parts[k + 2, within, lanes] for k in ks}, {})
                    if m < 3:
                        extra = el[(0, 1, 1)[m], at, lanes]
                        value += extra if m < 2 else THIRD_UP * extra
                    if m >= nx - 3:
                        extra = er[(0, 1, 1)[nx - 1 - m], at, lanes]
                        value += extra if m > nx - 3 else THIRD_DOWN * extra
                    out[m, at, lanes] = value
            return carry

        lax.fori_loop(0, step_rows // 8, tile, 0)

    block = pl.BlockSpec((nx, step_rows, nz), lambda i: (0, i, 0))
    side = pl.BlockSpec((2, step_rows, nz), lambda i: (0, i, 0))
    return call(
        kernel,
        (ny // step_rows,),
        [whole(approx), whole(left), whole(right), block, side, side]
        + [whole(m) for m in z_matrix + y_matrix],
        block,
        shape(nx, ny, nz),
        [approx, left, right, detail, e_left, e_right, *z_matrix, *y_matrix],
        8 * nx * ny * nz,
        8 * nx * ny * nz,
        scratch=[pltpu.VMEM((planes, rows, half_z), F32), pltpu.VMEM((planes, ny, nz), F32)],
        name="final",
    )


def to_next(array, axis):
    size = lax.axis_size(axis)
    return lax.ppermute(array, axis, [(i, (i + 1) % size) for i in range(size)])


def to_previous(array, axis):
    size = lax.axis_size(axis)
    return lax.ppermute(array, axis, [((i + 1) % size, i) for i in range(size)])


def local(velocity, table, index):
    nx, ny, nz = velocity.shape
    y1, y2, y3 = ny // 2, ny // 4, ny // 8
    ghost = 24
    cells0 = list(range(-8, ny + 8))
    rows0 = up_to(y1 + 4, 8)
    ks0 = fill(list(range(y1)) + [-2, -1, y1, y1 + 1], rows0)
    cells1 = list(range(y1)) + list(range(-ghost, 0)) + list(range(y1, y1 + ghost))
    rows1 = up_to(y2 + 18, 8)
    ks1 = fill(list(range(-9, y2 + 9)), rows1)
    rows2 = up_to(y3 + 6, 8)
    ks2 = fill(list(range(-3, y3 + 3)), rows2)
    ya0 = pieces(analysis_rows(cells0, ks0))
    ys0_matrix = synthesis_rows(list(range(ny)), ks0)
    ys0 = pieces(ys0_matrix)
    ys0_low = pieces(ys0_matrix[:, :rows0])
    ya1 = pieces(analysis_rows(cells1, ks1))
    ys1 = pieces(synthesis_rows(ks0, ks1)) + [rows0]
    ya2 = pieces(analysis_rows(ks1, ks2))
    ys2 = pieces(synthesis_rows(ks1, ks2))
    z0 = periodic(nz, nz)
    z1 = periodic(nz // 2, nz // 2)
    z2 = periodic(nz // 4, nz // 2)
    za0, zs0, zs0_low = pieces(z0), pieces(z0.T), pieces(z0.T[: nz // 2])
    za1, zs1 = pieces(z1), pieces(z1.T)
    za2, zs2 = pieces(z2), pieces(z2.T)

    x_up, x_down, y_up, y_down = first_messages(velocity)
    x_left = to_next(x_up, "gx")
    x_right = to_previous(x_down, "gx")
    y_left = to_next(y_up, "gy")
    y_right = to_previous(y_down, "gy")
    zed = depth_analysis(velocity, za0)
    c_up, c_down = corner_messages(y_left, y_right)
    c_left = to_next(c_up, "gx")
    c_right = to_previous(c_down, "gx")
    bands = y_analysis(zed, y_left, y_right, za0, ya0)
    halo, approx, a_up, a_down = first_approx(
        bands, x_left, x_right, c_left, c_right, za0, ya0, y1, ghost
    )
    a_left = to_next(a_up, "gy")
    a_right = to_previous(a_down, "gy")
    coeffs = detail_bands(bands, halo, table, index)
    bands1, b_up, b_down = second_bands(approx, a_left, a_right, za1, ya1, rows1)
    b_left = to_next(b_up, "gx")
    b_right = to_previous(b_down, "gx")
    parts, e_up, e_down = detail_yz(coeffs, zs0, ys0)
    e_left = to_next(e_up, "gx")
    e_right = to_previous(e_down, "gx")
    approx1, s_up, s_down = coarse(
        bands1, b_left, b_right, table, index, zs1, za2 + zs2, ya2, ys2, ys1, rows1, nz // 2
    )
    s_left = to_next(s_up, "gx")
    s_right = to_previous(s_down, "gx")
    detail = detail_x(parts)
    return final(approx1, s_left, s_right, detail, e_left, e_right, zs0_low, ys0_low)


def solution(mesh):
    return jax.shard_map(
        local,
        mesh=mesh,
        in_specs=(P("gx", "gy", None), P(), P()),
        out_specs=P("gx", "gy", None),
        check_vma=False,
    )
```

```python
import functools

import jax
import jax.numpy as jnp
import ml_dtypes
import numpy as np
from jax import lax
from jax.experimental import pallas as pl
from jax.experimental.pallas import tpu as pltpu
from jax.sharding import PartitionSpec as P

H = [
    0.23037781330885523,
    0.7148465705525415,
    0.6308807679295904,
    -0.02798376941698385,
    -0.18703481171888114,
    0.030841381835986965,
    0.032883011666982945,
    -0.010597401784997278,
]
G = [(-1.0) ** j * H[7 - j] for j in range(8)]
F32 = jnp.float32
BF16 = jnp.bfloat16
NOTHING = 3.0e38
VMEM_BYTES = 16 * 1024 * 1024


def tap(filt, j):
    return filt[j] if 0 <= j < 8 else 0.0


def analysis_rows(cells, ks):
    matrix = np.zeros((2 * len(ks), len(cells)))
    for row, k in enumerate(ks):
        for col, cell in enumerate(cells):
            if k is not None and cell is not None:
                matrix[row, col] = tap(H, cell - 2 * k + 3)
                matrix[len(ks) + row, col] = tap(G, cell - 2 * k + 3)
    return matrix


def synthesis_rows(cells, ks):
    return analysis_rows(cells, ks).T


def periodic(length, padded_to):
    matrix = np.zeros((padded_to, padded_to))
    for k in range(length // 2):
        for j in range(8):
            matrix[(2 * k + j - 3) % length, k] += H[j]
            matrix[(2 * k + j - 3) % length, length // 2 + k] += G[j]
    return matrix


def fill(items, length):
    return items + [None] * (length - len(items))


def up_to(count, step):
    return -(-count // step) * step


def pieces(matrix):
    rows, cols = matrix.shape
    matrix = np.pad(matrix, ((0, up_to(rows, 16) - rows), (0, up_to(cols, 16) - cols))).astype(np.float32)
    high = matrix.astype(ml_dtypes.bfloat16)
    low = (matrix - high.astype(np.float32)).astype(ml_dtypes.bfloat16)
    return [high, low]


def halves(values):
    high = values.astype(BF16)
    return high, (values - high.astype(F32)).astype(BF16)


def dot(left, right):
    return jnp.dot(left, right, preferred_element_type=F32)


def times(values, matrix):
    high, low = halves(values)
    return dot(high, matrix[0][...]) + (dot(low, matrix[0][...]) + dot(high, matrix[1][...]))


def left_times(matrix, values):
    missing = matrix[0].shape[1] - values.shape[0]
    if missing:
        values = jnp.concatenate([values, jnp.zeros((missing, values.shape[1]), F32)], axis=0)
    high, low = halves(values)
    return dot(matrix[0][...], high) + (dot(matrix[0][...], low) + dot(matrix[1][...], high))


def added(terms):
    total = None
    for coef, value in terms:
        part = value if coef == 1.0 else coef * value
        total = part if total is None else total + part
    return total


def x_terms(k, n):
    terms = []
    for j in range(8):
        cell = 2 * k + j - 3
        if 0 <= cell < n:
            terms.append((cell, H[j], G[j]))
        elif cell == -1:
            terms.append(("l1", H[j], G[j]))
        elif cell == n:
            terms.append(("r1", H[j], G[j]))
    if k == 0:
        terms.append(("l2", 1.0, G[0] / H[0]))
    if k == n // 2 - 1:
        terms.append(("r2", 1.0, G[6] / H[6]))
    return terms


def x_low(get, k, n):
    return added([(low, get(key)) for key, low, _ in x_terms(k, n)])


def x_high(get, k, n):
    return added([(high, get(key)) for key, _, high in x_terms(k, n)])


def x_synth(m, lows, highs):
    terms = [(H[m + 3 - 2 * k], v) for k, v in lows.items() if 0 <= m + 3 - 2 * k < 8]
    terms += [(G[m + 3 - 2 * k], v) for k, v in highs.items() if 0 <= m + 3 - 2 * k < 8]
    return added(terms)


def spill_up(low, high, n):
    first = added([(H[5], low[n - 1]), (G[5], high[n - 1]), (H[7], low[n - 2]), (G[7], high[n - 2])])
    return first, added([(H[6], low[n - 1]), (G[6], high[n - 1])])


def spill_down(low, high):
    first = added([(H[2], low[0]), (G[2], high[0]), (H[0], low[1]), (G[0], high[1])])
    return first, added([(H[1], low[0]), (G[1], high[0])])


THIRD_UP = H[7] / H[6]
THIRD_DOWN = H[0] / H[1]


def shrink(values, thresh):
    return values - jnp.minimum(jnp.maximum(values, -thresh), thresh)


def call(kernel, grid, in_specs, out_specs, out_shapes, args, flops, moved, scratch=(), name=None):
    return pl.pallas_call(
        kernel,
        grid=grid,
        in_specs=in_specs,
        out_specs=out_specs,
        out_shape=out_shapes,
        scratch_shapes=list(scratch),
        name=name,
        cost_estimate=pl.CostEstimate(flops=int(flops), bytes_accessed=int(moved), transcendentals=0),
        compiler_params=pltpu.CompilerParams(vmem_limit_bytes=VMEM_BYTES),
    )(*args)


def shape(*dims):
    return jax.ShapeDtypeStruct(dims, F32)


def whole(array):
    dims = array.shape
    return pl.BlockSpec(dims, lambda *_: (0,) * len(dims))


def whole_out(*dims):
    return pl.BlockSpec(dims, lambda *_: (0,) * len(dims))


SMEM = pl.BlockSpec(memory_space=pltpu.SMEM)


def x_messages(last, first, up, down):
    up[0] = last[3]
    up[1] = H[0] * last[1] + H[1] * last[2]
    down[0] = first[0]
    down[1] = H[6] * first[1] + H[7] * first[2]


def first_messages(v):
    nx, ny, nz = v.shape

    def kernel(last, first, y_last, y_first, up, down, y_up, y_down):
        x_messages(last, first, up, down)
        y_up[...] = y_last[...]
        y_down[...] = y_first[...]

    return call(
        kernel,
        (1,),
        [
            pl.BlockSpec((4, ny, nz), lambda i: (nx // 4 - 1, 0, 0)),
            pl.BlockSpec((4, ny, nz), lambda i: (0, 0, 0)),
            pl.BlockSpec((nx, 8, nz), lambda i: (0, ny // 8 - 1, 0)),
            pl.BlockSpec((nx, 8, nz), lambda i: (0, 0, 0)),
        ],
        [whole_out(2, ny, nz)] * 2 + [whole_out(nx, 8, nz)] * 2,
        [shape(2, ny, nz)] * 2 + [shape(nx, 8, nz)] * 2,
        [v] * 4,
        1e6,
        3e6,
        name="first_messages",
    )


def corner_messages(y_left, y_right):
    nx, rows, nz = y_left.shape

    def kernel(last_l, first_l, last_r, first_r, up, down):
        for part, last, first in ((0, last_l, first_l), (1, last_r, first_r)):
            at = pl.ds(8 * part, 8)
            up[0, at] = last[3]
            up[1, at] = H[0] * last[1] + H[1] * last[2]
            down[0, at] = first[0]
            down[1, at] = H[6] * first[1] + H[7] * first[2]

    last = pl.BlockSpec((4, rows, nz), lambda i: (nx // 4 - 1, 0, 0))
    first = pl.BlockSpec((4, rows, nz), lambda i: (0, 0, 0))
    return call(
        kernel,
        (1,),
        [last, first, last, first],
        [whole_out(2, 16, nz)] * 2,
        [shape(2, 16, nz)] * 2,
        [y_left, y_left, y_right, y_right],
        1e5,
        2e5,
        name="corner_messages",
    )


def depth_analysis(v, z_matrix):
    nx, ny, nz = v.shape

    def kernel(v_ref, z0, z1, out):
        out[...] = times(v_ref[...].reshape(4 * ny, nz), (z0, z1)).reshape(4, ny, nz)

    block = pl.BlockSpec((4, ny, nz), lambda i: (i, 0, 0))
    return call(
        kernel,
        (nx // 4,),
        [block, whole(z_matrix[0]), whole(z_matrix[1])],
        block,
        shape(nx, ny, nz),
        [v, *z_matrix],
        6 * nx * ny * nz * nz,
        8 * nx * ny * nz,
        name="depth_analysis",
    )


def y_analysis(zed, y_left, y_right, z_matrix, y_matrix):
    nx, ny, nz = zed.shape
    rows = y_matrix[0].shape[0]

    def kernel(zed_ref, left, right, z0, z1, y0, y1, out):
        sides = jnp.concatenate([left[...].reshape(32, nz), right[...].reshape(32, nz)], axis=0)
        sides = times(sides, (z0, z1))
        for i in range(4):
            plane = jnp.concatenate(
                [sides[8 * i : 8 * i + 8], zed_ref[i], sides[32 + 8 * i : 40 + 8 * i]], axis=0
            )
            out[i] = left_times((y0, y1), plane)

    return call(
        kernel,
        (nx // 4,),
        [
            pl.BlockSpec((4, ny, nz), lambda i: (i, 0, 0)),
            pl.BlockSpec((4, 8, nz), lambda i: (i, 0, 0)),
            pl.BlockSpec((4, 8, nz), lambda i: (i, 0, 0)),
        ]
        + [whole(m) for m in z_matrix + y_matrix],
        pl.BlockSpec((4, rows, nz), lambda i: (i, 0, 0)),
        shape(nx, rows, nz),
        [zed, y_left, y_right, *z_matrix, *y_matrix],
        6 * nx * rows * (ny + 16) * nz,
        4 * nx * nz * (ny + rows + 16),
        name="y_analysis",
    )


def first_approx(bands, x_left, x_right, c_left, c_right, z_matrix, y_matrix, own, ghost_rows):
    nx, rows, nz = bands.shape
    ny = x_left.shape[1]
    half_rows = rows // 2
    half_z = nz // 2
    n1 = nx // 2

    def kernel(b_ref, xl, xr, cl, cr, z0, z1, y0, y1, halo, approx, up, down):
        for side, (main, corner) in enumerate(((xl, cl), (xr, cr))):
            for i in range(2):
                plane = jnp.concatenate([corner[i, :8], main[i], corner[i, 8:]], axis=0)
                halo[2 * side + i] = left_times((y0, y1), times(plane, (z0, z1)))
        place = {"l1": 0, "l2": 1, "r1": 2, "r2": 3}

        def tile(t, carry):
            at = pl.ds(pl.multiple_of(t * 8, 8), 8)

            def get(key):
                if isinstance(key, str):
                    return halo[place[key], at, :half_z]
                return b_ref[key, at]

            for k in range(n1):
                approx[k, at] = x_low(get, k, nx)
            return carry

        lax.fori_loop(0, own // 8, tile, 0)
        up[...] = approx[:, own - ghost_rows :]
        down[...] = approx[:, :ghost_rows]

    return call(
        kernel,
        (1,),
        [pl.BlockSpec((nx, half_rows, half_z), lambda i: (0, 0, 0))]
        + [whole(a) for a in (x_left, x_right, c_left, c_right, *z_matrix, *y_matrix)],
        [
            whole_out(4, rows, nz),
            whole_out(n1, own, half_z),
            whole_out(n1, ghost_rows, half_z),
            whole_out(n1, ghost_rows, half_z),
        ],
        [
            shape(4, rows, nz),
            shape(n1, own, half_z),
            shape(n1, ghost_rows, half_z),
            shape(n1, ghost_rows, half_z),
        ],
        [bands, x_left, x_right, c_left, c_right, *z_matrix, *y_matrix],
        24 * rows * (ny + 16) * nz + 24 * (ny + 16) * nz * nz,
        6e6,
        name="first_approx",
    )


def detail_bands(bands, halo, table, index):
    nx, rows, nz = bands.shape
    n1 = nx // 2
    step_rows = 24 if (rows // 2) % 24 == 0 else 8
    steps = rows // step_rows
    half_z = nz // 2

    def kernel(table_ref, index_ref, b_ref, h_ref, out):
        by = (pl.program_id(0) >= steps // 2).astype(jnp.int32)
        place = {"l1": 0, "l2": 1, "r1": 2, "r2": 3}
        limits = {}
        for bx in range(2):
            for bz in range(2):
                band = 4 * bx + 2 * by + bz
                found = table_ref[index_ref[0, jnp.maximum(band - 1, 0)]]
                limits[bx, bz] = jnp.where(band == 0, NOTHING, found)

        def tile(t, carry):
            at = pl.ds(pl.multiple_of(t * 8, 8), 8)
            for bz in range(2):
                lanes = pl.ds(bz * half_z, half_z)

                def get(key):
                    if isinstance(key, str):
                        return h_ref[place[key], at, lanes]
                    return b_ref[key, at, lanes]

                for k in range(n1):
                    out[k, at, lanes] = shrink(x_low(get, k, nx), limits[0, bz])
                    out[n1 + k, at, lanes] = shrink(x_high(get, k, nx), limits[1, bz])
            return carry

        lax.fori_loop(0, step_rows // 8, tile, 0)

    block = pl.BlockSpec((nx, step_rows, nz), lambda i: (0, i, 0))
    return call(
        kernel,
        (steps,),
        [SMEM, SMEM, block, pl.BlockSpec((4, step_rows, nz), lambda i: (0, i, 0))],
        block,
        shape(nx, rows, nz),
        [table, index, bands, halo],
        40 * nx * rows * nz,
        8 * nx * rows * nz,
        name="detail_bands",
    )


def detail_yz(coeffs, z_matrix, y_matrix):
    nx, rows, nz = coeffs.shape
    ny = y_matrix[0].shape[0]
    blocks = nx // 8

    def kernel(c_ref, z0, z1, y0, y1, out, up, down):
        step = pl.program_id(0)
        zed = times(c_ref[...].reshape(4 * rows, nz), (z0, z1))
        for i in range(4):
            out[i] = left_times((y0, y1), zed[i * rows : (i + 1) * rows])

        @pl.when(step == 0)
        def _():
            down[0] = H[2] * out[0] + H[0] * out[1]
            down[1] = H[1] * out[0]

        @pl.when(step == blocks)
        def _():
            down[0] += G[2] * out[0] + G[0] * out[1]
            down[1] += G[1] * out[0]

        @pl.when(step == blocks - 1)
        def _():
            up[0] = H[5] * out[3] + H[7] * out[2]
            up[1] = H[6] * out[3]

        @pl.when(step == 2 * blocks - 1)
        def _():
            up[0] += G[5] * out[3] + G[7] * out[2]
            up[1] += G[6] * out[3]

    return call(
        kernel,
        (2 * blocks,),
        [pl.BlockSpec((4, rows, nz), lambda i: (i, 0, 0))] + [whole(m) for m in z_matrix + y_matrix],
        [pl.BlockSpec((4, ny, nz), lambda i: (i, 0, 0)), whole_out(2, ny, nz), whole_out(2, ny, nz)],
        [shape(nx, ny, nz), shape(2, ny, nz), shape(2, ny, nz)],
        [coeffs, *z_matrix, *y_matrix],
        6 * nx * rows * nz * nz + 6 * nx * rows * ny * nz,
        4 * nx * nz * (rows + ny),
        name="detail_yz",
    )


def detail_x(parts):
    nx, ny, nz = parts.shape
    n1 = nx // 2
    step_rows = 16

    def kernel(p_ref, out):
        def tile(t, carry):
            at = pl.ds(pl.multiple_of(t * 8, 8), 8)
            for lane in range(0, nz, 128):
                lanes = pl.ds(lane, 128)
                for m in range(nx):
                    ks = [k for k in range(n1) if 0 <= m + 3 - 2 * k < 8]
                    lows = {k: p_ref[k, at, lanes] for k in ks}
                    highs = {k: p_ref[n1 + k, at, lanes] for k in ks}
                    out[m, at, lanes] = x_synth(m, lows, highs)
            return carry

        lax.fori_loop(0, step_rows // 8, tile, 0)

    block = pl.BlockSpec((nx, step_rows, nz), lambda i: (0, i, 0))
    return call(
        kernel,
        (ny // step_rows,),
        [block],
        block,
        shape(nx, ny, nz),
        [parts],
        16 * nx * ny * nz,
        8 * nx * ny * nz,
        name="detail_x",
    )


def second_bands(own, left, right, z_matrix, y_matrix, low_rows):
    n1, own_rows, nz = own.shape
    ghost_rows = left.shape[1]
    in_rows = own_rows + 2 * ghost_rows
    rows = 2 * low_rows
    lane_half = nz // 2

    def kernel(o_ref, l_ref, r_ref, z0, z1, y0, y1, out, up, down):
        for i in range(0, n1, 4):
            stack = jnp.concatenate(
                [part[j] for j in range(i, i + 4) for part in (o_ref, l_ref, r_ref)], axis=0
            )
            zed = times(stack, (z0, z1))
            for j in range(4):
                out[i + j] = left_times((y0, y1), zed[j * in_rows : (j + 1) * in_rows])
        low = lambda c: out[c, :low_rows]
        up[0:rows] = out[n1 - 1]
        up[rows : 2 * rows] = H[0] * out[n1 - 3] + H[1] * out[n1 - 2]
        first = added([(H[j], low(n1 - 5 + j)) for j in range(5)])
        second = added([(H[0] * H[j], low(n1 - 9 + j)) for j in range(8)])
        second += added([(H[1] * H[j], low(n1 - 7 + j)) for j in range(7)])
        lane = lax.broadcasted_iota(jnp.int32, first.shape, 1)
        up[2 * rows :] = jnp.where(lane < lane_half, first, pltpu.roll(second, lane_half, 1))
        down[0:rows] = out[0]
        down[rows : 2 * rows] = H[6] * out[1] + H[7] * out[2]
        first = added([(H[j], low(j - 3)) for j in range(3, 8)])
        second = added([(H[6] * H[j], low(j - 1)) for j in range(1, 8)])
        second += added([(H[7] * H[j], low(j + 1)) for j in range(8)])
        down[2 * rows :] = jnp.where(lane < lane_half, first, pltpu.roll(second, lane_half, 1))

    message = 2 * rows + low_rows
    return call(
        kernel,
        (1,),
        [whole(a) for a in (own, left, right, *z_matrix, *y_matrix)],
        [whole_out(n1, rows, nz), whole_out(message, nz), whole_out(message, nz)],
        [shape(n1, rows, nz), shape(message, nz), shape(message, nz)],
        [own, left, right, *z_matrix, *y_matrix],
        6 * n1 * in_rows * nz * (nz + rows),
        4 * n1 * nz * (in_rows + rows),
        name="second_bands",
    )


def limits_plane(table_ref, index_ref, level, bx, dims, row_split, lane_split, zeroth):
    row_high = lax.broadcasted_iota(jnp.int32, dims, 0) >= row_split
    lane_high = lax.broadcasted_iota(jnp.int32, dims, 1) >= lane_split

    def limit(by, bz):
        band = 4 * bx + 2 * by + bz
        return zeroth if band == 0 else table_ref[index_ref[level, band - 1]]

    low_y = jnp.where(lane_high, limit(0, 1), limit(0, 0))
    return jnp.where(row_high, jnp.where(lane_high, limit(1, 1), limit(1, 0)), low_y)


def coarse(bands, left, right, table, index, z1_mats, z2_mats, ya2, ys2, ys1, low_rows, z1_len):
    n1, rows, nz = bands.shape
    n2, n3 = n1 // 2, n1 // 4
    rows2 = ya2[0].shape[0]
    out_rows = up_to(ys1[0].shape[0], 8)
    out_rows = ys1[2]
    mats = [*z1_mats, *z2_mats, *ya2[:2], *ys2[:2], *ys1[:2]]
    lane_half = z1_len // 2

    def kernel(table_ref, index_ref, b_ref, l_ref, r_ref, *refs):
        z1s, z2a, z2s, a2, s2, s1 = [refs[2 * i : 2 * i + 2] for i in range(6)]
        approx, up, down, c1, p1 = refs[12:]
        sides = {
            "l1": lambda: l_ref[0:rows],
            "l2": lambda: l_ref[rows : 2 * rows],
            "r1": lambda: r_ref[0:rows],
            "r2": lambda: r_ref[rows : 2 * rows],
        }
        get = lambda key: sides[key]() if isinstance(key, str) else b_ref[key]
        lowpart = lambda c: b_ref[c, :low_rows]
        dims = (rows, nz)
        quiet = limits_plane(table_ref, index_ref, 1, 0, dims, low_rows, lane_half, NOTHING)
        loud = limits_plane(table_ref, index_ref, 1, 1, dims, low_rows, lane_half, NOTHING)
        planes = []
        for k in range(n2):
            low = x_low(get, k, n1)
            planes.append(low[:low_rows])
            c1[k] = shrink(low, quiet)
            c1[n2 + k] = shrink(x_high(get, k, n1), loud)
        packed = l_ref[2 * rows :]
        planes.append(packed + added([(H[5 + i], lowpart(i)) for i in range(3)]))
        planes.append(pltpu.roll(packed, lane_half, 1) + H[1] * H[7] * lowpart(0))
        packed = r_ref[2 * rows :]
        planes.append(packed + added([(H[i], lowpart(n1 - 3 + i)) for i in range(3)]))
        planes.append(pltpu.roll(packed, lane_half, 1) + H[6] * H[0] * lowpart(n1 - 1))
        zed = times(jnp.concatenate(planes, axis=0), z2a)
        third = [left_times(a2, zed[i * low_rows : (i + 1) * low_rows]) for i in range(len(planes))]
        keys = {"l1": n2, "l2": n2 + 1, "r1": n2 + 2, "r2": n2 + 3}
        get2 = lambda key: third[keys.get(key, key)]
        dims = (rows2, nz)
        quiet = limits_plane(table_ref, index_ref, 2, 0, dims, rows2 // 2, lane_half // 2, 0.0)
        loud = limits_plane(table_ref, index_ref, 2, 1, dims, rows2 // 2, lane_half // 2, 0.0)
        kept = [shrink(x_low(get2, k, n2), quiet) for k in range(n3)]
        kept += [shrink(x_high(get2, k, n2), loud) for k in range(n3)]
        zed = times(jnp.concatenate(kept, axis=0), z2s)
        parts = [left_times(s2, zed[i * rows2 : (i + 1) * rows2])[:low_rows] for i in range(2 * n3)]
        lows = dict(enumerate(parts[:n3]))
        highs = dict(enumerate(parts[n3:]))
        ghosts = [-3, -2, -1, n2, n2 + 1, n2 + 2]
        for k in range(n2):
            c1[k, :low_rows] += x_synth(k, lows, highs)
        stack = [x_synth(k, lows, highs) for k in ghosts]
        pad = jnp.zeros((rows - low_rows, nz), F32)
        stack_zed = times(jnp.concatenate(stack, axis=0), z1s)
        for i in range(6):
            plane = jnp.concatenate([stack_zed[i * low_rows : (i + 1) * low_rows], pad], axis=0)
            p1[2 * n2 + i] = left_times(s1, plane)[:out_rows]
        for i in range(0, 2 * n2, 4):
            zed = times(c1[i : i + 4].reshape(4 * rows, nz), z1s)
            for j in range(4):
                p1[i + j] = left_times(s1, zed[j * rows : (j + 1) * rows])[:out_rows]
        lows = {k: p1.at[k] for k in range(n2)}
        highs = {k: p1.at[n2 + k] for k in range(n2)}
        for i, k in enumerate(ghosts):
            lows[k] = p1.at[2 * n2 + i]

        def cell(m):
            near = lambda part: {k: ref[...] for k, ref in part.items() if 0 <= m + 3 - 2 * k < 8}
            return x_synth(m, near(lows), near(highs))

        for m in range(-2, n1 + 2):
            approx[m + 2] = cell(m)
        value = lambda part, ks: {k: part[k][...] for k in ks}
        ends = (n2 - 2, n2 - 1)
        up[0], up[1] = approx[n1], approx[n1 + 1]
        up[2], up[3] = spill_up(value(lows, ends), value(highs, ends), n2)
        up[4], up[5] = lows[n2][...], lows[n2 + 1][...]
        down[0], down[1] = approx[2], approx[3]
        down[2], down[3] = spill_down(value(lows, (0, 1)), value(highs, (0, 1)))
        down[4], down[5] = lows[-1][...], lows[-2][...]

    return call(
        kernel,
        (1,),
        [SMEM, SMEM] + [whole(a) for a in (bands, left, right, *mats)],
        [whole_out(n1 + 4, out_rows, nz), whole_out(6, out_rows, nz), whole_out(6, out_rows, nz)],
        [shape(n1 + 4, out_rows, nz), shape(6, out_rows, nz), shape(6, out_rows, nz)],
        [table, index, bands, left, right, *mats],
        1.5e9,
        8 * n1 * rows * nz,
        scratch=[pltpu.VMEM((2 * n2, rows, nz), F32), pltpu.VMEM((2 * n2 + 6, out_rows, nz), F32)],
        name="coarse",
    )


def final(approx, left, right, detail, e_left, e_right, z_matrix, y_matrix):
    planes, rows, half_z = approx.shape
    nx, ny, nz = detail.shape
    n1 = nx // 2
    n2 = n1 // 2
    step_rows = 16

    def kernel(a_ref, l_ref, r_ref, d_ref, el, er, z0, z1, y0, y1, out, total, parts):
        @pl.when(pl.program_id(0) == 0)
        def _():
            for m in range(n1):
                terms = [(1.0, a_ref[m + 2])]
                for k, coef, source in ((0, 1.0, 4), (1, 1.0, 5), (2, THIRD_UP, 5)):
                    if 0 <= m + 3 - 2 * k < 8:
                        terms.append((coef * H[m + 3 - 2 * k], l_ref[source]))
                for k, coef, source in ((n2 - 1, 1.0, 4), (n2 - 2, 1.0, 5), (n2 - 3, THIRD_DOWN, 5)):
                    if 0 <= m + 3 - 2 * k < 8:
                        terms.append((coef * H[m + 3 - 2 * k], r_ref[source]))
                if m < 3:
                    terms.append(((1.0, 1.0, THIRD_UP)[m], l_ref[(2, 3, 3)[m]]))
                if m >= n1 - 3:
                    terms.append(((1.0, 1.0, THIRD_DOWN)[n1 - 1 - m], r_ref[(2, 3, 3)[n1 - 1 - m]]))
                total[m + 2] = added(terms)
            total[0] = a_ref[0] + l_ref[0]
            total[1] = a_ref[1] + l_ref[1]
            total[n1 + 2] = a_ref[n1 + 2] + r_ref[0]
            total[n1 + 3] = a_ref[n1 + 3] + r_ref[1]
            for i in range(0, planes, 4):
                zed = times(total[i : i + 4].reshape(4 * rows, half_z), (z0, z1))
                for j in range(4):
                    parts[i + j] = left_times((y0, y1), zed[j * rows : (j + 1) * rows])

        start = pl.program_id(0) * step_rows

        def tile(t, carry):
            at = pl.ds(pl.multiple_of(t * 8, 8), 8)
            within = pl.ds(pl.multiple_of(start + t * 8, 8), 8)
            for lane in range(0, nz, 128):
                lanes = pl.ds(lane, 128)
                for m in range(nx):
                    ks = [k for k in range(-2, n1 + 2) if 0 <= m + 3 - 2 * k < 8]
                    value = d_ref[m, at, lanes] + x_synth(m, {k: parts[k + 2, within, lanes] for k in ks}, {})
                    if m < 3:
                        extra = el[(0, 1, 1)[m], at, lanes]
                        value += extra if m < 2 else THIRD_UP * extra
                    if m >= nx - 3:
                        extra = er[(0, 1, 1)[nx - 1 - m], at, lanes]
                        value += extra if m > nx - 3 else THIRD_DOWN * extra
                    out[m, at, lanes] = value
            return carry

        lax.fori_loop(0, step_rows // 8, tile, 0)

    block = pl.BlockSpec((nx, step_rows, nz), lambda i: (0, i, 0))
    side = pl.BlockSpec((2, step_rows, nz), lambda i: (0, i, 0))
    return call(
        kernel,
        (ny // step_rows,),
        [whole(approx), whole(left), whole(right), block, side, side]
        + [whole(m) for m in z_matrix + y_matrix],
        block,
        shape(nx, ny, nz),
        [approx, left, right, detail, e_left, e_right, *z_matrix, *y_matrix],
        8 * nx * ny * nz,
        8 * nx * ny * nz,
        scratch=[pltpu.VMEM((planes, rows, half_z), F32), pltpu.VMEM((planes, ny, nz), F32)],
        name="final",
    )


def to_next(array, axis):
    size = lax.axis_size(axis)
    return lax.ppermute(array, axis, [(i, (i + 1) % size) for i in range(size)])


def to_previous(array, axis):
    size = lax.axis_size(axis)
    return lax.ppermute(array, axis, [((i + 1) % size, i) for i in range(size)])


def local(velocity, table, index):
    nx, ny, nz = velocity.shape
    y1, y2, y3 = ny // 2, ny // 4, ny // 8
    ghost = 24
    cells0 = list(range(-8, ny + 8))
    rows0 = up_to(y1 + 4, 8)
    ks0 = fill(list(range(y1)) + [-2, -1, y1, y1 + 1], rows0)
    cells1 = list(range(y1)) + list(range(-ghost, 0)) + list(range(y1, y1 + ghost))
    rows1 = up_to(y2 + 18, 8)
    ks1 = fill(list(range(-9, y2 + 9)), rows1)
    rows2 = up_to(y3 + 6, 8)
    ks2 = fill(list(range(-3, y3 + 3)), rows2)
    ya0 = pieces(analysis_rows(cells0, ks0))
    ys0_matrix = synthesis_rows(list(range(ny)), ks0)
    ys0 = pieces(ys0_matrix)
    ys0_low = pieces(ys0_matrix[:, :rows0])
    ya1 = pieces(analysis_rows(cells1, ks1))
    ys1 = pieces(synthesis_rows(ks0, ks1)) + [rows0]
    ya2 = pieces(analysis_rows(ks1, ks2))
    ys2 = pieces(synthesis_rows(ks1, ks2))
    z0 = periodic(nz, nz)
    z1 = periodic(nz // 2, nz // 2)
    z2 = periodic(nz // 4, nz // 2)
    za0, zs0, zs0_low = pieces(z0), pieces(z0.T), pieces(z0.T[: nz // 2])
    za1, zs1 = pieces(z1), pieces(z1.T)
    za2, zs2 = pieces(z2), pieces(z2.T)

    x_up, x_down, y_up, y_down = first_messages(velocity)
    x_left = to_next(x_up, "gx")
    x_right = to_previous(x_down, "gx")
    y_left = to_next(y_up, "gy")
    y_right = to_previous(y_down, "gy")
    zed = depth_analysis(velocity, za0)
    c_up, c_down = corner_messages(y_left, y_right)
    c_left = to_next(c_up, "gx")
    c_right = to_previous(c_down, "gx")
    bands = y_analysis(zed, y_left, y_right, za0, ya0)
    halo, approx, a_up, a_down = first_approx(
        bands, x_left, x_right, c_left, c_right, za0, ya0, y1, ghost
    )
    a_left = to_next(a_up, "gy")
    a_right = to_previous(a_down, "gy")
    coeffs = detail_bands(bands, halo, table, index)
    bands1, b_up, b_down = second_bands(approx, a_left, a_right, za1, ya1, rows1)
    b_left = to_next(b_up, "gx")
    b_right = to_previous(b_down, "gx")
    parts, e_up, e_down = detail_yz(coeffs, zs0, ys0)
    e_left = to_next(e_up, "gx")
    e_right = to_previous(e_down, "gx")
    approx1, s_up, s_down = coarse(
        bands1, b_left, b_right, table, index, zs1, za2 + zs2, ya2, ys2, ys1, rows1, nz // 2
    )
    s_left = to_next(s_up, "gx")
    s_right = to_previous(s_down, "gx")
    detail = detail_x(parts)
    return final(approx1, s_left, s_right, detail, e_left, e_right, zs0_low, ys0_low)


def solution(mesh):
    return jax.shard_map(
        local,
        mesh=mesh,
        in_specs=(P("gx", "gy", None), P(), P()),
        out_specs=P("gx", "gy", None),
        check_vma=False,
    )
```

```python
import functools

import jax
import jax.numpy as jnp
import ml_dtypes
import numpy as np
from jax import lax
from jax.experimental import pallas as pl
from jax.experimental.pallas import tpu as pltpu
from jax.sharding import PartitionSpec as P

H = [
    0.23037781330885523,
    0.7148465705525415,
    0.6308807679295904,
    -0.02798376941698385,
    -0.18703481171888114,
    0.030841381835986965,
    0.032883011666982945,
    -0.010597401784997278,
]
G = [(-1.0) ** j * H[7 - j] for j in range(8)]
F32 = jnp.float32
BF16 = jnp.bfloat16
NOTHING = 3.0e38
VMEM_BYTES = 16 * 1024 * 1024


def tap(filt, j):
    return filt[j] if 0 <= j < 8 else 0.0


def analysis_rows(cells, low_ks, high_ks):
    matrix = np.zeros((len(low_ks) + len(high_ks), len(cells)))
    rows = [(H, k) for k in low_ks] + [(G, k) for k in high_ks]
    for row, (filt, k) in enumerate(rows):
        for col, cell in enumerate(cells):
            if k is not None and cell is not None:
                matrix[row, col] = tap(filt, cell - 2 * k + 3)
    return matrix


def synthesis_rows(cells, low_ks, high_ks):
    return analysis_rows(cells, low_ks, high_ks).T


def periodic(length, padded_to):
    matrix = np.zeros((padded_to, padded_to))
    for k in range(length // 2):
        for j in range(8):
            matrix[(2 * k + j - 3) % length, k] += H[j]
            matrix[(2 * k + j - 3) % length, length // 2 + k] += G[j]
    return matrix


def fill(items, length):
    return items + [None] * (length - len(items))


def up_to(count, step):
    return -(-count // step) * step


def pieces(matrix, axis):
    rows, cols = matrix.shape
    matrix = np.pad(matrix, ((0, up_to(rows, 16) - rows), (0, up_to(cols, 16) - cols))).astype(np.float32)
    high = matrix.astype(ml_dtypes.bfloat16)
    low = (matrix - high.astype(np.float32)).astype(ml_dtypes.bfloat16)
    return np.concatenate([high, high, low], axis=axis)


def from_left(matrix):
    return pieces(matrix, 1)


def from_right(matrix):
    return pieces(matrix, 0)


def halves(values):
    high = values.astype(BF16)
    return high, (values - high.astype(F32)).astype(BF16)


def times(values, matrix):
    high, low = halves(values)
    return jnp.dot(jnp.concatenate([high, low, high], axis=1), matrix[...], preferred_element_type=F32)


def left_times(matrix, values):
    missing = matrix.shape[1] // 3 - values.shape[0]
    if missing:
        values = jnp.concatenate([values, jnp.zeros((missing, values.shape[1]), F32)], axis=0)
    high, low = halves(values)
    return jnp.dot(matrix[...], jnp.concatenate([high, low, high], axis=0), preferred_element_type=F32)


def added(terms):
    total = None
    for coef, value in terms:
        part = value if coef == 1.0 else coef * value
        total = part if total is None else total + part
    return total


def x_terms(k, n):
    terms = []
    for j in range(8):
        cell = 2 * k + j - 3
        if 0 <= cell < n:
            terms.append((cell, H[j], G[j]))
        elif cell == -1:
            terms.append(("l1", H[j], G[j]))
        elif cell == n:
            terms.append(("r1", H[j], G[j]))
    if k == 0:
        terms.append(("l2", 1.0, G[0] / H[0]))
    if k == n // 2 - 1:
        terms.append(("r2", 1.0, G[6] / H[6]))
    return terms


def lattice():
    low = np.array(H).reshape(4, 2)
    high = np.array(G).reshape(4, 2)
    tangents = []
    for _ in range(3):
        t = (low[0] @ high[0]) / (high[0] @ high[0])
        tangents.append(float(t))
        low, high = (low - t * high)[1:] / (1 + t * t), (high + t * low)[:-1] / (1 + t * t)
    return low[0].tolist(), high[0].tolist(), tangents[::-1]


def x_interior(get, n):
    first, second, tangents = lattice()
    a, b = {}, {}
    for i in range(1, n // 2):
        x, y = get(2 * i - 1), get(2 * i)
        a[i] = first[0] * x + first[1] * y
        b[i] = second[0] * x + second[1] * y
    for t in tangents:
        shared = [i for i in a if i + 1 in a]
        a, b = {i: a[i + 1] + t * b[i] for i in shared}, {i: b[i] - t * a[i + 1] for i in shared}
    return {i + 1: (a[i], b[i]) for i in a}


def x_low(get, k, n):
    return added([(low, get(key)) for key, low, _ in x_terms(k, n)])


def x_high(get, k, n):
    return added([(high, get(key)) for key, _, high in x_terms(k, n)])


def x_synth(m, lows, highs):
    terms = [(H[m + 3 - 2 * k], v) for k, v in lows.items() if 0 <= m + 3 - 2 * k < 8]
    terms += [(G[m + 3 - 2 * k], v) for k, v in highs.items() if 0 <= m + 3 - 2 * k < 8]
    return added(terms)


def spill_up(low, high, n):
    first = added([(H[5], low[n - 1]), (G[5], high[n - 1]), (H[7], low[n - 2]), (G[7], high[n - 2])])
    return first, added([(H[6], low[n - 1]), (G[6], high[n - 1])])


def spill_down(low, high):
    first = added([(H[2], low[0]), (G[2], high[0]), (H[0], low[1]), (G[0], high[1])])
    return first, added([(H[1], low[0]), (G[1], high[0])])


THIRD_UP = H[7] / H[6]
THIRD_DOWN = H[0] / H[1]


def shrink(values, thresh):
    return values - jnp.minimum(jnp.maximum(values, -thresh), thresh)


def whole_call(kernel, out_shapes, args, flops, moved, scratch=(), name=None):
    specs = [SMEM if a.ndim == 1 or a.dtype == jnp.int32 else VMEM for a in args]
    outs = [VMEM] * len(out_shapes) if isinstance(out_shapes, list) else VMEM
    return pl.pallas_call(
        kernel,
        in_specs=specs,
        out_specs=outs,
        out_shape=out_shapes,
        scratch_shapes=list(scratch),
        name=name,
        cost_estimate=pl.CostEstimate(flops=int(flops), bytes_accessed=int(moved), transcendentals=0),
        compiler_params=pltpu.CompilerParams(vmem_limit_bytes=VMEM_BYTES),
    )(*args)


def call(kernel, grid, in_specs, out_specs, out_shapes, args, flops, moved, scratch=(), name=None):
    return pl.pallas_call(
        kernel,
        grid=grid,
        in_specs=in_specs,
        out_specs=out_specs,
        out_shape=out_shapes,
        scratch_shapes=list(scratch),
        name=name,
        cost_estimate=pl.CostEstimate(flops=int(flops), bytes_accessed=int(moved), transcendentals=0),
        compiler_params=pltpu.CompilerParams(vmem_limit_bytes=VMEM_BYTES),
    )(*args)


def shape(*dims):
    return jax.ShapeDtypeStruct(dims, F32)


def whole(array):
    dims = array.shape
    return pl.BlockSpec(dims, lambda *_: (0,) * len(dims))


def whole_out(*dims):
    return pl.BlockSpec(dims, lambda *_: (0,) * len(dims))


SMEM = pl.BlockSpec(memory_space=pltpu.SMEM)
VMEM = pl.BlockSpec(memory_space=pltpu.VMEM)


def x_messages(last, first, up, down):
    up[0] = last[3]
    up[1] = H[0] * last[1] + H[1] * last[2]
    down[0] = first[0]
    down[1] = H[6] * first[1] + H[7] * first[2]


def first_messages(v):
    nx, ny, nz = v.shape

    def kernel(last, first, y_last, y_first, up, down, y_up, y_down):
        x_messages(last, first, up, down)
        y_up[...] = y_last[...]
        y_down[...] = y_first[...]

    return call(
        kernel,
        (1,),
        [
            pl.BlockSpec((4, ny, nz), lambda i: (nx // 4 - 1, 0, 0)),
            pl.BlockSpec((4, ny, nz), lambda i: (0, 0, 0)),
            pl.BlockSpec((nx, 8, nz), lambda i: (0, ny // 8 - 1, 0)),
            pl.BlockSpec((nx, 8, nz), lambda i: (0, 0, 0)),
        ],
        [whole_out(2, ny, nz)] * 2 + [whole_out(nx, 8, nz)] * 2,
        [shape(2, ny, nz)] * 2 + [shape(nx, 8, nz)] * 2,
        [v] * 4,
        1e6,
        3e6,
        name="first_messages",
    )


def corner_messages(y_left, y_right):
    nx, rows, nz = y_left.shape

    def kernel(last_l, first_l, last_r, first_r, up, down):
        for part, last, first in ((0, last_l, first_l), (1, last_r, first_r)):
            at = pl.ds(8 * part, 8)
            up[0, at] = last[3]
            up[1, at] = H[0] * last[1] + H[1] * last[2]
            down[0, at] = first[0]
            down[1, at] = H[6] * first[1] + H[7] * first[2]

    last = pl.BlockSpec((4, rows, nz), lambda i: (nx // 4 - 1, 0, 0))
    first = pl.BlockSpec((4, rows, nz), lambda i: (0, 0, 0))
    return call(
        kernel,
        (1,),
        [last, first, last, first],
        [whole_out(2, 16, nz)] * 2,
        [shape(2, 16, nz)] * 2,
        [y_left, y_left, y_right, y_right],
        1e5,
        2e5,
        name="corner_messages",
    )


def over_planes(count, group, body):
    def step(i, carry):
        body(i * group)
        return carry

    lax.fori_loop(0, count // group, step, 0)


def depth(v, z_matrix, group, name):
    nx, rows, nz = v.shape

    def kernel(v_ref, z, out):
        def body(first):
            at = pl.ds(first, group)
            out[at] = times(v_ref[at].reshape(group * rows, nz), z).reshape(group, rows, nz)

        over_planes(nx, group, body)

    return whole_call(
        kernel, shape(nx, rows, nz), [v, z_matrix], 6 * nx * rows * nz * nz, 8 * nx * rows * nz, name=name
    )


def y_analysis(zed, y_left, y_right, z_matrix, y_matrix):
    nx, ny, nz = zed.shape
    rows = y_matrix.shape[0]
    group = 8

    def kernel(zed_ref, left, right, z, y, out, left_z, right_z):
        left_z[...] = times(left[...].reshape(8 * nx, nz), z).reshape(nx, 8, nz)
        right_z[...] = times(right[...].reshape(8 * nx, nz), z).reshape(nx, 8, nz)

        def body(first):
            for j in range(group):
                i = first + j
                out[i] = left_times(y, jnp.concatenate([left_z[i], zed_ref[i], right_z[i]], axis=0))

        over_planes(nx, group, body)

    return whole_call(
        kernel,
        shape(nx, rows, nz),
        [zed, y_left, y_right, z_matrix, y_matrix],
        6 * nx * rows * (ny + 16) * nz,
        4 * nx * nz * (ny + rows + 16),
        scratch=[pltpu.VMEM((nx, 8, nz), F32)] * 2,
        name="y_analysis",
    )


def first_approx(bands, x_left, x_right, c_left, c_right, z_matrix, y_matrix, own, ghost_rows):
    nx, rows, nz = bands.shape
    ny = x_left.shape[1]
    half_z = nz // 2
    n1 = nx // 2

    def kernel(b_ref, xl, xr, cl, cr, z, y, halo, approx, up, down):
        planes = [
            jnp.concatenate([corner[i, :8], main[i], corner[i, 8:]], axis=0)
            for main, corner in ((xl, cl), (xr, cr))
            for i in range(2)
        ]
        zed = times(jnp.concatenate(planes, axis=0), z)
        for i in range(4):
            halo[i] = left_times(y, zed[i * (ny + 16) : (i + 1) * (ny + 16)])
        place = {"l1": 0, "l2": 1, "r1": 2, "r2": 3}

        def tile(t, carry):
            at = pl.ds(pl.multiple_of(t * 8, 8), 8)
            values = {key: halo[i, at, :half_z] for key, i in place.items()}
            values.update({i: b_ref[i, at, :half_z] for i in range(nx)})
            for k in range(n1):
                approx[k, at] = x_low(values.get, k, nx)
            return carry

        lax.fori_loop(0, own // 8, tile, 0)
        up[...] = approx[:, own - ghost_rows :]
        down[...] = approx[:, :ghost_rows]

    return whole_call(
        kernel,
        [
            shape(4, rows, nz),
            shape(n1, own, half_z),
            shape(n1, ghost_rows, half_z),
            shape(n1, ghost_rows, half_z),
        ],
        [bands, x_left, x_right, c_left, c_right, z_matrix, y_matrix],
        24 * rows * (ny + 16) * nz + 24 * (ny + 16) * nz * nz,
        3e6,
        name="first_approx",
    )


def detail_bands(bands, halo, table, index):
    nx, rows, nz = bands.shape
    n1 = nx // 2
    half_z = nz // 2
    half_tiles = rows // 16

    def kernel(table_ref, index_ref, b_ref, h_ref, out):
        place = {"l1": 0, "l2": 1, "r1": 2, "r2": 3}

        def tiles(by):
            def tile(t, carry):
                at = pl.ds(pl.multiple_of((t + by * half_tiles) * 8, 8), 8)
                for bz in range(2):
                    lanes = pl.ds(bz * half_z, half_z)
                    band = 2 * by + bz
                    quiet = table_ref[index_ref[0, band - 1]] if band else NOTHING
                    loud = table_ref[index_ref[0, band + 3]]
                    values = {key: h_ref[i, at, lanes] for key, i in place.items()}
                    values.update({i: b_ref[i, at, lanes] for i in range(nx)})
                    coeffs = x_interior(values.get, nx)
                    for k in (0, 1, n1 - 2, n1 - 1):
                        coeffs[k] = (x_low(values.get, k, nx), x_high(values.get, k, nx))
                    for k, (low, high) in coeffs.items():
                        out[k, at, lanes] = shrink(low, quiet) if band else jnp.zeros_like(low)
                        out[n1 + k, at, lanes] = shrink(high, loud)
                return carry

            return tile

        lax.fori_loop(0, half_tiles, tiles(0), 0)
        lax.fori_loop(0, half_tiles, tiles(1), 0)

    return whole_call(
        kernel,
        shape(nx, rows, nz),
        [table, index, bands, halo],
        40 * nx * rows * nz,
        8 * nx * rows * nz,
        name="detail_bands",
    )


def detail_yz(coeffs, z_matrix, y_matrix):
    nx, rows, nz = coeffs.shape
    ny = y_matrix.shape[0]
    n1 = nx // 2

    def kernel(c_ref, z, y, out, up, down, zed):
        def z_body(first):
            at = pl.ds(first, 8)
            zed[at] = times(c_ref[at].reshape(8 * rows, nz), z).reshape(8, rows, nz)

        def y_body(first):
            for j in range(8):
                out[first + j] = left_times(y, zed[first + j])

        over_planes(nx, 8, z_body)
        over_planes(nx, 8, y_body)
        lows = {k: out.at[k] for k in range(n1)}
        highs = {k: out.at[n1 + k] for k in range(n1)}
        value = lambda part, ks: {k: part[k][...] for k in ks}
        ends = (n1 - 2, n1 - 1)
        up[0], up[1] = spill_up(value(lows, ends), value(highs, ends), n1)
        down[0], down[1] = spill_down(value(lows, (0, 1)), value(highs, (0, 1)))

    return whole_call(
        kernel,
        [shape(nx, ny, nz), shape(2, ny, nz), shape(2, ny, nz)],
        [coeffs, z_matrix, y_matrix],
        6 * nx * rows * nz * nz + 6 * nx * rows * ny * nz,
        4 * nx * nz * (rows + ny),
        scratch=[pltpu.VMEM((nx, rows, nz), F32)],
        name="detail_yz",
    )


def detail_x(parts):
    nx, ny, nz = parts.shape
    n1 = nx // 2

    def kernel(p_ref, out):
        def tile(t, carry):
            at = pl.ds(pl.multiple_of(t * 8, 8), 8)
            for lane in range(0, nz, 128):
                lanes = pl.ds(lane, 128)
                lows = {k: p_ref[k, at, lanes] for k in range(n1)}
                highs = {k: p_ref[n1 + k, at, lanes] for k in range(n1)}
                for m in range(nx):
                    out[m, at, lanes] = x_synth(m, lows, highs)
            return carry

        lax.fori_loop(0, ny // 8, tile, 0)

    return whole_call(
        kernel, shape(nx, ny, nz), [parts], 16 * nx * ny * nz, 8 * nx * ny * nz, name="detail_x"
    )


def in_pairs(matrix, planes):
    results = []
    for i in range(0, len(planes), 2):
        both = left_times(matrix, jnp.concatenate(planes[i : i + 2], axis=1))
        width = both.shape[1] // 2
        results += [both[:, :width], both[:, width:]]
    return results


def cut(values, rows):
    return [values[i : i + rows] for i in range(0, values.shape[0], rows)]


def packed(first, second):
    half = first.shape[1] // 2
    lane = lax.broadcasted_iota(jnp.int32, first.shape, 1)
    return jnp.where(lane < half, first, pltpu.roll(second, half, 1))


def unpacked(both):
    half = both.shape[1] // 2
    lane = lax.broadcasted_iota(jnp.int32, both.shape, 1)
    return [jnp.where(lane < half, part, 0.0) for part in (both, pltpu.roll(both, half, 1))]


def second_bands(own, left, right, z_matrix, y_matrix, low_rows):
    n1, own_rows, nz = own.shape
    in_rows = own_rows + 2 * left.shape[1]
    rows = y_matrix.shape[0]

    def kernel(o_ref, l_ref, r_ref, z, y, out, up, down):
        for i in range(0, n1, 8):
            stack = [part[j] for j in range(i, i + 8) for part in (o_ref, l_ref, r_ref)]
            zed = times(jnp.concatenate(stack, axis=0), z)
            for j, plane in enumerate(in_pairs(y, cut(zed, in_rows))):
                out[i + j] = plane
        low = lambda c: out[c, :low_rows]
        up[0:rows] = out[n1 - 1]
        up[rows : 2 * rows] = H[0] * out[n1 - 3] + H[1] * out[n1 - 2]
        first = added([(H[j], low(n1 - 5 + j)) for j in range(5)])
        second = added([(H[0] * H[j], low(n1 - 9 + j)) for j in range(8)])
        second += added([(H[1] * H[j], low(n1 - 7 + j)) for j in range(7)])
        up[2 * rows :] = packed(first, second)
        down[0:rows] = out[0]
        down[rows : 2 * rows] = H[6] * out[1] + H[7] * out[2]
        first = added([(H[j], low(j - 3)) for j in range(3, 8)])
        second = added([(H[6] * H[j], low(j - 1)) for j in range(1, 8)])
        second += added([(H[7] * H[j], low(j + 1)) for j in range(8)])
        down[2 * rows :] = packed(first, second)

    message = 2 * rows + low_rows
    return whole_call(
        kernel,
        [shape(n1, rows, nz), shape(message, nz), shape(message, nz)],
        [own, left, right, z_matrix, y_matrix],
        6 * n1 * in_rows * nz * (nz + rows),
        4 * n1 * nz * (in_rows + rows),
        name="second_bands",
    )


def limits_plane(table_ref, index_ref, level, bx, dims, row_split, lane_split, zeroth):
    row_high = lax.broadcasted_iota(jnp.int32, dims, 0) >= row_split
    lane_high = lax.broadcasted_iota(jnp.int32, dims, 1) >= lane_split

    def limit(by, bz):
        band = 4 * bx + 2 * by + bz
        return zeroth if band == 0 else table_ref[index_ref[level, band - 1]]

    low_y = jnp.where(lane_high, limit(0, 1), limit(0, 0))
    return jnp.where(row_high, jnp.where(lane_high, limit(1, 1), limit(1, 0)), low_y)


def coarse(bands, left, right, table, index, zs1, za2, zs2, ya2, ys2, ys1, low_rows, out_rows):
    n1, rows, nz = bands.shape
    n2, n3 = n1 // 2, n1 // 4
    rows2 = ya2.shape[0]
    lane_half = nz // 2

    def kernel(table_ref, index_ref, b_ref, l_ref, r_ref, z1, z2a, z2s, a2, s2, s1, approx, up, down, c1, p1):
        sides = {
            "l1": lambda: l_ref[0:rows],
            "l2": lambda: l_ref[rows : 2 * rows],
            "r1": lambda: r_ref[0:rows],
            "r2": lambda: r_ref[rows : 2 * rows],
        }
        get = lambda key: sides[key]() if isinstance(key, str) else b_ref[key]
        low_part = lambda c: b_ref[c, :low_rows]
        dims = (rows, nz)
        quiet = limits_plane(table_ref, index_ref, 1, 0, dims, low_rows, lane_half, NOTHING)
        loud = limits_plane(table_ref, index_ref, 1, 1, dims, low_rows, lane_half, NOTHING)
        planes = []
        for k in range(n2):
            low = x_low(get, k, n1)
            planes.append(low[:low_rows])
            c1[k] = shrink(low, quiet)
            c1[n2 + k] = shrink(x_high(get, k, n1), loud)
        first, second = unpacked(l_ref[2 * rows :])
        planes.append(first + added([(H[5 + i], low_part(i)) for i in range(3)]))
        planes.append(second + H[1] * H[7] * low_part(0))
        first, second = unpacked(r_ref[2 * rows :])
        planes.append(first + added([(H[i], low_part(n1 - 3 + i)) for i in range(3)]))
        planes.append(second + H[6] * H[0] * low_part(n1 - 1))
        third = in_pairs(a2, cut(times(jnp.concatenate(planes, axis=0), z2a), low_rows))
        keys = {"l1": n2, "l2": n2 + 1, "r1": n2 + 2, "r2": n2 + 3}
        get2 = lambda key: third[keys.get(key, key)]
        dims = (rows2, nz)
        quiet = limits_plane(table_ref, index_ref, 2, 0, dims, rows2 // 2, lane_half // 2, 0.0)
        loud = limits_plane(table_ref, index_ref, 2, 1, dims, rows2 // 2, lane_half // 2, 0.0)
        kept = [shrink(x_low(get2, k, n2), quiet) for k in range(n3)]
        kept += [shrink(x_high(get2, k, n2), loud) for k in range(n3)]
        parts = in_pairs(s2, cut(times(jnp.concatenate(kept, axis=0), z2s), rows2))
        parts = [part[:low_rows] for part in parts]
        lows = dict(enumerate(parts[:n3]))
        highs = dict(enumerate(parts[n3:]))
        ghosts = [-3, -2, -1, n2, n2 + 1, n2 + 2]
        for k in range(n2):
            c1[k, :low_rows] += x_synth(k, lows, highs)
        stack = [x_synth(k, lows, highs) for k in ghosts]
        beyond = dict(zip(ghosts, stack))
        zed = times(jnp.concatenate(stack, axis=0), z1)
        for i, plane in enumerate(in_pairs(s1, cut(zed, low_rows))):
            p1[2 * n2 + i] = plane[:out_rows]
        for i in range(0, 2 * n2, 8):
            zed = times(c1[i : i + 8].reshape(8 * rows, nz), z1)
            for j, plane in enumerate(in_pairs(s1, cut(zed, rows))):
                p1[i + j] = plane[:out_rows]
        lows = {k: p1.at[k] for k in range(n2)}
        highs = {k: p1.at[n2 + k] for k in range(n2)}
        for i, k in enumerate(ghosts):
            lows[k] = p1.at[2 * n2 + i]

        def cell(m):
            near = lambda part: {k: ref[...] for k, ref in part.items() if 0 <= m + 3 - 2 * k < 8}
            return x_synth(m, near(lows), near(highs))

        for m in range(-2, n1 + 2):
            approx[m + 2] = cell(m)
        value = lambda part, ks: {k: part[k][...] for k in ks}
        ends = (n2 - 2, n2 - 1)
        slot = lambda i: pl.ds(i * out_rows, out_rows)
        up[slot(0)], up[slot(1)] = approx[n1], approx[n1 + 1]
        up[slot(2)], up[slot(3)] = spill_up(value(lows, ends), value(highs, ends), n2)
        up[4 * out_rows :] = packed(beyond[n2], beyond[n2 + 1])
        down[slot(0)], down[slot(1)] = approx[2], approx[3]
        down[slot(2)], down[slot(3)] = spill_down(value(lows, (0, 1)), value(highs, (0, 1)))
        down[4 * out_rows :] = packed(beyond[-1], beyond[-2])

    message = 4 * out_rows + low_rows
    return whole_call(
        kernel,
        [shape(n1 + 4, out_rows, nz), shape(message, nz), shape(message, nz)],
        [table, index, bands, left, right, zs1, za2, zs2, ya2, ys2, ys1],
        1.5e9,
        8 * n1 * rows * nz,
        scratch=[pltpu.VMEM((2 * n2, rows, nz), F32), pltpu.VMEM((2 * n2 + 6, out_rows, nz), F32)],
        name="coarse",
    )


def final(approx, left, right, detail, e_left, e_right, zs1, ys1, z_matrix, y_matrix, low_rows):
    planes, rows, half_z = approx.shape
    nx, ny, nz = detail.shape
    n1 = nx // 2
    n2 = n1 // 2
    step_rows = 16
    steps = ny // step_rows

    def kernel(a_ref, l_ref, r_ref, d_ref, el, er, z1, s1, z, y, out, total, parts, done, sems):
        stack = [p for ref in (l_ref, r_ref) for p in unpacked(ref[4 * rows :])]
        zed = times(jnp.concatenate(stack, axis=0), z1)
        spilled = [p[:rows] for p in in_pairs(s1, cut(zed, low_rows))]
        slot = lambda ref, i: ref[pl.ds(i * rows, rows)]
        for m in range(n1):
            terms = [(1.0, a_ref[m + 2])]
            for k, coef, source in (
                (0, 1.0, 0),
                (1, 1.0, 1),
                (2, THIRD_UP, 1),
                (n2 - 1, 1.0, 2),
                (n2 - 2, 1.0, 3),
                (n2 - 3, THIRD_DOWN, 3),
            ):
                if 0 <= m + 3 - 2 * k < 8:
                    terms.append((coef * H[m + 3 - 2 * k], spilled[source]))
            if m < 3:
                terms.append(((1.0, 1.0, THIRD_UP)[m], slot(l_ref, (2, 3, 3)[m])))
            if m >= n1 - 3:
                terms.append(((1.0, 1.0, THIRD_DOWN)[n1 - 1 - m], slot(r_ref, (2, 3, 3)[n1 - 1 - m])))
            total[m + 2] = added(terms)
        total[0] = a_ref[0] + slot(l_ref, 0)
        total[1] = a_ref[1] + slot(l_ref, 1)
        total[n1 + 2] = a_ref[n1 + 2] + slot(r_ref, 0)
        total[n1 + 3] = a_ref[n1 + 3] + slot(r_ref, 1)

        def body(first):
            zed = times(total[pl.ds(first, 4)].reshape(4 * rows, half_z), z)
            for j, plane in enumerate(cut(zed, rows)):
                parts[first + j] = left_times(y, plane)

        over_planes(planes, 4, body)

        def copy(i):
            at = pl.ds(pl.multiple_of(i * step_rows, step_rows), step_rows)
            return pltpu.make_async_copy(done.at[:, at], out.at[:, at], sems.at[i])

        def step(i, carry):
            for t in range(step_rows // 8):
                at = pl.ds(pl.multiple_of(i * step_rows + 8 * t, 8), 8)
                for lane in range(0, nz, 128):
                    lanes = pl.ds(lane, 128)
                    lows = {k: parts[k + 2, at, lanes] for k in range(-2, n1 + 2)}
                    for m in range(nx):
                        value = d_ref[m, at, lanes] + x_synth(m, lows, {})
                        if m < 3:
                            extra = el[(0, 1, 1)[m], at, lanes]
                            value += extra if m < 2 else THIRD_UP * extra
                        if m >= nx - 3:
                            extra = er[(0, 1, 1)[nx - 1 - m], at, lanes]
                            value += extra if m > nx - 3 else THIRD_DOWN * extra
                        done[m, at, lanes] = value
            copy(i).start()
            return carry

        lax.fori_loop(0, steps, step, 0)

        def finish(i, carry):
            copy(i).wait()
            return carry

        lax.fori_loop(0, steps, finish, 0)

    return pl.pallas_call(
        kernel,
        in_specs=[VMEM] * 10,
        out_specs=pl.BlockSpec(memory_space=pl.ANY),
        out_shape=shape(nx, ny, nz),
        scratch_shapes=[
            pltpu.VMEM((planes, rows, half_z), F32),
            pltpu.VMEM((planes, ny, nz), F32),
            pltpu.VMEM((nx, ny, nz), F32),
            pltpu.SemaphoreType.DMA((steps,)),
        ],
        name="final",
        cost_estimate=pl.CostEstimate(flops=8 * nx * ny * nz, bytes_accessed=8 * nx * ny * nz, transcendentals=0),
        compiler_params=pltpu.CompilerParams(vmem_limit_bytes=VMEM_BYTES),
    )(approx, left, right, detail, e_left, e_right, zs1, ys1, z_matrix, y_matrix)


def to_next(array, axis):
    size = lax.axis_size(axis)
    return lax.ppermute(array, axis, [(i, (i + 1) % size) for i in range(size)])


def to_previous(array, axis):
    size = lax.axis_size(axis)
    return lax.ppermute(array, axis, [((i + 1) % size, i) for i in range(size)])


def local(velocity, table, index):
    nx, ny, nz = velocity.shape
    y1, y2, y3 = ny // 2, ny // 4, ny // 8
    ghost = 24
    cells0 = list(range(-8, ny + 8))
    rows0 = up_to(y1 + 4, 8)
    ks0 = fill(list(range(y1)) + [-2, -1, y1, y1 + 1], rows0)
    cells1 = list(range(y1)) + list(range(-ghost, 0)) + list(range(y1, y1 + ghost))
    rows1 = up_to(y2 + 18, 8)
    low1 = fill(list(range(-9, y2 + 9)), rows1)
    high1 = fill(list(range(-3, y2 + 3)), up_to(y2 + 6, 8))
    ks2 = fill(list(range(-3, y3 + 3)), up_to(y3 + 6, 8))
    ya0 = from_left(analysis_rows(cells0, ks0, ks0))
    ys0_matrix = synthesis_rows(list(range(ny)), ks0, ks0)
    ys0 = from_left(ys0_matrix)
    ys0_low = from_left(ys0_matrix[:, :rows0])
    ya1 = from_left(analysis_rows(cells1, low1, high1))
    ys1 = from_left(synthesis_rows(ks0, low1, high1))
    ya2 = from_left(analysis_rows(low1, ks2, ks2))
    ys2 = from_left(synthesis_rows(low1, ks2, ks2))
    z0 = periodic(nz, nz)
    z1 = periodic(nz // 2, nz // 2)
    z2 = periodic(nz // 4, nz // 2)
    za0, zs0, zs0_low = from_right(z0), from_right(z0.T), from_right(z0.T[: nz // 2])
    za1, zs1 = from_right(z1), from_right(z1.T)
    za2, zs2 = from_right(z2), from_right(z2.T)

    x_up, x_down, y_up, y_down = first_messages(velocity)
    y_left = to_next(y_up, "gy")
    y_right = to_previous(y_down, "gy")
    x_left = to_next(x_up, "gx")
    x_right = to_previous(x_down, "gx")
    zed = depth(velocity, za0, 16, "depth_analysis")
    c_up, c_down = corner_messages(y_left, y_right)
    c_left = to_next(c_up, "gx")
    c_right = to_previous(c_down, "gx")
    bands = y_analysis(zed, y_left, y_right, za0, ya0)
    halo, approx, a_up, a_down = first_approx(
        bands, x_left, x_right, c_left, c_right, za0, ya0, y1, ghost
    )
    a_left = to_next(a_up, "gy")
    a_right = to_previous(a_down, "gy")
    coeffs = detail_bands(bands, halo, table, index)
    bands1, b_up, b_down = second_bands(approx, a_left, a_right, za1, ya1, rows1)
    b_left = to_next(b_up, "gx")
    b_right = to_previous(b_down, "gx")
    parts, e_up, e_down = detail_yz(coeffs, zs0, ys0)
    e_left = to_next(e_up, "gx")
    e_right = to_previous(e_down, "gx")
    approx1, s_up, s_down = coarse(
        bands1, b_left, b_right, table, index, zs1, za2, zs2, ya2, ys2, ys1, rows1, rows0
    )
    s_left = to_next(s_up, "gx")
    s_right = to_previous(s_down, "gx")
    detail = detail_x(parts)
    return final(
        approx1, s_left, s_right, detail, e_left, e_right, zs1, ys1, zs0_low, ys0_low, rows1
    )


def solution(mesh):
    return jax.shard_map(
        local,
        mesh=mesh,
        in_specs=(P("gx", "gy", None), P(), P()),
        out_specs=P("gx", "gy", None),
        check_vma=False,
    )
```

```python
import functools

import jax
import jax.numpy as jnp
import ml_dtypes
import numpy as np
from jax import lax
from jax.experimental import pallas as pl
from jax.experimental.pallas import tpu as pltpu
from jax.sharding import PartitionSpec as P

H = [
    0.23037781330885523,
    0.7148465705525415,
    0.6308807679295904,
    -0.02798376941698385,
    -0.18703481171888114,
    0.030841381835986965,
    0.032883011666982945,
    -0.010597401784997278,
]
G = [(-1.0) ** j * H[7 - j] for j in range(8)]
F32 = jnp.float32
BF16 = jnp.bfloat16
NOTHING = 3.0e38
VMEM_BYTES = 16 * 1024 * 1024


def tap(filt, j):
    return filt[j] if 0 <= j < 8 else 0.0


def analysis_rows(cells, low_ks, high_ks):
    matrix = np.zeros((len(low_ks) + len(high_ks), len(cells)))
    rows = [(H, k) for k in low_ks] + [(G, k) for k in high_ks]
    for row, (filt, k) in enumerate(rows):
        for col, cell in enumerate(cells):
            if k is not None and cell is not None:
                matrix[row, col] = tap(filt, cell - 2 * k + 3)
    return matrix


def synthesis_rows(cells, low_ks, high_ks):
    return analysis_rows(cells, low_ks, high_ks).T


def periodic(length, padded_to):
    matrix = np.zeros((padded_to, padded_to))
    for k in range(length // 2):
        for j in range(8):
            matrix[(2 * k + j - 3) % length, k] += H[j]
            matrix[(2 * k + j - 3) % length, length // 2 + k] += G[j]
    return matrix


def fill(items, length):
    return items + [None] * (length - len(items))


def up_to(count, step):
    return -(-count // step) * step


def pieces(matrix, axis):
    rows, cols = matrix.shape
    matrix = np.pad(matrix, ((0, up_to(rows, 16) - rows), (0, up_to(cols, 16) - cols))).astype(np.float32)
    high = matrix.astype(ml_dtypes.bfloat16)
    low = (matrix - high.astype(np.float32)).astype(ml_dtypes.bfloat16)
    return np.concatenate([high, high, low], axis=axis)


def from_left(matrix):
    return pieces(matrix, 1)


def from_right(matrix):
    return pieces(matrix, 0)


def halves(values):
    high = values.astype(BF16)
    return high, (values - high.astype(F32)).astype(BF16)


def times(values, matrix):
    high, low = halves(values)
    return jnp.dot(jnp.concatenate([high, low, high], axis=1), matrix[...], preferred_element_type=F32)


def left_times(matrix, values):
    missing = matrix.shape[1] // 3 - values.shape[0]
    if missing:
        values = jnp.concatenate([values, jnp.zeros((missing, values.shape[1]), F32)], axis=0)
    high, low = halves(values)
    return jnp.dot(matrix[...], jnp.concatenate([high, low, high], axis=0), preferred_element_type=F32)


def added(terms):
    total = None
    for coef, value in terms:
        part = value if coef == 1.0 else coef * value
        total = part if total is None else total + part
    return total


def x_terms(k, n):
    terms = []
    for j in range(8):
        cell = 2 * k + j - 3
        if 0 <= cell < n:
            terms.append((cell, H[j], G[j]))
        elif cell == -1:
            terms.append(("l1", H[j], G[j]))
        elif cell == n:
            terms.append(("r1", H[j], G[j]))
    if k == 0:
        terms.append(("l2", 1.0, G[0] / H[0]))
    if k == n // 2 - 1:
        terms.append(("r2", 1.0, G[6] / H[6]))
    return terms


def lattice():
    low = np.array(H).reshape(4, 2)
    high = np.array(G).reshape(4, 2)
    tangents = []
    for _ in range(3):
        t = (low[0] @ high[0]) / (high[0] @ high[0])
        tangents.append(float(t))
        low, high = (low - t * high)[1:] / (1 + t * t), (high + t * low)[:-1] / (1 + t * t)
    return low[0].tolist(), high[0].tolist(), tangents[::-1]


def x_interior(get, n):
    first, second, tangents = lattice()
    a, b = {}, {}
    for i in range(1, n // 2):
        x, y = get(2 * i - 1), get(2 * i)
        a[i] = first[0] * x + first[1] * y
        b[i] = second[0] * x + second[1] * y
    for t in tangents:
        shared = [i for i in a if i + 1 in a]
        a, b = {i: a[i + 1] + t * b[i] for i in shared}, {i: b[i] - t * a[i + 1] for i in shared}
    return {i + 1: (a[i], b[i]) for i in a}


def x_low(get, k, n):
    return added([(low, get(key)) for key, low, _ in x_terms(k, n)])


def x_high(get, k, n):
    return added([(high, get(key)) for key, _, high in x_terms(k, n)])


def x_synth(m, lows, highs):
    terms = [(H[m + 3 - 2 * k], v) for k, v in lows.items() if 0 <= m + 3 - 2 * k < 8]
    terms += [(G[m + 3 - 2 * k], v) for k, v in highs.items() if 0 <= m + 3 - 2 * k < 8]
    return added(terms)


def spill_up(low, high, n):
    first = added([(H[5], low[n - 1]), (G[5], high[n - 1]), (H[7], low[n - 2]), (G[7], high[n - 2])])
    return first, added([(H[6], low[n - 1]), (G[6], high[n - 1])])


def spill_down(low, high):
    first = added([(H[2], low[0]), (G[2], high[0]), (H[0], low[1]), (G[0], high[1])])
    return first, added([(H[1], low[0]), (G[1], high[0])])


THIRD_UP = H[7] / H[6]
THIRD_DOWN = H[0] / H[1]


def shrink(values, thresh):
    return values - jnp.minimum(jnp.maximum(values, -thresh), thresh)


def whole_call(kernel, out_shapes, args, flops, moved, scratch=(), name=None):
    specs = [SMEM if a.ndim == 1 or a.dtype == jnp.int32 else VMEM for a in args]
    outs = [VMEM] * len(out_shapes) if isinstance(out_shapes, list) else VMEM
    return pl.pallas_call(
        kernel,
        in_specs=specs,
        out_specs=outs,
        out_shape=out_shapes,
        scratch_shapes=list(scratch),
        name=name,
        cost_estimate=pl.CostEstimate(flops=int(flops), bytes_accessed=int(moved), transcendentals=0),
        compiler_params=pltpu.CompilerParams(vmem_limit_bytes=VMEM_BYTES),
    )(*args)


def call(kernel, grid, in_specs, out_specs, out_shapes, args, flops, moved, scratch=(), name=None):
    return pl.pallas_call(
        kernel,
        grid=grid,
        in_specs=in_specs,
        out_specs=out_specs,
        out_shape=out_shapes,
        scratch_shapes=list(scratch),
        name=name,
        cost_estimate=pl.CostEstimate(flops=int(flops), bytes_accessed=int(moved), transcendentals=0),
        compiler_params=pltpu.CompilerParams(vmem_limit_bytes=VMEM_BYTES),
    )(*args)


def shape(*dims):
    return jax.ShapeDtypeStruct(dims, F32)


def whole(array):
    dims = array.shape
    return pl.BlockSpec(dims, lambda *_: (0,) * len(dims))


def whole_out(*dims):
    return pl.BlockSpec(dims, lambda *_: (0,) * len(dims))


SMEM = pl.BlockSpec(memory_space=pltpu.SMEM)
VMEM = pl.BlockSpec(memory_space=pltpu.VMEM)


def x_messages(last, first, up, down):
    up[0] = last[3]
    up[1] = H[0] * last[1] + H[1] * last[2]
    down[0] = first[0]
    down[1] = H[6] * first[1] + H[7] * first[2]


def first_messages(v):
    nx, ny, nz = v.shape

    def kernel(last, first, y_last, y_first, up, down, y_up, y_down):
        x_messages(last, first, up, down)
        y_up[...] = y_last[...]
        y_down[...] = y_first[...]

    return call(
        kernel,
        (1,),
        [
            pl.BlockSpec((4, ny, nz), lambda i: (nx // 4 - 1, 0, 0)),
            pl.BlockSpec((4, ny, nz), lambda i: (0, 0, 0)),
            pl.BlockSpec((nx, 8, nz), lambda i: (0, ny // 8 - 1, 0)),
            pl.BlockSpec((nx, 8, nz), lambda i: (0, 0, 0)),
        ],
        [whole_out(2, ny, nz)] * 2 + [whole_out(nx, 8, nz)] * 2,
        [shape(2, ny, nz)] * 2 + [shape(nx, 8, nz)] * 2,
        [v] * 4,
        1e6,
        3e6,
        name="first_messages",
    )


def over_planes(count, group, body):
    def step(i, carry):
        body(i * group)
        return carry

    lax.fori_loop(0, count // group, step, 0)


def depth(v, z_matrix, group, name):
    nx, rows, nz = v.shape

    def kernel(v_ref, z, out):
        def body(first):
            at = pl.ds(first, group)
            out[at] = times(v_ref[at].reshape(group * rows, nz), z).reshape(group, rows, nz)

        over_planes(nx, group, body)

    return whole_call(
        kernel, shape(nx, rows, nz), [v, z_matrix], 6 * nx * rows * nz * nz, 8 * nx * rows * nz, name=name
    )


def y_analysis(zed, y_left, y_right, z_matrix, y_matrix):
    nx, ny, nz = zed.shape
    rows = y_matrix.shape[0]
    group = 8

    def kernel(zed_ref, left, right, z, y, out, left_z, right_z):
        left_z[...] = times(left[...].reshape(8 * nx, nz), z).reshape(nx, 8, nz)
        right_z[...] = times(right[...].reshape(8 * nx, nz), z).reshape(nx, 8, nz)

        def body(first):
            for j in range(group):
                i = first + j
                out[i] = left_times(y, jnp.concatenate([left_z[i], zed_ref[i], right_z[i]], axis=0))

        over_planes(nx, group, body)

    return whole_call(
        kernel,
        shape(nx, rows, nz),
        [zed, y_left, y_right, z_matrix, y_matrix],
        6 * nx * rows * (ny + 16) * nz,
        4 * nx * nz * (ny + rows + 16),
        scratch=[pltpu.VMEM((nx, 8, nz), F32)] * 2,
        name="y_analysis",
    )


def own_approx(bands, own, ghost_rows):
    nx, rows, nz = bands.shape
    half_z = nz // 2
    n1 = nx // 2

    def kernel(b_ref, approx, up, down):
        def tile(t, carry):
            at = pl.ds(pl.multiple_of(t * 8, 8), 8)
            values = {i: b_ref[i, at, :half_z] for i in range(nx)}
            for k in range(n1):
                approx[k, at] = added([(c, values[i]) for i, c, _ in x_terms(k, nx) if i in values])
            return carry

        lax.fori_loop(0, own // 8, tile, 0)
        up[...] = approx[:, own - ghost_rows :]
        down[...] = approx[:, :ghost_rows]

    return whole_call(
        kernel,
        [shape(n1, own, half_z), shape(n1, ghost_rows, half_z), shape(n1, ghost_rows, half_z)],
        [bands],
        16 * n1 * own * half_z,
        3e6,
        name="own_approx",
    )


def x_halo_messages(x_left, x_right, z_matrix, wide):
    _, ny, nz = x_left.shape
    half_z = nz // 2

    def kernel(xl, xr, z, out, up, down):
        planes = jnp.concatenate([xl[0], xl[1], xr[0], xr[1]], axis=0)
        out[...] = times(planes, z).reshape(4, ny, nz)
        up[:, :wide] = out[:, ny - wide :, :half_z]
        up[:, wide:] = out[:, ny - 8 :, half_z:]
        down[:, :wide] = out[:, :wide, :half_z]
        down[:, wide:] = out[:, :8, half_z:]

    return whole_call(
        kernel,
        [shape(4, ny, nz), shape(4, wide + 8, half_z), shape(4, wide + 8, half_z)],
        [x_left, x_right, z_matrix],
        24 * ny * nz * nz,
        3e6,
        name="x_halo_messages",
    )


def edges_of(n):
    return [0, 1, n - 2, n - 1]


def detail_bands(bands, halo, h_left, h_right, table, index, y_matrix):
    nx, rows, nz = bands.shape
    n1 = nx // 2
    half_z = nz // 2
    half_tiles = rows // 16
    wide = h_left.shape[1] - 8
    ends = edges_of(n1)
    inner = [k for k in range(n1) if k not in ends]

    def kernel(table_ref, index_ref, b_ref, x_ref, hl, hr, y, edge, rest, h_ref):
        for i in range(4):
            low = jnp.concatenate([hl[i, wide - 8 : wide], x_ref[i, :, :half_z], hr[i, :8]], axis=0)
            high = jnp.concatenate([hl[i, wide:], x_ref[i, :, half_z:], hr[i, wide:]], axis=0)
            h_ref[i] = left_times(y, jnp.concatenate([low, high], axis=1))
        place = {"l1": 0, "l2": 1, "r1": 2, "r2": 3}

        def tiles(by):
            def tile(t, carry):
                at = pl.ds(pl.multiple_of((t + by * half_tiles) * 8, 8), 8)
                for bz in range(2):
                    lanes = pl.ds(bz * half_z, half_z)
                    band = 2 * by + bz
                    quiet = table_ref[index_ref[0, band - 1]] if band else NOTHING
                    loud = table_ref[index_ref[0, band + 3]]
                    values = {key: h_ref[i, at, lanes] for key, i in place.items()}
                    values.update({i: b_ref[i, at, lanes] for i in range(nx)})
                    coeffs = x_interior(values.get, nx)
                    for k in ends:
                        coeffs[k] = (x_low(values.get, k, nx), x_high(values.get, k, nx))
                    for k, (low, high) in coeffs.items():
                        target, place_k, count = (edge, ends.index(k), 4) if k in ends else (rest, k - 2, n1 - 4)
                        target[place_k, at, lanes] = shrink(low, quiet) if band else jnp.zeros_like(low)
                        target[count + place_k, at, lanes] = shrink(high, loud)
                return carry

            return tile

        lax.fori_loop(0, half_tiles, tiles(0), 0)
        lax.fori_loop(0, half_tiles, tiles(1), 0)

    return whole_call(
        kernel,
        [shape(8, rows, nz), shape(2 * len(inner), rows, nz)],
        [table, index, bands, halo, h_left, h_right, y_matrix],
        40 * nx * rows * nz,
        8 * nx * rows * nz,
        scratch=[pltpu.VMEM((4, rows, nz), F32)],
        name="detail_bands",
    )


def yz_synthesis(coeffs, z, y, out, zed):
    count, rows, nz = coeffs.shape

    def z_body(first):
        at = pl.ds(first, 8)
        zed[at] = times(coeffs[at].reshape(8 * rows, nz), z).reshape(8, rows, nz)

    def y_body(first):
        for j in range(8):
            out[first + j] = left_times(y, zed[first + j])

    over_planes(count, 8, z_body)
    over_planes(count, 8, y_body)


def detail_edges(coeffs, z_matrix, y_matrix):
    count, rows, nz = coeffs.shape
    ny = y_matrix.shape[0]

    def kernel(c_ref, z, y, out, up, down, zed):
        yz_synthesis(c_ref, z, y, out, zed)
        part = lambda ks, at: {k: out[i] for k, i in zip(ks, at)}
        up[0], up[1] = spill_up(part((0, 1), (2, 3)), part((0, 1), (6, 7)), 2)
        down[0], down[1] = spill_down(part((0, 1), (0, 1)), part((0, 1), (4, 5)))

    return whole_call(
        kernel,
        [shape(count, ny, nz), shape(2, ny, nz), shape(2, ny, nz)],
        [coeffs, z_matrix, y_matrix],
        6 * count * rows * nz * (nz + ny),
        4 * count * nz * (rows + ny),
        scratch=[pltpu.VMEM((count, rows, nz), F32)],
        name="detail_edges",
    )


def detail_rest(coeffs, z_matrix, y_matrix):
    count, rows, nz = coeffs.shape
    ny = y_matrix.shape[0]
    return whole_call(
        yz_synthesis,
        shape(count, ny, nz),
        [coeffs, z_matrix, y_matrix],
        6 * count * rows * nz * (nz + ny),
        4 * count * nz * (rows + ny),
        scratch=[pltpu.VMEM((count, rows, nz), F32)],
        name="detail_rest",
    )


def detail_x(edge, rest):
    count, ny, nz = rest.shape
    n1 = (count + 8) // 2
    nx = 2 * n1
    ends = edges_of(n1)

    def kernel(e_ref, r_ref, out):
        def tile(t, carry):
            at = pl.ds(pl.multiple_of(t * 8, 8), 8)
            for lane in range(0, nz, 128):
                lanes = pl.ds(lane, 128)

                def coeff(k, high):
                    if k in ends:
                        return e_ref[4 * high + ends.index(k), at, lanes]
                    return r_ref[(n1 - 4) * high + k - 2, at, lanes]

                lows = {k: coeff(k, 0) for k in range(n1)}
                highs = {k: coeff(k, 1) for k in range(n1)}
                for m in range(nx):
                    out[m, at, lanes] = x_synth(m, lows, highs)
            return carry

        lax.fori_loop(0, ny // 8, tile, 0)

    return whole_call(
        kernel, shape(nx, ny, nz), [edge, rest], 16 * nx * ny * nz, 8 * nx * ny * nz, name="detail_x"
    )


def in_pairs(matrix, planes):
    results = []
    for i in range(0, len(planes), 2):
        both = left_times(matrix, jnp.concatenate(planes[i : i + 2], axis=1))
        width = both.shape[1] // 2
        results += [both[:, :width], both[:, width:]]
    return results


def cut(values, rows):
    return [values[i : i + rows] for i in range(0, values.shape[0], rows)]


def packed(first, second):
    half = first.shape[1] // 2
    lane = lax.broadcasted_iota(jnp.int32, first.shape, 1)
    return jnp.where(lane < half, first, pltpu.roll(second, half, 1))


def unpacked(both):
    half = both.shape[1] // 2
    lane = lax.broadcasted_iota(jnp.int32, both.shape, 1)
    return [jnp.where(lane < half, part, 0.0) for part in (both, pltpu.roll(both, half, 1))]


def second_bands(own, left, right, halo, h_left, h_right, z_matrix, yx_matrix, y_matrix, low_rows):
    n1, own_rows, nz = own.shape
    in_rows = own_rows + 2 * left.shape[1]
    rows = y_matrix.shape[0]

    wide = h_left.shape[1] - 8

    def kernel(o_ref, l_ref, r_ref, x_ref, hl, hr, z, yx, y, out, up, down):
        planes = [jnp.concatenate([hl[i, :wide], x_ref[i, :, :nz], hr[i, :wide]], axis=0) for i in range(4)]
        l1, l2, r1, r2 = [plane[:in_rows] for plane in in_pairs(yx, planes)]
        beyond = {
            0: l2 + H[2] * l1,
            1: H[0] * l1,
            n1 - 2: H[7] * r1,
            n1 - 1: r2 + H[5] * r1,
        }
        for i in range(0, n1, 8):
            stack = []
            for j in range(i, i + 8):
                plane = jnp.concatenate([o_ref[j], l_ref[j], r_ref[j]], axis=0)
                stack.append(plane + beyond[j] if j in beyond else plane)
            zed = times(jnp.concatenate(stack, axis=0), z)
            for j, plane in enumerate(in_pairs(y, cut(zed, in_rows))):
                out[i + j] = plane
        low = lambda c: out[c, :low_rows]
        up[0:rows] = out[n1 - 1]
        up[rows : 2 * rows] = H[0] * out[n1 - 3] + H[1] * out[n1 - 2]
        first = added([(H[j], low(n1 - 5 + j)) for j in range(5)])
        second = added([(H[0] * H[j], low(n1 - 9 + j)) for j in range(8)])
        second += added([(H[1] * H[j], low(n1 - 7 + j)) for j in range(7)])
        up[2 * rows :] = packed(first, second)
        down[0:rows] = out[0]
        down[rows : 2 * rows] = H[6] * out[1] + H[7] * out[2]
        first = added([(H[j], low(j - 3)) for j in range(3, 8)])
        second = added([(H[6] * H[j], low(j - 1)) for j in range(1, 8)])
        second += added([(H[7] * H[j], low(j + 1)) for j in range(8)])
        down[2 * rows :] = packed(first, second)

    message = 2 * rows + low_rows
    return whole_call(
        kernel,
        [shape(n1, rows, nz), shape(message, nz), shape(message, nz)],
        [own, left, right, halo, h_left, h_right, z_matrix, yx_matrix, y_matrix],
        6 * n1 * in_rows * nz * (nz + rows),
        4 * n1 * nz * (in_rows + rows),
        name="second_bands",
    )


def limits_plane(table_ref, index_ref, level, bx, dims, row_split, lane_split, zeroth):
    row_high = lax.broadcasted_iota(jnp.int32, dims, 0) >= row_split
    lane_high = lax.broadcasted_iota(jnp.int32, dims, 1) >= lane_split

    def limit(by, bz):
        band = 4 * bx + 2 * by + bz
        return zeroth if band == 0 else table_ref[index_ref[level, band - 1]]

    low_y = jnp.where(lane_high, limit(0, 1), limit(0, 0))
    return jnp.where(row_high, jnp.where(lane_high, limit(1, 1), limit(1, 0)), low_y)


def coarse(bands, left, right, table, index, zs1, za2, zs2, ya2, ys2, ys1, low_rows, out_rows):
    n1, rows, nz = bands.shape
    n2, n3 = n1 // 2, n1 // 4
    rows2 = ya2.shape[0]
    lane_half = nz // 2

    def kernel(table_ref, index_ref, b_ref, l_ref, r_ref, z1, z2a, z2s, a2, s2, s1, approx, up, down, c1, p1):
        sides = {
            "l1": lambda: l_ref[0:rows],
            "l2": lambda: l_ref[rows : 2 * rows],
            "r1": lambda: r_ref[0:rows],
            "r2": lambda: r_ref[rows : 2 * rows],
        }
        get = lambda key: sides[key]() if isinstance(key, str) else b_ref[key]
        low_part = lambda c: b_ref[c, :low_rows]
        dims = (rows, nz)
        quiet = limits_plane(table_ref, index_ref, 1, 0, dims, low_rows, lane_half, NOTHING)
        loud = limits_plane(table_ref, index_ref, 1, 1, dims, low_rows, lane_half, NOTHING)
        planes = []
        for k in range(n2):
            low = x_low(get, k, n1)
            planes.append(low[:low_rows])
            c1[k] = shrink(low, quiet)
            c1[n2 + k] = shrink(x_high(get, k, n1), loud)
        first, second = unpacked(l_ref[2 * rows :])
        planes.append(first + added([(H[5 + i], low_part(i)) for i in range(3)]))
        planes.append(second + H[1] * H[7] * low_part(0))
        first, second = unpacked(r_ref[2 * rows :])
        planes.append(first + added([(H[i], low_part(n1 - 3 + i)) for i in range(3)]))
        planes.append(second + H[6] * H[0] * low_part(n1 - 1))
        third = in_pairs(a2, cut(times(jnp.concatenate(planes, axis=0), z2a), low_rows))
        keys = {"l1": n2, "l2": n2 + 1, "r1": n2 + 2, "r2": n2 + 3}
        get2 = lambda key: third[keys.get(key, key)]
        dims = (rows2, nz)
        quiet = limits_plane(table_ref, index_ref, 2, 0, dims, rows2 // 2, lane_half // 2, 0.0)
        loud = limits_plane(table_ref, index_ref, 2, 1, dims, rows2 // 2, lane_half // 2, 0.0)
        kept = [shrink(x_low(get2, k, n2), quiet) for k in range(n3)]
        kept += [shrink(x_high(get2, k, n2), loud) for k in range(n3)]
        parts = in_pairs(s2, cut(times(jnp.concatenate(kept, axis=0), z2s), rows2))
        parts = [part[:low_rows] for part in parts]
        lows = dict(enumerate(parts[:n3]))
        highs = dict(enumerate(parts[n3:]))
        ghosts = [-3, -2, -1, n2, n2 + 1, n2 + 2]
        for k in range(n2):
            c1[k, :low_rows] += x_synth(k, lows, highs)
        stack = [x_synth(k, lows, highs) for k in ghosts]
        beyond = dict(zip(ghosts, stack))
        zed = times(jnp.concatenate(stack, axis=0), z1)
        for i, plane in enumerate(in_pairs(s1, cut(zed, low_rows))):
            p1[2 * n2 + i] = plane[:out_rows]
        for i in range(0, 2 * n2, 8):
            zed = times(c1[i : i + 8].reshape(8 * rows, nz), z1)
            for j, plane in enumerate(in_pairs(s1, cut(zed, rows))):
                p1[i + j] = plane[:out_rows]
        lows = {k: p1.at[k] for k in range(n2)}
        highs = {k: p1.at[n2 + k] for k in range(n2)}
        for i, k in enumerate(ghosts):
            lows[k] = p1.at[2 * n2 + i]

        def cell(m):
            near = lambda part: {k: ref[...] for k, ref in part.items() if 0 <= m + 3 - 2 * k < 8}
            return x_synth(m, near(lows), near(highs))

        for m in range(-2, n1 + 2):
            approx[m + 2] = cell(m)
        value = lambda part, ks: {k: part[k][...] for k in ks}
        ends = (n2 - 2, n2 - 1)
        slot = lambda i: pl.ds(i * out_rows, out_rows)
        up[slot(0)], up[slot(1)] = approx[n1], approx[n1 + 1]
        up[slot(2)], up[slot(3)] = spill_up(value(lows, ends), value(highs, ends), n2)
        up[4 * out_rows :] = packed(beyond[n2], beyond[n2 + 1])
        down[slot(0)], down[slot(1)] = approx[2], approx[3]
        down[slot(2)], down[slot(3)] = spill_down(value(lows, (0, 1)), value(highs, (0, 1)))
        down[4 * out_rows :] = packed(beyond[-1], beyond[-2])

    message = 4 * out_rows + low_rows
    return whole_call(
        kernel,
        [shape(n1 + 4, out_rows, nz), shape(message, nz), shape(message, nz)],
        [table, index, bands, left, right, zs1, za2, zs2, ya2, ys2, ys1],
        1.5e9,
        8 * n1 * rows * nz,
        scratch=[pltpu.VMEM((2 * n2, rows, nz), F32), pltpu.VMEM((2 * n2 + 6, out_rows, nz), F32)],
        name="coarse",
    )


def final(approx, left, right, detail, e_left, e_right, zs1, ys1, z_matrix, y_matrix, low_rows):
    planes, rows, half_z = approx.shape
    nx, ny, nz = detail.shape
    n1 = nx // 2
    n2 = n1 // 2
    step_rows = 16
    steps = ny // step_rows

    def kernel(a_ref, l_ref, r_ref, d_ref, el, er, z1, s1, z, y, out, total, parts, done, sems):
        stack = [p for ref in (l_ref, r_ref) for p in unpacked(ref[4 * rows :])]
        zed = times(jnp.concatenate(stack, axis=0), z1)
        spilled = [p[:rows] for p in in_pairs(s1, cut(zed, low_rows))]
        slot = lambda ref, i: ref[pl.ds(i * rows, rows)]
        for m in range(n1):
            terms = [(1.0, a_ref[m + 2])]
            for k, coef, source in (
                (0, 1.0, 0),
                (1, 1.0, 1),
                (2, THIRD_UP, 1),
                (n2 - 1, 1.0, 2),
                (n2 - 2, 1.0, 3),
                (n2 - 3, THIRD_DOWN, 3),
            ):
                if 0 <= m + 3 - 2 * k < 8:
                    terms.append((coef * H[m + 3 - 2 * k], spilled[source]))
            if m < 3:
                terms.append(((1.0, 1.0, THIRD_UP)[m], slot(l_ref, (2, 3, 3)[m])))
            if m >= n1 - 3:
                terms.append(((1.0, 1.0, THIRD_DOWN)[n1 - 1 - m], slot(r_ref, (2, 3, 3)[n1 - 1 - m])))
            total[m + 2] = added(terms)
        total[0] = a_ref[0] + slot(l_ref, 0)
        total[1] = a_ref[1] + slot(l_ref, 1)
        total[n1 + 2] = a_ref[n1 + 2] + slot(r_ref, 0)
        total[n1 + 3] = a_ref[n1 + 3] + slot(r_ref, 1)

        def body(first):
            zed = times(total[pl.ds(first, 4)].reshape(4 * rows, half_z), z)
            for j, plane in enumerate(cut(zed, rows)):
                parts[first + j] = left_times(y, plane)

        over_planes(planes, 4, body)

        def copy(i):
            at = pl.ds(pl.multiple_of(i * step_rows, step_rows), step_rows)
            return pltpu.make_async_copy(done.at[:, at], out.at[:, at], sems.at[i])

        def step(i, carry):
            for t in range(step_rows // 8):
                at = pl.ds(pl.multiple_of(i * step_rows + 8 * t, 8), 8)
                for lane in range(0, nz, 128):
                    lanes = pl.ds(lane, 128)
                    lows = {k: parts[k + 2, at, lanes] for k in range(-2, n1 + 2)}
                    for m in range(nx):
                        value = d_ref[m, at, lanes] + x_synth(m, lows, {})
                        if m < 3:
                            extra = el[(0, 1, 1)[m], at, lanes]
                            value += extra if m < 2 else THIRD_UP * extra
                        if m >= nx - 3:
                            extra = er[(0, 1, 1)[nx - 1 - m], at, lanes]
                            value += extra if m > nx - 3 else THIRD_DOWN * extra
                        done[m, at, lanes] = value
            copy(i).start()
            return carry

        lax.fori_loop(0, steps, step, 0)

        def finish(i, carry):
            copy(i).wait()
            return carry

        lax.fori_loop(0, steps, finish, 0)

    return pl.pallas_call(
        kernel,
        in_specs=[VMEM] * 10,
        out_specs=pl.BlockSpec(memory_space=pl.ANY),
        out_shape=shape(nx, ny, nz),
        scratch_shapes=[
            pltpu.VMEM((planes, rows, half_z), F32),
            pltpu.VMEM((planes, ny, nz), F32),
            pltpu.VMEM((nx, ny, nz), F32),
            pltpu.SemaphoreType.DMA((steps,)),
        ],
        name="final",
        cost_estimate=pl.CostEstimate(flops=8 * nx * ny * nz, bytes_accessed=8 * nx * ny * nz, transcendentals=0),
        compiler_params=pltpu.CompilerParams(vmem_limit_bytes=VMEM_BYTES),
    )(approx, left, right, detail, e_left, e_right, zs1, ys1, z_matrix, y_matrix)


def to_next(array, axis):
    size = lax.axis_size(axis)
    return lax.ppermute(array, axis, [(i, (i + 1) % size) for i in range(size)])


def to_previous(array, axis):
    size = lax.axis_size(axis)
    return lax.ppermute(array, axis, [((i + 1) % size, i) for i in range(size)])


def local(velocity, table, index):
    nx, ny, nz = velocity.shape
    y1, y2, y3 = ny // 2, ny // 4, ny // 8
    ghost, wide = 24, 48
    cells0 = list(range(-8, ny + 8))
    rows0 = up_to(y1 + 4, 8)
    ks0 = fill(list(range(y1)) + [-2, -1, y1, y1 + 1], rows0)
    cells1 = list(range(y1)) + list(range(-ghost, 0)) + list(range(y1, y1 + ghost))
    rows1 = up_to(y2 + 18, 8)
    low1 = fill(list(range(-9, y2 + 9)), rows1)
    high1 = fill(list(range(-3, y2 + 3)), up_to(y2 + 6, 8))
    ks2 = fill(list(range(-3, y3 + 3)), up_to(y3 + 6, 8))
    ya0 = from_left(analysis_rows(cells0, ks0, ks0))
    ys0_matrix = synthesis_rows(list(range(ny)), ks0, ks0)
    ys0 = from_left(ys0_matrix)
    ys0_low = from_left(ys0_matrix[:, :rows0])
    yx0 = from_left(analysis_rows(list(range(-wide, ny + wide)), cells1, []))
    ya1 = from_left(analysis_rows(cells1, low1, high1))
    ys1 = from_left(synthesis_rows(ks0, low1, high1))
    ya2 = from_left(analysis_rows(low1, ks2, ks2))
    ys2 = from_left(synthesis_rows(low1, ks2, ks2))
    z0 = periodic(nz, nz)
    z1 = periodic(nz // 2, nz // 2)
    z2 = periodic(nz // 4, nz // 2)
    za0, zs0, zs0_low = from_right(z0), from_right(z0.T), from_right(z0.T[: nz // 2])
    za1, zs1 = from_right(z1), from_right(z1.T)
    za2, zs2 = from_right(z2), from_right(z2.T)

    x_up, x_down, y_up, y_down = first_messages(velocity)
    x_left = to_next(x_up, "gx")
    x_right = to_previous(x_down, "gx")
    y_left = to_next(y_up, "gy")
    y_right = to_previous(y_down, "gy")
    zed = depth(velocity, za0, 16, "depth_analysis")
    bands = y_analysis(zed, y_left, y_right, za0, ya0)
    approx, a_up, a_down = own_approx(bands, y1, ghost)
    a_left = to_next(a_up, "gy")
    a_right = to_previous(a_down, "gy")
    halo, h_up, h_down = x_halo_messages(x_left, x_right, za0, wide)
    h_left = to_next(h_up, "gy")
    h_right = to_previous(h_down, "gy")
    bands1, b_up, b_down = second_bands(
        approx, a_left, a_right, halo, h_left, h_right, za1, yx0, ya1, rows1
    )
    b_left = to_next(b_up, "gx")
    b_right = to_previous(b_down, "gx")
    h_left, h_right, bands1 = lax.optimization_barrier((h_left, h_right, bands1))
    edge, rest = detail_bands(bands, halo, h_left, h_right, table, index, ya0)
    edge, e_up, e_down = detail_edges(edge, zs0, ys0)
    e_left = to_next(e_up, "gx")
    e_right = to_previous(e_down, "gx")
    bands1, edge = lax.optimization_barrier((bands1, edge))
    approx1, s_up, s_down = coarse(
        bands1, b_left, b_right, table, index, zs1, za2, zs2, ya2, ys2, ys1, rows1, rows0
    )
    s_left = to_next(s_up, "gx")
    s_right = to_previous(s_down, "gx")
    rest, approx1 = lax.optimization_barrier((rest, approx1))
    detail = detail_x(edge, detail_rest(rest, zs0, ys0))
    return final(
        approx1, s_left, s_right, detail, e_left, e_right, zs1, ys1, zs0_low, ys0_low, rows1
    )


def solution(mesh):
    return jax.shard_map(
        local,
        mesh=mesh,
        in_specs=(P("gx", "gy", None), P(), P()),
        out_specs=P("gx", "gy", None),
        check_vma=False,
    )
```

```python
import functools

import jax
import jax.numpy as jnp
import ml_dtypes
import numpy as np
from jax import lax
from jax.experimental import pallas as pl
from jax.experimental.pallas import tpu as pltpu
from jax.sharding import PartitionSpec as P

H = [
    0.23037781330885523,
    0.7148465705525415,
    0.6308807679295904,
    -0.02798376941698385,
    -0.18703481171888114,
    0.030841381835986965,
    0.032883011666982945,
    -0.010597401784997278,
]
G = [(-1.0) ** j * H[7 - j] for j in range(8)]
F32 = jnp.float32
BF16 = jnp.bfloat16
NOTHING = 3.0e38
VMEM_BYTES = 16 * 1024 * 1024


def tap(filt, j):
    return filt[j] if 0 <= j < 8 else 0.0


def analysis_rows(cells, low_ks, high_ks):
    matrix = np.zeros((len(low_ks) + len(high_ks), len(cells)))
    rows = [(H, k) for k in low_ks] + [(G, k) for k in high_ks]
    for row, (filt, k) in enumerate(rows):
        for col, cell in enumerate(cells):
            if k is not None and cell is not None:
                matrix[row, col] = tap(filt, cell - 2 * k + 3)
    return matrix


def synthesis_rows(cells, low_ks, high_ks):
    return analysis_rows(cells, low_ks, high_ks).T


def periodic(length, padded_to):
    matrix = np.zeros((padded_to, padded_to))
    for k in range(length // 2):
        for j in range(8):
            matrix[(2 * k + j - 3) % length, k] += H[j]
            matrix[(2 * k + j - 3) % length, length // 2 + k] += G[j]
    return matrix


def fill(items, length):
    return items + [None] * (length - len(items))


def up_to(count, step):
    return -(-count // step) * step


def pieces(matrix, axis):
    rows, cols = matrix.shape
    matrix = np.pad(matrix, ((0, up_to(rows, 16) - rows), (0, up_to(cols, 16) - cols))).astype(np.float32)
    high = matrix.astype(ml_dtypes.bfloat16)
    low = (matrix - high.astype(np.float32)).astype(ml_dtypes.bfloat16)
    return np.concatenate([high, high, low], axis=axis)


def from_left(matrix):
    return pieces(matrix, 1)


def from_right(matrix):
    return pieces(matrix, 0)


def halves(values):
    high = values.astype(BF16)
    return high, (values - high.astype(F32)).astype(BF16)


def times(values, matrix):
    high, low = halves(values)
    return jnp.dot(jnp.concatenate([high, low, high], axis=1), matrix[...], preferred_element_type=F32)


def left_times(matrix, values):
    missing = matrix.shape[1] // 3 - values.shape[0]
    if missing:
        values = jnp.concatenate([values, jnp.zeros((missing, values.shape[1]), F32)], axis=0)
    high, low = halves(values)
    return jnp.dot(matrix[...], jnp.concatenate([high, low, high], axis=0), preferred_element_type=F32)


def added(terms):
    total = None
    for coef, value in terms:
        part = value if coef == 1.0 else coef * value
        total = part if total is None else total + part
    return total


def x_terms(k, n):
    terms = []
    for j in range(8):
        cell = 2 * k + j - 3
        if 0 <= cell < n:
            terms.append((cell, H[j], G[j]))
        elif cell == -1:
            terms.append(("l1", H[j], G[j]))
        elif cell == n:
            terms.append(("r1", H[j], G[j]))
    if k == 0:
        terms.append(("l2", 1.0, G[0] / H[0]))
    if k == n // 2 - 1:
        terms.append(("r2", 1.0, G[6] / H[6]))
    return terms


def lattice():
    low = np.array(H).reshape(4, 2)
    high = np.array(G).reshape(4, 2)
    tangents = []
    for _ in range(3):
        t = (low[0] @ high[0]) / (high[0] @ high[0])
        tangents.append(float(t))
        low, high = (low - t * high)[1:] / (1 + t * t), (high + t * low)[:-1] / (1 + t * t)
    return low[0].tolist(), high[0].tolist(), tangents[::-1]


def x_interior(get, n):
    first, second, tangents = lattice()
    a, b = {}, {}
    for i in range(1, n // 2):
        x, y = get(2 * i - 1), get(2 * i)
        a[i] = first[0] * x + first[1] * y
        b[i] = second[0] * x + second[1] * y
    for t in tangents:
        shared = [i for i in a if i + 1 in a]
        a, b = {i: a[i + 1] + t * b[i] for i in shared}, {i: b[i] - t * a[i + 1] for i in shared}
    return {i + 1: (a[i], b[i]) for i in a}


def x_low(get, k, n):
    return added([(low, get(key)) for key, low, _ in x_terms(k, n)])


def x_high(get, k, n):
    return added([(high, get(key)) for key, _, high in x_terms(k, n)])


def x_synth(m, lows, highs):
    terms = [(H[m + 3 - 2 * k], v) for k, v in lows.items() if 0 <= m + 3 - 2 * k < 8]
    terms += [(G[m + 3 - 2 * k], v) for k, v in highs.items() if 0 <= m + 3 - 2 * k < 8]
    return added(terms)


def spill_up(low, high, n):
    first = added([(H[5], low[n - 1]), (G[5], high[n - 1]), (H[7], low[n - 2]), (G[7], high[n - 2])])
    return first, added([(H[6], low[n - 1]), (G[6], high[n - 1])])


def spill_down(low, high):
    first = added([(H[2], low[0]), (G[2], high[0]), (H[0], low[1]), (G[0], high[1])])
    return first, added([(H[1], low[0]), (G[1], high[0])])


THIRD_UP = H[7] / H[6]
THIRD_DOWN = H[0] / H[1]


def shrink(values, thresh):
    return values - jnp.minimum(jnp.maximum(values, -thresh), thresh)


def whole_call(kernel, out_shapes, args, flops, moved, scratch=(), name=None):
    specs = [SMEM if a.ndim == 1 or a.dtype == jnp.int32 else VMEM for a in args]
    outs = [VMEM] * len(out_shapes) if isinstance(out_shapes, list) else VMEM
    return pl.pallas_call(
        kernel,
        in_specs=specs,
        out_specs=outs,
        out_shape=out_shapes,
        scratch_shapes=list(scratch),
        name=name,
        cost_estimate=pl.CostEstimate(flops=int(flops), bytes_accessed=int(moved), transcendentals=0),
        compiler_params=pltpu.CompilerParams(vmem_limit_bytes=VMEM_BYTES),
    )(*args)


def shape(*dims):
    return jax.ShapeDtypeStruct(dims, F32)


SMEM = pl.BlockSpec(memory_space=pltpu.SMEM)
VMEM = pl.BlockSpec(memory_space=pltpu.VMEM)


def first_messages(v):
    nx, ny, nz = v.shape

    def kernel(v_ref, up, down, y_up, y_down, last, first, sems):
        copies = [
            pltpu.make_async_copy(source, target, sems.at[i])
            for i, (source, target) in enumerate(
                (
                    (v_ref.at[pl.ds(nx - 3, 3)], last),
                    (v_ref.at[pl.ds(0, 3)], first),
                    (v_ref.at[:, pl.ds(ny - 8, 8)], y_up),
                    (v_ref.at[:, pl.ds(0, 8)], y_down),
                )
            )
        ]
        for copy in copies:
            copy.start()
        for copy in copies:
            copy.wait()
        up[0] = last[2]
        up[1] = H[0] * last[0] + H[1] * last[1]
        down[0] = first[0]
        down[1] = H[6] * first[1] + H[7] * first[2]

    return pl.pallas_call(
        kernel,
        in_specs=[pl.BlockSpec(memory_space=pltpu.HBM)],
        out_specs=[VMEM] * 4,
        out_shape=[shape(2, ny, nz)] * 2 + [shape(nx, 8, nz)] * 2,
        scratch_shapes=[pltpu.VMEM((3, ny, nz), F32)] * 2 + [pltpu.SemaphoreType.DMA((4,))],
        name="first_messages",
        cost_estimate=pl.CostEstimate(flops=1000000, bytes_accessed=3000000, transcendentals=0),
        compiler_params=pltpu.CompilerParams(vmem_limit_bytes=50 * 1024 * 1024),
    )(v)


def over_planes(count, group, body):
    def step(i, carry):
        body(i * group)
        return carry

    lax.fori_loop(0, count // group, step, 0)


def depth(v, z_matrix, group, name):
    nx, rows, nz = v.shape

    def kernel(v_ref, z, out):
        def body(first):
            at = pl.ds(first, group)
            out[at] = times(v_ref[at].reshape(group * rows, nz), z).reshape(group, rows, nz)

        over_planes(nx, group, body)

    return whole_call(
        kernel, shape(nx, rows, nz), [v, z_matrix], 6 * nx * rows * nz * nz, 8 * nx * rows * nz, name=name
    )


def y_analysis(zed, y_left, y_right, z_matrix, y_matrix):
    nx, ny, nz = zed.shape
    rows = y_matrix.shape[0]
    group = 8

    def kernel(zed_ref, left, right, z, y, out, left_z, right_z):
        left_z[...] = times(left[...].reshape(8 * nx, nz), z).reshape(nx, 8, nz)
        right_z[...] = times(right[...].reshape(8 * nx, nz), z).reshape(nx, 8, nz)

        def body(first):
            for j in range(group):
                i = first + j
                out[i] = left_times(y, jnp.concatenate([left_z[i], zed_ref[i], right_z[i]], axis=0))

        over_planes(nx, group, body)

    return whole_call(
        kernel,
        shape(nx, rows, nz),
        [zed, y_left, y_right, z_matrix, y_matrix],
        6 * nx * rows * (ny + 16) * nz,
        4 * nx * nz * (ny + rows + 16),
        scratch=[pltpu.VMEM((nx, 8, nz), F32)] * 2,
        name="y_analysis",
    )


def own_approx(bands, own, ghost_rows):
    nx, rows, nz = bands.shape
    half_z = nz // 2
    n1 = nx // 2

    def kernel(b_ref, approx, up, down):
        def tile(t, carry):
            at = pl.ds(pl.multiple_of(t * 8, 8), 8)
            values = {i: b_ref[i, at, :half_z] for i in range(nx)}
            for k in range(n1):
                approx[k, at] = added([(c, values[i]) for i, c, _ in x_terms(k, nx) if i in values])
            return carry

        lax.fori_loop(0, own // 8, tile, 0)
        up[...] = approx[:, own - ghost_rows :]
        down[...] = approx[:, :ghost_rows]

    return whole_call(
        kernel,
        [shape(n1, own, half_z), shape(n1, ghost_rows, half_z), shape(n1, ghost_rows, half_z)],
        [bands],
        16 * n1 * own * half_z,
        3e6,
        name="own_approx",
    )


def x_halo_messages(x_left, x_right, z_matrix, wide):
    _, ny, nz = x_left.shape
    half_z = nz // 2

    def kernel(xl, xr, z, out, up, down):
        planes = jnp.concatenate([xl[0], xl[1], xr[0], xr[1]], axis=0)
        out[...] = times(planes, z).reshape(4, ny, nz)
        up[:, :wide] = out[:, ny - wide :, :half_z]
        up[:, wide:] = out[:, ny - 8 :, half_z:]
        down[:, :wide] = out[:, :wide, :half_z]
        down[:, wide:] = out[:, :8, half_z:]

    return whole_call(
        kernel,
        [shape(4, ny, nz), shape(4, wide + 8, half_z), shape(4, wide + 8, half_z)],
        [x_left, x_right, z_matrix],
        24 * ny * nz * nz,
        3e6,
        name="x_halo_messages",
    )


def edges_of(n):
    return [0, 1, n - 2, n - 1]


def band_limits(table_ref, index_ref, by, bz):
    band = 2 * by + bz
    quiet = table_ref[index_ref[0, band - 1]] if band else NOTHING
    return quiet, table_ref[index_ref[0, band + 3]]


def over_tiles(rows, nz, body):
    half_z, half_tiles = nz // 2, rows // 16
    for by in range(2):

        def tile(t, carry, by=by):
            at = pl.ds(pl.multiple_of((t + by * half_tiles) * 8, 8), 8)
            for bz in range(2):
                body(at, pl.ds(bz * half_z, half_z), by, bz)
            return carry

        lax.fori_loop(0, half_tiles, tile, 0)


def inner_bands(bands, table, index):
    nx, rows, nz = bands.shape
    count = nx // 2 - 4

    def kernel(table_ref, index_ref, b_ref, out):
        def body(at, lanes, by, bz):
            quiet, loud = band_limits(table_ref, index_ref, by, bz)
            values = {i: b_ref[i, at, lanes] for i in range(nx)}
            for k, (low, high) in x_interior(values.get, nx).items():
                out[k - 2, at, lanes] = shrink(low, quiet) if by + bz else jnp.zeros_like(low)
                out[count + k - 2, at, lanes] = shrink(high, loud)

        over_tiles(rows, nz, body)

    return whole_call(
        kernel,
        shape(2 * count, rows, nz),
        [table, index, bands],
        30 * nx * rows * nz,
        8 * nx * rows * nz,
        name="inner_bands",
    )


def edge_bands(bands, halo, h_left, h_right, table, index, y_matrix):
    nx, rows, nz = bands.shape
    n1 = nx // 2
    half_z = nz // 2
    wide = h_left.shape[1] - 8
    ends = edges_of(n1)

    def kernel(table_ref, index_ref, b_ref, x_ref, hl, hr, y, out, h_ref):
        for i in range(4):
            low = jnp.concatenate([hl[i, wide - 8 : wide], x_ref[i, :, :half_z], hr[i, :8]], axis=0)
            high = jnp.concatenate([hl[i, wide:], x_ref[i, :, half_z:], hr[i, wide:]], axis=0)
            h_ref[i] = left_times(y, jnp.concatenate([low, high], axis=1))
        place = {"l1": 0, "l2": 1, "r1": 2, "r2": 3}

        def body(at, lanes, by, bz):
            quiet, loud = band_limits(table_ref, index_ref, by, bz)
            values = {key: h_ref[i, at, lanes] for key, i in place.items()}
            values.update({i: b_ref[i, at, lanes] for i in [*range(7), *range(nx - 7, nx)]})
            for i, k in enumerate(ends):
                low, high = x_low(values.get, k, nx), x_high(values.get, k, nx)
                out[i, at, lanes] = shrink(low, quiet) if by + bz else jnp.zeros_like(low)
                out[4 + i, at, lanes] = shrink(high, loud)

        over_tiles(rows, nz, body)

    return whole_call(
        kernel,
        shape(8, rows, nz),
        [table, index, bands, halo, h_left, h_right, y_matrix],
        20 * nx * rows * nz,
        4 * nx * rows * nz,
        scratch=[pltpu.VMEM((4, rows, nz), F32)],
        name="edge_bands",
    )


def yz_synthesis(coeffs, z, y, out, zed):
    count, rows, nz = coeffs.shape

    def z_body(first):
        at = pl.ds(first, 8)
        zed[at] = times(coeffs[at].reshape(8 * rows, nz), z).reshape(8, rows, nz)

    def y_body(first):
        for j in range(8):
            out[first + j] = left_times(y, zed[first + j])

    over_planes(count, 8, z_body)
    over_planes(count, 8, y_body)


def detail_edges(coeffs, z_matrix, y_matrix):
    count, rows, nz = coeffs.shape
    ny = y_matrix.shape[0]

    def kernel(c_ref, z, y, out, up, down, zed):
        yz_synthesis(c_ref, z, y, out, zed)
        part = lambda ks, at: {k: out[i] for k, i in zip(ks, at)}
        up[0], up[1] = spill_up(part((0, 1), (2, 3)), part((0, 1), (6, 7)), 2)
        down[0], down[1] = spill_down(part((0, 1), (0, 1)), part((0, 1), (4, 5)))

    return whole_call(
        kernel,
        [shape(count, ny, nz), shape(2, ny, nz), shape(2, ny, nz)],
        [coeffs, z_matrix, y_matrix],
        6 * count * rows * nz * (nz + ny),
        4 * count * nz * (rows + ny),
        scratch=[pltpu.VMEM((count, rows, nz), F32)],
        name="detail_edges",
    )


def detail_rest(coeffs, z_matrix, y_matrix):
    count, rows, nz = coeffs.shape
    ny = y_matrix.shape[0]
    return whole_call(
        yz_synthesis,
        shape(count, ny, nz),
        [coeffs, z_matrix, y_matrix],
        6 * count * rows * nz * (nz + ny),
        4 * count * nz * (rows + ny),
        scratch=[pltpu.VMEM((count, rows, nz), F32)],
        name="detail_rest",
    )


def own_result(edge, rest, approx, z_matrix, y_matrix):
    count, ny, nz = rest.shape
    n1 = (count + 8) // 2
    nx = 2 * n1
    ends = edges_of(n1)
    planes, rows, half_z = approx.shape

    def kernel(e_ref, r_ref, a_ref, z, y, out, parts):
        def body(first):
            zed = times(a_ref[pl.ds(first, 4)].reshape(4 * rows, half_z), z)
            for j, plane in enumerate(cut(zed, rows)):
                parts[first + j] = left_times(y, plane)

        over_planes(planes, 4, body)

        def tile(t, carry):
            at = pl.ds(pl.multiple_of(t * 8, 8), 8)
            for lane in range(0, nz, 128):
                lanes = pl.ds(lane, 128)

                def coeff(k, high):
                    if k in ends:
                        return e_ref[4 * high + ends.index(k), at, lanes]
                    return r_ref[(n1 - 4) * high + k - 2, at, lanes]

                lows = {k: parts[k + 2, at, lanes] for k in range(-2, n1 + 2)}
                for k in range(n1):
                    lows[k] = lows[k] + coeff(k, 0)
                highs = {k: coeff(k, 1) for k in range(n1)}
                for m in range(nx):
                    out[m, at, lanes] = x_synth(m, lows, highs)
            return carry

        lax.fori_loop(0, ny // 8, tile, 0)

    return whole_call(
        kernel,
        shape(nx, ny, nz),
        [edge, rest, approx, z_matrix, y_matrix],
        16 * nx * ny * nz,
        8 * nx * ny * nz,
        scratch=[pltpu.VMEM((planes, ny, nz), F32)],
        name="own_result",
    )


def in_pairs(matrix, planes):
    results = []
    for i in range(0, len(planes), 2):
        both = left_times(matrix, jnp.concatenate(planes[i : i + 2], axis=1))
        width = both.shape[1] // 2
        results += [both[:, :width], both[:, width:]]
    return results


def cut(values, rows):
    return [values[i : i + rows] for i in range(0, values.shape[0], rows)]


def packed(first, second):
    half = first.shape[1] // 2
    lane = lax.broadcasted_iota(jnp.int32, first.shape, 1)
    return jnp.where(lane < half, first, pltpu.roll(second, half, 1))


def unpacked(both):
    half = both.shape[1] // 2
    lane = lax.broadcasted_iota(jnp.int32, both.shape, 1)
    return [jnp.where(lane < half, part, 0.0) for part in (both, pltpu.roll(both, half, 1))]


def second_bands(own, left, right, halo, h_left, h_right, z_matrix, yx_matrix, y_matrix, low_rows):
    n1, own_rows, nz = own.shape
    in_rows = own_rows + 2 * left.shape[1]
    rows = y_matrix.shape[0]

    wide = h_left.shape[1] - 8

    def kernel(o_ref, l_ref, r_ref, x_ref, hl, hr, z, yx, y, out, up, down):
        planes = [jnp.concatenate([hl[i, :wide], x_ref[i, :, :nz], hr[i, :wide]], axis=0) for i in range(4)]
        l1, l2, r1, r2 = [plane[:in_rows] for plane in in_pairs(yx, planes)]
        beyond = {
            0: l2 + H[2] * l1,
            1: H[0] * l1,
            n1 - 2: H[7] * r1,
            n1 - 1: r2 + H[5] * r1,
        }
        for i in range(0, n1, 8):
            stack = []
            for j in range(i, i + 8):
                plane = jnp.concatenate([o_ref[j], l_ref[j], r_ref[j]], axis=0)
                stack.append(plane + beyond[j] if j in beyond else plane)
            zed = times(jnp.concatenate(stack, axis=0), z)
            for j, plane in enumerate(in_pairs(y, cut(zed, in_rows))):
                out[i + j] = plane
        low = lambda c: out[c, :low_rows]
        up[0:rows] = out[n1 - 1]
        up[rows : 2 * rows] = H[0] * out[n1 - 3] + H[1] * out[n1 - 2]
        first = added([(H[j], low(n1 - 5 + j)) for j in range(5)])
        second = added([(H[0] * H[j], low(n1 - 9 + j)) for j in range(8)])
        second += added([(H[1] * H[j], low(n1 - 7 + j)) for j in range(7)])
        up[2 * rows :] = packed(first, second)
        down[0:rows] = out[0]
        down[rows : 2 * rows] = H[6] * out[1] + H[7] * out[2]
        first = added([(H[j], low(j - 3)) for j in range(3, 8)])
        second = added([(H[6] * H[j], low(j - 1)) for j in range(1, 8)])
        second += added([(H[7] * H[j], low(j + 1)) for j in range(8)])
        down[2 * rows :] = packed(first, second)

    message = 2 * rows + low_rows
    return whole_call(
        kernel,
        [shape(n1, rows, nz), shape(message, nz), shape(message, nz)],
        [own, left, right, halo, h_left, h_right, z_matrix, yx_matrix, y_matrix],
        6 * n1 * in_rows * nz * (nz + rows),
        4 * n1 * nz * (in_rows + rows),
        name="second_bands",
    )


def limits_plane(table_ref, index_ref, level, bx, dims, row_split, lane_split, zeroth):
    row_high = lax.broadcasted_iota(jnp.int32, dims, 0) >= row_split
    lane_high = lax.broadcasted_iota(jnp.int32, dims, 1) >= lane_split

    def limit(by, bz):
        band = 4 * bx + 2 * by + bz
        return zeroth if band == 0 else table_ref[index_ref[level, band - 1]]

    low_y = jnp.where(lane_high, limit(0, 1), limit(0, 0))
    return jnp.where(row_high, jnp.where(lane_high, limit(1, 1), limit(1, 0)), low_y)


def coarse(bands, left, right, table, index, zs1, za2, zs2, ya2, ys2, ys1, low_rows, out_rows):
    n1, rows, nz = bands.shape
    n2, n3 = n1 // 2, n1 // 4
    rows2 = ya2.shape[0]
    lane_half = nz // 2

    def kernel(table_ref, index_ref, b_ref, l_ref, r_ref, z1, z2a, z2s, a2, s2, s1, approx, up, down, c1, p1):
        sides = {
            "l1": lambda: l_ref[0:rows],
            "l2": lambda: l_ref[rows : 2 * rows],
            "r1": lambda: r_ref[0:rows],
            "r2": lambda: r_ref[rows : 2 * rows],
        }
        get = lambda key: sides[key]() if isinstance(key, str) else b_ref[key]
        low_part = lambda c: b_ref[c, :low_rows]
        dims = (rows, nz)
        quiet = limits_plane(table_ref, index_ref, 1, 0, dims, low_rows, lane_half, NOTHING)
        loud = limits_plane(table_ref, index_ref, 1, 1, dims, low_rows, lane_half, NOTHING)
        planes = []
        for k in range(n2):
            low = x_low(get, k, n1)
            planes.append(low[:low_rows])
            c1[k] = shrink(low, quiet)
            c1[n2 + k] = shrink(x_high(get, k, n1), loud)
        first, second = unpacked(l_ref[2 * rows :])
        planes.append(first + added([(H[5 + i], low_part(i)) for i in range(3)]))
        planes.append(second + H[1] * H[7] * low_part(0))
        first, second = unpacked(r_ref[2 * rows :])
        planes.append(first + added([(H[i], low_part(n1 - 3 + i)) for i in range(3)]))
        planes.append(second + H[6] * H[0] * low_part(n1 - 1))
        third = in_pairs(a2, cut(times(jnp.concatenate(planes, axis=0), z2a), low_rows))
        keys = {"l1": n2, "l2": n2 + 1, "r1": n2 + 2, "r2": n2 + 3}
        get2 = lambda key: third[keys.get(key, key)]
        dims = (rows2, nz)
        quiet = limits_plane(table_ref, index_ref, 2, 0, dims, rows2 // 2, lane_half // 2, 0.0)
        loud = limits_plane(table_ref, index_ref, 2, 1, dims, rows2 // 2, lane_half // 2, 0.0)
        kept = [shrink(x_low(get2, k, n2), quiet) for k in range(n3)]
        kept += [shrink(x_high(get2, k, n2), loud) for k in range(n3)]
        parts = in_pairs(s2, cut(times(jnp.concatenate(kept, axis=0), z2s), rows2))
        parts = [part[:low_rows] for part in parts]
        lows = dict(enumerate(parts[:n3]))
        highs = dict(enumerate(parts[n3:]))
        ghosts = [-3, -2, -1, n2, n2 + 1, n2 + 2]
        for k in range(n2):
            c1[k, :low_rows] += x_synth(k, lows, highs)
        stack = [x_synth(k, lows, highs) for k in ghosts]
        beyond = dict(zip(ghosts, stack))
        zed = times(jnp.concatenate(stack, axis=0), z1)
        for i, plane in enumerate(in_pairs(s1, cut(zed, low_rows))):
            p1[2 * n2 + i] = plane[:out_rows]
        for i in range(0, 2 * n2, 8):
            zed = times(c1[i : i + 8].reshape(8 * rows, nz), z1)
            for j, plane in enumerate(in_pairs(s1, cut(zed, rows))):
                p1[i + j] = plane[:out_rows]
        lows = {k: p1.at[k] for k in range(n2)}
        highs = {k: p1.at[n2 + k] for k in range(n2)}
        for i, k in enumerate(ghosts):
            lows[k] = p1.at[2 * n2 + i]

        def cell(m):
            near = lambda part: {k: ref[...] for k, ref in part.items() if 0 <= m + 3 - 2 * k < 8}
            return x_synth(m, near(lows), near(highs))

        for m in range(-2, n1 + 2):
            approx[m + 2] = cell(m)
        value = lambda part, ks: {k: part[k][...] for k in ks}
        ends = (n2 - 2, n2 - 1)
        slot = lambda i: pl.ds(i * out_rows, out_rows)
        up[slot(0)], up[slot(1)] = approx[n1], approx[n1 + 1]
        up[slot(2)], up[slot(3)] = spill_up(value(lows, ends), value(highs, ends), n2)
        up[4 * out_rows :] = packed(beyond[n2], beyond[n2 + 1])
        down[slot(0)], down[slot(1)] = approx[2], approx[3]
        down[slot(2)], down[slot(3)] = spill_down(value(lows, (0, 1)), value(highs, (0, 1)))
        down[4 * out_rows :] = packed(beyond[-1], beyond[-2])

    message = 4 * out_rows + low_rows
    return whole_call(
        kernel,
        [shape(n1 + 4, out_rows, nz), shape(message, nz), shape(message, nz)],
        [table, index, bands, left, right, zs1, za2, zs2, ya2, ys2, ys1],
        1.5e9,
        8 * n1 * rows * nz,
        scratch=[pltpu.VMEM((2 * n2, rows, nz), F32), pltpu.VMEM((2 * n2 + 6, out_rows, nz), F32)],
        name="coarse",
    )


def received_taps(n1):
    n2, nx = n1 // 2, 2 * n1
    from_approx = np.zeros((nx, n1 + 4))
    for m in range(nx):
        for k in range(-2, n1 + 2):
            from_approx[m, k + 2] = tap(H, m + 3 - 2 * k)
    approx = np.zeros((n1 + 4, 12))
    third = {0: THIRD_UP, 6: THIRD_DOWN}
    for first, cell, second in ((0, lambda i: i, lambda i: i), (6, lambda i: n1 - 1 - i, lambda i: n2 - 1 - i)):
        ghost = (-2, -1) if first == 0 else (n1, n1 + 1)
        for i in range(2):
            approx[ghost[i] + 2, first + i] = 1.0
        for place, source, coef in ((0, 0, 1.0), (1, 1, 1.0), (2, 1, third[first])):
            approx[cell(place) + 2, first + 2 + source] += coef
            for m in range(n1):
                approx[m + 2, first + 4 + source] += coef * tap(H, m + 3 - 2 * second(place))
    return from_approx @ approx


def final(left, right, own, e_left, e_right, zs1, ys1, z_matrix, y_matrix, low_rows):
    nx, ny, nz = own.shape
    half_z = nz // 2
    rows = (left.shape[0] - low_rows) // 4
    step_rows = 16
    steps = ny // step_rows
    taps = received_taps(nx // 2)

    def kernel(l_ref, r_ref, d_ref, el, er, z1, s1, z, y, out, parts, done, sems):
        stack = [p for ref in (l_ref, r_ref) for p in unpacked(ref[4 * rows :])]
        zed = times(jnp.concatenate(stack, axis=0), z1)
        spilled = [p[:rows] for p in in_pairs(s1, cut(zed, low_rows))]
        planes = []
        for side, ref in enumerate((l_ref, r_ref)):
            planes += [ref[pl.ds(i * rows, rows)] for i in range(4)] + spilled[2 * side : 2 * side + 2]
        for i, plane in enumerate(cut(times(jnp.concatenate(planes, axis=0), z), rows)):
            parts[i] = left_times(y, plane)

        def copy(i):
            at = pl.ds(pl.multiple_of(i * step_rows, step_rows), step_rows)
            return pltpu.make_async_copy(done.at[:, at], out.at[:, at], sems.at[i])

        def step(i, carry):
            for t in range(step_rows // 8):
                at = pl.ds(pl.multiple_of(i * step_rows + 8 * t, 8), 8)
                for lane in range(0, nz, 128):
                    lanes = pl.ds(lane, 128)
                    values = [parts[i, at, lanes] for i in range(12)]
                    for m in range(nx):
                        value = d_ref[m, at, lanes]
                        value += added([(float(c), v) for c, v in zip(taps[m], values) if c != 0.0])
                        if m < 3:
                            extra = el[(0, 1, 1)[m], at, lanes]
                            value += extra if m < 2 else THIRD_UP * extra
                        if m >= nx - 3:
                            extra = er[(0, 1, 1)[nx - 1 - m], at, lanes]
                            value += extra if m > nx - 3 else THIRD_DOWN * extra
                        done[m, at, lanes] = value
            copy(i).start()
            return carry

        lax.fori_loop(0, steps, step, 0)

        def finish(i, carry):
            copy(i).wait()
            return carry

        lax.fori_loop(0, steps, finish, 0)

    return pl.pallas_call(
        kernel,
        in_specs=[VMEM] * 9,
        out_specs=pl.BlockSpec(memory_space=pl.ANY),
        out_shape=shape(nx, ny, nz),
        scratch_shapes=[
            pltpu.VMEM((12, ny, nz), F32),
            pltpu.VMEM((nx, ny, nz), F32),
            pltpu.SemaphoreType.DMA((steps,)),
        ],
        name="final",
        cost_estimate=pl.CostEstimate(flops=8 * nx * ny * nz, bytes_accessed=8 * nx * ny * nz, transcendentals=0),
        compiler_params=pltpu.CompilerParams(vmem_limit_bytes=VMEM_BYTES),
    )(left, right, own, e_left, e_right, zs1, ys1, z_matrix, y_matrix)


def to_next(array, axis):
    size = lax.axis_size(axis)
    return lax.ppermute(array, axis, [(i, (i + 1) % size) for i in range(size)])


def to_previous(array, axis):
    size = lax.axis_size(axis)
    return lax.ppermute(array, axis, [((i + 1) % size, i) for i in range(size)])


def local(velocity, table, index):
    nx, ny, nz = velocity.shape
    y1, y2, y3 = ny // 2, ny // 4, ny // 8
    ghost, wide = 24, 48
    cells0 = list(range(-8, ny + 8))
    rows0 = up_to(y1 + 4, 8)
    ks0 = fill(list(range(y1)) + [-2, -1, y1, y1 + 1], rows0)
    cells1 = list(range(y1)) + list(range(-ghost, 0)) + list(range(y1, y1 + ghost))
    rows1 = up_to(y2 + 18, 8)
    low1 = fill(list(range(-9, y2 + 9)), rows1)
    high1 = fill(list(range(-3, y2 + 3)), up_to(y2 + 6, 8))
    ks2 = fill(list(range(-3, y3 + 3)), up_to(y3 + 6, 8))
    ya0 = from_left(analysis_rows(cells0, ks0, ks0))
    ys0_matrix = synthesis_rows(list(range(ny)), ks0, ks0)
    ys0 = from_left(ys0_matrix)
    ys0_low = from_left(ys0_matrix[:, :rows0])
    yx0 = from_left(analysis_rows(list(range(-wide, ny + wide)), cells1, []))
    ya1 = from_left(analysis_rows(cells1, low1, high1))
    ys1 = from_left(synthesis_rows(ks0, low1, high1))
    ya2 = from_left(analysis_rows(low1, ks2, ks2))
    ys2 = from_left(synthesis_rows(low1, ks2, ks2))
    z0 = periodic(nz, nz)
    z1 = periodic(nz // 2, nz // 2)
    z2 = periodic(nz // 4, nz // 2)
    za0, zs0, zs0_low = from_right(z0), from_right(z0.T), from_right(z0.T[: nz // 2])
    za1, zs1 = from_right(z1), from_right(z1.T)
    za2, zs2 = from_right(z2), from_right(z2.T)

    x_up, x_down, y_up, y_down = first_messages(velocity)
    x_left = to_next(x_up, "gx")
    x_right = to_previous(x_down, "gx")
    y_left = to_next(y_up, "gy")
    y_right = to_previous(y_down, "gy")
    zed = depth(velocity, za0, 16, "depth_analysis")
    bands = y_analysis(zed, y_left, y_right, za0, ya0)
    approx, a_up, a_down = own_approx(bands, y1, ghost)
    a_left = to_next(a_up, "gy")
    a_right = to_previous(a_down, "gy")
    halo, h_up, h_down = x_halo_messages(x_left, x_right, za0, wide)
    h_left = to_next(h_up, "gy")
    h_right = to_previous(h_down, "gy")
    bands, halo = lax.optimization_barrier((bands, halo))
    rest = inner_bands(bands, table, index)
    rest, approx = lax.optimization_barrier((rest, approx))
    bands1, b_up, b_down = second_bands(
        approx, a_left, a_right, halo, h_left, h_right, za1, yx0, ya1, rows1
    )
    b_left = to_next(b_up, "gx")
    b_right = to_previous(b_down, "gx")
    h_left, h_right, bands1 = lax.optimization_barrier((h_left, h_right, bands1))
    edge = edge_bands(bands, halo, h_left, h_right, table, index, ya0)
    edge, e_up, e_down = detail_edges(edge, zs0, ys0)
    e_left = to_next(e_up, "gx")
    e_right = to_previous(e_down, "gx")
    bands1, edge = lax.optimization_barrier((bands1, edge))
    approx1, s_up, s_down = coarse(
        bands1, b_left, b_right, table, index, zs1, za2, zs2, ya2, ys2, ys1, rows1, rows0
    )
    s_left = to_next(s_up, "gx")
    s_right = to_previous(s_down, "gx")
    rest, approx1 = lax.optimization_barrier((rest, approx1))
    own = own_result(edge, detail_rest(rest, zs0, ys0), approx1, zs0_low, ys0_low)
    return final(s_left, s_right, own, e_left, e_right, zs1, ys1, zs0_low, ys0_low, rows1)


def solution(mesh):
    return jax.shard_map(
        local,
        mesh=mesh,
        in_specs=(P("gx", "gy", None), P(), P()),
        out_specs=P("gx", "gy", None),
        check_vma=False,
    )
```

```python
import functools

import jax
import jax.numpy as jnp
import ml_dtypes
import numpy as np
from jax import lax
from jax.experimental import pallas as pl
from jax.experimental.pallas import tpu as pltpu
from jax.sharding import PartitionSpec as P

H = [
    0.23037781330885523,
    0.7148465705525415,
    0.6308807679295904,
    -0.02798376941698385,
    -0.18703481171888114,
    0.030841381835986965,
    0.032883011666982945,
    -0.010597401784997278,
]
G = [(-1.0) ** j * H[7 - j] for j in range(8)]
F32 = jnp.float32
BF16 = jnp.bfloat16
NOTHING = 3.0e38
VMEM_BYTES = 16 * 1024 * 1024


def tap(filt, j):
    return filt[j] if 0 <= j < 8 else 0.0


def analysis_rows(cells, low_ks, high_ks):
    matrix = np.zeros((len(low_ks) + len(high_ks), len(cells)))
    rows = [(H, k) for k in low_ks] + [(G, k) for k in high_ks]
    for row, (filt, k) in enumerate(rows):
        for col, cell in enumerate(cells):
            if k is not None and cell is not None:
                matrix[row, col] = tap(filt, cell - 2 * k + 3)
    return matrix


def synthesis_rows(cells, low_ks, high_ks):
    return analysis_rows(cells, low_ks, high_ks).T


def periodic(length, padded_to):
    matrix = np.zeros((padded_to, padded_to))
    for k in range(length // 2):
        for j in range(8):
            matrix[(2 * k + j - 3) % length, k] += H[j]
            matrix[(2 * k + j - 3) % length, length // 2 + k] += G[j]
    return matrix


def fill(items, length):
    return items + [None] * (length - len(items))


def up_to(count, step):
    return -(-count // step) * step


def pieces(matrix, axis):
    rows, cols = matrix.shape
    matrix = np.pad(matrix, ((0, up_to(rows, 16) - rows), (0, up_to(cols, 16) - cols))).astype(np.float32)
    high = matrix.astype(ml_dtypes.bfloat16)
    low = (matrix - high.astype(np.float32)).astype(ml_dtypes.bfloat16)
    return np.concatenate([high, high, low], axis=axis)


def from_left(matrix):
    return pieces(matrix, 1)


def from_right(matrix):
    return pieces(matrix, 0)


def halves(values):
    high = values.astype(BF16)
    return high, (values - high.astype(F32)).astype(BF16)


def times(values, matrix):
    high, low = halves(values)
    return jnp.dot(jnp.concatenate([high, low, high], axis=1), matrix[...], preferred_element_type=F32)


def left_times(matrix, values):
    missing = matrix.shape[1] // 3 - values.shape[0]
    if missing:
        values = jnp.concatenate([values, jnp.zeros((missing, values.shape[1]), F32)], axis=0)
    high, low = halves(values)
    return jnp.dot(matrix[...], jnp.concatenate([high, low, high], axis=0), preferred_element_type=F32)


def added(terms):
    total = None
    for coef, value in terms:
        part = value if coef == 1.0 else coef * value
        total = part if total is None else total + part
    return total


def x_terms(k, n):
    terms = []
    for j in range(8):
        cell = 2 * k + j - 3
        if 0 <= cell < n:
            terms.append((cell, H[j], G[j]))
        elif cell == -1:
            terms.append(("l1", H[j], G[j]))
        elif cell == n:
            terms.append(("r1", H[j], G[j]))
    if k == 0:
        terms.append(("l2", 1.0, G[0] / H[0]))
    if k == n // 2 - 1:
        terms.append(("r2", 1.0, G[6] / H[6]))
    return terms


def lattice():
    low = np.array(H).reshape(4, 2)
    high = np.array(G).reshape(4, 2)
    tangents = []
    for _ in range(3):
        t = (low[0] @ high[0]) / (high[0] @ high[0])
        tangents.append(float(t))
        low, high = (low - t * high)[1:] / (1 + t * t), (high + t * low)[:-1] / (1 + t * t)
    return low[0].tolist(), high[0].tolist(), tangents[::-1]


def x_interior(get, n):
    first, second, tangents = lattice()
    a, b = {}, {}
    for i in range(1, n // 2):
        x, y = get(2 * i - 1), get(2 * i)
        a[i] = first[0] * x + first[1] * y
        b[i] = second[0] * x + second[1] * y
    for t in tangents:
        shared = [i for i in a if i + 1 in a]
        a, b = {i: a[i + 1] + t * b[i] for i in shared}, {i: b[i] - t * a[i + 1] for i in shared}
    return {i + 1: (a[i], b[i]) for i in a}


def x_low(get, k, n):
    return added([(low, get(key)) for key, low, _ in x_terms(k, n)])


def x_high(get, k, n):
    return added([(high, get(key)) for key, _, high in x_terms(k, n)])


def x_synth(m, lows, highs):
    terms = [(H[m + 3 - 2 * k], v) for k, v in lows.items() if 0 <= m + 3 - 2 * k < 8]
    terms += [(G[m + 3 - 2 * k], v) for k, v in highs.items() if 0 <= m + 3 - 2 * k < 8]
    return added(terms)


def x_synth_interior(lows, highs, n):
    first, second, tangents = lattice()
    a = {k - 1: lows[k] for k in range(n)}
    b = {k - 1: highs[k] for k in range(n)}
    for t in reversed(tangents):
        a, b = {i + 1: a[i] - t * b[i] for i in a}, {i: b[i] + t * a[i] for i in b}
        both = [i for i in a if i in b]
        a, b = {i: a[i] for i in both}, {i: b[i] for i in both}
    cells = {}
    for i in a:
        cells[2 * i - 1] = first[0] * a[i] + second[0] * b[i]
        cells[2 * i] = first[1] * a[i] + second[1] * b[i]
    return cells


def spill_up(low, high, n):
    first = added([(H[5], low[n - 1]), (G[5], high[n - 1]), (H[7], low[n - 2]), (G[7], high[n - 2])])
    return first, added([(H[6], low[n - 1]), (G[6], high[n - 1])])


def spill_down(low, high):
    first = added([(H[2], low[0]), (G[2], high[0]), (H[0], low[1]), (G[0], high[1])])
    return first, added([(H[1], low[0]), (G[1], high[0])])


THIRD_UP = H[7] / H[6]
THIRD_DOWN = H[0] / H[1]


def shrink(values, thresh):
    return values - jnp.minimum(jnp.maximum(values, -thresh), thresh)


def whole_call(kernel, out_shapes, args, flops, moved, scratch=(), name=None):
    specs = [SMEM if a.ndim == 1 or a.dtype == jnp.int32 else VMEM for a in args]
    outs = [VMEM] * len(out_shapes) if isinstance(out_shapes, list) else VMEM
    return pl.pallas_call(
        kernel,
        in_specs=specs,
        out_specs=outs,
        out_shape=out_shapes,
        scratch_shapes=list(scratch),
        name=name,
        cost_estimate=pl.CostEstimate(flops=int(flops), bytes_accessed=int(moved), transcendentals=0),
        compiler_params=pltpu.CompilerParams(vmem_limit_bytes=VMEM_BYTES),
    )(*args)


def shape(*dims):
    return jax.ShapeDtypeStruct(dims, F32)


SMEM = pl.BlockSpec(memory_space=pltpu.SMEM)
VMEM = pl.BlockSpec(memory_space=pltpu.VMEM)


def first_messages(v):
    nx, ny, nz = v.shape

    kept = nx - nx // 8

    def kernel(v_ref, up, down, y_up, y_down, last, first, rows_up, rows_down, sems):
        copies = [
            pltpu.make_async_copy(source, target, sems.at[i])
            for i, (source, target) in enumerate(
                (
                    (v_ref.at[pl.ds(nx - 3, 3)], last),
                    (v_ref.at[pl.ds(0, 3)], first),
                    (v_ref.at[:, pl.ds(ny - 8, 8)], rows_up),
                    (v_ref.at[:, pl.ds(0, 8)], rows_down),
                )
            )
        ]
        for copy in copies:
            copy.start()
        for copy in copies:
            copy.wait()
        up[0] = last[2]
        up[1] = H[0] * last[0] + H[1] * last[1]
        down[0] = first[0]
        down[1] = H[6] * first[1] + H[7] * first[2]
        y_up[...] = rows_up[:kept]
        y_down[...] = rows_down[:kept]
        for i in range(kept):
            plane, row = kept + i // 7, i % 7
            y_up[i, 0:1] = rows_up[plane, row + 1 : row + 2]
            y_down[i, 7:8] = rows_down[plane, row : row + 1]

    return pl.pallas_call(
        kernel,
        in_specs=[pl.BlockSpec(memory_space=pltpu.HBM)],
        out_specs=[VMEM] * 4,
        out_shape=[shape(2, ny, nz)] * 2 + [shape(kept, 8, nz)] * 2,
        scratch_shapes=[pltpu.VMEM((3, ny, nz), F32)] * 2
        + [pltpu.VMEM((nx, 8, nz), F32)] * 2
        + [pltpu.SemaphoreType.DMA((4,))],
        name="first_messages",
        cost_estimate=pl.CostEstimate(flops=1000000, bytes_accessed=3000000, transcendentals=0),
        compiler_params=pltpu.CompilerParams(vmem_limit_bytes=50 * 1024 * 1024),
    )(v)


def over_planes(count, group, body):
    def step(i, carry):
        body(i * group)
        return carry

    lax.fori_loop(0, count // group, step, 0)


def depth(v, z_matrix, group, name):
    nx, rows, nz = v.shape

    def kernel(v_ref, z, out):
        def body(first):
            at = pl.ds(first, group)
            out[at] = times(v_ref[at].reshape(group * rows, nz), z).reshape(group, rows, nz)

        over_planes(nx, group, body)

    return whole_call(
        kernel, shape(nx, rows, nz), [v, z_matrix], 6 * nx * rows * nz * nz, 8 * nx * rows * nz, name=name
    )


def y_analysis(zed, y_left, y_right, z_matrix, y_matrix):
    nx, ny, nz = zed.shape
    rows = y_matrix.shape[0]
    kept = y_left.shape[0]
    group = 8

    def kernel(zed_ref, left, right, z, y, out, left_z, right_z):
        for part, out_z in ((left, left_z), (right, right_z)):
            out_z[:kept] = times(part[...].reshape(8 * kept, nz), z).reshape(kept, 8, nz)
            out_z[kept:] = jnp.zeros((nx - kept, 8, nz), F32)
        for i in range(kept):
            plane, row = kept + i // 7, i % 7
            left_z[plane, row + 1 : row + 2] = left_z[i, 0:1]
            right_z[plane, row : row + 1] = right_z[i, 7:8]

        def body(first):
            for j in range(group):
                i = first + j
                out[i] = left_times(y, jnp.concatenate([left_z[i], zed_ref[i], right_z[i]], axis=0))

        over_planes(nx, group, body)

    return whole_call(
        kernel,
        shape(nx, rows, nz),
        [zed, y_left, y_right, z_matrix, y_matrix],
        1000,
        1000,
        scratch=[pltpu.VMEM((nx, 8, nz), F32)] * 2,
        name="y_analysis",
    )


def own_approx(bands, own, ghost_rows):
    nx, rows, nz = bands.shape
    half_z = nz // 2
    n1 = nx // 2

    def kernel(b_ref, approx, up, down):
        def tile(t, carry):
            at = pl.ds(pl.multiple_of(t * 8, 8), 8)
            values = {i: b_ref[i, at, :half_z] for i in range(nx)}
            for k in range(n1):
                approx[k, at] = added([(c, values[i]) for i, c, _ in x_terms(k, nx) if i in values])
            approx[n1, at] = added([(H[5 + i], values[i]) for i in range(3)])
            approx[n1 + 1, at] = H[1] * H[7] * values[0]
            approx[n1 + 2, at] = added([(H[i], values[nx - 3 + i]) for i in range(3)])
            approx[n1 + 3, at] = H[6] * H[0] * values[nx - 1]
            return carry

        lax.fori_loop(0, own // 8, tile, 0)
        up[...] = approx[:, own - ghost_rows :]
        down[...] = approx[:, :ghost_rows]

    return whole_call(
        kernel,
        [shape(n1 + 4, own, half_z), shape(n1 + 4, ghost_rows, half_z), shape(n1 + 4, ghost_rows, half_z)],
        [bands],
        1000,
        1000,
        name="own_approx",
    )


def x_halo_messages(x_left, x_right, z_matrix, wide):
    _, ny, nz = x_left.shape
    half_z = nz // 2

    def kernel(xl, xr, z, out, up, down):
        planes = jnp.concatenate([xl[0], xl[1], xr[0], xr[1]], axis=0)
        out[...] = times(planes, z).reshape(4, ny, nz)
        up[:, :wide] = out[:, ny - wide :, :half_z]
        up[:, wide:] = out[:, ny - 8 :, half_z:]
        down[:, :wide] = out[:, :wide, :half_z]
        down[:, wide:] = out[:, :8, half_z:]

    return whole_call(
        kernel,
        [shape(4, ny, nz), shape(4, wide + 8, half_z), shape(4, wide + 8, half_z)],
        [x_left, x_right, z_matrix],
        24 * ny * nz * nz,
        3e6,
        name="x_halo_messages",
    )


def edges_of(n):
    return [0, 1, n - 2, n - 1]


def band_limits(table_ref, index_ref, by, bz):
    band = 2 * by + bz
    quiet = table_ref[index_ref[0, band - 1]] if band else NOTHING
    return quiet, table_ref[index_ref[0, band + 3]]


def over_tiles(rows, nz, body):
    half_z, half_tiles = nz // 2, rows // 16
    for by in range(2):

        def tile(t, carry, by=by):
            at = pl.ds(pl.multiple_of((t + by * half_tiles) * 8, 8), 8)
            for bz in range(2):
                body(at, pl.ds(bz * half_z, half_z), by, bz)
            return carry

        lax.fori_loop(0, half_tiles, tile, 0)


def inner_bands(bands, table, index):
    nx, rows, nz = bands.shape
    count = nx // 2 - 4

    def kernel(table_ref, index_ref, b_ref, out):
        def body(at, lanes, by, bz):
            quiet, loud = band_limits(table_ref, index_ref, by, bz)
            values = {i: b_ref[i, at, lanes] for i in range(nx)}
            for k, (low, high) in x_interior(values.get, nx).items():
                out[k - 2, at, lanes] = shrink(low, quiet) if by + bz else jnp.zeros_like(low)
                out[count + k - 2, at, lanes] = shrink(high, loud)

        over_tiles(rows, nz, body)

    return whole_call(
        kernel,
        shape(2 * count, rows, nz),
        [table, index, bands],
        30 * nx * rows * nz,
        8 * nx * rows * nz,
        name="inner_bands",
    )


def edge_bands(bands, halo, h_left, h_right, table, index, y_matrix):
    nx, rows, nz = bands.shape
    n1 = nx // 2
    half_z = nz // 2
    wide = h_left.shape[1] - 8
    ends = edges_of(n1)

    def kernel(table_ref, index_ref, b_ref, x_ref, hl, hr, y, out, h_ref):
        for i in range(4):
            low = jnp.concatenate([hl[i, wide - 8 : wide], x_ref[i, :, :half_z], hr[i, :8]], axis=0)
            high = jnp.concatenate([hl[i, wide:], x_ref[i, :, half_z:], hr[i, wide:]], axis=0)
            h_ref[i] = left_times(y, jnp.concatenate([low, high], axis=1))
        place = {"l1": 0, "l2": 1, "r1": 2, "r2": 3}

        def body(at, lanes, by, bz):
            quiet, loud = band_limits(table_ref, index_ref, by, bz)
            values = {key: h_ref[i, at, lanes] for key, i in place.items()}
            values.update({i: b_ref[i, at, lanes] for i in [*range(7), *range(nx - 7, nx)]})
            for i, k in enumerate(ends):
                low, high = x_low(values.get, k, nx), x_high(values.get, k, nx)
                out[i, at, lanes] = shrink(low, quiet) if by + bz else jnp.zeros_like(low)
                out[4 + i, at, lanes] = shrink(high, loud)

        over_tiles(rows, nz, body)

    return whole_call(
        kernel,
        shape(8, rows, nz),
        [table, index, bands, halo, h_left, h_right, y_matrix],
        20 * nx * rows * nz,
        4 * nx * rows * nz,
        scratch=[pltpu.VMEM((4, rows, nz), F32)],
        name="edge_bands",
    )


def yz_synthesis(planes, z, y, out, zed):
    count, rows, nz = zed.shape
    group = max(g for g in range(1, 13) if count % g == 0)
    for first in range(0, count, group):
        zed[first : first + group] = times(planes(first, group), z).reshape(group, rows, nz)

    def y_body(first):
        for j in range(4):
            out[first + j] = left_times(y, zed[first + j])

    over_planes(count, 4, y_body)


def detail_edges(coeffs, z_matrix, y_matrix):
    count, rows, nz = coeffs.shape
    ny = y_matrix.shape[0]

    def kernel(c_ref, z, y, out, up, down, zed):
        yz_synthesis(lambda first, n: c_ref[first : first + n].reshape(n * rows, nz), z, y, out, zed)
        part = lambda ks, at: {k: out[i] for k, i in zip(ks, at)}
        up[0], up[1] = spill_up(part((0, 1), (2, 3)), part((0, 1), (6, 7)), 2)
        down[0], down[1] = spill_down(part((0, 1), (0, 1)), part((0, 1), (4, 5)))

    return whole_call(
        kernel,
        [shape(count, ny, nz), shape(2, ny, nz), shape(2, ny, nz)],
        [coeffs, z_matrix, y_matrix],
        6 * count * rows * nz * (nz + ny),
        4 * count * nz * (rows + ny),
        scratch=[pltpu.VMEM((count, rows, nz), F32)],
        name="detail_edges",
    )


def inner_yz(coeffs, approx, z_matrix, y_matrix):
    count, rows, nz = coeffs.shape
    ny = y_matrix.shape[0]
    _, low_rows, half_z = approx.shape
    lows = count // 2

    def kernel(c_ref, a_ref, z, y, out, zed):
        def plane(i):
            if i >= lows:
                return c_ref[i]
            corner = c_ref[i, :low_rows, :half_z] + a_ref[i + 4]
            top = jnp.concatenate([corner, c_ref[i, :low_rows, half_z:]], axis=1)
            return jnp.concatenate([top, c_ref[i, low_rows:]], axis=0)

        def planes(first, n):
            return jnp.concatenate([plane(i) for i in range(first, first + n)], axis=0)

        yz_synthesis(planes, z, y, out, zed)

    return whole_call(
        kernel,
        shape(count, ny, nz),
        [coeffs, approx, z_matrix, y_matrix],
        6 * count * rows * nz * (nz + ny),
        4 * count * nz * (rows + ny),
        scratch=[pltpu.VMEM((count, rows, nz), F32)],
        name="inner_yz",
    )


def own_result(edge, rest, approx, z_matrix, y_matrix):
    count, ny, nz = rest.shape
    n1 = (count + 8) // 2
    nx = 2 * n1
    ends = edges_of(n1)
    planes, rows, half_z = approx.shape

    def kernel(e_ref, r_ref, a_ref, z, y, out, parts):
        for first in (0, 4):
            start = first and n1
            zed = times(a_ref[start : start + 4].reshape(4 * rows, half_z), z)
            for j, plane in enumerate(cut(zed, rows)):
                parts[first + j] = left_times(y, plane)
        place = {k: i for i, k in enumerate([-2, -1, 0, 1, n1 - 2, n1 - 1, n1, n1 + 1])}

        def tile(t, carry):
            at = pl.ds(pl.multiple_of(t * 8, 8), 8)
            for lane in range(0, nz, 128):
                lanes = pl.ds(lane, 128)

                def coeff(k, high):
                    if k in ends:
                        return e_ref[4 * high + ends.index(k), at, lanes]
                    return r_ref[(n1 - 4) * high + k - 2, at, lanes]

                lows = {k: coeff(k, 0) for k in range(n1)}
                highs = {k: coeff(k, 1) for k in range(n1)}
                for k, i in place.items():
                    part = parts[i, at, lanes]
                    lows[k] = lows[k] + part if k in lows else part
                cells = x_synth_interior(lows, highs, n1)
                for m in range(nx):
                    out[m, at, lanes] = cells[m] if m in cells else x_synth(m, lows, highs)
            return carry

        lax.fori_loop(0, ny // 8, tile, 0)

    return whole_call(
        kernel,
        shape(nx, ny, nz),
        [edge, rest, approx, z_matrix, y_matrix],
        16 * nx * ny * nz,
        8 * nx * ny * nz,
        scratch=[pltpu.VMEM((8, ny, nz), F32)],
        name="own_result",
    )


def in_pairs(matrix, planes):
    results = []
    for i in range(0, len(planes), 2):
        both = left_times(matrix, jnp.concatenate(planes[i : i + 2], axis=1))
        width = both.shape[1] // 2
        results += [both[:, :width], both[:, width:]]
    return results


def cut(values, rows):
    return [values[i : i + rows] for i in range(0, values.shape[0], rows)]


def packed(first, second):
    half = first.shape[1] // 2
    lane = lax.broadcasted_iota(jnp.int32, first.shape, 1)
    return jnp.where(lane < half, first, pltpu.roll(second, half, 1))


def unpacked(both):
    half = both.shape[1] // 2
    lane = lax.broadcasted_iota(jnp.int32, both.shape, 1)
    return [jnp.where(lane < half, part, 0.0) for part in (both, pltpu.roll(both, half, 1))]


def second_bands(own, left, right, z_matrix, y_matrix, low_rows):
    planes, own_rows, nz = own.shape
    n1 = planes - 4
    in_rows = own_rows + 2 * left.shape[1]
    rows = y_matrix.shape[0]


    def kernel(o_ref, l_ref, r_ref, z, y, out, up, down):
        for i in range(0, planes, 10):
            stack = [part[j] for j in range(i, i + 10) for part in (o_ref, l_ref, r_ref)]
            zed = times(jnp.concatenate(stack, axis=0), z)
            for j, plane in enumerate(in_pairs(y, cut(zed, in_rows))):
                out[i + j] = plane
        low = lambda c: out[c, :low_rows]
        up[0:rows] = out[n1 - 1]
        up[rows : 2 * rows] = H[0] * out[n1 - 3] + H[1] * out[n1 - 2]
        first = added([(H[j], low(n1 - 5 + j)) for j in range(5)])
        second = added([(H[0] * H[j], low(n1 - 9 + j)) for j in range(8)])
        second += added([(H[1] * H[j], low(n1 - 7 + j)) for j in range(7)])
        up[2 * rows :] = packed(first, second)
        down[0:rows] = out[0]
        down[rows : 2 * rows] = H[6] * out[1] + H[7] * out[2]
        first = added([(H[j], low(j - 3)) for j in range(3, 8)])
        second = added([(H[6] * H[j], low(j - 1)) for j in range(1, 8)])
        second += added([(H[7] * H[j], low(j + 1)) for j in range(8)])
        down[2 * rows :] = packed(first, second)

    message = 2 * rows + low_rows
    return whole_call(
        kernel,
        [shape(planes, rows, nz), shape(message, nz), shape(message, nz)],
        [own, left, right, z_matrix, y_matrix],
        6 * n1 * in_rows * nz * (nz + rows),
        4 * n1 * nz * (in_rows + rows),
        name="second_bands",
    )


def limits_plane(table_ref, index_ref, level, bx, dims, row_split, lane_split, zeroth):
    row_high = lax.broadcasted_iota(jnp.int32, dims, 0) >= row_split
    lane_high = lax.broadcasted_iota(jnp.int32, dims, 1) >= lane_split

    def limit(by, bz):
        band = 4 * bx + 2 * by + bz
        return zeroth if band == 0 else table_ref[index_ref[level, band - 1]]

    low_y = jnp.where(lane_high, limit(0, 1), limit(0, 0))
    return jnp.where(row_high, jnp.where(lane_high, limit(1, 1), limit(1, 0)), low_y)


def coarse(
    bands, left, right, halo, h_left, h_right, table, index, za1, yx0, ya1, zs1, za2, zs2, ya2, ys2, ys1, low_rows, out_rows
):
    planes_in, rows, nz = bands.shape
    n1 = planes_in - 4
    in_rows = yx0.shape[0]
    wide = h_left.shape[1] - 8
    n2, n3 = n1 // 2, n1 // 4
    rows2 = ya2.shape[0]
    lane_half = nz // 2

    def kernel(
        table_ref, index_ref, b_ref, l_ref, r_ref, x_ref, hl, hr, z1a, yx, a1, z1, z2a, z2s, a2, s2, s1,
        approx, up, down, c1, p1,
    ):
        halo_planes = [jnp.concatenate([hl[i, :wide], x_ref[i, :, :nz], hr[i, :wide]], axis=0) for i in range(4)]
        halo_planes = jnp.concatenate([plane[:in_rows] for plane in in_pairs(yx, halo_planes)], axis=0)
        hl1, hl2, hr1, hr2 = in_pairs(a1, cut(times(halo_planes, z1a), in_rows))
        values = {k: b_ref[k] for k in range(2, n1 - 2)}
        values[0] = b_ref[0] + (hl2 + H[2] * hl1)
        values[1] = b_ref[1] + H[0] * hl1
        values[n1 - 2] = b_ref[n1 - 2] + H[7] * hr1
        values[n1 - 1] = b_ref[n1 - 1] + (hr2 + H[5] * hr1)
        xl1, xl2, xr1, xr2 = [b_ref[n1 + i] for i in range(4)]
        values["l1"] = l_ref[0:rows] + xl1
        values["l2"] = l_ref[rows : 2 * rows] + xl2
        values["r1"] = r_ref[0:rows] + xr1
        values["r2"] = r_ref[rows : 2 * rows] + xr2
        get = values.get
        low_part = lambda c: values[c][:low_rows]
        xl1, xl2, xr1, xr2 = [part[:low_rows] for part in (xl1, xl2, xr1, xr2)]
        dims = (rows, nz)
        quiet = limits_plane(table_ref, index_ref, 1, 0, dims, low_rows, lane_half, NOTHING)
        loud = limits_plane(table_ref, index_ref, 1, 1, dims, low_rows, lane_half, NOTHING)
        planes = []
        for k in range(n2):
            low = x_low(get, k, n1)
            planes.append(low[:low_rows])
            c1[k] = shrink(low, quiet)
            c1[n2 + k] = shrink(x_high(get, k, n1), loud)
        first, second = unpacked(l_ref[2 * rows :])
        own = [(H[5 + i], low_part(i)) for i in range(3)]
        planes.append(first + added([(H[3] / H[1], xl2), (H[4], xl1)] + own))
        own = [((H[0] * H[7] + H[1] * H[5]) / H[1], xl2), (H[1] * H[6], xl1), (H[1] * H[7], low_part(0))]
        planes.append(second + added(own))
        first, second = unpacked(r_ref[2 * rows :])
        own = [(H[i], low_part(n1 - 3 + i)) for i in range(3)]
        planes.append(first + added([(H[3], xr1), (H[4] / H[6], xr2)] + own))
        own = [((H[6] * H[2] + H[7] * H[0]) / H[6], xr2), (H[6] * H[1], xr1), (H[6] * H[0], low_part(n1 - 1))]
        planes.append(second + added(own))
        third = in_pairs(a2, cut(times(jnp.concatenate(planes, axis=0), z2a), low_rows))
        keys = {"l1": n2, "l2": n2 + 1, "r1": n2 + 2, "r2": n2 + 3}
        get2 = lambda key: third[keys.get(key, key)]
        dims = (rows2, nz)
        quiet = limits_plane(table_ref, index_ref, 2, 0, dims, rows2 // 2, lane_half // 2, 0.0)
        loud = limits_plane(table_ref, index_ref, 2, 1, dims, rows2 // 2, lane_half // 2, 0.0)
        kept = [shrink(x_low(get2, k, n2), quiet) for k in range(n3)]
        kept += [shrink(x_high(get2, k, n2), loud) for k in range(n3)]
        parts = in_pairs(s2, cut(times(jnp.concatenate(kept, axis=0), z2s), rows2))
        parts = [part[:low_rows] for part in parts]
        lows = dict(enumerate(parts[:n3]))
        highs = dict(enumerate(parts[n3:]))
        ghosts = [-3, -2, -1, n2, n2 + 1, n2 + 2]
        for k in range(n2):
            c1[k, :low_rows] += x_synth(k, lows, highs)
        stack = [x_synth(k, lows, highs) for k in ghosts]
        beyond = dict(zip(ghosts, stack))
        zed = times(jnp.concatenate(stack, axis=0), z1)
        for i, plane in enumerate(in_pairs(s1, cut(zed, low_rows))):
            p1[2 * n2 + i] = plane[:out_rows]
        for i in range(0, 2 * n2, 8):
            zed = times(c1[i : i + 8].reshape(8 * rows, nz), z1)
            for j, plane in enumerate(in_pairs(s1, cut(zed, rows))):
                p1[i + j] = plane[:out_rows]
        lows = {k: p1.at[k] for k in range(n2)}
        highs = {k: p1.at[n2 + k] for k in range(n2)}
        for i, k in enumerate(ghosts):
            lows[k] = p1.at[2 * n2 + i]

        def cell(m):
            near = lambda part: {k: ref[...] for k, ref in part.items() if 0 <= m + 3 - 2 * k < 8}
            return x_synth(m, near(lows), near(highs))

        for m in range(-2, n1 + 2):
            approx[m + 2] = cell(m)
        value = lambda part, ks: {k: part[k][...] for k in ks}
        ends = (n2 - 2, n2 - 1)
        slot = lambda i: pl.ds(i * out_rows, out_rows)
        up[slot(0)], up[slot(1)] = approx[n1], approx[n1 + 1]
        up[slot(2)], up[slot(3)] = spill_up(value(lows, ends), value(highs, ends), n2)
        up[4 * out_rows :] = packed(beyond[n2], beyond[n2 + 1])
        down[slot(0)], down[slot(1)] = approx[2], approx[3]
        down[slot(2)], down[slot(3)] = spill_down(value(lows, (0, 1)), value(highs, (0, 1)))
        down[4 * out_rows :] = packed(beyond[-1], beyond[-2])

    message = 4 * out_rows + low_rows
    return whole_call(
        kernel,
        [shape(n1 + 4, out_rows, nz), shape(message, nz), shape(message, nz)],
        [table, index, bands, left, right, halo, h_left, h_right, za1, yx0, ya1, zs1, za2, zs2, ya2, ys2, ys1],
        1.5e9,
        8 * n1 * rows * nz,
        scratch=[pltpu.VMEM((2 * n2, rows, nz), F32), pltpu.VMEM((2 * n2 + 6, out_rows, nz), F32)],
        name="coarse",
    )


def received_taps(n1):
    n2, nx = n1 // 2, 2 * n1
    from_approx = np.zeros((nx, n1 + 4))
    for m in range(nx):
        for k in range(-2, n1 + 2):
            from_approx[m, k + 2] = tap(H, m + 3 - 2 * k)
    approx = np.zeros((n1 + 4, 12))
    third = {0: THIRD_UP, 6: THIRD_DOWN}
    for first, cell, second in ((0, lambda i: i, lambda i: i), (6, lambda i: n1 - 1 - i, lambda i: n2 - 1 - i)):
        ghost = (-2, -1) if first == 0 else (n1, n1 + 1)
        for i in range(2):
            approx[ghost[i] + 2, first + i] = 1.0
        for place, source, coef in ((0, 0, 1.0), (1, 1, 1.0), (2, 1, third[first])):
            approx[cell(place) + 2, first + 2 + source] += coef
            for m in range(n1):
                approx[m + 2, first + 4 + source] += coef * tap(H, m + 3 - 2 * second(place))
    return from_approx @ approx


def final(left, right, own, e_left, e_right, zs1, ys1, z_matrix, y_matrix, low_rows):
    nx, ny, nz = own.shape
    half_z = nz // 2
    rows = (left.shape[0] - low_rows) // 4
    step_rows = 16
    steps = ny // step_rows
    taps = received_taps(nx // 2)

    def kernel(l_ref, r_ref, d_ref, el, er, z1, s1, z, y, out, parts, done, sems):
        stack = [p for ref in (l_ref, r_ref) for p in unpacked(ref[4 * rows :])]
        zed = times(jnp.concatenate(stack, axis=0), z1)
        spilled = [p[:rows] for p in in_pairs(s1, cut(zed, low_rows))]
        planes = []
        for side, ref in enumerate((l_ref, r_ref)):
            planes += [ref[pl.ds(i * rows, rows)] for i in range(4)] + spilled[2 * side : 2 * side + 2]
        for i, plane in enumerate(cut(times(jnp.concatenate(planes, axis=0), z), rows)):
            parts[i] = left_times(y, plane)

        def copy(i):
            at = pl.ds(pl.multiple_of(i * step_rows, step_rows), step_rows)
            return pltpu.make_async_copy(done.at[:, at], out.at[:, at], sems.at[i])

        def step(i, carry):
            for t in range(step_rows // 8):
                at = pl.ds(pl.multiple_of(i * step_rows + 8 * t, 8), 8)
                for lane in range(0, nz, 128):
                    lanes = pl.ds(lane, 128)
                    values = [parts[i, at, lanes] for i in range(12)]
                    for m in range(nx):
                        value = d_ref[m, at, lanes]
                        value += added([(float(c), v) for c, v in zip(taps[m], values) if c != 0.0])
                        if m < 3:
                            extra = el[(0, 1, 1)[m], at, lanes]
                            value += extra if m < 2 else THIRD_UP * extra
                        if m >= nx - 3:
                            extra = er[(0, 1, 1)[nx - 1 - m], at, lanes]
                            value += extra if m > nx - 3 else THIRD_DOWN * extra
                        done[m, at, lanes] = value
            copy(i).start()
            return carry

        lax.fori_loop(0, steps, step, 0)

        def finish(i, carry):
            copy(i).wait()
            return carry

        lax.fori_loop(0, steps, finish, 0)

    return pl.pallas_call(
        kernel,
        in_specs=[VMEM] * 9,
        out_specs=pl.BlockSpec(memory_space=pl.ANY),
        out_shape=shape(nx, ny, nz),
        scratch_shapes=[
            pltpu.VMEM((12, ny, nz), F32),
            pltpu.VMEM((nx, ny, nz), F32),
            pltpu.SemaphoreType.DMA((steps,)),
        ],
        name="final",
        cost_estimate=pl.CostEstimate(flops=8 * nx * ny * nz, bytes_accessed=8 * nx * ny * nz, transcendentals=0),
        compiler_params=pltpu.CompilerParams(vmem_limit_bytes=VMEM_BYTES),
    )(left, right, own, e_left, e_right, zs1, ys1, z_matrix, y_matrix)


def to_next(array, axis):
    size = lax.axis_size(axis)
    return lax.ppermute(array, axis, [(i, (i + 1) % size) for i in range(size)])


def to_previous(array, axis):
    size = lax.axis_size(axis)
    return lax.ppermute(array, axis, [((i + 1) % size, i) for i in range(size)])


def local(velocity, table, index):
    nx, ny, nz = velocity.shape
    y1, y2, y3 = ny // 2, ny // 4, ny // 8
    ghost, wide = 24, 48
    cells0 = list(range(-8, ny + 8))
    rows0 = up_to(y1 + 4, 8)
    ks0 = fill(list(range(y1)) + [-2, -1, y1, y1 + 1], rows0)
    cells1 = list(range(y1)) + list(range(-ghost, 0)) + list(range(y1, y1 + ghost))
    rows1 = up_to(y2 + 18, 8)
    low1 = fill(list(range(-9, y2 + 9)), rows1)
    high1 = fill(list(range(-3, y2 + 3)), up_to(y2 + 6, 8))
    ks2 = fill(list(range(-3, y3 + 3)), up_to(y3 + 6, 8))
    ya0 = from_left(analysis_rows(cells0, ks0, ks0))
    ys0_matrix = synthesis_rows(list(range(ny)), ks0, ks0)
    ys0 = from_left(ys0_matrix)
    ys0_low = from_left(ys0_matrix[:, :rows0])
    yx0 = from_left(analysis_rows(list(range(-wide, ny + wide)), cells1, []))
    ya1 = from_left(analysis_rows(cells1, low1, high1))
    ys1 = from_left(synthesis_rows(ks0, low1, high1))
    ya2 = from_left(analysis_rows(low1, ks2, ks2))
    ys2 = from_left(synthesis_rows(low1, ks2, ks2))
    z0 = periodic(nz, nz)
    z1 = periodic(nz // 2, nz // 2)
    z2 = periodic(nz // 4, nz // 2)
    za0, zs0, zs0_low = from_right(z0), from_right(z0.T), from_right(z0.T[: nz // 2])
    za1, zs1 = from_right(z1), from_right(z1.T)
    za2, zs2 = from_right(z2), from_right(z2.T)

    x_up, x_down, y_up, y_down = first_messages(velocity)
    x_left = to_next(x_up, "gx")
    x_right = to_previous(x_down, "gx")
    y_left = to_next(y_up, "gy")
    y_right = to_previous(y_down, "gy")
    zed = depth(velocity, za0, 16, "depth_analysis")
    bands = y_analysis(zed, y_left, y_right, za0, ya0)
    approx, a_up, a_down = own_approx(bands, y1, ghost)
    a_left = to_next(a_up, "gy")
    a_right = to_previous(a_down, "gy")
    inner = inner_bands(bands, table, index)
    x_left, x_right, inner = lax.optimization_barrier((x_left, x_right, inner))
    halo, h_up, h_down = x_halo_messages(x_left, x_right, za0, wide)
    h_left = to_next(h_up, "gy")
    h_right = to_previous(h_down, "gy")
    approx, halo = lax.optimization_barrier((approx, halo))
    bands1, b_up, b_down = second_bands(approx, a_left, a_right, za1, ya1, rows1)
    b_left = to_next(b_up, "gx")
    b_right = to_previous(b_down, "gx")
    h_left, h_right, bands1 = lax.optimization_barrier((h_left, h_right, bands1))
    edge = edge_bands(bands, halo, h_left, h_right, table, index, ya0)
    edge, e_up, e_down = detail_edges(edge, zs0, ys0)
    e_left = to_next(e_up, "gx")
    e_right = to_previous(e_down, "gx")
    bands1, edge = lax.optimization_barrier((bands1, edge))
    approx1, s_up, s_down = coarse(
        bands1, b_left, b_right, halo, h_left, h_right, table, index,
        za1, yx0, ya1, zs1, za2, zs2, ya2, ys2, ys1, rows1, rows0,
    )
    s_left = to_next(s_up, "gx")
    s_right = to_previous(s_down, "gx")
    rest = inner_yz(inner, approx1, zs0, ys0)
    own = own_result(edge, rest, approx1, zs0_low, ys0_low)
    return final(s_left, s_right, own, e_left, e_right, zs1, ys1, zs0_low, ys0_low, rows1)


def solution(mesh):
    return jax.shard_map(
        local,
        mesh=mesh,
        in_specs=(P("gx", "gy", None), P(), P()),
        out_specs=P("gx", "gy", None),
        check_vma=False,
    )
```

```python
import functools

import jax
import jax.numpy as jnp
import ml_dtypes
import numpy as np
from jax import lax
from jax.experimental import pallas as pl
from jax.experimental.pallas import tpu as pltpu
from jax.sharding import PartitionSpec as P

H = [
    0.23037781330885523,
    0.7148465705525415,
    0.6308807679295904,
    -0.02798376941698385,
    -0.18703481171888114,
    0.030841381835986965,
    0.032883011666982945,
    -0.010597401784997278,
]
G = [(-1.0) ** j * H[7 - j] for j in range(8)]
F32 = jnp.float32
BF16 = jnp.bfloat16
NOTHING = 3.0e38
VMEM_BYTES = 16 * 1024 * 1024


def tap(filt, j):
    return filt[j] if 0 <= j < 8 else 0.0


def analysis_rows(cells, low_ks, high_ks):
    matrix = np.zeros((len(low_ks) + len(high_ks), len(cells)))
    rows = [(H, k) for k in low_ks] + [(G, k) for k in high_ks]
    for row, (filt, k) in enumerate(rows):
        for col, cell in enumerate(cells):
            if k is not None and cell is not None:
                matrix[row, col] = tap(filt, cell - 2 * k + 3)
    return matrix


def synthesis_rows(cells, low_ks, high_ks):
    return analysis_rows(cells, low_ks, high_ks).T


def periodic(length, padded_to):
    matrix = np.zeros((padded_to, padded_to))
    for k in range(length // 2):
        for j in range(8):
            matrix[(2 * k + j - 3) % length, k] += H[j]
            matrix[(2 * k + j - 3) % length, length // 2 + k] += G[j]
    return matrix


def fill(items, length):
    return items + [None] * (length - len(items))


def up_to(count, step):
    return -(-count // step) * step


def pieces(matrix, axis):
    rows, cols = matrix.shape
    matrix = np.pad(matrix, ((0, up_to(rows, 16) - rows), (0, up_to(cols, 16) - cols))).astype(np.float32)
    high = matrix.astype(ml_dtypes.bfloat16)
    low = (matrix - high.astype(np.float32)).astype(ml_dtypes.bfloat16)
    return np.concatenate([high, high, low], axis=axis)


def from_left(matrix):
    return pieces(matrix, 1)


def from_right(matrix):
    return pieces(matrix, 0)


def halves(values):
    high = values.astype(BF16)
    return high, (values - high.astype(F32)).astype(BF16)


def times(values, matrix):
    high, low = halves(values)
    return jnp.dot(jnp.concatenate([high, low, high], axis=1), matrix[...], preferred_element_type=F32)


def left_times(matrix, values):
    missing = matrix.shape[1] // 3 - values.shape[0]
    if missing:
        values = jnp.concatenate([values, jnp.zeros((missing, values.shape[1]), F32)], axis=0)
    high, low = halves(values)
    return jnp.dot(matrix[...], jnp.concatenate([high, low, high], axis=0), preferred_element_type=F32)


def added(terms):
    total = None
    for coef, value in terms:
        part = value if coef == 1.0 else coef * value
        total = part if total is None else total + part
    return total


def x_terms(k, n):
    terms = []
    for j in range(8):
        cell = 2 * k + j - 3
        if 0 <= cell < n:
            terms.append((cell, H[j], G[j]))
        elif cell == -1:
            terms.append(("l1", H[j], G[j]))
        elif cell == n:
            terms.append(("r1", H[j], G[j]))
    if k == 0:
        terms.append(("l2", 1.0, G[0] / H[0]))
    if k == n // 2 - 1:
        terms.append(("r2", 1.0, G[6] / H[6]))
    return terms


def lattice():
    low = np.array(H).reshape(4, 2)
    high = np.array(G).reshape(4, 2)
    tangents = []
    for _ in range(3):
        t = (low[0] @ high[0]) / (high[0] @ high[0])
        tangents.append(float(t))
        low, high = (low - t * high)[1:] / (1 + t * t), (high + t * low)[:-1] / (1 + t * t)
    return low[0].tolist(), high[0].tolist(), tangents[::-1]


def x_interior(get, n):
    first, second, tangents = lattice()
    a, b = {}, {}
    for i in range(1, n // 2):
        x, y = get(2 * i - 1), get(2 * i)
        a[i] = first[0] * x + first[1] * y
        b[i] = second[0] * x + second[1] * y
    for t in tangents:
        shared = [i for i in a if i + 1 in a]
        a, b = {i: a[i + 1] + t * b[i] for i in shared}, {i: b[i] - t * a[i + 1] for i in shared}
    return {i + 1: (a[i], b[i]) for i in a}


def x_low(get, k, n):
    return added([(low, get(key)) for key, low, _ in x_terms(k, n)])


def x_high(get, k, n):
    return added([(high, get(key)) for key, _, high in x_terms(k, n)])


def x_synth(m, lows, highs):
    terms = [(H[m + 3 - 2 * k], v) for k, v in lows.items() if 0 <= m + 3 - 2 * k < 8]
    terms += [(G[m + 3 - 2 * k], v) for k, v in highs.items() if 0 <= m + 3 - 2 * k < 8]
    return added(terms)


def x_synth_interior(lows, highs, n):
    first, second, tangents = lattice()
    a = {k - 1: lows[k] for k in range(n)}
    b = {k - 1: highs[k] for k in range(n)}
    for t in reversed(tangents):
        a, b = {i + 1: a[i] - t * b[i] for i in a}, {i: b[i] + t * a[i] for i in b}
        both = [i for i in a if i in b]
        a, b = {i: a[i] for i in both}, {i: b[i] for i in both}
    cells = {}
    for i in a:
        cells[2 * i - 1] = first[0] * a[i] + second[0] * b[i]
        cells[2 * i] = first[1] * a[i] + second[1] * b[i]
    return cells


def spill_up(low, high, n):
    first = added([(H[5], low[n - 1]), (G[5], high[n - 1]), (H[7], low[n - 2]), (G[7], high[n - 2])])
    return first, added([(H[6], low[n - 1]), (G[6], high[n - 1])])


def spill_down(low, high):
    first = added([(H[2], low[0]), (G[2], high[0]), (H[0], low[1]), (G[0], high[1])])
    return first, added([(H[1], low[0]), (G[1], high[0])])


THIRD_UP = H[7] / H[6]
THIRD_DOWN = H[0] / H[1]


def shrink(values, thresh):
    return values - jnp.minimum(jnp.maximum(values, -thresh), thresh)


def whole_call(kernel, out_shapes, args, flops, moved, scratch=(), name=None):
    specs = [SMEM if a.ndim == 1 or a.dtype == jnp.int32 else VMEM for a in args]
    outs = [VMEM] * len(out_shapes) if isinstance(out_shapes, list) else VMEM
    return pl.pallas_call(
        kernel,
        in_specs=specs,
        out_specs=outs,
        out_shape=out_shapes,
        scratch_shapes=list(scratch),
        name=name,
        cost_estimate=pl.CostEstimate(flops=int(flops), bytes_accessed=int(moved), transcendentals=0),
        compiler_params=pltpu.CompilerParams(vmem_limit_bytes=VMEM_BYTES),
    )(*args)


def shape(*dims):
    return jax.ShapeDtypeStruct(dims, F32)


SMEM = pl.BlockSpec(memory_space=pltpu.SMEM)
VMEM = pl.BlockSpec(memory_space=pltpu.VMEM)


def first_messages(v):
    nx, ny, nz = v.shape

    kept = nx - nx // 8

    def kernel(v_ref, up, down, y_up, y_down, last, first, rows_up, rows_down, sems):
        copies = [
            pltpu.make_async_copy(source, target, sems.at[i])
            for i, (source, target) in enumerate(
                (
                    (v_ref.at[pl.ds(nx - 3, 3)], last),
                    (v_ref.at[pl.ds(0, 3)], first),
                    (v_ref.at[:, pl.ds(ny - 8, 8)], rows_up),
                    (v_ref.at[:, pl.ds(0, 8)], rows_down),
                )
            )
        ]
        for copy in copies:
            copy.start()
        for copy in copies:
            copy.wait()
        up[0] = last[2]
        up[1] = H[0] * last[0] + H[1] * last[1]
        down[0] = first[0]
        down[1] = H[6] * first[1] + H[7] * first[2]
        y_up[...] = rows_up[:kept]
        y_down[...] = rows_down[:kept]
        for i in range(kept):
            plane, row = kept + i // 7, i % 7
            y_up[i, 0:1] = rows_up[plane, row + 1 : row + 2]
            y_down[i, 7:8] = rows_down[plane, row : row + 1]

    return pl.pallas_call(
        kernel,
        in_specs=[pl.BlockSpec(memory_space=pltpu.HBM)],
        out_specs=[VMEM] * 4,
        out_shape=[shape(2, ny, nz)] * 2 + [shape(kept, 8, nz)] * 2,
        scratch_shapes=[pltpu.VMEM((3, ny, nz), F32)] * 2
        + [pltpu.VMEM((nx, 8, nz), F32)] * 2
        + [pltpu.SemaphoreType.DMA((4,))],
        name="first_messages",
        cost_estimate=pl.CostEstimate(flops=1000000, bytes_accessed=3000000, transcendentals=0),
        compiler_params=pltpu.CompilerParams(vmem_limit_bytes=50 * 1024 * 1024),
    )(v)


def over_planes(count, group, body):
    def step(i, carry):
        body(i * group)
        return carry

    lax.fori_loop(0, count // group, step, 0)


def depth(v, z_matrix, group, name):
    nx, rows, nz = v.shape

    def kernel(v_ref, z, out):
        def body(first):
            at = pl.ds(first, group)
            out[at] = times(v_ref[at].reshape(group * rows, nz), z).reshape(group, rows, nz)

        over_planes(nx, group, body)

    return whole_call(
        kernel, shape(nx, rows, nz), [v, z_matrix], 6 * nx * rows * nz * nz, 8 * nx * rows * nz, name=name
    )


def y_analysis(zed, y_left, y_right, z_matrix, y_matrix):
    nx, ny, nz = zed.shape
    rows = y_matrix.shape[0]
    kept = y_left.shape[0]
    group = 8

    def kernel(zed_ref, left, right, z, y, out, left_z, right_z):
        for part, out_z in ((left, left_z), (right, right_z)):
            out_z[:kept] = times(part[...].reshape(8 * kept, nz), z).reshape(kept, 8, nz)
            out_z[kept:] = jnp.zeros((nx - kept, 8, nz), F32)
        for i in range(kept):
            plane, row = kept + i // 7, i % 7
            left_z[plane, row + 1 : row + 2] = left_z[i, 0:1]
            right_z[plane, row : row + 1] = right_z[i, 7:8]

        def body(first):
            for j in range(group):
                i = first + j
                out[i] = left_times(y, jnp.concatenate([left_z[i], zed_ref[i], right_z[i]], axis=0))

        over_planes(nx, group, body)

    return whole_call(
        kernel,
        shape(nx, rows, nz),
        [zed, y_left, y_right, z_matrix, y_matrix],
        1000,
        1000,
        scratch=[pltpu.VMEM((nx, 8, nz), F32)] * 2,
        name="y_analysis",
    )


def own_approx(zed, y_matrix, own, rows, ghost_rows):
    nx, ny, nz = zed.shape
    half_z = nz // 2
    n1 = nx // 2

    def kernel(zed_ref, y, approx, up, down, low):
        def y_body(first):
            planes = [zed_ref[first + i, :, :half_z] for i in range(8)]
            for i, plane in enumerate(in_pairs(y, planes)):
                low[first + i] = plane[:rows]

        over_planes(nx, 8, y_body)

        def tile(t, carry):
            at = pl.ds(pl.multiple_of(t * 8, 8), 8)
            values = {i: low[i, at] for i in range(nx)}
            for k in range(n1):
                approx[k, at] = added([(c, values[i]) for i, c, _ in x_terms(k, nx) if i in values])
            approx[n1, at] = added([(H[5 + i], values[i]) for i in range(3)])
            approx[n1 + 1, at] = H[1] * H[7] * values[0]
            approx[n1 + 2, at] = added([(H[i], values[nx - 3 + i]) for i in range(3)])
            approx[n1 + 3, at] = H[6] * H[0] * values[nx - 1]
            return carry

        lax.fori_loop(0, rows // 8, tile, 0)
        inside = ghost_rows - 2
        up[:, :inside] = approx[:, own - inside : own]
        up[:, inside:] = approx[:, own + 2 : own + 4]
        down[:, :2] = approx[:, own : own + 2]
        down[:, 2:] = approx[:, :inside]

    return whole_call(
        kernel,
        [shape(n1 + 4, rows, half_z), shape(n1 + 4, ghost_rows, half_z), shape(n1 + 4, ghost_rows, half_z)],
        [zed, y_matrix],
        1000,
        1000,
        scratch=[pltpu.VMEM((nx, rows, half_z), F32)],
        name="own_approx",
    )


def x_halo_messages(x_left, x_right, z_matrix, wide):
    _, ny, nz = x_left.shape
    half_z = nz // 2

    def kernel(xl, xr, z, out, up, down):
        planes = jnp.concatenate([xl[0], xl[1], xr[0], xr[1]], axis=0)
        out[...] = times(planes, z).reshape(4, ny, nz)
        up[:, :wide] = out[:, ny - wide :, :half_z]
        up[:, wide:] = out[:, ny - 8 :, half_z:]
        down[:, :wide] = out[:, :wide, :half_z]
        down[:, wide:] = out[:, :8, half_z:]

    return whole_call(
        kernel,
        [shape(4, ny, nz), shape(4, wide + 8, half_z), shape(4, wide + 8, half_z)],
        [x_left, x_right, z_matrix],
        24 * ny * nz * nz,
        3e6,
        name="x_halo_messages",
    )


def edges_of(n):
    return [0, 1, n - 2, n - 1]


def band_limits(table_ref, index_ref, by, bz):
    band = 2 * by + bz
    quiet = table_ref[index_ref[0, band - 1]] if band else NOTHING
    return quiet, table_ref[index_ref[0, band + 3]]


def over_tiles(rows, nz, body):
    half_z, half_tiles = nz // 2, rows // 16
    for by in range(2):

        def tile(t, carry, by=by):
            at = pl.ds(pl.multiple_of((t + by * half_tiles) * 8, 8), 8)
            for bz in range(2):
                body(at, pl.ds(bz * half_z, half_z), by, bz)
            return carry

        lax.fori_loop(0, half_tiles, tile, 0, unroll=3 if half_tiles % 3 == 0 else 1)


def inner_bands(bands, table, index):
    nx, rows, nz = bands.shape
    count = nx // 2 - 4

    def kernel(table_ref, index_ref, b_ref, out):
        def body(at, lanes, by, bz):
            quiet, loud = band_limits(table_ref, index_ref, by, bz)
            values = {i: b_ref[i, at, lanes] for i in range(nx)}
            for k, (low, high) in x_interior(values.get, nx).items():
                out[k - 2, at, lanes] = shrink(low, quiet) if by + bz else jnp.zeros_like(low)
                out[count + k - 2, at, lanes] = shrink(high, loud)

        over_tiles(rows, nz, body)

    return whole_call(
        kernel,
        shape(2 * count, rows, nz),
        [table, index, bands],
        30 * nx * rows * nz,
        8 * nx * rows * nz,
        name="inner_bands",
    )


def edge_bands(bands, halo, h_left, h_right, table, index, y_matrix):
    nx, rows, nz = bands.shape
    n1 = nx // 2
    half_z = nz // 2
    wide = h_left.shape[1] - 8
    ends = edges_of(n1)

    def kernel(table_ref, index_ref, b_ref, x_ref, hl, hr, y, out, h_ref):
        for i in range(4):
            low = jnp.concatenate([hl[i, wide - 8 : wide], x_ref[i, :, :half_z], hr[i, :8]], axis=0)
            high = jnp.concatenate([hl[i, wide:], x_ref[i, :, half_z:], hr[i, wide:]], axis=0)
            h_ref[i] = left_times(y, jnp.concatenate([low, high], axis=1))
        place = {"l1": 0, "l2": 1, "r1": 2, "r2": 3}

        def body(at, lanes, by, bz):
            quiet, loud = band_limits(table_ref, index_ref, by, bz)
            values = {key: h_ref[i, at, lanes] for key, i in place.items()}
            values.update({i: b_ref[i, at, lanes] for i in [*range(7), *range(nx - 7, nx)]})
            for i, k in enumerate(ends):
                low, high = x_low(values.get, k, nx), x_high(values.get, k, nx)
                out[i, at, lanes] = shrink(low, quiet) if by + bz else jnp.zeros_like(low)
                out[4 + i, at, lanes] = shrink(high, loud)

        over_tiles(rows, nz, body)

    return whole_call(
        kernel,
        shape(8, rows, nz),
        [table, index, bands, halo, h_left, h_right, y_matrix],
        20 * nx * rows * nz,
        4 * nx * rows * nz,
        scratch=[pltpu.VMEM((4, rows, nz), F32)],
        name="edge_bands",
    )


def yz_synthesis(planes, z, y, out, zed):
    count, rows, nz = zed.shape
    group = max(g for g in range(1, 13) if count % g == 0)
    for first in range(0, count, group):
        zed[first : first + group] = times(planes(first, group), z).reshape(group, rows, nz)

    def y_body(first):
        for j in range(4):
            out[first + j] = left_times(y, zed[first + j])

    over_planes(count, 4, y_body)


def detail_edges(coeffs, z_matrix, y_matrix):
    count, rows, nz = coeffs.shape
    ny = y_matrix.shape[0]

    def kernel(c_ref, z, y, out, up, down, zed):
        yz_synthesis(lambda first, n: c_ref[first : first + n].reshape(n * rows, nz), z, y, out, zed)
        part = lambda ks, at: {k: out[i] for k, i in zip(ks, at)}
        up[0], up[1] = spill_up(part((0, 1), (2, 3)), part((0, 1), (6, 7)), 2)
        down[0], down[1] = spill_down(part((0, 1), (0, 1)), part((0, 1), (4, 5)))

    return whole_call(
        kernel,
        [shape(count, ny, nz), shape(2, ny, nz), shape(2, ny, nz)],
        [coeffs, z_matrix, y_matrix],
        6 * count * rows * nz * (nz + ny),
        4 * count * nz * (rows + ny),
        scratch=[pltpu.VMEM((count, rows, nz), F32)],
        name="detail_edges",
    )


def inner_yz(coeffs, approx, z_matrix, y_matrix):
    count, rows, nz = coeffs.shape
    ny = y_matrix.shape[0]
    _, low_rows, half_z = approx.shape
    lows = count // 2

    def kernel(c_ref, a_ref, z, y, out, zed):
        def plane(i):
            if i >= lows:
                return c_ref[i]
            corner = c_ref[i, :low_rows, :half_z] + a_ref[i + 4]
            top = jnp.concatenate([corner, c_ref[i, :low_rows, half_z:]], axis=1)
            return jnp.concatenate([top, c_ref[i, low_rows:]], axis=0)

        def planes(first, n):
            return jnp.concatenate([plane(i) for i in range(first, first + n)], axis=0)

        yz_synthesis(planes, z, y, out, zed)

    return whole_call(
        kernel,
        shape(count, ny, nz),
        [coeffs, approx, z_matrix, y_matrix],
        6 * count * rows * nz * (nz + ny),
        4 * count * nz * (rows + ny),
        scratch=[pltpu.VMEM((count, rows, nz), F32)],
        name="inner_yz",
    )


def own_result(edge, rest, approx, z_matrix, y_matrix):
    count, ny, nz = rest.shape
    n1 = (count + 8) // 2
    nx = 2 * n1
    ends = edges_of(n1)
    planes, rows, half_z = approx.shape

    def kernel(e_ref, r_ref, a_ref, z, y, out, parts):
        for first in (0, 4):
            start = first and n1
            zed = times(a_ref[start : start + 4].reshape(4 * rows, half_z), z)
            for j, plane in enumerate(cut(zed, rows)):
                parts[first + j] = left_times(y, plane)
        place = {k: i for i, k in enumerate([-2, -1, 0, 1, n1 - 2, n1 - 1, n1, n1 + 1])}

        def tile(t, carry):
            at = pl.ds(pl.multiple_of(t * 8, 8), 8)
            for lane in range(0, nz, 128):
                lanes = pl.ds(lane, 128)

                def coeff(k, high):
                    if k in ends:
                        return e_ref[4 * high + ends.index(k), at, lanes]
                    return r_ref[(n1 - 4) * high + k - 2, at, lanes]

                lows = {k: coeff(k, 0) for k in range(n1)}
                highs = {k: coeff(k, 1) for k in range(n1)}
                for k, i in place.items():
                    part = parts[i, at, lanes]
                    lows[k] = lows[k] + part if k in lows else part
                cells = x_synth_interior(lows, highs, n1)
                for m in range(nx):
                    out[m, at, lanes] = cells[m] if m in cells else x_synth(m, lows, highs)
            return carry

        lax.fori_loop(0, ny // 8, tile, 0)

    return whole_call(
        kernel,
        shape(nx, ny, nz),
        [edge, rest, approx, z_matrix, y_matrix],
        16 * nx * ny * nz,
        8 * nx * ny * nz,
        scratch=[pltpu.VMEM((8, ny, nz), F32)],
        name="own_result",
    )


def in_pairs(matrix, planes):
    results = []
    for i in range(0, len(planes), 2):
        both = left_times(matrix, jnp.concatenate(planes[i : i + 2], axis=1))
        width = both.shape[1] // 2
        results += [both[:, :width], both[:, width:]]
    return results


def cut(values, rows):
    return [values[i : i + rows] for i in range(0, values.shape[0], rows)]


def packed(first, second):
    half = first.shape[1] // 2
    lane = lax.broadcasted_iota(jnp.int32, first.shape, 1)
    return jnp.where(lane < half, first, pltpu.roll(second, half, 1))


def unpacked(both):
    half = both.shape[1] // 2
    lane = lax.broadcasted_iota(jnp.int32, both.shape, 1)
    return [jnp.where(lane < half, part, 0.0) for part in (both, pltpu.roll(both, half, 1))]


def second_bands(own, left, right, z_matrix, y_matrix, low_rows):
    planes, own_rows, nz = own.shape
    n1 = planes - 4
    in_rows = own_rows + 2 * left.shape[1]
    rows = y_matrix.shape[0]


    def kernel(o_ref, l_ref, r_ref, z, y, out, up, down):
        for i in range(0, planes, 10):
            stack = [part[j] for j in range(i, i + 10) for part in (o_ref, l_ref, r_ref)]
            zed = times(jnp.concatenate(stack, axis=0), z)
            for j, plane in enumerate(in_pairs(y, cut(zed, in_rows))):
                out[i + j] = plane
        low = lambda c: out[c, :low_rows]
        up[0:rows] = out[n1 - 1]
        up[rows : 2 * rows] = H[0] * out[n1 - 3] + H[1] * out[n1 - 2]
        first = added([(H[j], low(n1 - 5 + j)) for j in range(5)])
        second = added([(H[0] * H[j], low(n1 - 9 + j)) for j in range(8)])
        second += added([(H[1] * H[j], low(n1 - 7 + j)) for j in range(7)])
        up[2 * rows :] = packed(first, second)
        down[0:rows] = out[0]
        down[rows : 2 * rows] = H[6] * out[1] + H[7] * out[2]
        first = added([(H[j], low(j - 3)) for j in range(3, 8)])
        second = added([(H[6] * H[j], low(j - 1)) for j in range(1, 8)])
        second += added([(H[7] * H[j], low(j + 1)) for j in range(8)])
        down[2 * rows :] = packed(first, second)

    message = 2 * rows + low_rows
    return whole_call(
        kernel,
        [shape(planes, rows, nz), shape(message, nz), shape(message, nz)],
        [own, left, right, z_matrix, y_matrix],
        6 * n1 * in_rows * nz * (nz + rows),
        4 * n1 * nz * (in_rows + rows),
        name="second_bands",
    )


def limits_plane(table_ref, index_ref, level, bx, dims, row_split, lane_split, zeroth):
    row_high = lax.broadcasted_iota(jnp.int32, dims, 0) >= row_split
    lane_high = lax.broadcasted_iota(jnp.int32, dims, 1) >= lane_split

    def limit(by, bz):
        band = 4 * bx + 2 * by + bz
        return zeroth if band == 0 else table_ref[index_ref[level, band - 1]]

    low_y = jnp.where(lane_high, limit(0, 1), limit(0, 0))
    return jnp.where(row_high, jnp.where(lane_high, limit(1, 1), limit(1, 0)), low_y)


def coarse(
    bands, left, right, halo, h_left, h_right, table, index, za1, yx0, ya1, zs1, za2, zs2, ya2, ys2, ys1,
    in_rows1, low_rows, out_rows,
):
    planes_in, rows, nz = bands.shape
    n1 = planes_in - 4
    in_rows = in_rows1
    wide = h_left.shape[1] - 8
    n2, n3 = n1 // 2, n1 // 4
    rows2 = ya2.shape[0]
    lane_half = nz // 2

    def kernel(
        table_ref, index_ref, b_ref, l_ref, r_ref, x_ref, hl, hr, z1a, yx, a1, z1, z2a, z2s, a2, s2, s1,
        approx, up, down, c1, p1,
    ):
        halo_planes = [jnp.concatenate([hl[i, :wide], x_ref[i, :, :nz], hr[i, :wide]], axis=0) for i in range(4)]
        halo_planes = jnp.concatenate([plane[:in_rows] for plane in in_pairs(yx, halo_planes)], axis=0)
        hl1, hl2, hr1, hr2 = in_pairs(a1, cut(times(halo_planes, z1a), in_rows))
        values = {k: b_ref[k] for k in range(2, n1 - 2)}
        values[0] = b_ref[0] + (hl2 + H[2] * hl1)
        values[1] = b_ref[1] + H[0] * hl1
        values[n1 - 2] = b_ref[n1 - 2] + H[7] * hr1
        values[n1 - 1] = b_ref[n1 - 1] + (hr2 + H[5] * hr1)
        xl1, xl2, xr1, xr2 = [b_ref[n1 + i] for i in range(4)]
        values["l1"] = l_ref[0:rows] + xl1
        values["l2"] = l_ref[rows : 2 * rows] + xl2
        values["r1"] = r_ref[0:rows] + xr1
        values["r2"] = r_ref[rows : 2 * rows] + xr2
        get = values.get
        low_part = lambda c: values[c][:low_rows]
        xl1, xl2, xr1, xr2 = [part[:low_rows] for part in (xl1, xl2, xr1, xr2)]
        dims = (rows, nz)
        quiet = limits_plane(table_ref, index_ref, 1, 0, dims, low_rows, lane_half, NOTHING)
        loud = limits_plane(table_ref, index_ref, 1, 1, dims, low_rows, lane_half, NOTHING)
        planes = []
        for k in range(n2):
            low = x_low(get, k, n1)
            planes.append(low[:low_rows])
            c1[k] = shrink(low, quiet)
            c1[n2 + k] = shrink(x_high(get, k, n1), loud)
        first, second = unpacked(l_ref[2 * rows :])
        own = [(H[5 + i], low_part(i)) for i in range(3)]
        planes.append(first + added([(H[3] / H[1], xl2), (H[4], xl1)] + own))
        own = [((H[0] * H[7] + H[1] * H[5]) / H[1], xl2), (H[1] * H[6], xl1), (H[1] * H[7], low_part(0))]
        planes.append(second + added(own))
        first, second = unpacked(r_ref[2 * rows :])
        own = [(H[i], low_part(n1 - 3 + i)) for i in range(3)]
        planes.append(first + added([(H[3], xr1), (H[4] / H[6], xr2)] + own))
        own = [((H[6] * H[2] + H[7] * H[0]) / H[6], xr2), (H[6] * H[1], xr1), (H[6] * H[0], low_part(n1 - 1))]
        planes.append(second + added(own))
        third = in_pairs(a2, cut(times(jnp.concatenate(planes, axis=0), z2a), low_rows))
        keys = {"l1": n2, "l2": n2 + 1, "r1": n2 + 2, "r2": n2 + 3}
        get2 = lambda key: third[keys.get(key, key)]
        dims = (rows2, nz)
        quiet = limits_plane(table_ref, index_ref, 2, 0, dims, rows2 // 2, lane_half // 2, 0.0)
        loud = limits_plane(table_ref, index_ref, 2, 1, dims, rows2 // 2, lane_half // 2, 0.0)
        kept = [shrink(x_low(get2, k, n2), quiet) for k in range(n3)]
        kept += [shrink(x_high(get2, k, n2), loud) for k in range(n3)]
        parts = in_pairs(s2, cut(times(jnp.concatenate(kept, axis=0), z2s), rows2))
        parts = [part[:low_rows] for part in parts]
        lows = dict(enumerate(parts[:n3]))
        highs = dict(enumerate(parts[n3:]))
        ghosts = [-3, -2, -1, n2, n2 + 1, n2 + 2]
        for k in range(n2):
            c1[k, :low_rows] += x_synth(k, lows, highs)
        stack = [x_synth(k, lows, highs) for k in ghosts]
        beyond = dict(zip(ghosts, stack))
        zed = times(jnp.concatenate(stack, axis=0), z1)
        for i, plane in enumerate(in_pairs(s1, cut(zed, low_rows))):
            p1[2 * n2 + i] = plane[:out_rows]
        for i in range(0, 2 * n2, 8):
            zed = times(c1[i : i + 8].reshape(8 * rows, nz), z1)
            for j, plane in enumerate(in_pairs(s1, cut(zed, rows))):
                p1[i + j] = plane[:out_rows]
        lows = {k: p1.at[k] for k in range(n2)}
        highs = {k: p1.at[n2 + k] for k in range(n2)}
        for i, k in enumerate(ghosts):
            lows[k] = p1.at[2 * n2 + i]

        def cell(m):
            near = lambda part: {k: ref[...] for k, ref in part.items() if 0 <= m + 3 - 2 * k < 8}
            return x_synth(m, near(lows), near(highs))

        for m in range(-2, n1 + 2):
            approx[m + 2] = cell(m)
        value = lambda part, ks: {k: part[k][...] for k in ks}
        ends = (n2 - 2, n2 - 1)
        slot = lambda i: pl.ds(i * out_rows, out_rows)
        up[slot(0)], up[slot(1)] = approx[n1], approx[n1 + 1]
        up[slot(2)], up[slot(3)] = spill_up(value(lows, ends), value(highs, ends), n2)
        up[4 * out_rows :] = packed(beyond[n2], beyond[n2 + 1])
        down[slot(0)], down[slot(1)] = approx[2], approx[3]
        down[slot(2)], down[slot(3)] = spill_down(value(lows, (0, 1)), value(highs, (0, 1)))
        down[4 * out_rows :] = packed(beyond[-1], beyond[-2])

    message = 4 * out_rows + low_rows
    return whole_call(
        kernel,
        [shape(n1 + 4, out_rows, nz), shape(message, nz), shape(message, nz)],
        [table, index, bands, left, right, halo, h_left, h_right, za1, yx0, ya1, zs1, za2, zs2, ya2, ys2, ys1],
        1.5e9,
        8 * n1 * rows * nz,
        scratch=[pltpu.VMEM((2 * n2, rows, nz), F32), pltpu.VMEM((2 * n2 + 6, out_rows, nz), F32)],
        name="coarse",
    )


def received_taps(n1):
    n2, nx = n1 // 2, 2 * n1
    from_approx = np.zeros((nx, n1 + 4))
    for m in range(nx):
        for k in range(-2, n1 + 2):
            from_approx[m, k + 2] = tap(H, m + 3 - 2 * k)
    approx = np.zeros((n1 + 4, 12))
    third = {0: THIRD_UP, 6: THIRD_DOWN}
    for first, cell, second in ((0, lambda i: i, lambda i: i), (6, lambda i: n1 - 1 - i, lambda i: n2 - 1 - i)):
        ghost = (-2, -1) if first == 0 else (n1, n1 + 1)
        for i in range(2):
            approx[ghost[i] + 2, first + i] = 1.0
        for place, source, coef in ((0, 0, 1.0), (1, 1, 1.0), (2, 1, third[first])):
            approx[cell(place) + 2, first + 2 + source] += coef
            for m in range(n1):
                approx[m + 2, first + 4 + source] += coef * tap(H, m + 3 - 2 * second(place))
    return from_approx @ approx


def final(left, right, own, e_left, e_right, zs1, ys1, z_matrix, y_matrix, low_rows):
    nx, ny, nz = own.shape
    half_z = nz // 2
    rows = (left.shape[0] - low_rows) // 4
    step_rows = 16
    steps = ny // step_rows
    taps = received_taps(nx // 2)

    def kernel(l_ref, r_ref, d_ref, el, er, z1, s1, z, y, out, parts, done, sems):
        stack = [p for ref in (l_ref, r_ref) for p in unpacked(ref[4 * rows :])]
        zed = times(jnp.concatenate(stack, axis=0), z1)
        spilled = [p[:rows] for p in in_pairs(s1, cut(zed, low_rows))]
        planes = []
        for side, ref in enumerate((l_ref, r_ref)):
            planes += [ref[pl.ds(i * rows, rows)] for i in range(4)] + spilled[2 * side : 2 * side + 2]
        for i, plane in enumerate(cut(times(jnp.concatenate(planes, axis=0), z), rows)):
            parts[i] = left_times(y, plane)

        def copy(i):
            at = pl.ds(pl.multiple_of(i * step_rows, step_rows), step_rows)
            return pltpu.make_async_copy(done.at[:, at], out.at[:, at], sems.at[i])

        def step(i, carry):
            for t in range(step_rows // 8):
                at = pl.ds(pl.multiple_of(i * step_rows + 8 * t, 8), 8)
                for lane in range(0, nz, 128):
                    lanes = pl.ds(lane, 128)
                    values = [parts[i, at, lanes] for i in range(12)]
                    for m in range(nx):
                        value = d_ref[m, at, lanes]
                        value += added([(float(c), v) for c, v in zip(taps[m], values) if c != 0.0])
                        if m < 3:
                            extra = el[(0, 1, 1)[m], at, lanes]
                            value += extra if m < 2 else THIRD_UP * extra
                        if m >= nx - 3:
                            extra = er[(0, 1, 1)[nx - 1 - m], at, lanes]
                            value += extra if m > nx - 3 else THIRD_DOWN * extra
                        done[m, at, lanes] = value
            copy(i).start()
            return carry

        lax.fori_loop(0, steps, step, 0)

        def finish(i, carry):
            copy(i).wait()
            return carry

        lax.fori_loop(0, steps, finish, 0)

    return pl.pallas_call(
        kernel,
        in_specs=[VMEM] * 9,
        out_specs=pl.BlockSpec(memory_space=pl.ANY),
        out_shape=shape(nx, ny, nz),
        scratch_shapes=[
            pltpu.VMEM((12, ny, nz), F32),
            pltpu.VMEM((nx, ny, nz), F32),
            pltpu.SemaphoreType.DMA((steps,)),
        ],
        name="final",
        cost_estimate=pl.CostEstimate(flops=8 * nx * ny * nz, bytes_accessed=8 * nx * ny * nz, transcendentals=0),
        compiler_params=pltpu.CompilerParams(vmem_limit_bytes=VMEM_BYTES),
    )(left, right, own, e_left, e_right, zs1, ys1, z_matrix, y_matrix)


def to_next(array, axis):
    size = lax.axis_size(axis)
    return lax.ppermute(array, axis, [(i, (i + 1) % size) for i in range(size)])


def to_previous(array, axis):
    size = lax.axis_size(axis)
    return lax.ppermute(array, axis, [((i + 1) % size, i) for i in range(size)])


def local(velocity, table, index):
    nx, ny, nz = velocity.shape
    y1, y2, y3 = ny // 2, ny // 4, ny // 8
    ghost, wide = 24, 48
    cells0 = list(range(-8, ny + 8))
    rows0 = up_to(y1 + 4, 8)
    ks0 = fill(list(range(y1)) + [-2, -1, y1, y1 + 1], rows0)
    cells1 = ks0 + list(range(2 - ghost, 2)) + list(range(y1 - 2, y1 + ghost - 2))
    once = [c if cells1.index(c) == i else None for i, c in enumerate(cells1)]
    rows1 = up_to(y2 + 18, 8)
    low1 = fill(list(range(-9, y2 + 9)), rows1)
    high1 = fill(list(range(-3, y2 + 3)), up_to(y2 + 6, 8))
    ks2 = fill(list(range(-3, y3 + 3)), up_to(y3 + 6, 8))
    ya0 = from_left(analysis_rows(cells0, ks0, ks0))
    ys0_matrix = synthesis_rows(list(range(ny)), ks0, ks0)
    ys0 = from_left(ys0_matrix)
    ys0_low = from_left(ys0_matrix[:, :rows0])
    yl0 = from_left(analysis_rows(list(range(ny)), ks0, []))
    yx0 = from_left(analysis_rows(list(range(-wide, ny + wide)), once, []))
    ya1 = from_left(analysis_rows(cells1, low1, high1))
    ys1 = from_left(synthesis_rows(ks0, low1, high1))
    ya2 = from_left(analysis_rows(low1, ks2, ks2))
    ys2 = from_left(synthesis_rows(low1, ks2, ks2))
    z0 = periodic(nz, nz)
    z1 = periodic(nz // 2, nz // 2)
    z2 = periodic(nz // 4, nz // 2)
    za0, zs0, zs0_low = from_right(z0), from_right(z0.T), from_right(z0.T[: nz // 2])
    za1, zs1 = from_right(z1), from_right(z1.T)
    za2, zs2 = from_right(z2), from_right(z2.T)

    x_up, x_down, y_up, y_down = first_messages(velocity)
    x_left = to_next(x_up, "gx")
    x_right = to_previous(x_down, "gx")
    y_left = to_next(y_up, "gy")
    y_right = to_previous(y_down, "gy")
    zed = depth(velocity, za0, 16, "depth_analysis")
    approx, a_up, a_down = own_approx(zed, yl0, y1, rows0, ghost)
    a_left = to_next(a_up, "gy")
    a_right = to_previous(a_down, "gy")
    zed, a_up = lax.optimization_barrier((zed, a_up))
    bands = y_analysis(zed, y_left, y_right, za0, ya0)
    inner = inner_bands(bands, table, index)
    x_left, x_right, inner = lax.optimization_barrier((x_left, x_right, inner))
    halo, h_up, h_down = x_halo_messages(x_left, x_right, za0, wide)
    h_left = to_next(h_up, "gy")
    h_right = to_previous(h_down, "gy")
    approx, halo = lax.optimization_barrier((approx, halo))
    bands1, b_up, b_down = second_bands(approx, a_left, a_right, za1, ya1, rows1)
    b_left = to_next(b_up, "gx")
    b_right = to_previous(b_down, "gx")
    h_left, h_right, bands1 = lax.optimization_barrier((h_left, h_right, bands1))
    edge = edge_bands(bands, halo, h_left, h_right, table, index, ya0)
    edge, e_up, e_down = detail_edges(edge, zs0, ys0)
    e_left = to_next(e_up, "gx")
    e_right = to_previous(e_down, "gx")
    bands1, edge = lax.optimization_barrier((bands1, edge))
    approx1, s_up, s_down = coarse(
        bands1, b_left, b_right, halo, h_left, h_right, table, index,
        za1, yx0, ya1, zs1, za2, zs2, ya2, ys2, ys1, len(cells1), rows1, rows0,
    )
    s_left = to_next(s_up, "gx")
    s_right = to_previous(s_down, "gx")
    rest = inner_yz(inner, approx1, zs0, ys0)
    own = own_result(edge, rest, approx1, zs0_low, ys0_low)
    return final(s_left, s_right, own, e_left, e_right, zs1, ys1, zs0_low, ys0_low, rows1)


def solution(mesh):
    return jax.shard_map(
        local,
        mesh=mesh,
        in_specs=(P("gx", "gy", None), P(), P()),
        out_specs=P("gx", "gy", None),
        check_vma=False,
    )
```

```python
import functools

import jax
import jax.numpy as jnp
import ml_dtypes
import numpy as np
from jax import lax
from jax.experimental import pallas as pl
from jax.experimental.pallas import tpu as pltpu
from jax.sharding import PartitionSpec as P

H = [
    0.23037781330885523,
    0.7148465705525415,
    0.6308807679295904,
    -0.02798376941698385,
    -0.18703481171888114,
    0.030841381835986965,
    0.032883011666982945,
    -0.010597401784997278,
]
G = [(-1.0) ** j * H[7 - j] for j in range(8)]
F32 = jnp.float32
BF16 = jnp.bfloat16
NOTHING = 3.0e38
VMEM_BYTES = 16 * 1024 * 1024


def tap(filt, j):
    return filt[j] if 0 <= j < 8 else 0.0


def analysis_rows(cells, low_ks, high_ks):
    matrix = np.zeros((len(low_ks) + len(high_ks), len(cells)))
    rows = [(H, k) for k in low_ks] + [(G, k) for k in high_ks]
    for row, (filt, k) in enumerate(rows):
        for col, cell in enumerate(cells):
            if k is not None and cell is not None:
                matrix[row, col] = tap(filt, cell - 2 * k + 3)
    return matrix


def synthesis_rows(cells, low_ks, high_ks):
    return analysis_rows(cells, low_ks, high_ks).T


def periodic(length, padded_to):
    matrix = np.zeros((padded_to, padded_to))
    for k in range(length // 2):
        for j in range(8):
            matrix[(2 * k + j - 3) % length, k] += H[j]
            matrix[(2 * k + j - 3) % length, length // 2 + k] += G[j]
    return matrix


def fill(items, length):
    return items + [None] * (length - len(items))


def up_to(count, step):
    return -(-count // step) * step


def pieces(matrix, axis):
    rows, cols = matrix.shape
    matrix = np.pad(matrix, ((0, up_to(rows, 16) - rows), (0, up_to(cols, 16) - cols))).astype(np.float32)
    high = matrix.astype(ml_dtypes.bfloat16)
    low = (matrix - high.astype(np.float32)).astype(ml_dtypes.bfloat16)
    return np.concatenate([high, high, low], axis=axis)


def from_left(matrix):
    return pieces(matrix, 1)


def from_right(matrix):
    return pieces(matrix, 0)


def wide_right(matrix):
    rows, cols = matrix.shape
    both = pieces(matrix, 0)
    high, low = both[:rows], both[2 * rows :]
    return np.block([[high, low], [high, np.zeros_like(low)]])


def tall_left(matrix):
    return np.ascontiguousarray(wide_right(np.ascontiguousarray(padded_to_tiles(matrix).T)).T)


def padded_to_tiles(matrix):
    rows, cols = matrix.shape
    return np.pad(matrix, ((0, up_to(rows, 16) - rows), (0, up_to(cols, 16) - cols)))


def halves(values):
    high = values.astype(BF16)
    return high, (values - high.astype(F32)).astype(BF16)


def times(values, matrix):
    high, low = halves(values)
    return jnp.dot(jnp.concatenate([high, low, high], axis=1), matrix[...], preferred_element_type=F32)


def left_times(matrix, values):
    missing = matrix.shape[1] // 3 - values.shape[0]
    if missing:
        values = jnp.concatenate([values, jnp.zeros((missing, values.shape[1]), F32)], axis=0)
    high, low = halves(values)
    return jnp.dot(matrix[...], jnp.concatenate([high, low, high], axis=0), preferred_element_type=F32)


def times_wide(values, matrix):
    both = jnp.dot(jnp.concatenate(halves(values), axis=1), matrix[...], preferred_element_type=F32)
    return both[:, : both.shape[1] // 2] + both[:, both.shape[1] // 2 :]


def left_times_tall(matrix, values):
    missing = matrix.shape[1] // 2 - values.shape[0]
    if missing:
        values = jnp.concatenate([values, jnp.zeros((missing, values.shape[1]), F32)], axis=0)
    both = jnp.dot(matrix[...], jnp.concatenate(halves(values), axis=0), preferred_element_type=F32)
    return both[: both.shape[0] // 2] + both[both.shape[0] // 2 :]


def added(terms):
    total = None
    for coef, value in terms:
        part = value if coef == 1.0 else coef * value
        total = part if total is None else total + part
    return total


def x_terms(k, n):
    terms = []
    for j in range(8):
        cell = 2 * k + j - 3
        if 0 <= cell < n:
            terms.append((cell, H[j], G[j]))
        elif cell == -1:
            terms.append(("l1", H[j], G[j]))
        elif cell == n:
            terms.append(("r1", H[j], G[j]))
    if k == 0:
        terms.append(("l2", 1.0, G[0] / H[0]))
    if k == n // 2 - 1:
        terms.append(("r2", 1.0, G[6] / H[6]))
    return terms


def lattice():
    low = np.array(H).reshape(4, 2)
    high = np.array(G).reshape(4, 2)
    tangents = []
    for _ in range(3):
        t = (low[0] @ high[0]) / (high[0] @ high[0])
        tangents.append(float(t))
        low, high = (low - t * high)[1:] / (1 + t * t), (high + t * low)[:-1] / (1 + t * t)
    return low[0].tolist(), high[0].tolist(), tangents[::-1]


def x_interior(get, n):
    first, second, tangents = lattice()
    a, b = {}, {}
    for i in range(1, n // 2):
        x, y = get(2 * i - 1), get(2 * i)
        a[i] = first[0] * x + first[1] * y
        b[i] = second[0] * x + second[1] * y
    for t in tangents:
        shared = [i for i in a if i + 1 in a]
        a, b = {i: a[i + 1] + t * b[i] for i in shared}, {i: b[i] - t * a[i + 1] for i in shared}
    return {i + 1: (a[i], b[i]) for i in a}


def x_low(get, k, n):
    return added([(low, get(key)) for key, low, _ in x_terms(k, n)])


def x_high(get, k, n):
    return added([(high, get(key)) for key, _, high in x_terms(k, n)])


def x_synth(m, lows, highs):
    terms = [(H[m + 3 - 2 * k], v) for k, v in lows.items() if 0 <= m + 3 - 2 * k < 8]
    terms += [(G[m + 3 - 2 * k], v) for k, v in highs.items() if 0 <= m + 3 - 2 * k < 8]
    return added(terms)


def x_synth_interior(lows, highs, n):
    first, second, tangents = lattice()
    a = {k - 1: lows[k] for k in range(n)}
    b = {k - 1: highs[k] for k in range(n)}
    for t in reversed(tangents):
        a, b = {i + 1: a[i] - t * b[i] for i in a}, {i: b[i] + t * a[i] for i in b}
        both = [i for i in a if i in b]
        a, b = {i: a[i] for i in both}, {i: b[i] for i in both}
    cells = {}
    for i in a:
        cells[2 * i - 1] = first[0] * a[i] + second[0] * b[i]
        cells[2 * i] = first[1] * a[i] + second[1] * b[i]
    return cells


def spill_up(low, high, n):
    first = added([(H[5], low[n - 1]), (G[5], high[n - 1]), (H[7], low[n - 2]), (G[7], high[n - 2])])
    return first, added([(H[6], low[n - 1]), (G[6], high[n - 1])])


def spill_down(low, high):
    first = added([(H[2], low[0]), (G[2], high[0]), (H[0], low[1]), (G[0], high[1])])
    return first, added([(H[1], low[0]), (G[1], high[0])])


THIRD_UP = H[7] / H[6]
THIRD_DOWN = H[0] / H[1]


def shrink(values, thresh):
    return values - jnp.minimum(jnp.maximum(values, -thresh), thresh)


def whole_call(kernel, out_shapes, args, flops, moved, scratch=(), name=None):
    specs = [SMEM if a.ndim == 1 or a.dtype == jnp.int32 else VMEM for a in args]
    outs = [VMEM] * len(out_shapes) if isinstance(out_shapes, list) else VMEM
    return pl.pallas_call(
        kernel,
        in_specs=specs,
        out_specs=outs,
        out_shape=out_shapes,
        scratch_shapes=list(scratch),
        name=name,
        cost_estimate=pl.CostEstimate(flops=1000, bytes_accessed=1000, transcendentals=0),
        compiler_params=pltpu.CompilerParams(vmem_limit_bytes=VMEM_BYTES),
    )(*args)


def shape(*dims):
    return jax.ShapeDtypeStruct(dims, F32)


SMEM = pl.BlockSpec(memory_space=pltpu.SMEM)
VMEM = pl.BlockSpec(memory_space=pltpu.VMEM)


def first_messages(v):
    nx, ny, nz = v.shape

    kept = nx - nx // 8

    def kernel(v_ref, up, down, y_up, y_down, last, first, rows_up, rows_down, sems):
        copies = [
            pltpu.make_async_copy(source, target, sems.at[i])
            for i, (source, target) in enumerate(
                (
                    (v_ref.at[pl.ds(nx - 3, 3)], last),
                    (v_ref.at[pl.ds(0, 3)], first),
                    (v_ref.at[:, pl.ds(ny - 8, 8)], rows_up),
                    (v_ref.at[:, pl.ds(0, 8)], rows_down),
                )
            )
        ]
        for copy in copies:
            copy.start()
        for copy in copies:
            copy.wait()
        up[0] = last[2]
        up[1] = H[0] * last[0] + H[1] * last[1]
        down[0] = first[0]
        down[1] = H[6] * first[1] + H[7] * first[2]
        y_up[...] = rows_up[:kept]
        y_down[...] = rows_down[:kept]
        for i in range(kept):
            plane, row = kept + i // 7, i % 7
            y_up[i, 0:1] = rows_up[plane, row + 1 : row + 2]
            y_down[i, 7:8] = rows_down[plane, row : row + 1]

    return pl.pallas_call(
        kernel,
        in_specs=[pl.BlockSpec(memory_space=pltpu.HBM)],
        out_specs=[VMEM] * 4,
        out_shape=[shape(2, ny, nz)] * 2 + [shape(kept, 8, nz)] * 2,
        scratch_shapes=[pltpu.VMEM((3, ny, nz), F32)] * 2
        + [pltpu.VMEM((nx, 8, nz), F32)] * 2
        + [pltpu.SemaphoreType.DMA((4,))],
        name="first_messages",
        cost_estimate=pl.CostEstimate(flops=1000000, bytes_accessed=3000000, transcendentals=0),
        compiler_params=pltpu.CompilerParams(vmem_limit_bytes=50 * 1024 * 1024),
    )(v)


def over_planes(count, group, body):
    def step(i, carry):
        body(i * group)
        return carry

    lax.fori_loop(0, count // group, step, 0)


def depth(v, z_matrix, group, name):
    nx, rows, nz = v.shape

    def kernel(v_ref, z, out):
        def body(first):
            at = pl.ds(first, group)
            out[at] = times(v_ref[at].reshape(group * rows, nz), z).reshape(group, rows, nz)

        over_planes(nx, group, body)

    return whole_call(
        kernel, shape(nx, rows, nz), [v, z_matrix], 6 * nx * rows * nz * nz, 8 * nx * rows * nz, name=name
    )


def y_analysis(zed, y_left, y_right, z_matrix, y_matrix):
    nx, ny, nz = zed.shape
    rows = y_matrix.shape[0]
    kept = y_left.shape[0]
    group = 8

    def kernel(zed_ref, left, right, z, y, out, left_z, right_z):
        for part, out_z in ((left, left_z), (right, right_z)):
            out_z[:kept] = times(part[...].reshape(8 * kept, nz), z).reshape(kept, 8, nz)
            out_z[kept:] = jnp.zeros((nx - kept, 8, nz), F32)
        for i in range(kept):
            plane, row = kept + i // 7, i % 7
            left_z[plane, row + 1 : row + 2] = left_z[i, 0:1]
            right_z[plane, row : row + 1] = right_z[i, 7:8]

        def body(first):
            for j in range(group):
                i = first + j
                out[i] = left_times(y, jnp.concatenate([left_z[i], zed_ref[i], right_z[i]], axis=0))

        over_planes(nx, group, body)

    return whole_call(
        kernel,
        shape(nx, rows, nz),
        [zed, y_left, y_right, z_matrix, y_matrix],
        1000,
        1000,
        scratch=[pltpu.VMEM((nx, 8, nz), F32)] * 2,
        name="y_analysis",
    )


def own_approx(zed, y_matrix, own, rows, ghost_rows):
    nx, ny, nz = zed.shape
    half_z = nz // 2
    n1 = nx // 2

    def kernel(zed_ref, y, approx, up, down, low):
        def y_body(first):
            planes = [zed_ref[first + i, :, :half_z] for i in range(8)]
            for i, plane in enumerate(in_pairs(y, planes)):
                low[first + i] = plane[:rows]

        over_planes(nx, 8, y_body)

        def tile(t, carry):
            at = pl.ds(pl.multiple_of(t * 8, 8), 8)
            values = {i: low[i, at] for i in range(nx)}
            for k in range(n1):
                approx[k, at] = added([(c, values[i]) for i, c, _ in x_terms(k, nx) if i in values])
            approx[n1, at] = added([(H[5 + i], values[i]) for i in range(3)])
            approx[n1 + 1, at] = H[1] * H[7] * values[0]
            approx[n1 + 2, at] = added([(H[i], values[nx - 3 + i]) for i in range(3)])
            approx[n1 + 3, at] = H[6] * H[0] * values[nx - 1]
            return carry

        lax.fori_loop(0, rows // 8, tile, 0)
        inside = ghost_rows - 2
        up[:, :inside] = approx[:, own - inside : own]
        up[:, inside:] = approx[:, own + 2 : own + 4]
        down[:, :2] = approx[:, own : own + 2]
        down[:, 2:] = approx[:, :inside]

    return whole_call(
        kernel,
        [shape(n1 + 4, rows, half_z), shape(n1 + 4, ghost_rows, half_z), shape(n1 + 4, ghost_rows, half_z)],
        [zed, y_matrix],
        1000,
        1000,
        scratch=[pltpu.VMEM((nx, rows, half_z), F32)],
        name="own_approx",
    )


def x_halo_messages(x_left, x_right, z_matrix, wide):
    _, ny, nz = x_left.shape
    half_z = nz // 2

    def kernel(xl, xr, z, out, up, down):
        planes = jnp.concatenate([xl[0], xl[1], xr[0], xr[1]], axis=0)
        out[...] = times(planes, z).reshape(4, ny, nz)
        up[:, :wide] = out[:, ny - wide :, :half_z]
        up[:, wide:] = out[:, ny - 8 :, half_z:]
        down[:, :wide] = out[:, :wide, :half_z]
        down[:, wide:] = out[:, :8, half_z:]

    return whole_call(
        kernel,
        [shape(4, ny, nz), shape(4, wide + 8, half_z), shape(4, wide + 8, half_z)],
        [x_left, x_right, z_matrix],
        24 * ny * nz * nz,
        3e6,
        name="x_halo_messages",
    )


def edges_of(n):
    return [0, 1, n - 2, n - 1]


def band_limits(table_ref, index_ref, by, bz):
    band = 2 * by + bz
    quiet = table_ref[index_ref[0, band - 1]] if band else NOTHING
    return quiet, table_ref[index_ref[0, band + 3]]


def over_tiles(rows, nz, body):
    half_z, half_tiles = nz // 2, rows // 16
    for by in range(2):

        def tile(t, carry, by=by):
            at = pl.ds(pl.multiple_of((t + by * half_tiles) * 8, 8), 8)
            for bz in range(2):
                body(at, pl.ds(bz * half_z, half_z), by, bz)
            return carry

        lax.fori_loop(0, half_tiles, tile, 0, unroll=3 if half_tiles % 3 == 0 else 1)


def inner_bands(bands, table, index):
    nx, rows, nz = bands.shape
    count = nx // 2 - 4

    def kernel(table_ref, index_ref, b_ref, out):
        def body(at, lanes, by, bz):
            quiet, loud = band_limits(table_ref, index_ref, by, bz)
            values = {i: b_ref[i, at, lanes] for i in range(nx)}
            for k, (low, high) in x_interior(values.get, nx).items():
                out[k - 2, at, lanes] = shrink(low, quiet) if by + bz else jnp.zeros_like(low)
                out[count + k - 2, at, lanes] = shrink(high, loud)

        over_tiles(rows, nz, body)

    return whole_call(
        kernel,
        shape(2 * count, rows, nz),
        [table, index, bands],
        30 * nx * rows * nz,
        8 * nx * rows * nz,
        name="inner_bands",
    )


def yz_synthesis(planes, z, y, out, zed):
    count, rows, nz = zed.shape
    group = max(g for g in range(1, 13) if count % g == 0)
    for first in range(0, count, group):
        zed[first : first + group] = times(planes(first, group), z).reshape(group, rows, nz)

    def y_body(first):
        for j in range(4):
            out[first + j] = left_times(y, zed[first + j])

    over_planes(count, 4, y_body)


def edge_details(bands, halo, h_left, h_right, table, index, ya_matrix, z_matrix, y_matrix):
    nx, rows, nz = bands.shape
    ny = y_matrix.shape[0]
    n1 = nx // 2
    half_z = nz // 2
    wide = h_left.shape[1] - 8
    ends = edges_of(n1)

    def kernel(table_ref, index_ref, b_ref, x_ref, hl, hr, ya, z, y, out, up, down, h_ref, coeffs, zed):
        for i in range(4):
            low = jnp.concatenate([hl[i, wide - 8 : wide], x_ref[i, :, :half_z], hr[i, :8]], axis=0)
            high = jnp.concatenate([hl[i, wide:], x_ref[i, :, half_z:], hr[i, wide:]], axis=0)
            h_ref[i] = left_times(ya, jnp.concatenate([low, high], axis=1))
        place = {"l1": 0, "l2": 1, "r1": 2, "r2": 3}

        def body(at, lanes, by, bz):
            quiet, loud = band_limits(table_ref, index_ref, by, bz)
            values = {key: h_ref[i, at, lanes] for key, i in place.items()}
            values.update({i: b_ref[i, at, lanes] for i in [*range(7), *range(nx - 7, nx)]})
            for i, k in enumerate(ends):
                low, high = x_low(values.get, k, nx), x_high(values.get, k, nx)
                coeffs[i, at, lanes] = shrink(low, quiet) if by + bz else jnp.zeros_like(low)
                coeffs[4 + i, at, lanes] = shrink(high, loud)

        over_tiles(rows, nz, body)
        yz_synthesis(lambda first, n: coeffs[first : first + n].reshape(n * rows, nz), z, y, out, zed)
        part = lambda ks, at: {k: out[i] for k, i in zip(ks, at)}
        up[0], up[1] = spill_up(part((0, 1), (2, 3)), part((0, 1), (6, 7)), 2)
        down[0], down[1] = spill_down(part((0, 1), (0, 1)), part((0, 1), (4, 5)))

    return whole_call(
        kernel,
        [shape(8, ny, nz), shape(2, ny, nz), shape(2, ny, nz)],
        [table, index, bands, halo, h_left, h_right, ya_matrix, z_matrix, y_matrix],
        48 * rows * nz * (nz + ny),
        4 * nx * rows * nz,
        scratch=[pltpu.VMEM((4, rows, nz), F32)] + [pltpu.VMEM((8, rows, nz), F32)] * 2,
        name="edge_details",
    )


def inner_yz(coeffs, approx, z_matrix, y_matrix):
    count, rows, nz = coeffs.shape
    ny = y_matrix.shape[0]
    _, low_rows, half_z = approx.shape
    lows = count // 2

    def kernel(c_ref, a_ref, z, y, out, zed):
        def plane(i):
            if i >= lows:
                return c_ref[i]
            corner = c_ref[i, :low_rows, :half_z] + a_ref[i + 4]
            top = jnp.concatenate([corner, c_ref[i, :low_rows, half_z:]], axis=1)
            return jnp.concatenate([top, c_ref[i, low_rows:]], axis=0)

        def planes(first, n):
            return jnp.concatenate([plane(i) for i in range(first, first + n)], axis=0)

        yz_synthesis(planes, z, y, out, zed)

    return whole_call(
        kernel,
        shape(count, ny, nz),
        [coeffs, approx, z_matrix, y_matrix],
        6 * count * rows * nz * (nz + ny),
        4 * count * nz * (rows + ny),
        scratch=[pltpu.VMEM((count, rows, nz), F32)],
        name="inner_yz",
    )


def own_result(edge, rest, approx, z_matrix, y_matrix):
    count, ny, nz = rest.shape
    n1 = (count + 8) // 2
    nx = 2 * n1
    ends = edges_of(n1)
    planes, rows, half_z = approx.shape

    def kernel(e_ref, r_ref, a_ref, z, y, out, parts):
        for first in (0, 4):
            start = first and n1
            zed = times(a_ref[start : start + 4].reshape(4 * rows, half_z), z)
            for j, plane in enumerate(cut(zed, rows)):
                parts[first + j] = left_times(y, plane)
        place = {k: i for i, k in enumerate([-2, -1, 0, 1, n1 - 2, n1 - 1, n1, n1 + 1])}

        def tile(t, carry):
            at = pl.ds(pl.multiple_of(t * 8, 8), 8)
            for lane in range(0, nz, 128):
                lanes = pl.ds(lane, 128)

                def coeff(k, high):
                    if k in ends:
                        return e_ref[4 * high + ends.index(k), at, lanes]
                    return r_ref[(n1 - 4) * high + k - 2, at, lanes]

                lows = {k: coeff(k, 0) for k in range(n1)}
                highs = {k: coeff(k, 1) for k in range(n1)}
                for k, i in place.items():
                    part = parts[i, at, lanes]
                    lows[k] = lows[k] + part if k in lows else part
                cells = x_synth_interior(lows, highs, n1)
                for m in range(nx):
                    out[m, at, lanes] = cells[m] if m in cells else x_synth(m, lows, highs)
            return carry

        lax.fori_loop(0, ny // 8, tile, 0)

    return whole_call(
        kernel,
        shape(nx, ny, nz),
        [edge, rest, approx, z_matrix, y_matrix],
        16 * nx * ny * nz,
        8 * nx * ny * nz,
        scratch=[pltpu.VMEM((8, ny, nz), F32)],
        name="own_result",
    )


def in_pairs(matrix, planes):
    results = []
    for i in range(0, len(planes), 2):
        both = left_times(matrix, jnp.concatenate(planes[i : i + 2], axis=1))
        width = both.shape[1] // 2
        results += [both[:, :width], both[:, width:]]
    return results


def cut(values, rows):
    return [values[i : i + rows] for i in range(0, values.shape[0], rows)]


def packed(first, second):
    half = first.shape[1] // 2
    lane = lax.broadcasted_iota(jnp.int32, first.shape, 1)
    return jnp.where(lane < half, first, pltpu.roll(second, half, 1))


def unpacked(both):
    half = both.shape[1] // 2
    lane = lax.broadcasted_iota(jnp.int32, both.shape, 1)
    return [jnp.where(lane < half, part, 0.0) for part in (both, pltpu.roll(both, half, 1))]


def second_bands(own, left, right, z_matrix, y_matrix, low_rows):
    planes, own_rows, nz = own.shape
    n1 = planes - 4
    in_rows = own_rows + 2 * left.shape[1]
    rows = y_matrix.shape[0]


    def kernel(o_ref, l_ref, r_ref, z, y, out, up, down):
        for i in range(0, planes, 10):
            stack = [part[j] for j in range(i, i + 10) for part in (o_ref, l_ref, r_ref)]
            zed = times_wide(jnp.concatenate(stack, axis=0), z)
            for j, plane in enumerate(in_pairs(y, cut(zed, in_rows))):
                out[i + j] = plane
        low = lambda c: out[c, :low_rows]
        up[0:rows] = out[n1 - 1]
        up[rows : 2 * rows] = H[0] * out[n1 - 3] + H[1] * out[n1 - 2]
        first = added([(H[j], low(n1 - 5 + j)) for j in range(5)])
        second = added([(H[0] * H[j], low(n1 - 9 + j)) for j in range(8)])
        second += added([(H[1] * H[j], low(n1 - 7 + j)) for j in range(7)])
        up[2 * rows :] = packed(first, second)
        down[0:rows] = out[0]
        down[rows : 2 * rows] = H[6] * out[1] + H[7] * out[2]
        first = added([(H[j], low(j - 3)) for j in range(3, 8)])
        second = added([(H[6] * H[j], low(j - 1)) for j in range(1, 8)])
        second += added([(H[7] * H[j], low(j + 1)) for j in range(8)])
        down[2 * rows :] = packed(first, second)

    message = 2 * rows + low_rows
    return whole_call(
        kernel,
        [shape(planes, rows, nz), shape(message, nz), shape(message, nz)],
        [own, left, right, z_matrix, y_matrix],
        6 * n1 * in_rows * nz * (nz + rows),
        4 * n1 * nz * (in_rows + rows),
        name="second_bands",
    )


def limits_plane(table_ref, index_ref, level, bx, dims, row_split, lane_split, zeroth):
    row_high = lax.broadcasted_iota(jnp.int32, dims, 0) >= row_split
    lane_high = lax.broadcasted_iota(jnp.int32, dims, 1) >= lane_split

    def limit(by, bz):
        band = 4 * bx + 2 * by + bz
        return zeroth if band == 0 else table_ref[index_ref[level, band - 1]]

    low_y = jnp.where(lane_high, limit(0, 1), limit(0, 0))
    return jnp.where(row_high, jnp.where(lane_high, limit(1, 1), limit(1, 0)), low_y)


def coarse(
    bands, left, right, halo, h_left, h_right, table, index, za1, yx0, ya1, zs1, za2, zs2, ya2, ys2, ys1,
    in_rows1, low_rows, out_rows, own_rows, spill_at, spill_rows,
):
    planes_in, rows, nz = bands.shape
    n1 = planes_in - 4
    in_rows = in_rows1
    wide = h_left.shape[1] - 8
    n2, n3 = n1 // 2, n1 // 4
    rows2 = ya2.shape[0]
    lane_half = nz // 2

    def kernel(
        table_ref, index_ref, b_ref, l_ref, r_ref, x_ref, hl, hr, z1a, yx, a1, z1, z2a, z2s, a2, s2, s1,
        approx, up, down, c1, p1,
    ):
        halo_planes = [jnp.concatenate([hl[i, :wide], x_ref[i, :, :nz], hr[i, :wide]], axis=0) for i in range(4)]
        halo_planes = jnp.concatenate([plane[:in_rows] for plane in in_pairs(yx, halo_planes)], axis=0)
        hl1, hl2, hr1, hr2 = in_pairs(a1, cut(times_wide(halo_planes, z1a), in_rows))
        values = {k: b_ref[k] for k in range(2, n1 - 2)}
        values[0] = b_ref[0] + (hl2 + H[2] * hl1)
        values[1] = b_ref[1] + H[0] * hl1
        values[n1 - 2] = b_ref[n1 - 2] + H[7] * hr1
        values[n1 - 1] = b_ref[n1 - 1] + (hr2 + H[5] * hr1)
        xl1, xl2, xr1, xr2 = [b_ref[n1 + i] for i in range(4)]
        values["l1"] = l_ref[0:rows] + xl1
        values["l2"] = l_ref[rows : 2 * rows] + xl2
        values["r1"] = r_ref[0:rows] + xr1
        values["r2"] = r_ref[rows : 2 * rows] + xr2
        get = values.get
        low_part = lambda c: values[c][:low_rows]
        xl1, xl2, xr1, xr2 = [part[:low_rows] for part in (xl1, xl2, xr1, xr2)]
        dims = (rows, nz)
        quiet = limits_plane(table_ref, index_ref, 1, 0, dims, low_rows, lane_half, NOTHING)
        loud = limits_plane(table_ref, index_ref, 1, 1, dims, low_rows, lane_half, NOTHING)
        planes = []
        for k in range(n2):
            low = x_low(get, k, n1)
            planes.append(low[:low_rows])
            c1[k] = shrink(low, quiet)
            c1[n2 + k] = shrink(x_high(get, k, n1), loud)
        first, second = unpacked(l_ref[2 * rows :])
        own = [(H[5 + i], low_part(i)) for i in range(3)]
        planes.append(first + added([(H[3] / H[1], xl2), (H[4], xl1)] + own))
        own = [((H[0] * H[7] + H[1] * H[5]) / H[1], xl2), (H[1] * H[6], xl1), (H[1] * H[7], low_part(0))]
        planes.append(second + added(own))
        first, second = unpacked(r_ref[2 * rows :])
        own = [(H[i], low_part(n1 - 3 + i)) for i in range(3)]
        planes.append(first + added([(H[3], xr1), (H[4] / H[6], xr2)] + own))
        own = [((H[6] * H[2] + H[7] * H[0]) / H[6], xr2), (H[6] * H[1], xr1), (H[6] * H[0], low_part(n1 - 1))]
        planes.append(second + added(own))
        third = in_pairs(a2, cut(times_wide(jnp.concatenate(planes, axis=0), z2a), low_rows))
        keys = {"l1": n2, "l2": n2 + 1, "r1": n2 + 2, "r2": n2 + 3}
        get2 = lambda key: third[keys.get(key, key)]
        dims = (rows2, nz)
        quiet = limits_plane(table_ref, index_ref, 2, 0, dims, rows2 // 2, lane_half // 2, 0.0)
        loud = limits_plane(table_ref, index_ref, 2, 1, dims, rows2 // 2, lane_half // 2, 0.0)
        kept = [shrink(x_low(get2, k, n2), quiet) for k in range(n3)]
        kept += [shrink(x_high(get2, k, n2), loud) for k in range(n3)]
        parts = in_pairs(s2, cut(times_wide(jnp.concatenate(kept, axis=0), z2s), rows2))
        parts = [part[:low_rows] for part in parts]
        lows = dict(enumerate(parts[:n3]))
        highs = dict(enumerate(parts[n3:]))
        ghosts = [-3, -2, -1, n2, n2 + 1, n2 + 2]
        for k in range(n2):
            c1[k, :low_rows] += x_synth(k, lows, highs)
        stack = [x_synth(k, lows, highs) for k in ghosts]
        beyond = dict(zip(ghosts, stack))
        zed = times_wide(jnp.concatenate(stack, axis=0), z1)
        for i, plane in enumerate(in_pairs(s1, cut(zed, low_rows))):
            p1[2 * n2 + i] = plane[:out_rows]
        for i in range(0, 2 * n2, 8):
            zed = times_wide(c1[i : i + 8].reshape(8 * rows, nz), z1)
            for j, plane in enumerate(in_pairs(s1, cut(zed, rows))):
                p1[i + j] = plane[:out_rows]
        lows = {k: p1.at[k] for k in range(n2)}
        highs = {k: p1.at[n2 + k] for k in range(n2)}
        for i, k in enumerate(ghosts):
            lows[k] = p1.at[2 * n2 + i]

        def cell(m):
            near = lambda part: {k: ref[...] for k, ref in part.items() if 0 <= m + 3 - 2 * k < 8}
            return x_synth(m, near(lows), near(highs))

        for m in range(-2, n1 + 2):
            approx[m + 2] = cell(m)
        value = lambda part, ks: {k: part[k][...] for k in ks}
        ends = (n2 - 2, n2 - 1)

        def send(message, four, two):
            for i, plane in enumerate(four):
                message[i * own_rows : (i + 1) * own_rows] = plane[:own_rows]
                message[4 * own_rows + 4 * i : 4 * own_rows + 4 * i + 4] = plane[own_rows : own_rows + 4]
            message[4 * own_rows + 16 :] = packed(*two)[spill_at : spill_at + spill_rows]

        up_two = spill_up(value(lows, ends), value(highs, ends), n2)
        send(up, (approx[n1], approx[n1 + 1], *up_two), (beyond[n2], beyond[n2 + 1]))
        down_two = spill_down(value(lows, (0, 1)), value(highs, (0, 1)))
        send(down, (approx[2], approx[3], *down_two), (beyond[-1], beyond[-2]))

    message = 4 * own_rows + 16 + spill_rows
    return whole_call(
        kernel,
        [shape(n1 + 4, out_rows, nz), shape(message, nz), shape(message, nz)],
        [table, index, bands, left, right, halo, h_left, h_right, za1, yx0, ya1, zs1, za2, zs2, ya2, ys2, ys1],
        1.5e9,
        8 * n1 * rows * nz,
        scratch=[pltpu.VMEM((2 * n2, rows, nz), F32), pltpu.VMEM((2 * n2 + 6, out_rows, nz), F32)],
        name="coarse",
    )


def received_taps(n1):
    n2, nx = n1 // 2, 2 * n1
    from_approx = np.zeros((nx, n1 + 4))
    for m in range(nx):
        for k in range(-2, n1 + 2):
            from_approx[m, k + 2] = tap(H, m + 3 - 2 * k)
    approx = np.zeros((n1 + 4, 12))
    third = {0: THIRD_UP, 6: THIRD_DOWN}
    for first, cell, second in ((0, lambda i: i, lambda i: i), (6, lambda i: n1 - 1 - i, lambda i: n2 - 1 - i)):
        ghost = (-2, -1) if first == 0 else (n1, n1 + 1)
        for i in range(2):
            approx[ghost[i] + 2, first + i] = 1.0
        for place, source, coef in ((0, 0, 1.0), (1, 1, 1.0), (2, 1, third[first])):
            approx[cell(place) + 2, first + 2 + source] += coef
            for m in range(n1):
                approx[m + 2, first + 4 + source] += coef * tap(H, m + 3 - 2 * second(place))
    return from_approx @ approx


def final(left, right, own, e_left, e_right, zs1, ys1, z_matrix, y_matrix, rows, spill_rows):
    nx, ny, nz = own.shape
    half_z = nz // 2
    own_rows = ny // 2
    step_rows = 16
    steps = ny // step_rows
    taps = received_taps(nx // 2)

    def kernel(l_ref, r_ref, d_ref, el, er, z1, s1, z, y, out, planes, parts, done, sems):
        stack = [p for ref in (l_ref, r_ref) for p in unpacked(ref[4 * own_rows + 16 :])]
        zed = times_wide(jnp.concatenate(stack, axis=0), z1)
        spilled = [p[:rows] for p in in_pairs(s1, cut(zed, spill_rows))]
        for side, ref in enumerate((l_ref, r_ref)):
            for i in range(4):
                plane = planes.at[6 * side + i]
                plane[:own_rows] = ref[i * own_rows : (i + 1) * own_rows]
                plane[own_rows:] = jnp.zeros((rows - own_rows, half_z), F32)
                plane[own_rows : own_rows + 4] = ref[4 * own_rows + 4 * i : 4 * own_rows + 4 * i + 4]
            for i in range(2):
                planes[6 * side + 4 + i] = spilled[2 * side + i]
        for i, plane in enumerate(cut(times(planes[...].reshape(12 * rows, half_z), z), rows)):
            parts[i] = left_times(y, plane)

        def copy(i):
            at = pl.ds(pl.multiple_of(i * step_rows, step_rows), step_rows)
            return pltpu.make_async_copy(done.at[:, at], out.at[:, at], sems.at[i])

        def step(i, carry):
            for t in range(step_rows // 8):
                at = pl.ds(pl.multiple_of(i * step_rows + 8 * t, 8), 8)
                for lane in range(0, nz, 128):
                    lanes = pl.ds(lane, 128)
                    values = [parts[i, at, lanes] for i in range(12)]
                    for m in range(nx):
                        value = d_ref[m, at, lanes]
                        value += added([(float(c), v) for c, v in zip(taps[m], values) if c != 0.0])
                        if m < 3:
                            extra = el[(0, 1, 1)[m], at, lanes]
                            value += extra if m < 2 else THIRD_UP * extra
                        if m >= nx - 3:
                            extra = er[(0, 1, 1)[nx - 1 - m], at, lanes]
                            value += extra if m > nx - 3 else THIRD_DOWN * extra
                        done[m, at, lanes] = value
            copy(i).start()
            return carry

        lax.fori_loop(0, steps, step, 0)

        def finish(i, carry):
            copy(i).wait()
            return carry

        lax.fori_loop(0, steps, finish, 0)

    return pl.pallas_call(
        kernel,
        in_specs=[VMEM] * 9,
        out_specs=pl.BlockSpec(memory_space=pl.ANY),
        out_shape=shape(nx, ny, nz),
        scratch_shapes=[
            pltpu.VMEM((12, rows, half_z), F32),
            pltpu.VMEM((12, ny, nz), F32),
            pltpu.VMEM((nx, ny, nz), F32),
            pltpu.SemaphoreType.DMA((steps,)),
        ],
        name="final",
        cost_estimate=pl.CostEstimate(flops=8 * nx * ny * nz, bytes_accessed=8 * nx * ny * nz, transcendentals=0),
        compiler_params=pltpu.CompilerParams(vmem_limit_bytes=VMEM_BYTES),
    )(left, right, own, e_left, e_right, zs1, ys1, z_matrix, y_matrix)


def to_next(array, axis):
    size = lax.axis_size(axis)
    return lax.ppermute(array, axis, [(i, (i + 1) % size) for i in range(size)])


def to_previous(array, axis):
    size = lax.axis_size(axis)
    return lax.ppermute(array, axis, [((i + 1) % size, i) for i in range(size)])


def local(velocity, table, index):
    nx, ny, nz = velocity.shape
    y1, y2, y3 = ny // 2, ny // 4, ny // 8
    ghost, wide = 24, 48
    cells0 = list(range(-8, ny + 8))
    rows0 = up_to(y1 + 4, 8)
    ks0 = fill(list(range(y1)) + [-2, -1, y1, y1 + 1], rows0)
    cells1 = ks0 + list(range(2 - ghost, 2)) + list(range(y1 - 2, y1 + ghost - 2))
    once = [c if cells1.index(c) == i else None for i, c in enumerate(cells1)]
    rows1 = up_to(y2 + 18, 8)
    low1 = fill(list(range(-9, y2 + 9)), rows1)
    high1 = fill(list(range(-3, y2 + 3)), up_to(y2 + 6, 8))
    spill_at, spill_rows = 6, up_to(y2 + 6, 8)
    ks2 = fill(list(range(-3, y3 + 3)), up_to(y3 + 6, 8))
    ya0 = from_left(analysis_rows(cells0, ks0, ks0))
    ys0_matrix = synthesis_rows(list(range(ny)), ks0, ks0)
    ys0 = from_left(ys0_matrix)
    ys0_low = from_left(ys0_matrix[:, :rows0])
    yl0 = from_left(analysis_rows(list(range(ny)), ks0, []))
    yx0 = from_left(analysis_rows(list(range(-wide, ny + wide)), once, []))
    ya1 = from_left(analysis_rows(cells1, low1, high1))
    ys1 = from_left(synthesis_rows(ks0, low1, high1))
    ys1_spill = from_left(synthesis_rows(ks0, low1[spill_at : spill_at + spill_rows], []))
    ya2 = from_left(analysis_rows(low1, ks2, ks2))
    ys2 = from_left(synthesis_rows(low1, ks2, ks2))
    z0 = periodic(nz, nz)
    z1 = periodic(nz // 2, nz // 2)
    z2 = periodic(nz // 4, nz // 2)
    za0, zs0, zs0_low = from_right(z0), from_right(z0.T), from_right(z0.T[: nz // 2])
    za1, zs1 = wide_right(z1), wide_right(z1.T)
    za2, zs2 = wide_right(z2), wide_right(z2.T)

    x_up, x_down, y_up, y_down = first_messages(velocity)
    x_left = to_next(x_up, "gx")
    x_right = to_previous(x_down, "gx")
    y_left = to_next(y_up, "gy")
    y_right = to_previous(y_down, "gy")
    zed = depth(velocity, za0, 16, "depth_analysis")
    approx, a_up, a_down = own_approx(zed, yl0, y1, rows0, ghost)
    a_left = to_next(a_up, "gy")
    a_right = to_previous(a_down, "gy")
    zed, a_up = lax.optimization_barrier((zed, a_up))
    bands = y_analysis(zed, y_left, y_right, za0, ya0)
    inner = inner_bands(bands, table, index)
    x_left, x_right, inner = lax.optimization_barrier((x_left, x_right, inner))
    halo, h_up, h_down = x_halo_messages(x_left, x_right, za0, wide)
    h_left = to_next(h_up, "gy")
    h_right = to_previous(h_down, "gy")
    approx, halo = lax.optimization_barrier((approx, halo))
    bands1, b_up, b_down = second_bands(approx, a_left, a_right, za1, ya1, rows1)
    b_left = to_next(b_up, "gx")
    b_right = to_previous(b_down, "gx")
    h_left, h_right, bands1 = lax.optimization_barrier((h_left, h_right, bands1))
    edge, e_up, e_down = edge_details(bands, halo, h_left, h_right, table, index, ya0, zs0, ys0)
    e_left = to_next(e_up, "gx")
    e_right = to_previous(e_down, "gx")
    bands1, edge = lax.optimization_barrier((bands1, edge))
    approx1, s_up, s_down = coarse(
        bands1, b_left, b_right, halo, h_left, h_right, table, index,
        za1, yx0, ya1, zs1, za2, zs2, ya2, ys2, ys1, len(cells1), rows1, rows0, y1, spill_at, spill_rows,
    )
    s_left = to_next(s_up, "gx")
    s_right = to_previous(s_down, "gx")
    rest = inner_yz(inner, approx1, zs0, ys0)
    own = own_result(edge, rest, approx1, zs0_low, ys0_low)
    return final(s_left, s_right, own, e_left, e_right, zs1, ys1_spill, zs0_low, ys0_low, rows0, spill_rows)


def solution(mesh):
    return jax.shard_map(
        local,
        mesh=mesh,
        in_specs=(P("gx", "gy", None), P(), P()),
        out_specs=P("gx", "gy", None),
        check_vma=False,
    )
```

```python
import functools

import jax
import jax.numpy as jnp
import ml_dtypes
import numpy as np
from jax import lax
from jax.experimental import pallas as pl
from jax.experimental.pallas import tpu as pltpu
from jax.sharding import PartitionSpec as P

H = [
    0.23037781330885523,
    0.7148465705525415,
    0.6308807679295904,
    -0.02798376941698385,
    -0.18703481171888114,
    0.030841381835986965,
    0.032883011666982945,
    -0.010597401784997278,
]
G = [(-1.0) ** j * H[7 - j] for j in range(8)]
F32 = jnp.float32
BF16 = jnp.bfloat16
NOTHING = 3.0e38
VMEM_BYTES = 16 * 1024 * 1024


def tap(filt, j):
    return filt[j] if 0 <= j < 8 else 0.0


def analysis_rows(cells, low_ks, high_ks):
    matrix = np.zeros((len(low_ks) + len(high_ks), len(cells)))
    rows = [(H, k) for k in low_ks] + [(G, k) for k in high_ks]
    for row, (filt, k) in enumerate(rows):
        for col, cell in enumerate(cells):
            if k is not None and cell is not None:
                matrix[row, col] = tap(filt, cell - 2 * k + 3)
    return matrix


def synthesis_rows(cells, low_ks, high_ks):
    return analysis_rows(cells, low_ks, high_ks).T


def periodic(length, padded_to):
    matrix = np.zeros((padded_to, padded_to))
    for k in range(length // 2):
        for j in range(8):
            matrix[(2 * k + j - 3) % length, k] += H[j]
            matrix[(2 * k + j - 3) % length, length // 2 + k] += G[j]
    return matrix


def fill(items, length):
    return items + [None] * (length - len(items))


def up_to(count, step):
    return -(-count // step) * step


def pieces(matrix, axis):
    rows, cols = matrix.shape
    matrix = np.pad(matrix, ((0, up_to(rows, 16) - rows), (0, up_to(cols, 16) - cols))).astype(np.float32)
    high = matrix.astype(ml_dtypes.bfloat16)
    low = (matrix - high.astype(np.float32)).astype(ml_dtypes.bfloat16)
    return np.concatenate([high, high, low], axis=axis)


def from_left(matrix):
    return pieces(matrix, 1)


def from_right(matrix):
    return pieces(matrix, 0)


def wide_right(matrix):
    rows, cols = matrix.shape
    both = pieces(matrix, 0)
    high, low = both[:rows], both[2 * rows :]
    return np.block([[high, low], [high, np.zeros_like(low)]])


def tall_left(matrix):
    return np.ascontiguousarray(wide_right(np.ascontiguousarray(padded_to_tiles(matrix).T)).T)


def padded_to_tiles(matrix):
    rows, cols = matrix.shape
    return np.pad(matrix, ((0, up_to(rows, 16) - rows), (0, up_to(cols, 16) - cols)))


def halves(values):
    high = values.astype(BF16)
    return high, (values - high.astype(F32)).astype(BF16)


def times(values, matrix):
    high, low = halves(values)
    return jnp.dot(jnp.concatenate([high, low, high], axis=1), matrix[...], preferred_element_type=F32)


def left_times(matrix, values):
    missing = matrix.shape[1] // 3 - values.shape[0]
    if missing:
        values = jnp.concatenate([values, jnp.zeros((missing, values.shape[1]), F32)], axis=0)
    high, low = halves(values)
    return jnp.dot(matrix[...], jnp.concatenate([high, low, high], axis=0), preferred_element_type=F32)


def times_wide(values, matrix):
    both = jnp.dot(jnp.concatenate(halves(values), axis=1), matrix[...], preferred_element_type=F32)
    return both[:, : both.shape[1] // 2] + both[:, both.shape[1] // 2 :]


def left_times_tall(matrix, values):
    missing = matrix.shape[1] // 2 - values.shape[0]
    if missing:
        values = jnp.concatenate([values, jnp.zeros((missing, values.shape[1]), F32)], axis=0)
    both = jnp.dot(matrix[...], jnp.concatenate(halves(values), axis=0), preferred_element_type=F32)
    return both[: both.shape[0] // 2] + both[both.shape[0] // 2 :]


def added(terms):
    total = None
    for coef, value in terms:
        part = value if coef == 1.0 else coef * value
        total = part if total is None else total + part
    return total


def x_terms(k, n):
    terms = []
    for j in range(8):
        cell = 2 * k + j - 3
        if 0 <= cell < n:
            terms.append((cell, H[j], G[j]))
        elif cell == -1:
            terms.append(("l1", H[j], G[j]))
        elif cell == n:
            terms.append(("r1", H[j], G[j]))
    if k == 0:
        terms.append(("l2", 1.0, G[0] / H[0]))
    if k == n // 2 - 1:
        terms.append(("r2", 1.0, G[6] / H[6]))
    return terms


def lattice():
    low = np.array(H).reshape(4, 2)
    high = np.array(G).reshape(4, 2)
    tangents = []
    for _ in range(3):
        t = (low[0] @ high[0]) / (high[0] @ high[0])
        tangents.append(float(t))
        low, high = (low - t * high)[1:] / (1 + t * t), (high + t * low)[:-1] / (1 + t * t)
    return low[0].tolist(), high[0].tolist(), tangents[::-1]


def x_interior(get, n):
    first, second, tangents = lattice()
    a, b = {}, {}
    for i in range(1, n // 2):
        x, y = get(2 * i - 1), get(2 * i)
        a[i] = first[0] * x + first[1] * y
        b[i] = second[0] * x + second[1] * y
    for t in tangents:
        shared = [i for i in a if i + 1 in a]
        a, b = {i: a[i + 1] + t * b[i] for i in shared}, {i: b[i] - t * a[i + 1] for i in shared}
    return {i + 1: (a[i], b[i]) for i in a}


def x_low(get, k, n):
    return added([(low, get(key)) for key, low, _ in x_terms(k, n)])


def x_high(get, k, n):
    return added([(high, get(key)) for key, _, high in x_terms(k, n)])


def x_synth(m, lows, highs):
    terms = [(H[m + 3 - 2 * k], v) for k, v in lows.items() if 0 <= m + 3 - 2 * k < 8]
    terms += [(G[m + 3 - 2 * k], v) for k, v in highs.items() if 0 <= m + 3 - 2 * k < 8]
    return added(terms)


def x_synth_interior(lows, highs, n):
    first, second, tangents = lattice()
    a = {k - 1: lows[k] for k in range(n)}
    b = {k - 1: highs[k] for k in range(n)}
    for t in reversed(tangents):
        a, b = {i + 1: a[i] - t * b[i] for i in a}, {i: b[i] + t * a[i] for i in b}
        both = [i for i in a if i in b]
        a, b = {i: a[i] for i in both}, {i: b[i] for i in both}
    cells = {}
    for i in a:
        cells[2 * i - 1] = first[0] * a[i] + second[0] * b[i]
        cells[2 * i] = first[1] * a[i] + second[1] * b[i]
    return cells


def spill_up(low, high, n):
    first = added([(H[5], low[n - 1]), (G[5], high[n - 1]), (H[7], low[n - 2]), (G[7], high[n - 2])])
    return first, added([(H[6], low[n - 1]), (G[6], high[n - 1])])


def spill_down(low, high):
    first = added([(H[2], low[0]), (G[2], high[0]), (H[0], low[1]), (G[0], high[1])])
    return first, added([(H[1], low[0]), (G[1], high[0])])


THIRD_UP = H[7] / H[6]
THIRD_DOWN = H[0] / H[1]


def shrink(values, thresh):
    return values - jnp.minimum(jnp.maximum(values, -thresh), thresh)


def paired(kernel, args, outs, scratch, received, sent):
    extra = [pltpu.VMEM((2,) + args[i].shape, F32) for i, _ in received]
    extra += [pltpu.VMEM((2,) + outs[j].shape, F32) for j, _ in sent]

    def wrapped(*refs):
        refs, both = list(refs[: len(refs) - len(extra)]), refs[len(refs) - len(extra) :]
        for (i, axis), pair in zip(received, both):
            parity = lax.rem(lax.axis_index(axis), 2)
            pair[0], pair[1] = refs[i][...], refs[i + 1][...]
            refs[i], refs[i + 1] = pair.at[1 - parity], pair.at[parity]
        carried = []
        for (j, axis), pair in zip(sent, both[len(received) :]):
            parity = lax.rem(lax.axis_index(axis), 2)
            j += len(args)
            carried.append((refs[j], refs[j + 1], pair))
            refs[j], refs[j + 1] = pair.at[parity], pair.at[1 - parity]
        kernel(*refs)
        for first, second, pair in carried:
            first[...], second[...] = pair[0], pair[1]

    return wrapped, list(scratch) + extra


def whole_call(kernel, outs, args, scratch=(), received=(), sent=(), name=None, **changes):
    out_list = outs if isinstance(outs, list) else [outs]
    kernel, scratch = paired(kernel, args, out_list, scratch, received, sent)
    specs = [SMEM if a.ndim == 1 or a.dtype == jnp.int32 else VMEM for a in args]
    return pl.pallas_call(
        kernel,
        in_specs=changes.get("in_specs", specs),
        out_specs=changes.get("out_specs", [VMEM] * len(outs) if outs is out_list else VMEM),
        out_shape=outs,
        scratch_shapes=scratch,
        name=name,
        cost_estimate=pl.CostEstimate(flops=1000, bytes_accessed=1000, transcendentals=0),
        compiler_params=pltpu.CompilerParams(vmem_limit_bytes=changes.get("vmem", VMEM_BYTES)),
    )(*args)


def shape(*dims):
    return jax.ShapeDtypeStruct(dims, F32)


SMEM = pl.BlockSpec(memory_space=pltpu.SMEM)
VMEM = pl.BlockSpec(memory_space=pltpu.VMEM)


def first_messages(v):
    nx, ny, nz = v.shape

    kept = nx - nx // 8

    def kernel(v_ref, up, down, y_up, y_down, last, first, rows_up, rows_down, sems):
        copies = [
            pltpu.make_async_copy(source, target, sems.at[i])
            for i, (source, target) in enumerate(
                (
                    (v_ref.at[pl.ds(nx - 3, 3)], last),
                    (v_ref.at[pl.ds(0, 3)], first),
                    (v_ref.at[:, pl.ds(ny - 8, 8)], rows_up),
                    (v_ref.at[:, pl.ds(0, 8)], rows_down),
                )
            )
        ]
        for copy in copies:
            copy.start()
        for copy in copies:
            copy.wait()
        up[0] = last[2]
        up[1] = H[0] * last[0] + H[1] * last[1]
        down[0] = first[0]
        down[1] = H[6] * first[1] + H[7] * first[2]
        y_up[...] = rows_up[:kept]
        y_down[...] = rows_down[:kept]
        for i in range(kept):
            plane, row = kept + i // 7, i % 7
            y_up[i, 0:1] = rows_up[plane, row + 1 : row + 2]
            y_down[i, 7:8] = rows_down[plane, row : row + 1]

    return whole_call(
        kernel,
        [shape(2, ny, nz)] * 2 + [shape(kept, 8, nz)] * 2,
        [v],
        scratch=[pltpu.VMEM((3, ny, nz), F32)] * 2
        + [pltpu.VMEM((nx, 8, nz), F32)] * 2
        + [pltpu.SemaphoreType.DMA((4,))],
        sent=[(0, "gx"), (2, "gy")],
        name="first_messages",
        in_specs=[pl.BlockSpec(memory_space=pltpu.HBM)],
        vmem=50 * 1024 * 1024,
    )


def over_planes(count, group, body):
    def step(i, carry):
        body(i * group)
        return carry

    lax.fori_loop(0, count // group, step, 0)


def depth(v, z_matrix, group, name):
    nx, rows, nz = v.shape

    def kernel(v_ref, z, out):
        def body(first):
            at = pl.ds(first, group)
            out[at] = times(v_ref[at].reshape(group * rows, nz), z).reshape(group, rows, nz)

        over_planes(nx, group, body)

    return whole_call(kernel, shape(nx, rows, nz), [v, z_matrix], name=name)


def y_analysis(zed, y_left, y_right, z_matrix, y_matrix):
    nx, ny, nz = zed.shape
    rows = y_matrix.shape[0]
    kept = y_left.shape[0]
    group = 8

    def kernel(zed_ref, left, right, z, y, out, left_z, right_z):
        for part, out_z in ((left, left_z), (right, right_z)):
            out_z[:kept] = times(part[...].reshape(8 * kept, nz), z).reshape(kept, 8, nz)
            out_z[kept:] = jnp.zeros((nx - kept, 8, nz), F32)
        for i in range(kept):
            plane, row = kept + i // 7, i % 7
            left_z[plane, row + 1 : row + 2] = left_z[i, 0:1]
            right_z[plane, row : row + 1] = right_z[i, 7:8]

        def body(first):
            for j in range(group):
                i = first + j
                out[i] = left_times(y, jnp.concatenate([left_z[i], zed_ref[i], right_z[i]], axis=0))

        over_planes(nx, group, body)

    return whole_call(
        kernel,
        shape(nx, rows, nz),
        [zed, y_left, y_right, z_matrix, y_matrix],
        scratch=[pltpu.VMEM((nx, 8, nz), F32)] * 2,
        received=[(1, "gy")],
        name="y_analysis",
    )


def own_approx(zed, y_matrix, own, rows, ghost_rows):
    nx, ny, nz = zed.shape
    half_z = nz // 2
    n1 = nx // 2

    def kernel(zed_ref, y, approx, up, down, low):
        def y_body(first):
            planes = [zed_ref[first + i, :, :half_z] for i in range(8)]
            for i, plane in enumerate(in_pairs(y, planes)):
                low[first + i] = plane[:rows]

        over_planes(nx, 8, y_body)

        def tile(t, carry):
            at = pl.ds(pl.multiple_of(t * 8, 8), 8)
            values = {i: low[i, at] for i in range(nx)}
            for k in range(n1):
                approx[k, at] = added([(c, values[i]) for i, c, _ in x_terms(k, nx) if i in values])
            approx[n1, at] = added([(H[5 + i], values[i]) for i in range(3)])
            approx[n1 + 1, at] = H[1] * H[7] * values[0]
            approx[n1 + 2, at] = added([(H[i], values[nx - 3 + i]) for i in range(3)])
            approx[n1 + 3, at] = H[6] * H[0] * values[nx - 1]
            return carry

        lax.fori_loop(0, rows // 8, tile, 0)
        inside = ghost_rows - 2
        up[:, :inside] = approx[:, own - inside : own]
        up[:, inside:] = approx[:, own + 2 : own + 4]
        down[:, :2] = approx[:, own : own + 2]
        down[:, 2:] = approx[:, :inside]

    return whole_call(
        kernel,
        [shape(n1 + 4, rows, half_z), shape(n1 + 4, ghost_rows, half_z), shape(n1 + 4, ghost_rows, half_z)],
        [zed, y_matrix],
        scratch=[pltpu.VMEM((nx, rows, half_z), F32)],
        sent=[(1, "gy")],
        name="own_approx",
    )


def x_halo_messages(x_left, x_right, z_matrix, wide):
    _, ny, nz = x_left.shape
    half_z = nz // 2

    def kernel(xl, xr, z, out, up, down):
        planes = jnp.concatenate([xl[0], xl[1], xr[0], xr[1]], axis=0)
        out[...] = times(planes, z).reshape(4, ny, nz)
        up[:, :wide] = out[:, ny - wide :, :half_z]
        up[:, wide:] = out[:, ny - 8 :, half_z:]
        down[:, :wide] = out[:, :wide, :half_z]
        down[:, wide:] = out[:, :8, half_z:]

    return whole_call(
        kernel,
        [shape(4, ny, nz), shape(4, wide + 8, half_z), shape(4, wide + 8, half_z)],
        [x_left, x_right, z_matrix],
        received=[(0, "gx")],
        sent=[(1, "gy")],
        name="x_halo_messages",
    )


def edges_of(n):
    return [0, 1, n - 2, n - 1]


def band_limits(table_ref, index_ref, by, bz):
    band = 2 * by + bz
    quiet = table_ref[index_ref[0, band - 1]] if band else NOTHING
    return quiet, table_ref[index_ref[0, band + 3]]


def over_tiles(rows, nz, body):
    half_z, half_tiles = nz // 2, rows // 16
    for by in range(2):

        def tile(t, carry, by=by):
            at = pl.ds(pl.multiple_of((t + by * half_tiles) * 8, 8), 8)
            for bz in range(2):
                body(at, pl.ds(bz * half_z, half_z), by, bz)
            return carry

        lax.fori_loop(0, half_tiles, tile, 0, unroll=3 if half_tiles % 3 == 0 else 1)


def inner_bands(bands, table, index):
    nx, rows, nz = bands.shape
    count = nx // 2 - 4

    def kernel(table_ref, index_ref, b_ref, out):
        def body(at, lanes, by, bz):
            quiet, loud = band_limits(table_ref, index_ref, by, bz)
            values = {i: b_ref[i, at, lanes] for i in range(nx)}
            for k, (low, high) in x_interior(values.get, nx).items():
                out[k - 2, at, lanes] = shrink(low, quiet) if by + bz else jnp.zeros_like(low)
                out[count + k - 2, at, lanes] = shrink(high, loud)

        over_tiles(rows, nz, body)

    return whole_call(
        kernel,
        shape(2 * count, rows, nz),
        [table, index, bands],
        name="inner_bands",
    )


def yz_synthesis(planes, z, y, out, zed):
    count, rows, nz = zed.shape
    group = max(g for g in range(1, 13) if count % g == 0)
    for first in range(0, count, group):
        zed[first : first + group] = times(planes(first, group), z).reshape(group, rows, nz)

    def y_body(first):
        for j in range(4):
            out[first + j] = left_times(y, zed[first + j])

    over_planes(count, 4, y_body)


def edge_details(bands, halo, h_left, h_right, table, index, ya_matrix, z_matrix, y_matrix):
    nx, rows, nz = bands.shape
    ny = y_matrix.shape[0]
    n1 = nx // 2
    half_z = nz // 2
    wide = h_left.shape[1] - 8
    ends = edges_of(n1)

    def kernel(table_ref, index_ref, b_ref, x_ref, hl, hr, ya, z, y, out, up, down, h_ref, coeffs, zed):
        for i in range(4):
            low = jnp.concatenate([hl[i, wide - 8 : wide], x_ref[i, :, :half_z], hr[i, :8]], axis=0)
            high = jnp.concatenate([hl[i, wide:], x_ref[i, :, half_z:], hr[i, wide:]], axis=0)
            h_ref[i] = left_times(ya, jnp.concatenate([low, high], axis=1))
        place = {"l1": 0, "l2": 1, "r1": 2, "r2": 3}

        def body(at, lanes, by, bz):
            quiet, loud = band_limits(table_ref, index_ref, by, bz)
            values = {key: h_ref[i, at, lanes] for key, i in place.items()}
            values.update({i: b_ref[i, at, lanes] for i in [*range(7), *range(nx - 7, nx)]})
            for i, k in enumerate(ends):
                low, high = x_low(values.get, k, nx), x_high(values.get, k, nx)
                coeffs[i, at, lanes] = shrink(low, quiet) if by + bz else jnp.zeros_like(low)
                coeffs[4 + i, at, lanes] = shrink(high, loud)

        over_tiles(rows, nz, body)
        yz_synthesis(lambda first, n: coeffs[first : first + n].reshape(n * rows, nz), z, y, out, zed)
        part = lambda ks, at: {k: out[i] for k, i in zip(ks, at)}
        up[0], up[1] = spill_up(part((0, 1), (2, 3)), part((0, 1), (6, 7)), 2)
        down[0], down[1] = spill_down(part((0, 1), (0, 1)), part((0, 1), (4, 5)))

    return whole_call(
        kernel,
        [shape(8, ny, nz), shape(2, ny, nz), shape(2, ny, nz)],
        [table, index, bands, halo, h_left, h_right, ya_matrix, z_matrix, y_matrix],
        scratch=[pltpu.VMEM((4, rows, nz), F32)] + [pltpu.VMEM((8, rows, nz), F32)] * 2,
        received=[(4, "gy")],
        sent=[(1, "gx")],
        name="edge_details",
    )


def inner_yz(coeffs, approx, z_matrix, y_matrix):
    count, rows, nz = coeffs.shape
    ny = y_matrix.shape[0]
    _, low_rows, half_z = approx.shape
    lows = count // 2

    def kernel(c_ref, a_ref, z, y, out, zed):
        def plane(i):
            if i >= lows:
                return c_ref[i]
            corner = c_ref[i, :low_rows, :half_z] + a_ref[i + 4]
            top = jnp.concatenate([corner, c_ref[i, :low_rows, half_z:]], axis=1)
            return jnp.concatenate([top, c_ref[i, low_rows:]], axis=0)

        def planes(first, n):
            return jnp.concatenate([plane(i) for i in range(first, first + n)], axis=0)

        yz_synthesis(planes, z, y, out, zed)

    return whole_call(
        kernel,
        shape(count, ny, nz),
        [coeffs, approx, z_matrix, y_matrix],
        scratch=[pltpu.VMEM((count, rows, nz), F32)],
        name="inner_yz",
    )


def own_result(edge, rest, approx, z_matrix, y_matrix):
    count, ny, nz = rest.shape
    n1 = (count + 8) // 2
    nx = 2 * n1
    ends = edges_of(n1)
    planes, rows, half_z = approx.shape

    def kernel(e_ref, r_ref, a_ref, z, y, out, parts):
        for first in (0, 4):
            start = first and n1
            zed = times(a_ref[start : start + 4].reshape(4 * rows, half_z), z)
            for j, plane in enumerate(cut(zed, rows)):
                parts[first + j] = left_times(y, plane)
        place = {k: i for i, k in enumerate([-2, -1, 0, 1, n1 - 2, n1 - 1, n1, n1 + 1])}

        def tile(t, carry):
            at = pl.ds(pl.multiple_of(t * 8, 8), 8)
            for lane in range(0, nz, 128):
                lanes = pl.ds(lane, 128)

                def coeff(k, high):
                    if k in ends:
                        return e_ref[4 * high + ends.index(k), at, lanes]
                    return r_ref[(n1 - 4) * high + k - 2, at, lanes]

                lows = {k: coeff(k, 0) for k in range(n1)}
                highs = {k: coeff(k, 1) for k in range(n1)}
                for k, i in place.items():
                    part = parts[i, at, lanes]
                    lows[k] = lows[k] + part if k in lows else part
                cells = x_synth_interior(lows, highs, n1)
                for m in range(nx):
                    out[m, at, lanes] = cells[m] if m in cells else x_synth(m, lows, highs)
            return carry

        lax.fori_loop(0, ny // 8, tile, 0)

    return whole_call(
        kernel,
        shape(nx, ny, nz),
        [edge, rest, approx, z_matrix, y_matrix],
        scratch=[pltpu.VMEM((8, ny, nz), F32)],
        name="own_result",
    )


def in_pairs(matrix, planes):
    results = []
    for i in range(0, len(planes), 2):
        both = left_times(matrix, jnp.concatenate(planes[i : i + 2], axis=1))
        width = both.shape[1] // 2
        results += [both[:, :width], both[:, width:]]
    return results


def cut(values, rows):
    return [values[i : i + rows] for i in range(0, values.shape[0], rows)]


def packed(first, second):
    half = first.shape[1] // 2
    lane = lax.broadcasted_iota(jnp.int32, first.shape, 1)
    return jnp.where(lane < half, first, pltpu.roll(second, half, 1))


def unpacked(both):
    half = both.shape[1] // 2
    lane = lax.broadcasted_iota(jnp.int32, both.shape, 1)
    return [jnp.where(lane < half, part, 0.0) for part in (both, pltpu.roll(both, half, 1))]


def second_bands(own, left, right, z_matrix, y_matrix, low_rows):
    planes, own_rows, nz = own.shape
    n1 = planes - 4
    in_rows = own_rows + 2 * left.shape[1]
    rows = y_matrix.shape[0]


    def kernel(o_ref, l_ref, r_ref, z, y, out, up, down):
        for i in range(0, planes, 10):
            stack = [part[j] for j in range(i, i + 10) for part in (o_ref, l_ref, r_ref)]
            zed = times_wide(jnp.concatenate(stack, axis=0), z)
            for j, plane in enumerate(in_pairs(y, cut(zed, in_rows))):
                out[i + j] = plane
        low = lambda c: out[c, :low_rows]
        up[0:rows] = out[n1 - 1]
        up[rows : 2 * rows] = H[0] * out[n1 - 3] + H[1] * out[n1 - 2]
        first = added([(H[j], low(n1 - 5 + j)) for j in range(5)])
        second = added([(H[0] * H[j], low(n1 - 9 + j)) for j in range(8)])
        second += added([(H[1] * H[j], low(n1 - 7 + j)) for j in range(7)])
        up[2 * rows :] = packed(first, second)
        down[0:rows] = out[0]
        down[rows : 2 * rows] = H[6] * out[1] + H[7] * out[2]
        first = added([(H[j], low(j - 3)) for j in range(3, 8)])
        second = added([(H[6] * H[j], low(j - 1)) for j in range(1, 8)])
        second += added([(H[7] * H[j], low(j + 1)) for j in range(8)])
        down[2 * rows :] = packed(first, second)

    message = 2 * rows + low_rows
    return whole_call(
        kernel,
        [shape(planes, rows, nz), shape(message, nz), shape(message, nz)],
        [own, left, right, z_matrix, y_matrix],
        received=[(1, "gy")],
        sent=[(1, "gx")],
        name="second_bands",
    )


def limits_plane(table_ref, index_ref, level, bx, dims, row_split, lane_split, zeroth):
    row_high = lax.broadcasted_iota(jnp.int32, dims, 0) >= row_split
    lane_high = lax.broadcasted_iota(jnp.int32, dims, 1) >= lane_split

    def limit(by, bz):
        band = 4 * bx + 2 * by + bz
        return zeroth if band == 0 else table_ref[index_ref[level, band - 1]]

    low_y = jnp.where(lane_high, limit(0, 1), limit(0, 0))
    return jnp.where(row_high, jnp.where(lane_high, limit(1, 1), limit(1, 0)), low_y)


def coarse(
    bands, left, right, halo, h_left, h_right, table, index, za1, yx0, ya1, zs1, za2, zs2, ya2, ys2, ys1,
    in_rows1, low_rows, out_rows, own_rows, spill_at, spill_rows,
):
    planes_in, rows, nz = bands.shape
    n1 = planes_in - 4
    in_rows = in_rows1
    wide = h_left.shape[1] - 8
    n2, n3 = n1 // 2, n1 // 4
    rows2 = ya2.shape[0]
    lane_half = nz // 2

    def kernel(
        table_ref, index_ref, b_ref, l_ref, r_ref, x_ref, hl, hr, z1a, yx, a1, z1, z2a, z2s, a2, s2, s1,
        approx, up, down, c1, p1,
    ):
        halo_planes = [jnp.concatenate([hl[i, :wide], x_ref[i, :, :nz], hr[i, :wide]], axis=0) for i in range(4)]
        halo_planes = jnp.concatenate([plane[:in_rows] for plane in in_pairs(yx, halo_planes)], axis=0)
        hl1, hl2, hr1, hr2 = in_pairs(a1, cut(times_wide(halo_planes, z1a), in_rows))
        values = {k: b_ref[k] for k in range(2, n1 - 2)}
        values[0] = b_ref[0] + (hl2 + H[2] * hl1)
        values[1] = b_ref[1] + H[0] * hl1
        values[n1 - 2] = b_ref[n1 - 2] + H[7] * hr1
        values[n1 - 1] = b_ref[n1 - 1] + (hr2 + H[5] * hr1)
        xl1, xl2, xr1, xr2 = [b_ref[n1 + i] for i in range(4)]
        values["l1"] = l_ref[0:rows] + xl1
        values["l2"] = l_ref[rows : 2 * rows] + xl2
        values["r1"] = r_ref[0:rows] + xr1
        values["r2"] = r_ref[rows : 2 * rows] + xr2
        get = values.get
        low_part = lambda c: values[c][:low_rows]
        xl1, xl2, xr1, xr2 = [part[:low_rows] for part in (xl1, xl2, xr1, xr2)]
        dims = (rows, nz)
        quiet = limits_plane(table_ref, index_ref, 1, 0, dims, low_rows, lane_half, NOTHING)
        loud = limits_plane(table_ref, index_ref, 1, 1, dims, low_rows, lane_half, NOTHING)
        planes = []
        for k in range(n2):
            low = x_low(get, k, n1)
            planes.append(low[:low_rows])
            c1[k] = shrink(low, quiet)
            c1[n2 + k] = shrink(x_high(get, k, n1), loud)
        first, second = unpacked(l_ref[2 * rows :])
        own = [(H[5 + i], low_part(i)) for i in range(3)]
        planes.append(first + added([(H[3] / H[1], xl2), (H[4], xl1)] + own))
        own = [((H[0] * H[7] + H[1] * H[5]) / H[1], xl2), (H[1] * H[6], xl1), (H[1] * H[7], low_part(0))]
        planes.append(second + added(own))
        first, second = unpacked(r_ref[2 * rows :])
        own = [(H[i], low_part(n1 - 3 + i)) for i in range(3)]
        planes.append(first + added([(H[3], xr1), (H[4] / H[6], xr2)] + own))
        own = [((H[6] * H[2] + H[7] * H[0]) / H[6], xr2), (H[6] * H[1], xr1), (H[6] * H[0], low_part(n1 - 1))]
        planes.append(second + added(own))
        third = in_pairs(a2, cut(times_wide(jnp.concatenate(planes, axis=0), z2a), low_rows))
        keys = {"l1": n2, "l2": n2 + 1, "r1": n2 + 2, "r2": n2 + 3}
        get2 = lambda key: third[keys.get(key, key)]
        dims = (rows2, nz)
        quiet = limits_plane(table_ref, index_ref, 2, 0, dims, rows2 // 2, lane_half // 2, 0.0)
        loud = limits_plane(table_ref, index_ref, 2, 1, dims, rows2 // 2, lane_half // 2, 0.0)
        kept = [shrink(x_low(get2, k, n2), quiet) for k in range(n3)]
        kept += [shrink(x_high(get2, k, n2), loud) for k in range(n3)]
        parts = in_pairs(s2, cut(times_wide(jnp.concatenate(kept, axis=0), z2s), rows2))
        parts = [part[:low_rows] for part in parts]
        lows = dict(enumerate(parts[:n3]))
        highs = dict(enumerate(parts[n3:]))
        ghosts = [-3, -2, -1, n2, n2 + 1, n2 + 2]
        for k in range(n2):
            c1[k, :low_rows] += x_synth(k, lows, highs)
        stack = [x_synth(k, lows, highs) for k in ghosts]
        beyond = dict(zip(ghosts, stack))
        zed = times_wide(jnp.concatenate(stack, axis=0), z1)
        for i, plane in enumerate(in_pairs(s1, cut(zed, low_rows))):
            p1[2 * n2 + i] = plane[:out_rows]
        for i in range(0, 2 * n2, 8):
            zed = times_wide(c1[i : i + 8].reshape(8 * rows, nz), z1)
            for j, plane in enumerate(in_pairs(s1, cut(zed, rows))):
                p1[i + j] = plane[:out_rows]
        lows = {k: p1.at[k] for k in range(n2)}
        highs = {k: p1.at[n2 + k] for k in range(n2)}
        for i, k in enumerate(ghosts):
            lows[k] = p1.at[2 * n2 + i]

        def cell(m):
            near = lambda part: {k: ref[...] for k, ref in part.items() if 0 <= m + 3 - 2 * k < 8}
            return x_synth(m, near(lows), near(highs))

        for m in range(-2, n1 + 2):
            approx[m + 2] = cell(m)
        value = lambda part, ks: {k: part[k][...] for k in ks}
        ends = (n2 - 2, n2 - 1)

        def send(message, four, two):
            for i, plane in enumerate(four):
                message[i * own_rows : (i + 1) * own_rows] = plane[:own_rows]
                message[4 * own_rows + 4 * i : 4 * own_rows + 4 * i + 4] = plane[own_rows : own_rows + 4]
            message[4 * own_rows + 16 :] = packed(*two)[spill_at : spill_at + spill_rows]

        up_two = spill_up(value(lows, ends), value(highs, ends), n2)
        send(up, (approx[n1], approx[n1 + 1], *up_two), (beyond[n2], beyond[n2 + 1]))
        down_two = spill_down(value(lows, (0, 1)), value(highs, (0, 1)))
        send(down, (approx[2], approx[3], *down_two), (beyond[-1], beyond[-2]))

    message = 4 * own_rows + 16 + spill_rows
    return whole_call(
        kernel,
        [shape(n1 + 4, out_rows, nz), shape(message, nz), shape(message, nz)],
        [table, index, bands, left, right, halo, h_left, h_right, za1, yx0, ya1, zs1, za2, zs2, ya2, ys2, ys1],
        scratch=[pltpu.VMEM((2 * n2, rows, nz), F32), pltpu.VMEM((2 * n2 + 6, out_rows, nz), F32)],
        received=[(3, "gx"), (6, "gy")],
        sent=[(1, "gx")],
        name="coarse",
    )


def received_taps(n1):
    n2, nx = n1 // 2, 2 * n1
    from_approx = np.zeros((nx, n1 + 4))
    for m in range(nx):
        for k in range(-2, n1 + 2):
            from_approx[m, k + 2] = tap(H, m + 3 - 2 * k)
    approx = np.zeros((n1 + 4, 12))
    third = {0: THIRD_UP, 6: THIRD_DOWN}
    for first, cell, second in ((0, lambda i: i, lambda i: i), (6, lambda i: n1 - 1 - i, lambda i: n2 - 1 - i)):
        ghost = (-2, -1) if first == 0 else (n1, n1 + 1)
        for i in range(2):
            approx[ghost[i] + 2, first + i] = 1.0
        for place, source, coef in ((0, 0, 1.0), (1, 1, 1.0), (2, 1, third[first])):
            approx[cell(place) + 2, first + 2 + source] += coef
            for m in range(n1):
                approx[m + 2, first + 4 + source] += coef * tap(H, m + 3 - 2 * second(place))
    return from_approx @ approx


def final(left, right, own, e_left, e_right, zs1, ys1, z_matrix, y_matrix, rows, spill_rows):
    nx, ny, nz = own.shape
    half_z = nz // 2
    own_rows = ny // 2
    step_rows = 16
    steps = ny // step_rows
    taps = received_taps(nx // 2)

    def kernel(l_ref, r_ref, d_ref, el, er, z1, s1, z, y, out, planes, parts, done, sems):
        stack = [p for ref in (l_ref, r_ref) for p in unpacked(ref[4 * own_rows + 16 :])]
        zed = times_wide(jnp.concatenate(stack, axis=0), z1)
        spilled = [p[:rows] for p in in_pairs(s1, cut(zed, spill_rows))]
        for side, ref in enumerate((l_ref, r_ref)):
            for i in range(4):
                plane = planes.at[6 * side + i]
                plane[:own_rows] = ref[i * own_rows : (i + 1) * own_rows]
                plane[own_rows:] = jnp.zeros((rows - own_rows, half_z), F32)
                plane[own_rows : own_rows + 4] = ref[4 * own_rows + 4 * i : 4 * own_rows + 4 * i + 4]
            for i in range(2):
                planes[6 * side + 4 + i] = spilled[2 * side + i]
        for i, plane in enumerate(cut(times(planes[...].reshape(12 * rows, half_z), z), rows)):
            parts[i] = left_times(y, plane)

        def copy(i):
            at = pl.ds(pl.multiple_of(i * step_rows, step_rows), step_rows)
            return pltpu.make_async_copy(done.at[:, at], out.at[:, at], sems.at[i])

        def step(i, carry):
            for t in range(step_rows // 8):
                at = pl.ds(pl.multiple_of(i * step_rows + 8 * t, 8), 8)
                for lane in range(0, nz, 128):
                    lanes = pl.ds(lane, 128)
                    values = [parts[i, at, lanes] for i in range(12)]
                    for m in range(nx):
                        value = d_ref[m, at, lanes]
                        value += added([(float(c), v) for c, v in zip(taps[m], values) if c != 0.0])
                        if m < 3:
                            extra = el[(0, 1, 1)[m], at, lanes]
                            value += extra if m < 2 else THIRD_UP * extra
                        if m >= nx - 3:
                            extra = er[(0, 1, 1)[nx - 1 - m], at, lanes]
                            value += extra if m > nx - 3 else THIRD_DOWN * extra
                        done[m, at, lanes] = value
            copy(i).start()
            return carry

        lax.fori_loop(0, steps, step, 0)

        def finish(i, carry):
            copy(i).wait()
            return carry

        lax.fori_loop(0, steps, finish, 0)

    return whole_call(
        kernel,
        shape(nx, ny, nz),
        [left, right, own, e_left, e_right, zs1, ys1, z_matrix, y_matrix],
        scratch=[
            pltpu.VMEM((12, rows, half_z), F32),
            pltpu.VMEM((12, ny, nz), F32),
            pltpu.VMEM((nx, ny, nz), F32),
            pltpu.SemaphoreType.DMA((steps,)),
        ],
        received=[(0, "gx"), (3, "gx")],
        name="final",
        out_specs=pl.BlockSpec(memory_space=pl.ANY),
    )


def exchange(first, second, axis):
    size = lax.axis_size(axis)
    assert size % 2 == 0
    here = [(i, i ^ 1) for i in range(size)]
    across = [(i, (i + 1) % size if i % 2 else (i - 1) % size) for i in range(size)]
    return lax.ppermute(first, axis, here), lax.ppermute(second, axis, across)


def local(velocity, table, index):
    nx, ny, nz = velocity.shape
    y1, y2, y3 = ny // 2, ny // 4, ny // 8
    ghost, wide = 24, 48
    cells0 = list(range(-8, ny + 8))
    rows0 = up_to(y1 + 4, 8)
    ks0 = fill(list(range(y1)) + [-2, -1, y1, y1 + 1], rows0)
    cells1 = ks0 + list(range(2 - ghost, 2)) + list(range(y1 - 2, y1 + ghost - 2))
    once = [c if cells1.index(c) == i else None for i, c in enumerate(cells1)]
    rows1 = up_to(y2 + 18, 8)
    low1 = fill(list(range(-9, y2 + 9)), rows1)
    high1 = fill(list(range(-3, y2 + 3)), up_to(y2 + 6, 8))
    spill_at, spill_rows = 6, up_to(y2 + 6, 8)
    ks2 = fill(list(range(-3, y3 + 3)), up_to(y3 + 6, 8))
    ya0 = from_left(analysis_rows(cells0, ks0, ks0))
    ys0_matrix = synthesis_rows(list(range(ny)), ks0, ks0)
    ys0 = from_left(ys0_matrix)
    ys0_low = from_left(ys0_matrix[:, :rows0])
    yl0 = from_left(analysis_rows(list(range(ny)), ks0, []))
    yx0 = from_left(analysis_rows(list(range(-wide, ny + wide)), once, []))
    ya1 = from_left(analysis_rows(cells1, low1, high1))
    ys1 = from_left(synthesis_rows(ks0, low1, high1))
    ys1_spill = from_left(synthesis_rows(ks0, low1[spill_at : spill_at + spill_rows], []))
    ya2 = from_left(analysis_rows(low1, ks2, ks2))
    ys2 = from_left(synthesis_rows(low1, ks2, ks2))
    z0 = periodic(nz, nz)
    z1 = periodic(nz // 2, nz // 2)
    z2 = periodic(nz // 4, nz // 2)
    za0, zs0, zs0_low = from_right(z0), from_right(z0.T), from_right(z0.T[: nz // 2])
    za1, zs1 = wide_right(z1), wide_right(z1.T)
    za2, zs2 = wide_right(z2), wide_right(z2.T)

    x_up, x_down, y_up, y_down = first_messages(velocity)
    x_left, x_right = exchange(x_up, x_down, "gx")
    y_left, y_right = exchange(y_up, y_down, "gy")
    zed = depth(velocity, za0, 16, "depth_analysis")
    approx, a_up, a_down = own_approx(zed, yl0, y1, rows0, ghost)
    a_left, a_right = exchange(a_up, a_down, "gy")
    zed, a_up = lax.optimization_barrier((zed, a_up))
    bands = y_analysis(zed, y_left, y_right, za0, ya0)
    x_left, x_right, bands = lax.optimization_barrier((x_left, x_right, bands))
    halo, h_up, h_down = x_halo_messages(x_left, x_right, za0, wide)
    h_left, h_right = exchange(h_up, h_down, "gy")
    approx, halo = lax.optimization_barrier((approx, halo))
    bands1, b_up, b_down = second_bands(approx, a_left, a_right, za1, ya1, rows1)
    b_left, b_right = exchange(b_up, b_down, "gx")
    h_left, h_right, bands1 = lax.optimization_barrier((h_left, h_right, bands1))
    edge, e_up, e_down = edge_details(bands, halo, h_left, h_right, table, index, ya0, zs0, ys0)
    e_left, e_right = exchange(e_up, e_down, "gx")
    bands1, edge = lax.optimization_barrier((bands1, edge))
    approx1, s_up, s_down = coarse(
        bands1, b_left, b_right, halo, h_left, h_right, table, index,
        za1, yx0, ya1, zs1, za2, zs2, ya2, ys2, ys1, len(cells1), rows1, rows0, y1, spill_at, spill_rows,
    )
    s_left, s_right = exchange(s_up, s_down, "gx")
    bands, approx1 = lax.optimization_barrier((bands, approx1))
    rest = inner_yz(inner_bands(bands, table, index), approx1, zs0, ys0)
    own = own_result(edge, rest, approx1, zs0_low, ys0_low)
    return final(s_left, s_right, own, e_left, e_right, zs1, ys1_spill, zs0_low, ys0_low, rows0, spill_rows)


def solution(mesh):
    return jax.shard_map(
        local,
        mesh=mesh,
        in_specs=(P("gx", "gy", None), P(), P()),
        out_specs=P("gx", "gy", None),
        check_vma=False,
    )
```

```python
import functools

import jax
import jax.numpy as jnp
import ml_dtypes
import numpy as np
from jax import lax
from jax.experimental import pallas as pl
from jax.experimental.pallas import tpu as pltpu
from jax.sharding import PartitionSpec as P

H = [
    0.23037781330885523,
    0.7148465705525415,
    0.6308807679295904,
    -0.02798376941698385,
    -0.18703481171888114,
    0.030841381835986965,
    0.032883011666982945,
    -0.010597401784997278,
]
G = [(-1.0) ** j * H[7 - j] for j in range(8)]
F32 = jnp.float32
BF16 = jnp.bfloat16
NOTHING = 3.0e38
VMEM_BYTES = 16 * 1024 * 1024


def tap(filt, j):
    return filt[j] if 0 <= j < 8 else 0.0


def analysis_rows(cells, low_ks, high_ks):
    matrix = np.zeros((len(low_ks) + len(high_ks), len(cells)))
    rows = [(H, k) for k in low_ks] + [(G, k) for k in high_ks]
    for row, (filt, k) in enumerate(rows):
        for col, cell in enumerate(cells):
            if k is not None and cell is not None:
                matrix[row, col] = tap(filt, cell - 2 * k + 3)
    return matrix


def synthesis_rows(cells, low_ks, high_ks):
    return analysis_rows(cells, low_ks, high_ks).T


def periodic(length, padded_to):
    matrix = np.zeros((padded_to, padded_to))
    for k in range(length // 2):
        for j in range(8):
            matrix[(2 * k + j - 3) % length, k] += H[j]
            matrix[(2 * k + j - 3) % length, length // 2 + k] += G[j]
    return matrix


def fill(items, length):
    return items + [None] * (length - len(items))


def up_to(count, step):
    return -(-count // step) * step


def pieces(matrix, axis):
    rows, cols = matrix.shape
    matrix = np.pad(matrix, ((0, up_to(rows, 16) - rows), (0, up_to(cols, 16) - cols))).astype(np.float32)
    high = matrix.astype(ml_dtypes.bfloat16)
    low = (matrix - high.astype(np.float32)).astype(ml_dtypes.bfloat16)
    return np.concatenate([high, high, low], axis=axis)


def from_left(matrix):
    return pieces(matrix, 1)


def from_right(matrix):
    return pieces(matrix, 0)


def wide_right(matrix):
    rows, cols = matrix.shape
    both = pieces(matrix, 0)
    high, low = both[:rows], both[2 * rows :]
    return np.block([[high, low], [high, np.zeros_like(low)]])


def tall_left(matrix):
    return np.ascontiguousarray(wide_right(np.ascontiguousarray(padded_to_tiles(matrix).T)).T)


def padded_to_tiles(matrix):
    rows, cols = matrix.shape
    return np.pad(matrix, ((0, up_to(rows, 16) - rows), (0, up_to(cols, 16) - cols)))


def halves(values):
    high = values.astype(BF16)
    return high, (values - high.astype(F32)).astype(BF16)


def times(values, matrix):
    high, low = halves(values)
    return jnp.dot(jnp.concatenate([high, low, high], axis=1), matrix[...], preferred_element_type=F32)


def left_times(matrix, values):
    missing = matrix.shape[1] // 3 - values.shape[0]
    if missing:
        values = jnp.concatenate([values, jnp.zeros((missing, values.shape[1]), F32)], axis=0)
    high, low = halves(values)
    return jnp.dot(matrix[...], jnp.concatenate([high, low, high], axis=0), preferred_element_type=F32)


def times_wide(values, matrix):
    both = jnp.dot(jnp.concatenate(halves(values), axis=1), matrix[...], preferred_element_type=F32)
    return both[:, : both.shape[1] // 2] + both[:, both.shape[1] // 2 :]


def left_times_tall(matrix, values):
    missing = matrix.shape[1] // 2 - values.shape[0]
    if missing:
        values = jnp.concatenate([values, jnp.zeros((missing, values.shape[1]), F32)], axis=0)
    both = jnp.dot(matrix[...], jnp.concatenate(halves(values), axis=0), preferred_element_type=F32)
    return both[: both.shape[0] // 2] + both[both.shape[0] // 2 :]


def added(terms):
    total = None
    for coef, value in terms:
        part = value if coef == 1.0 else coef * value
        total = part if total is None else total + part
    return total


def x_terms(k, n):
    terms = []
    for j in range(8):
        cell = 2 * k + j - 3
        if 0 <= cell < n:
            terms.append((cell, H[j], G[j]))
        elif cell == -1:
            terms.append(("l1", H[j], G[j]))
        elif cell == n:
            terms.append(("r1", H[j], G[j]))
    if k == 0:
        terms.append(("l2", 1.0, G[0] / H[0]))
    if k == n // 2 - 1:
        terms.append(("r2", 1.0, G[6] / H[6]))
    return terms


def lattice():
    low = np.array(H).reshape(4, 2)
    high = np.array(G).reshape(4, 2)
    tangents = []
    for _ in range(3):
        t = (low[0] @ high[0]) / (high[0] @ high[0])
        tangents.append(float(t))
        low, high = (low - t * high)[1:] / (1 + t * t), (high + t * low)[:-1] / (1 + t * t)
    return low[0].tolist(), high[0].tolist(), tangents[::-1]


def x_interior(get, n):
    first, second, tangents = lattice()
    a, b = {}, {}
    for i in range(1, n // 2):
        x, y = get(2 * i - 1), get(2 * i)
        a[i] = first[0] * x + first[1] * y
        b[i] = second[0] * x + second[1] * y
    for t in tangents:
        shared = [i for i in a if i + 1 in a]
        a, b = {i: a[i + 1] + t * b[i] for i in shared}, {i: b[i] - t * a[i + 1] for i in shared}
    return {i + 1: (a[i], b[i]) for i in a}


def x_low(get, k, n):
    return added([(low, get(key)) for key, low, _ in x_terms(k, n)])


def x_high(get, k, n):
    return added([(high, get(key)) for key, _, high in x_terms(k, n)])


def x_synth(m, lows, highs):
    terms = [(H[m + 3 - 2 * k], v) for k, v in lows.items() if 0 <= m + 3 - 2 * k < 8]
    terms += [(G[m + 3 - 2 * k], v) for k, v in highs.items() if 0 <= m + 3 - 2 * k < 8]
    return added(terms)


def x_synth_interior(lows, highs, n):
    first, second, tangents = lattice()
    a = {k - 1: lows[k] for k in range(n)}
    b = {k - 1: highs[k] for k in range(n)}
    for t in reversed(tangents):
        a, b = {i + 1: a[i] - t * b[i] for i in a}, {i: b[i] + t * a[i] for i in b}
        both = [i for i in a if i in b]
        a, b = {i: a[i] for i in both}, {i: b[i] for i in both}
    cells = {}
    for i in a:
        cells[2 * i - 1] = first[0] * a[i] + second[0] * b[i]
        cells[2 * i] = first[1] * a[i] + second[1] * b[i]
    return cells


def spill_up(low, high, n):
    first = added([(H[5], low[n - 1]), (G[5], high[n - 1]), (H[7], low[n - 2]), (G[7], high[n - 2])])
    return first, added([(H[6], low[n - 1]), (G[6], high[n - 1])])


def spill_down(low, high):
    first = added([(H[2], low[0]), (G[2], high[0]), (H[0], low[1]), (G[0], high[1])])
    return first, added([(H[1], low[0]), (G[1], high[0])])


THIRD_UP = H[7] / H[6]
THIRD_DOWN = H[0] / H[1]


def shrink(values, thresh):
    return values - jnp.minimum(jnp.maximum(values, -thresh), thresh)


def paired(kernel, args, outs, scratch, received, sent):
    extra = [pltpu.VMEM((2,) + args[i].shape, F32) for i, _ in received]
    extra += [pltpu.VMEM((2,) + outs[j].shape, F32) for j, _ in sent]

    def wrapped(*refs):
        refs, both = list(refs[: len(refs) - len(extra)]), refs[len(refs) - len(extra) :]
        for (i, axis), pair in zip(received, both):
            parity = lax.rem(lax.axis_index(axis), 2)
            pair[0], pair[1] = refs[i][...], refs[i + 1][...]
            refs[i], refs[i + 1] = pair.at[1 - parity], pair.at[parity]
        carried = []
        for (j, axis), pair in zip(sent, both[len(received) :]):
            parity = lax.rem(lax.axis_index(axis), 2)
            j += len(args)
            carried.append((refs[j], refs[j + 1], pair))
            refs[j], refs[j + 1] = pair.at[parity], pair.at[1 - parity]
        kernel(*refs)
        for first, second, pair in carried:
            first[...], second[...] = pair[0], pair[1]

    return wrapped, list(scratch) + extra


def whole_call(kernel, outs, args, scratch=(), received=(), sent=(), name=None, **changes):
    out_list = outs if isinstance(outs, list) else [outs]
    kernel, scratch = paired(kernel, args, out_list, scratch, received, sent)
    specs = [SMEM if a.ndim == 1 or a.dtype == jnp.int32 else VMEM for a in args]
    return pl.pallas_call(
        kernel,
        in_specs=changes.get("in_specs", specs),
        out_specs=changes.get("out_specs", [VMEM] * len(outs) if outs is out_list else VMEM),
        out_shape=outs,
        scratch_shapes=scratch,
        name=name,
        cost_estimate=pl.CostEstimate(flops=1000, bytes_accessed=1000, transcendentals=0),
        compiler_params=pltpu.CompilerParams(vmem_limit_bytes=changes.get("vmem", VMEM_BYTES)),
    )(*args)


def shape(*dims):
    return jax.ShapeDtypeStruct(dims, F32)


SMEM = pl.BlockSpec(memory_space=pltpu.SMEM)
VMEM = pl.BlockSpec(memory_space=pltpu.VMEM)


def first_messages(v):
    nx, ny, nz = v.shape

    kept = nx - nx // 8

    def kernel(v_ref, up, down, y_up, y_down, last, first, rows_up, rows_down, sems):
        copies = [
            pltpu.make_async_copy(source, target, sems.at[i])
            for i, (source, target) in enumerate(
                (
                    (v_ref.at[pl.ds(nx - 3, 3)], last),
                    (v_ref.at[pl.ds(0, 3)], first),
                    (v_ref.at[:, pl.ds(ny - 8, 8)], rows_up),
                    (v_ref.at[:, pl.ds(0, 8)], rows_down),
                )
            )
        ]
        for copy in copies:
            copy.start()
        for copy in copies:
            copy.wait()
        up[0] = last[2]
        up[1] = H[0] * last[0] + H[1] * last[1]
        down[0] = first[0]
        down[1] = H[6] * first[1] + H[7] * first[2]
        y_up[...] = rows_up[:kept]
        y_down[...] = rows_down[:kept]
        for i in range(kept):
            plane, row = kept + i // 7, i % 7
            y_up[i, 0:1] = rows_up[plane, row + 1 : row + 2]
            y_down[i, 7:8] = rows_down[plane, row : row + 1]

    return whole_call(
        kernel,
        [shape(2, ny, nz)] * 2 + [shape(kept, 8, nz)] * 2,
        [v],
        scratch=[pltpu.VMEM((3, ny, nz), F32)] * 2
        + [pltpu.VMEM((nx, 8, nz), F32)] * 2
        + [pltpu.SemaphoreType.DMA((4,))],
        sent=[(0, "gx"), (2, "gy")],
        name="first_messages",
        in_specs=[pl.BlockSpec(memory_space=pltpu.HBM)],
        vmem=50 * 1024 * 1024,
    )


def over_planes(count, group, body):
    def step(i, carry):
        body(i * group)
        return carry

    lax.fori_loop(0, count // group, step, 0)


def depth(v, z_matrix, group, name):
    nx, rows, nz = v.shape

    def kernel(v_ref, z, out):
        def body(first):
            at = pl.ds(first, group)
            out[at] = times(v_ref[at].reshape(group * rows, nz), z).reshape(group, rows, nz)

        over_planes(nx, group, body)

    return whole_call(kernel, shape(nx, rows, nz), [v, z_matrix], name=name)


def y_analysis(zed, y_across, y_here, z_matrix, y_matrix):
    nx, ny, nz = zed.shape
    rows = y_matrix.shape[0]
    kept = y_here.shape[0]
    group = 8

    def kernel(zed_ref, right, left, z, y, out, left_z, right_z):
        for part, out_z in ((left, left_z), (right, right_z)):
            out_z[:kept] = times(part[...].reshape(8 * kept, nz), z).reshape(kept, 8, nz)
            out_z[kept:] = jnp.zeros((nx - kept, 8, nz), F32)
        for i in range(kept):
            plane, row = kept + i // 7, i % 7
            left_z[plane, row + 1 : row + 2] = left_z[i, 0:1]
            right_z[plane, row : row + 1] = right_z[i, 7:8]

        def body(first):
            for j in range(group):
                i = first + j
                out[i] = left_times(y, jnp.concatenate([left_z[i], zed_ref[i], right_z[i]], axis=0))

        over_planes(nx, group, body)

    return whole_call(
        kernel,
        shape(nx, rows, nz),
        [zed, y_across, y_here, z_matrix, y_matrix],
        scratch=[pltpu.VMEM((nx, 8, nz), F32)] * 2,
        received=[(1, "gy")],
        name="y_analysis",
    )


def own_approx(zed, y_matrix, own, rows, ghost_rows):
    nx, ny, nz = zed.shape
    half_z = nz // 2
    n1 = nx // 2

    def kernel(zed_ref, y, approx, up, down, low):
        def y_body(first):
            planes = [zed_ref[first + i, :, :half_z] for i in range(8)]
            for i, plane in enumerate(in_pairs(y, planes)):
                low[first + i] = plane[:rows]

        over_planes(nx, 8, y_body)

        def tile(t, carry):
            at = pl.ds(pl.multiple_of(t * 8, 8), 8)
            values = {i: low[i, at] for i in range(nx)}
            for k in range(n1):
                approx[k, at] = added([(c, values[i]) for i, c, _ in x_terms(k, nx) if i in values])
            approx[n1, at] = added([(H[5 + i], values[i]) for i in range(3)])
            approx[n1 + 1, at] = H[1] * H[7] * values[0]
            approx[n1 + 2, at] = added([(H[i], values[nx - 3 + i]) for i in range(3)])
            approx[n1 + 3, at] = H[6] * H[0] * values[nx - 1]
            return carry

        lax.fori_loop(0, rows // 8, tile, 0)
        inside = ghost_rows - 2
        up[:, :inside] = approx[:n1, own - inside : own]
        up[:, inside:] = approx[:n1, own + 2 : own + 4]
        down[:, :2] = approx[:n1, own : own + 2]
        down[:, 2:] = approx[:n1, :inside]

    return whole_call(
        kernel,
        [shape(n1 + 4, rows, half_z), shape(n1, ghost_rows, half_z), shape(n1, ghost_rows, half_z)],
        [zed, y_matrix],
        scratch=[pltpu.VMEM((nx, rows, half_z), F32)],
        sent=[(1, "gy")],
        name="own_approx",
    )


def x_halo_messages(x_left, x_right, approx, z_matrix, wide, ghost_rows):
    _, ny, nz = x_left.shape
    half_z = nz // 2
    n1 = approx.shape[0] - 4
    own, inside = ny // 2, ghost_rows - 2
    message = wide + 8 + ghost_rows

    def kernel(xl, xr, a_ref, z, out, up, down):
        planes = jnp.concatenate([xl[0], xl[1], xr[0], xr[1]], axis=0)
        out[...] = times(planes, z).reshape(4, ny, nz)
        up[:, :wide] = out[:, ny - wide :, :half_z]
        up[:, wide : wide + 8] = out[:, ny - 8 :, half_z:]
        down[:, :wide] = out[:, :wide, :half_z]
        down[:, wide : wide + 8] = out[:, :8, half_z:]
        up[:, wide + 8 : wide + 8 + inside] = a_ref[n1:, own - inside : own]
        up[:, wide + 8 + inside :] = a_ref[n1:, own + 2 : own + 4]
        down[:, wide + 8 : wide + 10] = a_ref[n1:, own : own + 2]
        down[:, wide + 10 :] = a_ref[n1:, :inside]

    return whole_call(
        kernel,
        [shape(4, ny, nz), shape(4, message, half_z), shape(4, message, half_z)],
        [x_left, x_right, approx, z_matrix],
        received=[(0, "gx")],
        sent=[(1, "gy")],
        name="x_halo_messages",
    )


def edges_of(n):
    return [0, 1, n - 2, n - 1]


def band_limits(table_ref, index_ref, by, bz):
    band = 2 * by + bz
    quiet = table_ref[index_ref[0, band - 1]] if band else NOTHING
    return quiet, table_ref[index_ref[0, band + 3]]


def over_tiles(rows, nz, body):
    half_z, half_tiles = nz // 2, rows // 16
    for by in range(2):

        def tile(t, carry, by=by):
            at = pl.ds(pl.multiple_of((t + by * half_tiles) * 8, 8), 8)
            for bz in range(2):
                body(at, pl.ds(bz * half_z, half_z), by, bz)
            return carry

        lax.fori_loop(0, half_tiles, tile, 0, unroll=3 if half_tiles % 3 == 0 else 1)


def inner_bands(bands, table, index):
    nx, rows, nz = bands.shape
    count = nx // 2 - 4

    def kernel(table_ref, index_ref, b_ref, out):
        def body(at, lanes, by, bz):
            quiet, loud = band_limits(table_ref, index_ref, by, bz)
            values = {i: b_ref[i, at, lanes] for i in range(nx)}
            for k, (low, high) in x_interior(values.get, nx).items():
                out[k - 2, at, lanes] = shrink(low, quiet) if by + bz else jnp.zeros_like(low)
                out[count + k - 2, at, lanes] = shrink(high, loud)

        over_tiles(rows, nz, body)

    return whole_call(
        kernel,
        shape(2 * count, rows, nz),
        [table, index, bands],
        name="inner_bands",
    )


def yz_synthesis(planes, z, y, out, zed):
    count, rows, nz = zed.shape
    group = max(g for g in range(1, 17) if count % g == 0)
    for first in range(0, count, group):
        zed[first : first + group] = times(planes(first, group), z).reshape(group, rows, nz)

    def y_body(first):
        for j in range(4):
            out[first + j] = left_times(y, zed[first + j])

    over_planes(count, 4, y_body)


def edge_details(bands, halo, h_left, h_right, table, index, ya_matrix, z_matrix, y_matrix, wide):
    nx, rows, nz = bands.shape
    ny = y_matrix.shape[0]
    n1 = nx // 2
    half_z = nz // 2
    ends = edges_of(n1)

    def kernel(table_ref, index_ref, b_ref, x_ref, hl, hr, ya, z, y, coeffs, up, down, h_ref, beyond, zed):
        for i in range(4):
            low = jnp.concatenate([hl[i, wide - 8 : wide], x_ref[i, :, :half_z], hr[i, :8]], axis=0)
            high = jnp.concatenate(
                [hl[i, wide : wide + 8], x_ref[i, :, half_z:], hr[i, wide : wide + 8]], axis=0
            )
            h_ref[i] = left_times(ya, jnp.concatenate([low, high], axis=1))
        place = {"l1": 0, "l2": 1, "r1": 2, "r2": 3}

        def body(at, lanes, by, bz):
            quiet, loud = band_limits(table_ref, index_ref, by, bz)
            values = {key: h_ref[i, at, lanes] for key, i in place.items()}
            values.update({i: b_ref[i, at, lanes] for i in [*range(7), *range(nx - 7, nx)]})
            lows, highs = {}, {}
            for i, k in enumerate(ends):
                low, high = x_low(values.get, k, nx), x_high(values.get, k, nx)
                lows[k] = shrink(low, quiet) if by + bz else jnp.zeros_like(low)
                highs[k] = shrink(high, loud)
                coeffs[i, at, lanes] = lows[k]
                coeffs[4 + i, at, lanes] = highs[k]
            spilled = spill_up(lows, highs, n1) + spill_down(lows, highs)
            for i, part in enumerate(spilled):
                beyond[i, at, lanes] = part

        over_tiles(rows, nz, body)
        zed[...] = times(beyond[...].reshape(4 * rows, nz), z).reshape(4, rows, nz)
        for i, target in enumerate((up.at[0], up.at[1], down.at[0], down.at[1])):
            target[...] = left_times(y, zed[i])

    return whole_call(
        kernel,
        [shape(8, rows, nz), shape(2, ny, nz), shape(2, ny, nz)],
        [table, index, bands, halo, h_left, h_right, ya_matrix, z_matrix, y_matrix],
        scratch=[pltpu.VMEM((4, rows, nz), F32)] * 3,
        received=[(4, "gy")],
        sent=[(1, "gx")],
        name="edge_details",
    )


def detail_yz(edge, inner, approx, z_matrix, y_matrix):
    count, rows, nz = inner.shape
    ny = y_matrix.shape[0]
    _, low_rows, half_z = approx.shape
    n1 = count // 2 + 4
    ends = edges_of(n1)

    def kernel(e_ref, i_ref, a_ref, z, y, out, zed):
        def coeff(k, high):
            if k in ends:
                return e_ref.at[4 * high + ends.index(k)]
            return i_ref.at[(n1 - 4) * high + k - 2]

        def plane(i):
            ref = coeff(i % n1, i // n1)
            if i >= n1:
                return ref[...]
            corner = ref[:low_rows, :half_z] + a_ref[i + 2]
            top = jnp.concatenate([corner, ref[:low_rows, half_z:]], axis=1)
            return jnp.concatenate([top, ref[low_rows:]], axis=0)

        def planes(first, n):
            return jnp.concatenate([plane(i) for i in range(first, first + n)], axis=0)

        yz_synthesis(planes, z, y, out, zed)

    return whole_call(
        kernel,
        shape(2 * n1, ny, nz),
        [edge, inner, approx, z_matrix, y_matrix],
        scratch=[pltpu.VMEM((2 * n1, rows, nz), F32)],
        name="detail_yz",
    )


def own_result(parts, approx, left, right, z_matrix, y_matrix):
    nx, ny, nz = parts.shape
    n1 = nx // 2
    planes, rows, half_z = approx.shape

    def kernel(p_ref, a_ref, el, er, z, y, out, ghosts):
        stack = jnp.concatenate([a_ref[i] for i in (0, 1, n1 + 2, n1 + 3)], axis=0)
        for i, plane in enumerate(cut(times(stack, z), rows)):
            ghosts[i] = left_times(y, plane)

        def tile(t, carry):
            at = pl.ds(pl.multiple_of(t * 8, 8), 8)
            for lane in range(0, nz, 128):
                lanes = pl.ds(lane, 128)
                lows = {k: p_ref[k, at, lanes] for k in range(n1)}
                highs = {k: p_ref[n1 + k, at, lanes] for k in range(n1)}
                for i, k in enumerate((-2, -1, n1, n1 + 1)):
                    lows[k] = ghosts[i, at, lanes]
                cells = x_synth_interior(lows, highs, n1)
                for m in range(nx):
                    value = cells[m] if m in cells else x_synth(m, lows, highs)
                    if m < 3:
                        extra = el[(0, 1, 1)[m], at, lanes]
                        value += extra if m < 2 else THIRD_UP * extra
                    if m >= nx - 3:
                        extra = er[(0, 1, 1)[nx - 1 - m], at, lanes]
                        value += extra if m > nx - 3 else THIRD_DOWN * extra
                    out[m, at, lanes] = value
            return carry

        lax.fori_loop(0, ny // 8, tile, 0)

    return whole_call(
        kernel,
        shape(nx, ny, nz),
        [parts, approx, left, right, z_matrix, y_matrix],
        scratch=[pltpu.VMEM((4, ny, nz), F32)],
        received=[(2, "gx")],
        name="own_result",
    )


def in_pairs(matrix, planes):
    results = []
    for i in range(0, len(planes), 2):
        both = left_times(matrix, jnp.concatenate(planes[i : i + 2], axis=1))
        width = both.shape[1] // 2
        results += [both[:, :width], both[:, width:]]
    return results


def cut(values, rows):
    return [values[i : i + rows] for i in range(0, values.shape[0], rows)]


def packed(first, second):
    half = first.shape[1] // 2
    lane = lax.broadcasted_iota(jnp.int32, first.shape, 1)
    return jnp.where(lane < half, first, pltpu.roll(second, half, 1))


def unpacked(both):
    half = both.shape[1] // 2
    lane = lax.broadcasted_iota(jnp.int32, both.shape, 1)
    return [jnp.where(lane < half, part, 0.0) for part in (both, pltpu.roll(both, half, 1))]


def second_bands(own, left, right, z_matrix, y_matrix, low_rows):
    _, own_rows, nz = own.shape
    n1 = left.shape[0]
    in_rows = own_rows + 2 * left.shape[1]
    rows = y_matrix.shape[0]


    def kernel(o_ref, l_ref, r_ref, z, y, out, up, down):
        for i in range(0, n1, 8):
            stack = [part[j] for j in range(i, i + 8) for part in (o_ref, l_ref, r_ref)]
            zed = times_wide(jnp.concatenate(stack, axis=0), z)
            for j, plane in enumerate(in_pairs(y, cut(zed, in_rows))):
                out[i + j] = plane
        low = lambda c: out[c, :low_rows]
        up[0:rows] = out[n1 - 1]
        up[rows : 2 * rows] = H[0] * out[n1 - 3] + H[1] * out[n1 - 2]
        first = added([(H[j], low(n1 - 5 + j)) for j in range(5)])
        second = added([(H[0] * H[j], low(n1 - 9 + j)) for j in range(8)])
        second += added([(H[1] * H[j], low(n1 - 7 + j)) for j in range(7)])
        up[2 * rows :] = packed(first, second)
        down[0:rows] = out[0]
        down[rows : 2 * rows] = H[6] * out[1] + H[7] * out[2]
        first = added([(H[j], low(j - 3)) for j in range(3, 8)])
        second = added([(H[6] * H[j], low(j - 1)) for j in range(1, 8)])
        second += added([(H[7] * H[j], low(j + 1)) for j in range(8)])
        down[2 * rows :] = packed(first, second)

    message = 2 * rows + low_rows
    return whole_call(
        kernel,
        [shape(n1, rows, nz), shape(message, nz), shape(message, nz)],
        [own, left, right, z_matrix, y_matrix],
        received=[(1, "gy")],
        sent=[(1, "gx")],
        name="second_bands",
    )


def limits_plane(table_ref, index_ref, level, bx, dims, row_split, lane_split, zeroth):
    row_high = lax.broadcasted_iota(jnp.int32, dims, 0) >= row_split
    lane_high = lax.broadcasted_iota(jnp.int32, dims, 1) >= lane_split

    def limit(by, bz):
        band = 4 * bx + 2 * by + bz
        return zeroth if band == 0 else table_ref[index_ref[level, band - 1]]

    low_y = jnp.where(lane_high, limit(0, 1), limit(0, 0))
    return jnp.where(row_high, jnp.where(lane_high, limit(1, 1), limit(1, 0)), low_y)


def coarse(
    bands, left, right, halo, h_left, h_right, approx_in, table, index, za1, yx0, ya1, zs1, za2, zs2, ya2, ys2, ys1,
    in_rows1, low_rows, out_rows, own_rows, spill_at, spill_rows, wide,
):
    n1, rows, nz = bands.shape
    in_rows = in_rows1
    n2, n3 = n1 // 2, n1 // 4
    rows2 = ya2.shape[0]
    lane_half = nz // 2

    def kernel(
        table_ref, index_ref, b_ref, l_ref, r_ref, x_ref, hl, hr, a_ref, z1a, yx, a1, z1, z2a, z2s, a2, s2, s1,
        approx, up, down, c1, p1,
    ):
        halo_planes = [jnp.concatenate([hl[i, :wide], x_ref[i, :, :nz], hr[i, :wide]], axis=0) for i in range(4)]
        halo_planes = [plane[:in_rows] for plane in in_pairs(yx, halo_planes)]
        own_planes = [
            jnp.concatenate([a_ref[n1 + i], hl[i, wide + 8 :], hr[i, wide + 8 :]], axis=0) for i in range(4)
        ]
        both = times_wide(jnp.concatenate(halo_planes + own_planes, axis=0), z1a)
        hl1, hl2, hr1, hr2, xl1, xl2, xr1, xr2 = in_pairs(a1, cut(both, in_rows))
        values = {k: b_ref[k] for k in range(2, n1 - 2)}
        values[0] = b_ref[0] + (hl2 + H[2] * hl1)
        values[1] = b_ref[1] + H[0] * hl1
        values[n1 - 2] = b_ref[n1 - 2] + H[7] * hr1
        values[n1 - 1] = b_ref[n1 - 1] + (hr2 + H[5] * hr1)
        values["l1"] = l_ref[0:rows] + xl1
        values["l2"] = l_ref[rows : 2 * rows] + xl2
        values["r1"] = r_ref[0:rows] + xr1
        values["r2"] = r_ref[rows : 2 * rows] + xr2
        get = values.get
        low_part = lambda c: values[c][:low_rows]
        xl1, xl2, xr1, xr2 = [part[:low_rows] for part in (xl1, xl2, xr1, xr2)]
        dims = (rows, nz)
        quiet = limits_plane(table_ref, index_ref, 1, 0, dims, low_rows, lane_half, NOTHING)
        loud = limits_plane(table_ref, index_ref, 1, 1, dims, low_rows, lane_half, NOTHING)
        planes = []
        for k in range(n2):
            low = x_low(get, k, n1)
            planes.append(low[:low_rows])
            c1[k] = shrink(low, quiet)
            c1[n2 + k] = shrink(x_high(get, k, n1), loud)
        first, second = unpacked(l_ref[2 * rows :])
        own = [(H[5 + i], low_part(i)) for i in range(3)]
        planes.append(first + added([(H[3] / H[1], xl2), (H[4], xl1)] + own))
        own = [((H[0] * H[7] + H[1] * H[5]) / H[1], xl2), (H[1] * H[6], xl1), (H[1] * H[7], low_part(0))]
        planes.append(second + added(own))
        first, second = unpacked(r_ref[2 * rows :])
        own = [(H[i], low_part(n1 - 3 + i)) for i in range(3)]
        planes.append(first + added([(H[3], xr1), (H[4] / H[6], xr2)] + own))
        own = [((H[6] * H[2] + H[7] * H[0]) / H[6], xr2), (H[6] * H[1], xr1), (H[6] * H[0], low_part(n1 - 1))]
        planes.append(second + added(own))
        third = in_pairs(a2, cut(times_wide(jnp.concatenate(planes, axis=0), z2a), low_rows))
        keys = {"l1": n2, "l2": n2 + 1, "r1": n2 + 2, "r2": n2 + 3}
        get2 = lambda key: third[keys.get(key, key)]
        dims = (rows2, nz)
        quiet = limits_plane(table_ref, index_ref, 2, 0, dims, rows2 // 2, lane_half // 2, 0.0)
        loud = limits_plane(table_ref, index_ref, 2, 1, dims, rows2 // 2, lane_half // 2, 0.0)
        kept = [shrink(x_low(get2, k, n2), quiet) for k in range(n3)]
        kept += [shrink(x_high(get2, k, n2), loud) for k in range(n3)]
        parts = in_pairs(s2, cut(times_wide(jnp.concatenate(kept, axis=0), z2s), rows2))
        parts = [part[:low_rows] for part in parts]
        lows = dict(enumerate(parts[:n3]))
        highs = dict(enumerate(parts[n3:]))
        ghosts = [-3, -2, -1, n2, n2 + 1, n2 + 2]
        for k in range(n2):
            c1[k, :low_rows] += x_synth(k, lows, highs)
        stack = [x_synth(k, lows, highs) for k in ghosts]
        beyond = dict(zip(ghosts, stack))
        zed = times_wide(jnp.concatenate(stack, axis=0), z1)
        for i, plane in enumerate(in_pairs(s1, cut(zed, low_rows))):
            p1[2 * n2 + i] = plane[:out_rows]
        for i in range(0, 2 * n2, 8):
            zed = times_wide(c1[i : i + 8].reshape(8 * rows, nz), z1)
            for j, plane in enumerate(in_pairs(s1, cut(zed, rows))):
                p1[i + j] = plane[:out_rows]
        lows = {k: p1.at[k] for k in range(n2)}
        highs = {k: p1.at[n2 + k] for k in range(n2)}
        for i, k in enumerate(ghosts):
            lows[k] = p1.at[2 * n2 + i]

        def cell(m):
            near = lambda part: {k: ref[...] for k, ref in part.items() if 0 <= m + 3 - 2 * k < 8}
            return x_synth(m, near(lows), near(highs))

        for m in range(-2, n1 + 2):
            approx[m + 2] = cell(m)
        value = lambda part, ks: {k: part[k][...] for k in ks}
        ends = (n2 - 2, n2 - 1)

        def send(message, four, two):
            for i, plane in enumerate(four):
                message[i * own_rows : (i + 1) * own_rows] = plane[:own_rows]
                message[4 * own_rows + 4 * i : 4 * own_rows + 4 * i + 4] = plane[own_rows : own_rows + 4]
            message[4 * own_rows + 16 :] = packed(*two)[spill_at : spill_at + spill_rows]

        up_two = spill_up(value(lows, ends), value(highs, ends), n2)
        send(up, (approx[n1], approx[n1 + 1], *up_two), (beyond[n2], beyond[n2 + 1]))
        down_two = spill_down(value(lows, (0, 1)), value(highs, (0, 1)))
        send(down, (approx[2], approx[3], *down_two), (beyond[-1], beyond[-2]))

    message = 4 * own_rows + 16 + spill_rows
    return whole_call(
        kernel,
        [shape(n1 + 4, out_rows, nz), shape(message, nz), shape(message, nz)],
        [table, index, bands, left, right, halo, h_left, h_right, approx_in, za1, yx0, ya1, zs1, za2, zs2, ya2, ys2, ys1],
        scratch=[pltpu.VMEM((2 * n2, rows, nz), F32), pltpu.VMEM((2 * n2 + 6, out_rows, nz), F32)],
        received=[(3, "gx"), (6, "gy")],
        sent=[(1, "gx")],
        name="coarse",
    )


def received_taps(n1):
    n2, nx = n1 // 2, 2 * n1
    from_approx = np.zeros((nx, n1 + 4))
    for m in range(nx):
        for k in range(-2, n1 + 2):
            from_approx[m, k + 2] = tap(H, m + 3 - 2 * k)
    approx = np.zeros((n1 + 4, 12))
    third = {0: THIRD_UP, 6: THIRD_DOWN}
    for first, cell, second in ((0, lambda i: i, lambda i: i), (6, lambda i: n1 - 1 - i, lambda i: n2 - 1 - i)):
        ghost = (-2, -1) if first == 0 else (n1, n1 + 1)
        for i in range(2):
            approx[ghost[i] + 2, first + i] = 1.0
        for place, source, coef in ((0, 0, 1.0), (1, 1, 1.0), (2, 1, third[first])):
            approx[cell(place) + 2, first + 2 + source] += coef
            for m in range(n1):
                approx[m + 2, first + 4 + source] += coef * tap(H, m + 3 - 2 * second(place))
    return from_approx @ approx


def final(left, right, own, zs1, ys1, z_matrix, y_matrix, rows, spill_rows):
    nx, ny, nz = own.shape
    half_z = nz // 2
    own_rows = ny // 2
    step_rows = 16
    steps = ny // step_rows
    taps = received_taps(nx // 2)

    def kernel(l_ref, r_ref, d_ref, z1, s1, z, y, out, planes, parts, done, sems):
        stack = [p for ref in (l_ref, r_ref) for p in unpacked(ref[4 * own_rows + 16 :])]
        spilled = cut(times(jnp.concatenate(stack, axis=0), z1), spill_rows)
        for side, ref in enumerate((l_ref, r_ref)):
            for i in range(4):
                plane = planes.at[4 * side + i]
                plane[:own_rows] = ref[i * own_rows : (i + 1) * own_rows]
                plane[own_rows:] = jnp.zeros((rows - own_rows, half_z), F32)
                plane[own_rows : own_rows + 4] = ref[4 * own_rows + 4 * i : 4 * own_rows + 4 * i + 4]
        for i, plane in enumerate(cut(times(planes[...].reshape(8 * rows, half_z), z), rows)):
            parts[6 * (i // 4) + i % 4] = left_times(y, plane)
        for i, plane in enumerate(spilled):
            parts[6 * (i // 2) + 4 + i % 2] = left_times(s1, plane)

        def copy(i):
            at = pl.ds(pl.multiple_of(i * step_rows, step_rows), step_rows)
            return pltpu.make_async_copy(done.at[:, at], out.at[:, at], sems.at[i])

        def step(i, carry):
            for t in range(step_rows // 8):
                at = pl.ds(pl.multiple_of(i * step_rows + 8 * t, 8), 8)
                for lane in range(0, nz, 128):
                    lanes = pl.ds(lane, 128)
                    values = [parts[i, at, lanes] for i in range(12)]
                    for m in range(nx):
                        value = d_ref[m, at, lanes]
                        value += added([(float(c), v) for c, v in zip(taps[m], values) if c != 0.0])
                        done[m, at, lanes] = value
            copy(i).start()
            return carry

        lax.fori_loop(0, steps, step, 0)

        def finish(i, carry):
            copy(i).wait()
            return carry

        lax.fori_loop(0, steps, finish, 0)

    return whole_call(
        kernel,
        shape(nx, ny, nz),
        [left, right, own, zs1, ys1, z_matrix, y_matrix],
        scratch=[
            pltpu.VMEM((8, rows, half_z), F32),
            pltpu.VMEM((12, ny, nz), F32),
            pltpu.VMEM((nx, ny, nz), F32),
            pltpu.SemaphoreType.DMA((steps,)),
        ],
        received=[(0, "gx")],
        name="final",
        out_specs=pl.BlockSpec(memory_space=pl.ANY),
    )


def exchange(first, second, axis):
    size = lax.axis_size(axis)
    assert size % 2 == 0
    here = [(i, i ^ 1) for i in range(size)]
    across = [(i, (i + 1) % size if i % 2 else (i - 1) % size) for i in range(size)]
    return lax.ppermute(first, axis, here), lax.ppermute(second, axis, across)


def local(velocity, table, index):
    nx, ny, nz = velocity.shape
    y1, y2, y3 = ny // 2, ny // 4, ny // 8
    ghost, wide = 24, 48
    cells0 = list(range(-8, ny + 8))
    rows0 = up_to(y1 + 4, 8)
    ks0 = fill(list(range(y1)) + [-2, -1, y1, y1 + 1], rows0)
    cells1 = ks0 + list(range(2 - ghost, 2)) + list(range(y1 - 2, y1 + ghost - 2))
    once = [c if cells1.index(c) == i else None for i, c in enumerate(cells1)]
    rows1 = up_to(y2 + 18, 8)
    low1 = fill(list(range(-9, y2 + 9)), rows1)
    high1 = fill(list(range(-3, y2 + 3)), up_to(y2 + 6, 8))
    spill_at, spill_rows = 6, up_to(y2 + 6, 8)
    ks2 = fill(list(range(-3, y3 + 3)), up_to(y3 + 6, 8))
    ya0 = from_left(analysis_rows(cells0, ks0, ks0))
    ys0_matrix = synthesis_rows(list(range(ny)), ks0, ks0)
    ys0 = from_left(ys0_matrix)
    ys0_low = from_left(ys0_matrix[:, :rows0])
    yl0 = from_left(analysis_rows(list(range(ny)), ks0, []))
    yx0 = from_left(analysis_rows(list(range(-wide, ny + wide)), once, []))
    ya1 = from_left(analysis_rows(cells1, low1, high1))
    ys1 = from_left(synthesis_rows(ks0, low1, high1))
    spill_matrix = synthesis_rows(ks0, low1[spill_at : spill_at + spill_rows], [])
    ys_spill = from_left(ys0_matrix[:, :rows0] @ spill_matrix)
    ya2 = from_left(analysis_rows(low1, ks2, ks2))
    ys2 = from_left(synthesis_rows(low1, ks2, ks2))
    z0 = periodic(nz, nz)
    z1 = periodic(nz // 2, nz // 2)
    z2 = periodic(nz // 4, nz // 2)
    za0, zs0, zs0_low = from_right(z0), from_right(z0.T), from_right(z0.T[: nz // 2])
    za1, zs1 = wide_right(z1), wide_right(z1.T)
    za2, zs2 = wide_right(z2), wide_right(z2.T)
    zs_spill = from_right(z1.T @ z0.T[: nz // 2])

    x_up, x_down, y_up, y_down = first_messages(velocity)
    x_left, x_right = exchange(x_up, x_down, "gx")
    y_here, y_across = exchange(y_up, y_down, "gy")
    zed = depth(velocity, za0, 16, "depth_analysis")
    approx, a_up, a_down = own_approx(zed, yl0, y1, rows0, ghost)
    a_left, a_right = exchange(a_up, a_down, "gy")
    zed, a_up = lax.optimization_barrier((zed, a_up))
    bands = y_analysis(zed, y_across, y_here, za0, ya0)
    x_left, x_right, bands = lax.optimization_barrier((x_left, x_right, bands))
    halo, h_up, h_down = x_halo_messages(x_left, x_right, approx, za0, wide, ghost)
    h_left, h_right = exchange(h_up, h_down, "gy")
    approx, halo = lax.optimization_barrier((approx, halo))
    bands1, b_up, b_down = second_bands(approx, a_left, a_right, za1, ya1, rows1)
    b_left, b_right = exchange(b_up, b_down, "gx")
    h_left, h_right, bands1 = lax.optimization_barrier((h_left, h_right, bands1))
    edge, e_up, e_down = edge_details(bands, halo, h_left, h_right, table, index, ya0, zs0, ys0, wide)
    e_left, e_right = exchange(e_up, e_down, "gx")
    bands1, edge = lax.optimization_barrier((bands1, edge))
    approx1, s_up, s_down = coarse(
        bands1, b_left, b_right, halo, h_left, h_right, approx, table, index,
        za1, yx0, ya1, zs1, za2, zs2, ya2, ys2, ys1, len(cells1), rows1, rows0, y1, spill_at, spill_rows, wide,
    )
    s_left, s_right = exchange(s_up, s_down, "gx")
    bands, approx1 = lax.optimization_barrier((bands, approx1))
    parts = detail_yz(edge, inner_bands(bands, table, index), approx1, zs0, ys0)
    own = own_result(parts, approx1, e_left, e_right, zs0_low, ys0_low)
    return final(s_left, s_right, own, zs_spill, ys_spill, zs0_low, ys0_low, rows0, spill_rows)


def solution(mesh):
    return jax.shard_map(
        local,
        mesh=mesh,
        in_specs=(P("gx", "gy", None), P(), P()),
        out_specs=P("gx", "gy", None),
        check_vma=False,
    )
```

```python
import functools

import jax
import jax.numpy as jnp
import ml_dtypes
import numpy as np
from jax import lax
from jax.experimental import pallas as pl
from jax.experimental.pallas import tpu as pltpu
from jax.sharding import PartitionSpec as P

H = [
    0.23037781330885523,
    0.7148465705525415,
    0.6308807679295904,
    -0.02798376941698385,
    -0.18703481171888114,
    0.030841381835986965,
    0.032883011666982945,
    -0.010597401784997278,
]
G = [(-1.0) ** j * H[7 - j] for j in range(8)]
F32 = jnp.float32
BF16 = jnp.bfloat16
NOTHING = 3.0e38
VMEM_BYTES = 16 * 1024 * 1024


def tap(filt, j):
    return filt[j] if 0 <= j < 8 else 0.0


def analysis_rows(cells, low_ks, high_ks):
    matrix = np.zeros((len(low_ks) + len(high_ks), len(cells)))
    rows = [(H, k) for k in low_ks] + [(G, k) for k in high_ks]
    for row, (filt, k) in enumerate(rows):
        for col, cell in enumerate(cells):
            if k is not None and cell is not None:
                matrix[row, col] = tap(filt, cell - 2 * k + 3)
    return matrix


def synthesis_rows(cells, low_ks, high_ks):
    return analysis_rows(cells, low_ks, high_ks).T


def periodic(length, padded_to):
    matrix = np.zeros((padded_to, padded_to))
    for k in range(length // 2):
        for j in range(8):
            matrix[(2 * k + j - 3) % length, k] += H[j]
            matrix[(2 * k + j - 3) % length, length // 2 + k] += G[j]
    return matrix


def fill(items, length):
    return items + [None] * (length - len(items))


def up_to(count, step):
    return -(-count // step) * step


def pieces(matrix, axis):
    rows, cols = matrix.shape
    matrix = np.pad(matrix, ((0, up_to(rows, 16) - rows), (0, up_to(cols, 16) - cols))).astype(np.float32)
    high = matrix.astype(ml_dtypes.bfloat16)
    low = (matrix - high.astype(np.float32)).astype(ml_dtypes.bfloat16)
    return np.concatenate([high, high, low], axis=axis)


def from_left(matrix):
    return pieces(matrix, 1)


def from_right(matrix):
    return pieces(matrix, 0)


def wide_right(matrix):
    rows, cols = matrix.shape
    both = pieces(matrix, 0)
    high, low = both[:rows], both[2 * rows :]
    return np.block([[high, low], [high, np.zeros_like(low)]])


def tall_left(matrix):
    return np.ascontiguousarray(wide_right(np.ascontiguousarray(padded_to_tiles(matrix).T)).T)


def padded_to_tiles(matrix):
    rows, cols = matrix.shape
    return np.pad(matrix, ((0, up_to(rows, 16) - rows), (0, up_to(cols, 16) - cols)))


def halves(values):
    high = values.astype(BF16)
    return high, (values - high.astype(F32)).astype(BF16)


def times(values, matrix):
    high, low = halves(values)
    return jnp.dot(jnp.concatenate([high, low, high], axis=1), matrix[...], preferred_element_type=F32)


def left_times(matrix, values):
    missing = matrix.shape[1] // 3 - values.shape[0]
    if missing:
        values = jnp.concatenate([values, jnp.zeros((missing, values.shape[1]), F32)], axis=0)
    high, low = halves(values)
    return jnp.dot(matrix[...], jnp.concatenate([high, low, high], axis=0), preferred_element_type=F32)


def times_wide(values, matrix):
    both = jnp.dot(jnp.concatenate(halves(values), axis=1), matrix[...], preferred_element_type=F32)
    return both[:, : both.shape[1] // 2] + both[:, both.shape[1] // 2 :]


def left_times_tall(matrix, values):
    missing = matrix.shape[1] // 2 - values.shape[0]
    if missing:
        values = jnp.concatenate([values, jnp.zeros((missing, values.shape[1]), F32)], axis=0)
    both = jnp.dot(matrix[...], jnp.concatenate(halves(values), axis=0), preferred_element_type=F32)
    return both[: both.shape[0] // 2] + both[both.shape[0] // 2 :]


def added(terms):
    total = None
    for coef, value in terms:
        part = value if coef == 1.0 else coef * value
        total = part if total is None else total + part
    return total


def x_terms(k, n):
    terms = []
    for j in range(8):
        cell = 2 * k + j - 3
        if 0 <= cell < n:
            terms.append((cell, H[j], G[j]))
        elif cell == -1:
            terms.append(("l1", H[j], G[j]))
        elif cell == n:
            terms.append(("r1", H[j], G[j]))
    if k == 0:
        terms.append(("l2", 1.0, G[0] / H[0]))
    if k == n // 2 - 1:
        terms.append(("r2", 1.0, G[6] / H[6]))
    return terms


def lattice():
    low = np.array(H).reshape(4, 2)
    high = np.array(G).reshape(4, 2)
    tangents = []
    for _ in range(3):
        t = (low[0] @ high[0]) / (high[0] @ high[0])
        tangents.append(float(t))
        low, high = (low - t * high)[1:] / (1 + t * t), (high + t * low)[:-1] / (1 + t * t)
    return low[0].tolist(), high[0].tolist(), tangents[::-1]


def x_interior(get, n):
    first, second, tangents = lattice()
    a, b = {}, {}
    for i in range(1, n // 2):
        x, y = get(2 * i - 1), get(2 * i)
        a[i] = first[0] * x + first[1] * y
        b[i] = second[0] * x + second[1] * y
    for t in tangents:
        shared = [i for i in a if i + 1 in a]
        a, b = {i: a[i + 1] + t * b[i] for i in shared}, {i: b[i] - t * a[i + 1] for i in shared}
    return {i + 1: (a[i], b[i]) for i in a}


def x_low(get, k, n):
    return added([(low, get(key)) for key, low, _ in x_terms(k, n)])


def x_high(get, k, n):
    return added([(high, get(key)) for key, _, high in x_terms(k, n)])


def x_synth(m, lows, highs):
    terms = [(H[m + 3 - 2 * k], v) for k, v in lows.items() if 0 <= m + 3 - 2 * k < 8]
    terms += [(G[m + 3 - 2 * k], v) for k, v in highs.items() if 0 <= m + 3 - 2 * k < 8]
    return added(terms)


def x_synth_interior(lows, highs, n):
    first, second, tangents = lattice()
    a = {k - 1: lows[k] for k in range(n)}
    b = {k - 1: highs[k] for k in range(n)}
    for t in reversed(tangents):
        a, b = {i + 1: a[i] - t * b[i] for i in a}, {i: b[i] + t * a[i] for i in b}
        both = [i for i in a if i in b]
        a, b = {i: a[i] for i in both}, {i: b[i] for i in both}
    cells = {}
    for i in a:
        cells[2 * i - 1] = first[0] * a[i] + second[0] * b[i]
        cells[2 * i] = first[1] * a[i] + second[1] * b[i]
    return cells


def spill_up(low, high, n):
    first = added([(H[5], low[n - 1]), (G[5], high[n - 1]), (H[7], low[n - 2]), (G[7], high[n - 2])])
    return first, added([(H[6], low[n - 1]), (G[6], high[n - 1])])


def spill_down(low, high):
    first = added([(H[2], low[0]), (G[2], high[0]), (H[0], low[1]), (G[0], high[1])])
    return first, added([(H[1], low[0]), (G[1], high[0])])


THIRD_UP = H[7] / H[6]
THIRD_DOWN = H[0] / H[1]


def shrink(values, thresh):
    return values - jnp.minimum(jnp.maximum(values, -thresh), thresh)


def paired(kernel, args, outs, scratch, received, sent):
    extra = [pltpu.VMEM((2,) + args[i].shape, F32) for i, _ in received]
    extra += [pltpu.VMEM((2,) + outs[j].shape, F32) for j, _ in sent]

    def wrapped(*refs):
        refs, both = list(refs[: len(refs) - len(extra)]), refs[len(refs) - len(extra) :]
        for (i, axis), pair in zip(received, both):
            parity = lax.rem(lax.axis_index(axis), 2)
            pair[0], pair[1] = refs[i][...], refs[i + 1][...]
            refs[i], refs[i + 1] = pair.at[1 - parity], pair.at[parity]
        carried = []
        for (j, axis), pair in zip(sent, both[len(received) :]):
            parity = lax.rem(lax.axis_index(axis), 2)
            j += len(args)
            carried.append((refs[j], refs[j + 1], pair))
            refs[j], refs[j + 1] = pair.at[parity], pair.at[1 - parity]
        kernel(*refs)
        for first, second, pair in carried:
            first[...], second[...] = pair[0], pair[1]

    return wrapped, list(scratch) + extra


def whole_call(kernel, outs, args, scratch=(), received=(), sent=(), name=None, **changes):
    out_list = outs if isinstance(outs, list) else [outs]
    kernel, scratch = paired(kernel, args, out_list, scratch, received, sent)
    specs = [SMEM if a.ndim == 1 or a.dtype == jnp.int32 else VMEM for a in args]
    return pl.pallas_call(
        kernel,
        in_specs=changes.get("in_specs", specs),
        out_specs=changes.get("out_specs", [VMEM] * len(outs) if outs is out_list else VMEM),
        out_shape=outs,
        scratch_shapes=scratch,
        name=name,
        cost_estimate=pl.CostEstimate(flops=1000, bytes_accessed=1000, transcendentals=0),
        compiler_params=pltpu.CompilerParams(vmem_limit_bytes=changes.get("vmem", VMEM_BYTES)),
    )(*args)


def shape(*dims):
    return jax.ShapeDtypeStruct(dims, F32)


SMEM = pl.BlockSpec(memory_space=pltpu.SMEM)
VMEM = pl.BlockSpec(memory_space=pltpu.VMEM)


def first_messages(v):
    nx, ny, nz = v.shape

    kept = nx - nx // 8

    def kernel(v_ref, up, down, y_up, y_down, last, first, rows_up, rows_down, sems):
        copies = [
            pltpu.make_async_copy(source, target, sems.at[i])
            for i, (source, target) in enumerate(
                (
                    (v_ref.at[pl.ds(nx - 3, 3)], last),
                    (v_ref.at[pl.ds(0, 3)], first),
                    (v_ref.at[:, pl.ds(ny - 8, 8)], rows_up),
                    (v_ref.at[:, pl.ds(0, 8)], rows_down),
                )
            )
        ]
        for copy in copies:
            copy.start()
        for copy in copies:
            copy.wait()
        up[0] = last[2]
        up[1] = H[0] * last[0] + H[1] * last[1]
        down[0] = first[0]
        down[1] = H[6] * first[1] + H[7] * first[2]
        y_up[...] = rows_up[:kept]
        y_down[...] = rows_down[:kept]
        for i in range(kept):
            plane, row = kept + i // 7, i % 7
            y_up[i, 0:1] = rows_up[plane, row + 1 : row + 2]
            y_down[i, 7:8] = rows_down[plane, row : row + 1]

    return whole_call(
        kernel,
        [shape(2, ny, nz)] * 2 + [shape(kept, 8, nz)] * 2,
        [v],
        scratch=[pltpu.VMEM((3, ny, nz), F32)] * 2
        + [pltpu.VMEM((nx, 8, nz), F32)] * 2
        + [pltpu.SemaphoreType.DMA((4,))],
        sent=[(0, "gx"), (2, "gy")],
        name="first_messages",
        in_specs=[pl.BlockSpec(memory_space=pltpu.HBM)],
        vmem=50 * 1024 * 1024,
    )


def over_planes(count, group, body):
    def step(i, carry):
        body(i * group)
        return carry

    lax.fori_loop(0, count // group, step, 0)


def depth(v, z_matrix, group, name):
    nx, rows, nz = v.shape

    def kernel(v_ref, z, out):
        def body(first):
            at = pl.ds(first, group)
            out[at] = times(v_ref[at].reshape(group * rows, nz), z).reshape(group, rows, nz)

        over_planes(nx, group, body)

    return whole_call(kernel, shape(nx, rows, nz), [v, z_matrix], name=name)


def y_analysis(zed, y_across, y_here, z_matrix, y_matrix):
    nx, ny, nz = zed.shape
    rows = y_matrix.shape[0]
    kept = y_here.shape[0]
    group = 8

    def kernel(zed_ref, right, left, z, y, out, left_z, right_z):
        for part, out_z in ((left, left_z), (right, right_z)):
            out_z[:kept] = times(part[...].reshape(8 * kept, nz), z).reshape(kept, 8, nz)
            out_z[kept:] = jnp.zeros((nx - kept, 8, nz), F32)
        for i in range(kept):
            plane, row = kept + i // 7, i % 7
            left_z[plane, row + 1 : row + 2] = left_z[i, 0:1]
            right_z[plane, row : row + 1] = right_z[i, 7:8]

        def body(first):
            for j in range(group):
                i = first + j
                out[i] = left_times(y, jnp.concatenate([left_z[i], zed_ref[i], right_z[i]], axis=0))

        over_planes(nx, group, body)

    return whole_call(
        kernel,
        shape(nx, rows, nz),
        [zed, y_across, y_here, z_matrix, y_matrix],
        scratch=[pltpu.VMEM((nx, 8, nz), F32)] * 2,
        received=[(1, "gy")],
        name="y_analysis",
    )


def own_approx(zed, y_matrix, own, rows, ghost_rows):
    nx, ny, nz = zed.shape
    half_z = nz // 2
    n1 = nx // 2

    def kernel(zed_ref, y, approx, up, down, low):
        def y_body(first):
            planes = [zed_ref[first + i, :, :half_z] for i in range(8)]
            for i, plane in enumerate(in_pairs(y, planes)):
                low[first + i] = plane[:rows]

        over_planes(nx, 8, y_body)

        def tile(t, carry):
            at = pl.ds(pl.multiple_of(t * 8, 8), 8)
            values = {i: low[i, at] for i in range(nx)}
            for k in range(n1):
                approx[k, at] = added([(c, values[i]) for i, c, _ in x_terms(k, nx) if i in values])
            approx[n1, at] = added([(H[5 + i], values[i]) for i in range(3)])
            approx[n1 + 1, at] = H[1] * H[7] * values[0]
            approx[n1 + 2, at] = added([(H[i], values[nx - 3 + i]) for i in range(3)])
            approx[n1 + 3, at] = H[6] * H[0] * values[nx - 1]
            return carry

        lax.fori_loop(0, rows // 8, tile, 0)
        inside = ghost_rows - 2
        up[:, :inside] = approx[:n1, own - inside : own]
        up[:, inside:] = approx[:n1, own + 2 : own + 4]
        down[:, :2] = approx[:n1, own : own + 2]
        down[:, 2:] = approx[:n1, :inside]

    return whole_call(
        kernel,
        [shape(n1 + 4, rows, half_z), shape(n1, ghost_rows, half_z), shape(n1, ghost_rows, half_z)],
        [zed, y_matrix],
        scratch=[pltpu.VMEM((nx, rows, half_z), F32)],
        sent=[(1, "gy")],
        name="own_approx",
    )


def x_halo_messages(x_left, x_right, approx, z_matrix, wide, ghost_rows):
    _, ny, nz = x_left.shape
    half_z = nz // 2
    n1 = approx.shape[0] - 4
    own, inside = ny // 2, ghost_rows - 2
    message = wide + 8 + ghost_rows

    def kernel(xl, xr, a_ref, z, out, up, down):
        planes = jnp.concatenate([xl[0], xl[1], xr[0], xr[1]], axis=0)
        out[...] = times(planes, z).reshape(4, ny, nz)
        up[:, :wide] = out[:, ny - wide :, :half_z]
        up[:, wide : wide + 8] = out[:, ny - 8 :, half_z:]
        down[:, :wide] = out[:, :wide, :half_z]
        down[:, wide : wide + 8] = out[:, :8, half_z:]
        up[:, wide + 8 : wide + 8 + inside] = a_ref[n1:, own - inside : own]
        up[:, wide + 8 + inside :] = a_ref[n1:, own + 2 : own + 4]
        down[:, wide + 8 : wide + 10] = a_ref[n1:, own : own + 2]
        down[:, wide + 10 :] = a_ref[n1:, :inside]

    return whole_call(
        kernel,
        [shape(4, ny, nz), shape(4, message, half_z), shape(4, message, half_z)],
        [x_left, x_right, approx, z_matrix],
        received=[(0, "gx")],
        sent=[(1, "gy")],
        name="x_halo_messages",
    )


def edges_of(n):
    return [0, 1, n - 2, n - 1]


def band_limits(table_ref, index_ref, by, bz):
    band = 2 * by + bz
    quiet = table_ref[index_ref[0, band - 1]] if band else NOTHING
    return quiet, table_ref[index_ref[0, band + 3]]


def over_tiles(rows, nz, body):
    half_z, half_tiles = nz // 2, rows // 16
    for by in range(2):

        def tile(t, carry, by=by):
            at = pl.ds(pl.multiple_of((t + by * half_tiles) * 8, 8), 8)
            for bz in range(2):
                body(at, pl.ds(bz * half_z, half_z), by, bz)
            return carry

        lax.fori_loop(0, half_tiles, tile, 0, unroll=3 if half_tiles % 3 == 0 else 1)


def inner_bands(bands, table, index):
    nx, rows, nz = bands.shape
    count = nx // 2 - 4

    def kernel(table_ref, index_ref, b_ref, out):
        def body(at, lanes, by, bz):
            quiet, loud = band_limits(table_ref, index_ref, by, bz)
            values = {i: b_ref[i, at, lanes] for i in range(nx)}
            for k, (low, high) in x_interior(values.get, nx).items():
                out[k - 2, at, lanes] = shrink(low, quiet) if by + bz else jnp.zeros_like(low)
                out[count + k - 2, at, lanes] = shrink(high, loud)

        over_tiles(rows, nz, body)

    return whole_call(
        kernel,
        shape(2 * count, rows, nz),
        [table, index, bands],
        name="inner_bands",
    )


def yz_synthesis(planes, z, y, out, zed):
    count, rows, nz = zed.shape
    group = max(g for g in range(1, 17) if count % g == 0)
    for first in range(0, count, group):
        zed[first : first + group] = times(planes(first, group), z).reshape(group, rows, nz)

    def y_body(first):
        for j in range(4):
            out[first + j] = left_times(y, zed[first + j])

    over_planes(count, 4, y_body)


def edge_own(bands):
    nx, rows, nz = bands.shape

    def kernel(b_ref, out):
        def body(at, lanes, by, bz):
            values = {i: b_ref[i, at, lanes] for i in [*range(7), *range(nx - 7, nx)]}
            for i, k in enumerate(edges_of(nx // 2)):
                terms = [t for t in x_terms(k, nx) if t[0] in values]
                out[i, at, lanes] = added([(low, values[key]) for key, low, _ in terms])
                out[4 + i, at, lanes] = added([(high, values[key]) for key, _, high in terms])

        over_tiles(rows, nz, body)

    return whole_call(kernel, shape(8, rows, nz), [bands], name="edge_own")


def edge_details(nx, own, halo, h_left, h_right, table, index, ya_matrix, z_matrix, y_matrix, wide):
    _, rows, nz = own.shape
    ny = y_matrix.shape[0]
    n1 = nx // 2
    half_z = nz // 2
    ends = edges_of(n1)

    def kernel(table_ref, index_ref, b_ref, x_ref, hl, hr, ya, z, y, coeffs, up, down, h_ref, beyond, zed):
        for i in range(4):
            low = jnp.concatenate([hl[i, wide - 8 : wide], x_ref[i, :, :half_z], hr[i, :8]], axis=0)
            high = jnp.concatenate(
                [hl[i, wide : wide + 8], x_ref[i, :, half_z:], hr[i, wide : wide + 8]], axis=0
            )
            h_ref[i] = left_times(ya, jnp.concatenate([low, high], axis=1))
        place = {"l1": 0, "l2": 1, "r1": 2, "r2": 3}

        def body(at, lanes, by, bz):
            quiet, loud = band_limits(table_ref, index_ref, by, bz)
            values = {key: h_ref[i, at, lanes] for key, i in place.items()}
            lows, highs = {}, {}
            for i, k in enumerate(ends):
                terms = [t for t in x_terms(k, nx) if t[0] in values]
                low = b_ref[i, at, lanes] + added([(c, values[key]) for key, c, _ in terms])
                high = b_ref[4 + i, at, lanes] + added([(c, values[key]) for key, _, c in terms])
                lows[k] = shrink(low, quiet) if by + bz else jnp.zeros_like(low)
                highs[k] = shrink(high, loud)
                coeffs[i, at, lanes] = lows[k]
                coeffs[4 + i, at, lanes] = highs[k]
            spilled = spill_up(lows, highs, n1) + spill_down(lows, highs)
            for i, part in enumerate(spilled):
                beyond[i, at, lanes] = part

        over_tiles(rows, nz, body)
        zed[...] = times(beyond[...].reshape(4 * rows, nz), z).reshape(4, rows, nz)
        for i, target in enumerate((up.at[0], up.at[1], down.at[0], down.at[1])):
            target[...] = left_times(y, zed[i])

    return whole_call(
        kernel,
        [shape(8, rows, nz), shape(2, ny, nz), shape(2, ny, nz)],
        [table, index, own, halo, h_left, h_right, ya_matrix, z_matrix, y_matrix],
        scratch=[pltpu.VMEM((4, rows, nz), F32)] * 3,
        received=[(4, "gy")],
        sent=[(1, "gx")],
        name="edge_details",
    )


def detail_yz(edge, inner, approx, z_matrix, y_matrix):
    count, rows, nz = inner.shape
    ny = y_matrix.shape[0]
    _, low_rows, half_z = approx.shape
    n1 = count // 2 + 4
    ends = edges_of(n1)

    def kernel(e_ref, i_ref, a_ref, z, y, out, zed):
        def coeff(k, high):
            if k in ends:
                return e_ref.at[4 * high + ends.index(k)]
            return i_ref.at[(n1 - 4) * high + k - 2]

        def plane(i):
            ref = coeff(i % n1, i // n1)
            if i >= n1:
                return ref[...]
            corner = ref[:low_rows, :half_z] + a_ref[i + 2]
            top = jnp.concatenate([corner, ref[:low_rows, half_z:]], axis=1)
            return jnp.concatenate([top, ref[low_rows:]], axis=0)

        def planes(first, n):
            return jnp.concatenate([plane(i) for i in range(first, first + n)], axis=0)

        yz_synthesis(planes, z, y, out, zed)

    return whole_call(
        kernel,
        shape(2 * n1, ny, nz),
        [edge, inner, approx, z_matrix, y_matrix],
        scratch=[pltpu.VMEM((2 * n1, rows, nz), F32)],
        name="detail_yz",
    )


def own_result(parts, approx, left, right, z_matrix, y_matrix):
    nx, ny, nz = parts.shape
    n1 = nx // 2
    planes, rows, half_z = approx.shape

    def kernel(p_ref, a_ref, el, er, z, y, out, ghosts):
        stack = jnp.concatenate([a_ref[i] for i in (0, 1, n1 + 2, n1 + 3)], axis=0)
        for i, plane in enumerate(cut(times(stack, z), rows)):
            ghosts[i] = left_times(y, plane)

        def tile(t, carry):
            at = pl.ds(pl.multiple_of(t * 8, 8), 8)
            for lane in range(0, nz, 128):
                lanes = pl.ds(lane, 128)
                lows = {k: p_ref[k, at, lanes] for k in range(n1)}
                highs = {k: p_ref[n1 + k, at, lanes] for k in range(n1)}
                for i, k in enumerate((-2, -1, n1, n1 + 1)):
                    lows[k] = ghosts[i, at, lanes]
                cells = x_synth_interior(lows, highs, n1)
                for m in range(nx):
                    value = cells[m] if m in cells else x_synth(m, lows, highs)
                    if m < 3:
                        extra = el[(0, 1, 1)[m], at, lanes]
                        value += extra if m < 2 else THIRD_UP * extra
                    if m >= nx - 3:
                        extra = er[(0, 1, 1)[nx - 1 - m], at, lanes]
                        value += extra if m > nx - 3 else THIRD_DOWN * extra
                    out[m, at, lanes] = value
            return carry

        lax.fori_loop(0, ny // 8, tile, 0)

    return whole_call(
        kernel,
        shape(nx, ny, nz),
        [parts, approx, left, right, z_matrix, y_matrix],
        scratch=[pltpu.VMEM((4, ny, nz), F32)],
        received=[(2, "gx")],
        name="own_result",
    )


def in_pairs(matrix, planes):
    results = []
    for i in range(0, len(planes), 2):
        both = left_times(matrix, jnp.concatenate(planes[i : i + 2], axis=1))
        width = both.shape[1] // 2
        results += [both[:, :width], both[:, width:]]
    return results


def cut(values, rows):
    return [values[i : i + rows] for i in range(0, values.shape[0], rows)]


def packed(first, second):
    half = first.shape[1] // 2
    lane = lax.broadcasted_iota(jnp.int32, first.shape, 1)
    return jnp.where(lane < half, first, pltpu.roll(second, half, 1))


def unpacked(both):
    half = both.shape[1] // 2
    lane = lax.broadcasted_iota(jnp.int32, both.shape, 1)
    return [jnp.where(lane < half, part, 0.0) for part in (both, pltpu.roll(both, half, 1))]


def second_bands(own, left, right, z_matrix, y_matrix, low_rows):
    _, own_rows, nz = own.shape
    n1 = left.shape[0]
    in_rows = own_rows + 2 * left.shape[1]
    rows = y_matrix.shape[0]


    def kernel(o_ref, l_ref, r_ref, z, y, out, up, down):
        for i in range(0, n1, 8):
            stack = [part[j] for j in range(i, i + 8) for part in (o_ref, l_ref, r_ref)]
            zed = times_wide(jnp.concatenate(stack, axis=0), z)
            for j, plane in enumerate(in_pairs(y, cut(zed, in_rows))):
                out[i + j] = plane
        low = lambda c: out[c, :low_rows]
        up[0:rows] = out[n1 - 1]
        up[rows : 2 * rows] = H[0] * out[n1 - 3] + H[1] * out[n1 - 2]
        first = added([(H[j], low(n1 - 5 + j)) for j in range(5)])
        second = added([(H[0] * H[j], low(n1 - 9 + j)) for j in range(8)])
        second += added([(H[1] * H[j], low(n1 - 7 + j)) for j in range(7)])
        up[2 * rows :] = packed(first, second)
        down[0:rows] = out[0]
        down[rows : 2 * rows] = H[6] * out[1] + H[7] * out[2]
        first = added([(H[j], low(j - 3)) for j in range(3, 8)])
        second = added([(H[6] * H[j], low(j - 1)) for j in range(1, 8)])
        second += added([(H[7] * H[j], low(j + 1)) for j in range(8)])
        down[2 * rows :] = packed(first, second)

    message = 2 * rows + low_rows
    return whole_call(
        kernel,
        [shape(n1, rows, nz), shape(message, nz), shape(message, nz)],
        [own, left, right, z_matrix, y_matrix],
        received=[(1, "gy")],
        sent=[(1, "gx")],
        name="second_bands",
    )


def limits_plane(table_ref, index_ref, level, bx, dims, row_split, lane_split, zeroth):
    row_high = lax.broadcasted_iota(jnp.int32, dims, 0) >= row_split
    lane_high = lax.broadcasted_iota(jnp.int32, dims, 1) >= lane_split

    def limit(by, bz):
        band = 4 * bx + 2 * by + bz
        return zeroth if band == 0 else table_ref[index_ref[level, band - 1]]

    low_y = jnp.where(lane_high, limit(0, 1), limit(0, 0))
    return jnp.where(row_high, jnp.where(lane_high, limit(1, 1), limit(1, 0)), low_y)


def coarse(
    bands, left, right, halo, h_left, h_right, approx_in, table, index, za1, yx0, ya1, zs1, za2, zs2, ya2, ys2, ys1,
    in_rows1, low_rows, out_rows, own_rows, spill_at, spill_rows, wide,
):
    n1, rows, nz = bands.shape
    in_rows = in_rows1
    n2, n3 = n1 // 2, n1 // 4
    rows2 = ya2.shape[0]
    lane_half = nz // 2

    def kernel(
        table_ref, index_ref, b_ref, l_ref, r_ref, x_ref, hl, hr, a_ref, z1a, yx, a1, z1, z2a, z2s, a2, s2, s1,
        approx, up, down, c1, p1,
    ):
        halo_planes = [jnp.concatenate([hl[i, :wide], x_ref[i, :, :nz], hr[i, :wide]], axis=0) for i in range(4)]
        halo_planes = [plane[:in_rows] for plane in in_pairs(yx, halo_planes)]
        own_planes = [
            jnp.concatenate([a_ref[n1 + i], hl[i, wide + 8 :], hr[i, wide + 8 :]], axis=0) for i in range(4)
        ]
        both = times_wide(jnp.concatenate(halo_planes + own_planes, axis=0), z1a)
        hl1, hl2, hr1, hr2, xl1, xl2, xr1, xr2 = in_pairs(a1, cut(both, in_rows))
        values = {k: b_ref[k] for k in range(2, n1 - 2)}
        values[0] = b_ref[0] + (hl2 + H[2] * hl1)
        values[1] = b_ref[1] + H[0] * hl1
        values[n1 - 2] = b_ref[n1 - 2] + H[7] * hr1
        values[n1 - 1] = b_ref[n1 - 1] + (hr2 + H[5] * hr1)
        values["l1"] = l_ref[0:rows] + xl1
        values["l2"] = l_ref[rows : 2 * rows] + xl2
        values["r1"] = r_ref[0:rows] + xr1
        values["r2"] = r_ref[rows : 2 * rows] + xr2
        get = values.get
        low_part = lambda c: values[c][:low_rows]
        xl1, xl2, xr1, xr2 = [part[:low_rows] for part in (xl1, xl2, xr1, xr2)]
        dims = (rows, nz)
        quiet = limits_plane(table_ref, index_ref, 1, 0, dims, low_rows, lane_half, NOTHING)
        loud = limits_plane(table_ref, index_ref, 1, 1, dims, low_rows, lane_half, NOTHING)
        planes = []
        for k in range(n2):
            low = x_low(get, k, n1)
            planes.append(low[:low_rows])
            c1[k] = shrink(low, quiet)
            c1[n2 + k] = shrink(x_high(get, k, n1), loud)
        first, second = unpacked(l_ref[2 * rows :])
        own = [(H[5 + i], low_part(i)) for i in range(3)]
        planes.append(first + added([(H[3] / H[1], xl2), (H[4], xl1)] + own))
        own = [((H[0] * H[7] + H[1] * H[5]) / H[1], xl2), (H[1] * H[6], xl1), (H[1] * H[7], low_part(0))]
        planes.append(second + added(own))
        first, second = unpacked(r_ref[2 * rows :])
        own = [(H[i], low_part(n1 - 3 + i)) for i in range(3)]
        planes.append(first + added([(H[3], xr1), (H[4] / H[6], xr2)] + own))
        own = [((H[6] * H[2] + H[7] * H[0]) / H[6], xr2), (H[6] * H[1], xr1), (H[6] * H[0], low_part(n1 - 1))]
        planes.append(second + added(own))
        third = in_pairs(a2, cut(times_wide(jnp.concatenate(planes, axis=0), z2a), low_rows))
        keys = {"l1": n2, "l2": n2 + 1, "r1": n2 + 2, "r2": n2 + 3}
        get2 = lambda key: third[keys.get(key, key)]
        dims = (rows2, nz)
        quiet = limits_plane(table_ref, index_ref, 2, 0, dims, rows2 // 2, lane_half // 2, 0.0)
        loud = limits_plane(table_ref, index_ref, 2, 1, dims, rows2 // 2, lane_half // 2, 0.0)
        kept = [shrink(x_low(get2, k, n2), quiet) for k in range(n3)]
        kept += [shrink(x_high(get2, k, n2), loud) for k in range(n3)]
        parts = in_pairs(s2, cut(times_wide(jnp.concatenate(kept, axis=0), z2s), rows2))
        parts = [part[:low_rows] for part in parts]
        lows = dict(enumerate(parts[:n3]))
        highs = dict(enumerate(parts[n3:]))
        ghosts = [-3, -2, -1, n2, n2 + 1, n2 + 2]
        for k in range(n2):
            c1[k, :low_rows] += x_synth(k, lows, highs)
        stack = [x_synth(k, lows, highs) for k in ghosts]
        beyond = dict(zip(ghosts, stack))
        zed = times_wide(jnp.concatenate(stack, axis=0), z1)
        for i, plane in enumerate(in_pairs(s1, cut(zed, low_rows))):
            p1[2 * n2 + i] = plane[:out_rows]
        for i in range(0, 2 * n2, 8):
            zed = times_wide(c1[i : i + 8].reshape(8 * rows, nz), z1)
            for j, plane in enumerate(in_pairs(s1, cut(zed, rows))):
                p1[i + j] = plane[:out_rows]
        lows = {k: p1.at[k] for k in range(n2)}
        highs = {k: p1.at[n2 + k] for k in range(n2)}
        for i, k in enumerate(ghosts):
            lows[k] = p1.at[2 * n2 + i]

        def cell(m):
            near = lambda part: {k: ref[...] for k, ref in part.items() if 0 <= m + 3 - 2 * k < 8}
            return x_synth(m, near(lows), near(highs))

        for m in range(-2, n1 + 2):
            approx[m + 2] = cell(m)
        value = lambda part, ks: {k: part[k][...] for k in ks}
        ends = (n2 - 2, n2 - 1)

        def send(message, four, two):
            for i, plane in enumerate(four):
                message[i * own_rows : (i + 1) * own_rows] = plane[:own_rows]
                message[4 * own_rows + 4 * i : 4 * own_rows + 4 * i + 4] = plane[own_rows : own_rows + 4]
            message[4 * own_rows + 16 :] = packed(*two)[spill_at : spill_at + spill_rows]

        up_two = spill_up(value(lows, ends), value(highs, ends), n2)
        send(up, (approx[n1], approx[n1 + 1], *up_two), (beyond[n2], beyond[n2 + 1]))
        down_two = spill_down(value(lows, (0, 1)), value(highs, (0, 1)))
        send(down, (approx[2], approx[3], *down_two), (beyond[-1], beyond[-2]))

    message = 4 * own_rows + 16 + spill_rows
    return whole_call(
        kernel,
        [shape(n1 + 4, out_rows, nz), shape(message, nz), shape(message, nz)],
        [table, index, bands, left, right, halo, h_left, h_right, approx_in, za1, yx0, ya1, zs1, za2, zs2, ya2, ys2, ys1],
        scratch=[pltpu.VMEM((2 * n2, rows, nz), F32), pltpu.VMEM((2 * n2 + 6, out_rows, nz), F32)],
        received=[(3, "gx"), (6, "gy")],
        sent=[(1, "gx")],
        name="coarse",
    )


def received_taps(n1):
    n2, nx = n1 // 2, 2 * n1
    from_approx = np.zeros((nx, n1 + 4))
    for m in range(nx):
        for k in range(-2, n1 + 2):
            from_approx[m, k + 2] = tap(H, m + 3 - 2 * k)
    approx = np.zeros((n1 + 4, 12))
    third = {0: THIRD_UP, 6: THIRD_DOWN}
    for first, cell, second in ((0, lambda i: i, lambda i: i), (6, lambda i: n1 - 1 - i, lambda i: n2 - 1 - i)):
        ghost = (-2, -1) if first == 0 else (n1, n1 + 1)
        for i in range(2):
            approx[ghost[i] + 2, first + i] = 1.0
        for place, source, coef in ((0, 0, 1.0), (1, 1, 1.0), (2, 1, third[first])):
            approx[cell(place) + 2, first + 2 + source] += coef
            for m in range(n1):
                approx[m + 2, first + 4 + source] += coef * tap(H, m + 3 - 2 * second(place))
    return from_approx @ approx


def final(left, right, own, zs1, ys1, z_matrix, y_matrix, rows, spill_rows):
    nx, ny, nz = own.shape
    half_z = nz // 2
    own_rows = ny // 2
    step_rows = 16
    steps = ny // step_rows
    taps = received_taps(nx // 2)

    def kernel(l_ref, r_ref, d_ref, z1, s1, z, y, out, planes, parts, done, sems):
        stack = [p for ref in (l_ref, r_ref) for p in unpacked(ref[4 * own_rows + 16 :])]
        spilled = cut(times(jnp.concatenate(stack, axis=0), z1), spill_rows)
        for side, ref in enumerate((l_ref, r_ref)):
            for i in range(4):
                plane = planes.at[4 * side + i]
                plane[:own_rows] = ref[i * own_rows : (i + 1) * own_rows]
                plane[own_rows:] = jnp.zeros((rows - own_rows, half_z), F32)
                plane[own_rows : own_rows + 4] = ref[4 * own_rows + 4 * i : 4 * own_rows + 4 * i + 4]
        for i, plane in enumerate(cut(times(planes[...].reshape(8 * rows, half_z), z), rows)):
            parts[6 * (i // 4) + i % 4] = left_times(y, plane)
        for i, plane in enumerate(spilled):
            parts[6 * (i // 2) + 4 + i % 2] = left_times(s1, plane)

        def copy(i):
            at = pl.ds(pl.multiple_of(i * step_rows, step_rows), step_rows)
            return pltpu.make_async_copy(done.at[:, at], out.at[:, at], sems.at[i])

        def step(i, carry):
            for t in range(step_rows // 8):
                at = pl.ds(pl.multiple_of(i * step_rows + 8 * t, 8), 8)
                for lane in range(0, nz, 128):
                    lanes = pl.ds(lane, 128)
                    values = [parts[i, at, lanes] for i in range(12)]
                    for m in range(nx):
                        value = d_ref[m, at, lanes]
                        value += added([(float(c), v) for c, v in zip(taps[m], values) if c != 0.0])
                        done[m, at, lanes] = value
            copy(i).start()
            return carry

        lax.fori_loop(0, steps, step, 0)

        def finish(i, carry):
            copy(i).wait()
            return carry

        lax.fori_loop(0, steps, finish, 0)

    return whole_call(
        kernel,
        shape(nx, ny, nz),
        [left, right, own, zs1, ys1, z_matrix, y_matrix],
        scratch=[
            pltpu.VMEM((8, rows, half_z), F32),
            pltpu.VMEM((12, ny, nz), F32),
            pltpu.VMEM((nx, ny, nz), F32),
            pltpu.SemaphoreType.DMA((steps,)),
        ],
        received=[(0, "gx")],
        name="final",
        out_specs=pl.BlockSpec(memory_space=pl.ANY),
    )


def exchange(first, second, axis):
    size = lax.axis_size(axis)
    assert size % 2 == 0
    here = [(i, i ^ 1) for i in range(size)]
    across = [(i, (i + 1) % size if i % 2 else (i - 1) % size) for i in range(size)]
    return lax.ppermute(first, axis, here), lax.ppermute(second, axis, across)


def local(velocity, table, index):
    nx, ny, nz = velocity.shape
    y1, y2, y3 = ny // 2, ny // 4, ny // 8
    ghost, wide = 24, 48
    cells0 = list(range(-8, ny + 8))
    rows0 = up_to(y1 + 4, 8)
    ks0 = fill(list(range(y1)) + [-2, -1, y1, y1 + 1], rows0)
    cells1 = ks0 + list(range(2 - ghost, 2)) + list(range(y1 - 2, y1 + ghost - 2))
    once = [c if cells1.index(c) == i else None for i, c in enumerate(cells1)]
    rows1 = up_to(y2 + 18, 8)
    low1 = fill(list(range(-9, y2 + 9)), rows1)
    high1 = fill(list(range(-3, y2 + 3)), up_to(y2 + 6, 8))
    spill_at, spill_rows = 6, up_to(y2 + 6, 8)
    ks2 = fill(list(range(-3, y3 + 3)), up_to(y3 + 6, 8))
    ya0 = from_left(analysis_rows(cells0, ks0, ks0))
    ys0_matrix = synthesis_rows(list(range(ny)), ks0, ks0)
    ys0 = from_left(ys0_matrix)
    ys0_low = from_left(ys0_matrix[:, :rows0])
    yl0 = from_left(analysis_rows(list(range(ny)), ks0, []))
    yx0 = from_left(analysis_rows(list(range(-wide, ny + wide)), once, []))
    ya1 = from_left(analysis_rows(cells1, low1, high1))
    ys1 = from_left(synthesis_rows(ks0, low1, high1))
    spill_matrix = synthesis_rows(ks0, low1[spill_at : spill_at + spill_rows], [])
    ys_spill = from_left(ys0_matrix[:, :rows0] @ spill_matrix)
    ya2 = from_left(analysis_rows(low1, ks2, ks2))
    ys2 = from_left(synthesis_rows(low1, ks2, ks2))
    z0 = periodic(nz, nz)
    z1 = periodic(nz // 2, nz // 2)
    z2 = periodic(nz // 4, nz // 2)
    za0, zs0, zs0_low = from_right(z0), from_right(z0.T), from_right(z0.T[: nz // 2])
    za1, zs1 = wide_right(z1), wide_right(z1.T)
    za2, zs2 = wide_right(z2), wide_right(z2.T)
    zs_spill = from_right(z1.T @ z0.T[: nz // 2])

    x_up, x_down, y_up, y_down = first_messages(velocity)
    x_left, x_right = exchange(x_up, x_down, "gx")
    y_here, y_across = exchange(y_up, y_down, "gy")
    zed = depth(velocity, za0, 16, "depth_analysis")
    approx, a_up, a_down = own_approx(zed, yl0, y1, rows0, ghost)
    a_left, a_right = exchange(a_up, a_down, "gy")
    zed, a_up = lax.optimization_barrier((zed, a_up))
    bands = y_analysis(zed, y_across, y_here, za0, ya0)
    ends = edge_own(bands)
    x_left, x_right, ends = lax.optimization_barrier((x_left, x_right, ends))
    halo, h_up, h_down = x_halo_messages(x_left, x_right, approx, za0, wide, ghost)
    h_left, h_right = exchange(h_up, h_down, "gy")
    approx, halo = lax.optimization_barrier((approx, halo))
    bands1, b_up, b_down = second_bands(approx, a_left, a_right, za1, ya1, rows1)
    b_left, b_right = exchange(b_up, b_down, "gx")
    h_left, h_right, bands1 = lax.optimization_barrier((h_left, h_right, bands1))
    edge, e_up, e_down = edge_details(nx, ends, halo, h_left, h_right, table, index, ya0, zs0, ys0, wide)
    e_left, e_right = exchange(e_up, e_down, "gx")
    bands1, edge = lax.optimization_barrier((bands1, edge))
    approx1, s_up, s_down = coarse(
        bands1, b_left, b_right, halo, h_left, h_right, approx, table, index,
        za1, yx0, ya1, zs1, za2, zs2, ya2, ys2, ys1, len(cells1), rows1, rows0, y1, spill_at, spill_rows, wide,
    )
    s_left, s_right = exchange(s_up, s_down, "gx")
    bands, approx1 = lax.optimization_barrier((bands, approx1))
    parts = detail_yz(edge, inner_bands(bands, table, index), approx1, zs0, ys0)
    own = own_result(parts, approx1, e_left, e_right, zs0_low, ys0_low)
    return final(s_left, s_right, own, zs_spill, ys_spill, zs0_low, ys0_low, rows0, spill_rows)


def solution(mesh):
    return jax.shard_map(
        local,
        mesh=mesh,
        in_specs=(P("gx", "gy", None), P(), P()),
        out_specs=P("gx", "gy", None),
        check_vma=False,
    )
```

```python
import functools

import jax
import jax.numpy as jnp
import ml_dtypes
import numpy as np
from jax import lax
from jax.experimental import pallas as pl
from jax.experimental.pallas import tpu as pltpu
from jax.sharding import PartitionSpec as P

H = [
    0.23037781330885523,
    0.7148465705525415,
    0.6308807679295904,
    -0.02798376941698385,
    -0.18703481171888114,
    0.030841381835986965,
    0.032883011666982945,
    -0.010597401784997278,
]
G = [(-1.0) ** j * H[7 - j] for j in range(8)]
F32 = jnp.float32
BF16 = jnp.bfloat16
NOTHING = 3.0e38
VMEM_BYTES = 16 * 1024 * 1024


def tap(filt, j):
    return filt[j] if 0 <= j < 8 else 0.0


def analysis_rows(cells, low_ks, high_ks):
    matrix = np.zeros((len(low_ks) + len(high_ks), len(cells)))
    rows = [(H, k) for k in low_ks] + [(G, k) for k in high_ks]
    for row, (filt, k) in enumerate(rows):
        for col, cell in enumerate(cells):
            if k is not None and cell is not None:
                matrix[row, col] = tap(filt, cell - 2 * k + 3)
    return matrix


def synthesis_rows(cells, low_ks, high_ks):
    return analysis_rows(cells, low_ks, high_ks).T


def periodic(length, padded_to):
    matrix = np.zeros((padded_to, padded_to))
    for k in range(length // 2):
        for j in range(8):
            matrix[(2 * k + j - 3) % length, k] += H[j]
            matrix[(2 * k + j - 3) % length, length // 2 + k] += G[j]
    return matrix


def fill(items, length):
    return items + [None] * (length - len(items))


def up_to(count, step):
    return -(-count // step) * step


def pieces(matrix, axis):
    rows, cols = matrix.shape
    matrix = np.pad(matrix, ((0, up_to(rows, 16) - rows), (0, up_to(cols, 16) - cols))).astype(np.float32)
    high = matrix.astype(ml_dtypes.bfloat16)
    low = (matrix - high.astype(np.float32)).astype(ml_dtypes.bfloat16)
    return np.concatenate([high, high, low], axis=axis)


def from_left(matrix):
    return pieces(matrix, 1)


def from_right(matrix):
    return pieces(matrix, 0)


def wide_right(matrix):
    rows, cols = matrix.shape
    both = pieces(matrix, 0)
    high, low = both[:rows], both[2 * rows :]
    return np.block([[high, low], [high, np.zeros_like(low)]])


def tall_left(matrix):
    return np.ascontiguousarray(wide_right(np.ascontiguousarray(padded_to_tiles(matrix).T)).T)


def padded_to_tiles(matrix):
    rows, cols = matrix.shape
    return np.pad(matrix, ((0, up_to(rows, 16) - rows), (0, up_to(cols, 16) - cols)))


def halves(values):
    high = values.astype(BF16)
    return high, (values - high.astype(F32)).astype(BF16)


def times(values, matrix):
    high, low = halves(values)
    return jnp.dot(jnp.concatenate([high, low, high], axis=1), matrix[...], preferred_element_type=F32)


def left_times(matrix, values):
    missing = matrix.shape[1] // 3 - values.shape[0]
    if missing:
        values = jnp.concatenate([values, jnp.zeros((missing, values.shape[1]), F32)], axis=0)
    high, low = halves(values)
    return jnp.dot(matrix[...], jnp.concatenate([high, low, high], axis=0), preferred_element_type=F32)


def times_wide(values, matrix):
    both = jnp.dot(jnp.concatenate(halves(values), axis=1), matrix[...], preferred_element_type=F32)
    return both[:, : both.shape[1] // 2] + both[:, both.shape[1] // 2 :]


def left_times_tall(matrix, values):
    missing = matrix.shape[1] // 2 - values.shape[0]
    if missing:
        values = jnp.concatenate([values, jnp.zeros((missing, values.shape[1]), F32)], axis=0)
    both = jnp.dot(matrix[...], jnp.concatenate(halves(values), axis=0), preferred_element_type=F32)
    return both[: both.shape[0] // 2] + both[both.shape[0] // 2 :]


def added(terms):
    total = None
    for coef, value in terms:
        part = value if coef == 1.0 else coef * value
        total = part if total is None else total + part
    return total


def x_terms(k, n):
    terms = []
    for j in range(8):
        cell = 2 * k + j - 3
        if 0 <= cell < n:
            terms.append((cell, H[j], G[j]))
        elif cell == -1:
            terms.append(("l1", H[j], G[j]))
        elif cell == n:
            terms.append(("r1", H[j], G[j]))
    if k == 0:
        terms.append(("l2", 1.0, G[0] / H[0]))
    if k == n // 2 - 1:
        terms.append(("r2", 1.0, G[6] / H[6]))
    return terms


def lattice():
    low = np.array(H).reshape(4, 2)
    high = np.array(G).reshape(4, 2)
    tangents = []
    for _ in range(3):
        t = (low[0] @ high[0]) / (high[0] @ high[0])
        tangents.append(float(t))
        low, high = (low - t * high)[1:] / (1 + t * t), (high + t * low)[:-1] / (1 + t * t)
    return low[0].tolist(), high[0].tolist(), tangents[::-1]


def x_interior(get, n):
    first, second, tangents = lattice()
    a, b = {}, {}
    for i in range(1, n // 2):
        x, y = get(2 * i - 1), get(2 * i)
        a[i] = first[0] * x + first[1] * y
        b[i] = second[0] * x + second[1] * y
    for t in tangents:
        shared = [i for i in a if i + 1 in a]
        a, b = {i: a[i + 1] + t * b[i] for i in shared}, {i: b[i] - t * a[i + 1] for i in shared}
    return {i + 1: (a[i], b[i]) for i in a}


def x_low(get, k, n):
    return added([(low, get(key)) for key, low, _ in x_terms(k, n)])


def x_high(get, k, n):
    return added([(high, get(key)) for key, _, high in x_terms(k, n)])


def x_synth(m, lows, highs):
    terms = [(H[m + 3 - 2 * k], v) for k, v in lows.items() if 0 <= m + 3 - 2 * k < 8]
    terms += [(G[m + 3 - 2 * k], v) for k, v in highs.items() if 0 <= m + 3 - 2 * k < 8]
    return added(terms)


def x_synth_interior(lows, highs, n):
    first, second, tangents = lattice()
    a = {k - 1: lows[k] for k in range(n)}
    b = {k - 1: highs[k] for k in range(n)}
    for t in reversed(tangents):
        a, b = {i + 1: a[i] - t * b[i] for i in a}, {i: b[i] + t * a[i] for i in b}
        both = [i for i in a if i in b]
        a, b = {i: a[i] for i in both}, {i: b[i] for i in both}
    cells = {}
    for i in a:
        cells[2 * i - 1] = first[0] * a[i] + second[0] * b[i]
        cells[2 * i] = first[1] * a[i] + second[1] * b[i]
    return cells


def spill_up(low, high, n):
    first = added([(H[5], low[n - 1]), (G[5], high[n - 1]), (H[7], low[n - 2]), (G[7], high[n - 2])])
    return first, added([(H[6], low[n - 1]), (G[6], high[n - 1])])


def spill_down(low, high):
    first = added([(H[2], low[0]), (G[2], high[0]), (H[0], low[1]), (G[0], high[1])])
    return first, added([(H[1], low[0]), (G[1], high[0])])


THIRD_UP = H[7] / H[6]
THIRD_DOWN = H[0] / H[1]


def shrink(values, thresh):
    return values - jnp.minimum(jnp.maximum(values, -thresh), thresh)


def paired(kernel, args, outs, scratch, received, sent):
    extra = [pltpu.VMEM((2,) + args[i].shape, F32) for i, _ in received]
    extra += [pltpu.VMEM((2,) + outs[j].shape, F32) for j, _ in sent]

    def wrapped(*refs):
        refs, both = list(refs[: len(refs) - len(extra)]), refs[len(refs) - len(extra) :]
        for (i, axis), pair in zip(received, both):
            parity = lax.rem(lax.axis_index(axis), 2)
            pair[0], pair[1] = refs[i][...], refs[i + 1][...]
            refs[i], refs[i + 1] = pair.at[1 - parity], pair.at[parity]
        carried = []
        for (j, axis), pair in zip(sent, both[len(received) :]):
            parity = lax.rem(lax.axis_index(axis), 2)
            j += len(args)
            carried.append((refs[j], refs[j + 1], pair))
            refs[j], refs[j + 1] = pair.at[parity], pair.at[1 - parity]
        kernel(*refs)
        for first, second, pair in carried:
            first[...], second[...] = pair[0], pair[1]

    return wrapped, list(scratch) + extra


def whole_call(kernel, outs, args, scratch=(), received=(), sent=(), name=None, **changes):
    out_list = outs if isinstance(outs, list) else [outs]
    kernel, scratch = paired(kernel, args, out_list, scratch, received, sent)
    specs = [SMEM if a.ndim == 1 or a.dtype == jnp.int32 else VMEM for a in args]
    return pl.pallas_call(
        kernel,
        in_specs=changes.get("in_specs", specs),
        out_specs=changes.get("out_specs", [VMEM] * len(outs) if outs is out_list else VMEM),
        out_shape=outs,
        scratch_shapes=scratch,
        name=name,
        cost_estimate=pl.CostEstimate(flops=1000, bytes_accessed=1000, transcendentals=0),
        compiler_params=pltpu.CompilerParams(vmem_limit_bytes=changes.get("vmem", VMEM_BYTES)),
    )(*args)


def shape(*dims):
    return jax.ShapeDtypeStruct(dims, F32)


SMEM = pl.BlockSpec(memory_space=pltpu.SMEM)
VMEM = pl.BlockSpec(memory_space=pltpu.VMEM)


def first_messages(v):
    nx, ny, nz = v.shape

    kept = nx - nx // 8

    def kernel(v_ref, up, down, y_up, y_down, last, first, rows_up, rows_down, sems):
        copies = [
            pltpu.make_async_copy(source, target, sems.at[i])
            for i, (source, target) in enumerate(
                (
                    (v_ref.at[pl.ds(nx - 3, 3)], last),
                    (v_ref.at[pl.ds(0, 3)], first),
                    (v_ref.at[:, pl.ds(ny - 8, 8)], rows_up),
                    (v_ref.at[:, pl.ds(0, 8)], rows_down),
                )
            )
        ]
        for copy in copies:
            copy.start()
        for copy in copies:
            copy.wait()
        up[0] = last[2]
        up[1] = H[0] * last[0] + H[1] * last[1]
        down[0] = first[0]
        down[1] = H[6] * first[1] + H[7] * first[2]
        y_up[...] = rows_up[:kept]
        y_down[...] = rows_down[:kept]
        for i in range(kept):
            plane, row = kept + i // 7, i % 7
            y_up[i, 0:1] = rows_up[plane, row + 1 : row + 2]
            y_down[i, 7:8] = rows_down[plane, row : row + 1]

    return whole_call(
        kernel,
        [shape(2, ny, nz)] * 2 + [shape(kept, 8, nz)] * 2,
        [v],
        scratch=[pltpu.VMEM((3, ny, nz), F32)] * 2
        + [pltpu.VMEM((nx, 8, nz), F32)] * 2
        + [pltpu.SemaphoreType.DMA((4,))],
        sent=[(0, "gx"), (2, "gy")],
        name="first_messages",
        in_specs=[pl.BlockSpec(memory_space=pltpu.HBM)],
        vmem=50 * 1024 * 1024,
    )


def over_planes(count, group, body):
    def step(i, carry):
        body(i * group)
        return carry

    lax.fori_loop(0, count // group, step, 0)


def depth(v, z_matrix, group, name):
    nx, rows, nz = v.shape

    def kernel(v_ref, z, out):
        def body(first):
            at = pl.ds(first, group)
            out[at] = times(v_ref[at].reshape(group * rows, nz), z).reshape(group, rows, nz)

        over_planes(nx, group, body)

    return whole_call(kernel, shape(nx, rows, nz), [v, z_matrix], name=name)


def y_analysis(zed, y_across, y_here, z_matrix, y_matrix):
    nx, ny, nz = zed.shape
    rows = y_matrix.shape[0]
    kept = y_here.shape[0]
    group = 8

    def kernel(zed_ref, right, left, z, y, out, left_z, right_z):
        for part, out_z in ((left, left_z), (right, right_z)):
            out_z[:kept] = times(part[...].reshape(8 * kept, nz), z).reshape(kept, 8, nz)
            out_z[kept:] = jnp.zeros((nx - kept, 8, nz), F32)
        for i in range(kept):
            plane, row = kept + i // 7, i % 7
            left_z[plane, row + 1 : row + 2] = left_z[i, 0:1]
            right_z[plane, row : row + 1] = right_z[i, 7:8]

        def body(first):
            for j in range(group):
                i = first + j
                out[i] = left_times(y, jnp.concatenate([left_z[i], zed_ref[i], right_z[i]], axis=0))

        over_planes(nx, group, body)

    return whole_call(
        kernel,
        shape(nx, rows, nz),
        [zed, y_across, y_here, z_matrix, y_matrix],
        scratch=[pltpu.VMEM((nx, 8, nz), F32)] * 2,
        received=[(1, "gy")],
        name="y_analysis",
    )


def own_approx(zed, y_matrix, own, rows, ghost_rows):
    nx, ny, nz = zed.shape
    half_z = nz // 2
    n1 = nx // 2

    def kernel(zed_ref, y, approx, up, down, low):
        def y_body(first):
            planes = [zed_ref[first + i, :, :half_z] for i in range(8)]
            for i, plane in enumerate(in_pairs(y, planes)):
                low[first + i] = plane[:rows]

        over_planes(nx, 8, y_body)

        def tile(t, carry):
            at = pl.ds(pl.multiple_of(t * 8, 8), 8)
            values = {i: low[i, at] for i in range(nx)}
            for k in range(n1):
                approx[k, at] = added([(c, values[i]) for i, c, _ in x_terms(k, nx) if i in values])
            approx[n1, at] = added([(H[5 + i], values[i]) for i in range(3)])
            approx[n1 + 1, at] = H[1] * H[7] * values[0]
            approx[n1 + 2, at] = added([(H[i], values[nx - 3 + i]) for i in range(3)])
            approx[n1 + 3, at] = H[6] * H[0] * values[nx - 1]
            return carry

        lax.fori_loop(0, rows // 8, tile, 0)
        inside = ghost_rows - 2
        up[:, :inside] = approx[:n1, own - inside : own]
        up[:, inside:] = approx[:n1, own + 2 : own + 4]
        down[:, :2] = approx[:n1, own : own + 2]
        down[:, 2:] = approx[:n1, :inside]

    return whole_call(
        kernel,
        [shape(n1 + 4, rows, half_z), shape(n1, ghost_rows, half_z), shape(n1, ghost_rows, half_z)],
        [zed, y_matrix],
        scratch=[pltpu.VMEM((nx, rows, half_z), F32)],
        sent=[(1, "gy")],
        name="own_approx",
    )


def x_halo_messages(x_left, x_right, approx, z_matrix, wide, ghost_rows):
    _, ny, nz = x_left.shape
    half_z = nz // 2
    n1 = approx.shape[0] - 4
    own, inside = ny // 2, ghost_rows - 2
    message = wide + 8 + ghost_rows

    def kernel(xl, xr, a_ref, z, out, up, down):
        planes = jnp.concatenate([xl[0], xl[1], xr[0], xr[1]], axis=0)
        out[...] = times(planes, z).reshape(4, ny, nz)
        up[:, :wide] = out[:, ny - wide :, :half_z]
        up[:, wide : wide + 8] = out[:, ny - 8 :, half_z:]
        down[:, :wide] = out[:, :wide, :half_z]
        down[:, wide : wide + 8] = out[:, :8, half_z:]
        up[:, wide + 8 : wide + 8 + inside] = a_ref[n1:, own - inside : own]
        up[:, wide + 8 + inside :] = a_ref[n1:, own + 2 : own + 4]
        down[:, wide + 8 : wide + 10] = a_ref[n1:, own : own + 2]
        down[:, wide + 10 :] = a_ref[n1:, :inside]

    return whole_call(
        kernel,
        [shape(4, ny, nz), shape(4, message, half_z), shape(4, message, half_z)],
        [x_left, x_right, approx, z_matrix],
        received=[(0, "gx")],
        sent=[(1, "gy")],
        name="x_halo_messages",
    )


def edges_of(n):
    return [0, 1, n - 2, n - 1]


def band_limits(table_ref, index_ref, by, bz):
    band = 2 * by + bz
    quiet = table_ref[index_ref[0, band - 1]] if band else NOTHING
    return quiet, table_ref[index_ref[0, band + 3]]


def over_tiles(rows, nz, body, unroll=3):
    half_z, half_tiles = nz // 2, rows // 16
    for by in range(2):

        def tile(t, carry, by=by):
            at = pl.ds(pl.multiple_of((t + by * half_tiles) * 8, 8), 8)
            for bz in range(2):
                body(at, pl.ds(bz * half_z, half_z), by, bz)
            return carry

        lax.fori_loop(0, half_tiles, tile, 0, unroll=unroll if half_tiles % unroll == 0 else 1)


def inner_bands(bands, table, index):
    nx, rows, nz = bands.shape
    count = nx // 2 - 4

    def kernel(table_ref, index_ref, b_ref, out):
        def body(at, lanes, by, bz):
            quiet, loud = band_limits(table_ref, index_ref, by, bz)
            values = {i: b_ref[i, at, lanes] for i in range(nx)}
            for k, (low, high) in x_interior(values.get, nx).items():
                out[k - 2, at, lanes] = shrink(low, quiet) if by + bz else jnp.zeros_like(low)
                out[count + k - 2, at, lanes] = shrink(high, loud)

        over_tiles(rows, nz, body)

    return whole_call(
        kernel,
        shape(2 * count, rows, nz),
        [table, index, bands],
        name="inner_bands",
    )


def yz_synthesis(planes, z, y, out, zed):
    count, rows, nz = zed.shape
    group = max(g for g in range(1, 17) if count % g == 0)
    for first in range(0, count, group):
        zed[first : first + group] = times(planes(first, group), z).reshape(group, rows, nz)

    def y_body(first):
        for j in range(4):
            out[first + j] = left_times(y, zed[first + j])

    over_planes(count, 4, y_body)


def edge_own(bands):
    nx, rows, nz = bands.shape

    def kernel(b_ref, out):
        def body(at, lanes, by, bz):
            values = {i: b_ref[i, at, lanes] for i in [*range(7), *range(nx - 7, nx)]}
            for i, k in enumerate(edges_of(nx // 2)):
                terms = [t for t in x_terms(k, nx) if t[0] in values]
                out[i, at, lanes] = added([(low, values[key]) for key, low, _ in terms])
                out[4 + i, at, lanes] = added([(high, values[key]) for key, _, high in terms])

        over_tiles(rows, nz, body)

    return whole_call(kernel, shape(8, rows, nz), [bands], name="edge_own")


def edge_details(nx, own, halo, h_left, h_right, table, index, ya_matrix, z_matrix, y_matrix, wide):
    _, rows, nz = own.shape
    ny = y_matrix.shape[0]
    n1 = nx // 2
    half_z = nz // 2
    ends = edges_of(n1)

    def kernel(table_ref, index_ref, b_ref, x_ref, hl, hr, ya, z, y, coeffs, up, down, h_ref, beyond, zed):
        for i in range(4):
            low = jnp.concatenate([hl[i, wide - 8 : wide], x_ref[i, :, :half_z], hr[i, :8]], axis=0)
            high = jnp.concatenate(
                [hl[i, wide : wide + 8], x_ref[i, :, half_z:], hr[i, wide : wide + 8]], axis=0
            )
            h_ref[i] = left_times(ya, jnp.concatenate([low, high], axis=1))
        place = {"l1": 0, "l2": 1, "r1": 2, "r2": 3}

        def body(at, lanes, by, bz):
            quiet, loud = band_limits(table_ref, index_ref, by, bz)
            values = {key: h_ref[i, at, lanes] for key, i in place.items()}
            lows, highs = {}, {}
            for i, k in enumerate(ends):
                terms = [t for t in x_terms(k, nx) if t[0] in values]
                low = b_ref[i, at, lanes] + added([(c, values[key]) for key, c, _ in terms])
                high = b_ref[4 + i, at, lanes] + added([(c, values[key]) for key, _, c in terms])
                lows[k] = shrink(low, quiet) if by + bz else jnp.zeros_like(low)
                highs[k] = shrink(high, loud)
                coeffs[i, at, lanes] = lows[k]
                coeffs[4 + i, at, lanes] = highs[k]
            spilled = spill_up(lows, highs, n1) + spill_down(lows, highs)
            for i, part in enumerate(spilled):
                beyond[i, at, lanes] = part

        over_tiles(rows, nz, body, 9)
        zed[...] = times(beyond[...].reshape(4 * rows, nz), z).reshape(4, rows, nz)
        for i, target in enumerate((up.at[0], up.at[1], down.at[0], down.at[1])):
            target[...] = left_times(y, zed[i])

    return whole_call(
        kernel,
        [shape(8, rows, nz), shape(2, ny, nz), shape(2, ny, nz)],
        [table, index, own, halo, h_left, h_right, ya_matrix, z_matrix, y_matrix],
        scratch=[pltpu.VMEM((4, rows, nz), F32)] * 3,
        received=[(4, "gy")],
        sent=[(1, "gx")],
        name="edge_details",
    )


def detail_yz(edge, inner, approx, z_matrix, y_matrix):
    count, rows, nz = inner.shape
    ny = y_matrix.shape[0]
    _, low_rows, half_z = approx.shape
    n1 = count // 2 + 4
    ends = edges_of(n1)

    def kernel(e_ref, i_ref, a_ref, z, y, out, zed):
        def coeff(k, high):
            if k in ends:
                return e_ref.at[4 * high + ends.index(k)]
            return i_ref.at[(n1 - 4) * high + k - 2]

        def plane(i):
            ref = coeff(i % n1, i // n1)
            if i >= n1:
                return ref[...]
            corner = ref[:low_rows, :half_z] + a_ref[i + 2]
            top = jnp.concatenate([corner, ref[:low_rows, half_z:]], axis=1)
            return jnp.concatenate([top, ref[low_rows:]], axis=0)

        def planes(first, n):
            return jnp.concatenate([plane(i) for i in range(first, first + n)], axis=0)

        yz_synthesis(planes, z, y, out, zed)

    return whole_call(
        kernel,
        shape(2 * n1, ny, nz),
        [edge, inner, approx, z_matrix, y_matrix],
        scratch=[pltpu.VMEM((2 * n1, rows, nz), F32)],
        name="detail_yz",
    )


def own_result(parts, approx, left, right, z_matrix, y_matrix):
    nx, ny, nz = parts.shape
    n1 = nx // 2
    planes, rows, half_z = approx.shape

    def kernel(p_ref, a_ref, el, er, z, y, out, ghosts):
        stack = jnp.concatenate([a_ref[i] for i in (0, 1, n1 + 2, n1 + 3)], axis=0)
        for i, plane in enumerate(cut(times(stack, z), rows)):
            ghosts[i] = left_times(y, plane)

        def tile(t, carry):
            at = pl.ds(pl.multiple_of(t * 8, 8), 8)
            for lane in range(0, nz, 128):
                lanes = pl.ds(lane, 128)
                lows = {k: p_ref[k, at, lanes] for k in range(n1)}
                highs = {k: p_ref[n1 + k, at, lanes] for k in range(n1)}
                for i, k in enumerate((-2, -1, n1, n1 + 1)):
                    lows[k] = ghosts[i, at, lanes]
                cells = x_synth_interior(lows, highs, n1)
                for m in range(nx):
                    value = cells[m] if m in cells else x_synth(m, lows, highs)
                    if m < 3:
                        extra = el[(0, 1, 1)[m], at, lanes]
                        value += extra if m < 2 else THIRD_UP * extra
                    if m >= nx - 3:
                        extra = er[(0, 1, 1)[nx - 1 - m], at, lanes]
                        value += extra if m > nx - 3 else THIRD_DOWN * extra
                    out[m, at, lanes] = value
            return carry

        lax.fori_loop(0, ny // 8, tile, 0)

    return whole_call(
        kernel,
        shape(nx, ny, nz),
        [parts, approx, left, right, z_matrix, y_matrix],
        scratch=[pltpu.VMEM((4, ny, nz), F32)],
        received=[(2, "gx")],
        name="own_result",
    )


def in_pairs(matrix, planes):
    results = []
    for i in range(0, len(planes), 2):
        both = left_times(matrix, jnp.concatenate(planes[i : i + 2], axis=1))
        width = both.shape[1] // 2
        results += [both[:, :width], both[:, width:]]
    return results


def cut(values, rows):
    return [values[i : i + rows] for i in range(0, values.shape[0], rows)]


def packed(first, second):
    half = first.shape[1] // 2
    lane = lax.broadcasted_iota(jnp.int32, first.shape, 1)
    return jnp.where(lane < half, first, pltpu.roll(second, half, 1))


def unpacked(both):
    half = both.shape[1] // 2
    lane = lax.broadcasted_iota(jnp.int32, both.shape, 1)
    return [jnp.where(lane < half, part, 0.0) for part in (both, pltpu.roll(both, half, 1))]


def second_bands(own, left, right, z_matrix, y_matrix, low_rows):
    _, own_rows, nz = own.shape
    n1 = left.shape[0]
    in_rows = own_rows + 2 * left.shape[1]
    rows = y_matrix.shape[0]


    def kernel(o_ref, l_ref, r_ref, z, y, out, up, down):
        for i in range(0, n1, 8):
            stack = [part[j] for j in range(i, i + 8) for part in (o_ref, l_ref, r_ref)]
            zed = times_wide(jnp.concatenate(stack, axis=0), z)
            for j, plane in enumerate(in_pairs(y, cut(zed, in_rows))):
                out[i + j] = plane
        low = lambda c: out[c, :low_rows]
        up[0:rows] = out[n1 - 1]
        up[rows : 2 * rows] = H[0] * out[n1 - 3] + H[1] * out[n1 - 2]
        first = added([(H[j], low(n1 - 5 + j)) for j in range(5)])
        second = added([(H[0] * H[j], low(n1 - 9 + j)) for j in range(8)])
        second += added([(H[1] * H[j], low(n1 - 7 + j)) for j in range(7)])
        up[2 * rows :] = packed(first, second)
        down[0:rows] = out[0]
        down[rows : 2 * rows] = H[6] * out[1] + H[7] * out[2]
        first = added([(H[j], low(j - 3)) for j in range(3, 8)])
        second = added([(H[6] * H[j], low(j - 1)) for j in range(1, 8)])
        second += added([(H[7] * H[j], low(j + 1)) for j in range(8)])
        down[2 * rows :] = packed(first, second)

    message = 2 * rows + low_rows
    return whole_call(
        kernel,
        [shape(n1, rows, nz), shape(message, nz), shape(message, nz)],
        [own, left, right, z_matrix, y_matrix],
        received=[(1, "gy")],
        sent=[(1, "gx")],
        name="second_bands",
    )


def limits_plane(table_ref, index_ref, level, bx, dims, row_split, lane_split, zeroth):
    row_high = lax.broadcasted_iota(jnp.int32, dims, 0) >= row_split
    lane_high = lax.broadcasted_iota(jnp.int32, dims, 1) >= lane_split

    def limit(by, bz):
        band = 4 * bx + 2 * by + bz
        return zeroth if band == 0 else table_ref[index_ref[level, band - 1]]

    low_y = jnp.where(lane_high, limit(0, 1), limit(0, 0))
    return jnp.where(row_high, jnp.where(lane_high, limit(1, 1), limit(1, 0)), low_y)


def coarse(
    bands, left, right, halo, h_left, h_right, approx_in, table, index, za1, yx0, ya1, zs1, za2, zs2, ya2, ys2, ys1,
    in_rows1, low_rows, out_rows, own_rows, spill_at, spill_rows, wide,
):
    n1, rows, nz = bands.shape
    in_rows = in_rows1
    n2, n3 = n1 // 2, n1 // 4
    rows2 = ya2.shape[0]
    lane_half = nz // 2

    def kernel(
        table_ref, index_ref, b_ref, l_ref, r_ref, x_ref, hl, hr, a_ref, z1a, yx, a1, z1, z2a, z2s, a2, s2, s1,
        approx, up, down, c1, p1,
    ):
        halo_planes = [jnp.concatenate([hl[i, :wide], x_ref[i, :, :nz], hr[i, :wide]], axis=0) for i in range(4)]
        halo_planes = [plane[:in_rows] for plane in in_pairs(yx, halo_planes)]
        own_planes = [
            jnp.concatenate([a_ref[n1 + i], hl[i, wide + 8 :], hr[i, wide + 8 :]], axis=0) for i in range(4)
        ]
        both = times_wide(jnp.concatenate(halo_planes + own_planes, axis=0), z1a)
        hl1, hl2, hr1, hr2, xl1, xl2, xr1, xr2 = in_pairs(a1, cut(both, in_rows))
        values = {k: b_ref[k] for k in range(2, n1 - 2)}
        values[0] = b_ref[0] + (hl2 + H[2] * hl1)
        values[1] = b_ref[1] + H[0] * hl1
        values[n1 - 2] = b_ref[n1 - 2] + H[7] * hr1
        values[n1 - 1] = b_ref[n1 - 1] + (hr2 + H[5] * hr1)
        values["l1"] = l_ref[0:rows] + xl1
        values["l2"] = l_ref[rows : 2 * rows] + xl2
        values["r1"] = r_ref[0:rows] + xr1
        values["r2"] = r_ref[rows : 2 * rows] + xr2
        get = values.get
        low_part = lambda c: values[c][:low_rows]
        xl1, xl2, xr1, xr2 = [part[:low_rows] for part in (xl1, xl2, xr1, xr2)]
        dims = (rows, nz)
        quiet = limits_plane(table_ref, index_ref, 1, 0, dims, low_rows, lane_half, NOTHING)
        loud = limits_plane(table_ref, index_ref, 1, 1, dims, low_rows, lane_half, NOTHING)
        planes = []
        for k in range(n2):
            low = x_low(get, k, n1)
            planes.append(low[:low_rows])
            c1[k] = shrink(low, quiet)
            c1[n2 + k] = shrink(x_high(get, k, n1), loud)
        first, second = unpacked(l_ref[2 * rows :])
        own = [(H[5 + i], low_part(i)) for i in range(3)]
        planes.append(first + added([(H[3] / H[1], xl2), (H[4], xl1)] + own))
        own = [((H[0] * H[7] + H[1] * H[5]) / H[1], xl2), (H[1] * H[6], xl1), (H[1] * H[7], low_part(0))]
        planes.append(second + added(own))
        first, second = unpacked(r_ref[2 * rows :])
        own = [(H[i], low_part(n1 - 3 + i)) for i in range(3)]
        planes.append(first + added([(H[3], xr1), (H[4] / H[6], xr2)] + own))
        own = [((H[6] * H[2] + H[7] * H[0]) / H[6], xr2), (H[6] * H[1], xr1), (H[6] * H[0], low_part(n1 - 1))]
        planes.append(second + added(own))
        third = in_pairs(a2, cut(times_wide(jnp.concatenate(planes, axis=0), z2a), low_rows))
        keys = {"l1": n2, "l2": n2 + 1, "r1": n2 + 2, "r2": n2 + 3}
        get2 = lambda key: third[keys.get(key, key)]
        dims = (rows2, nz)
        quiet = limits_plane(table_ref, index_ref, 2, 0, dims, rows2 // 2, lane_half // 2, 0.0)
        loud = limits_plane(table_ref, index_ref, 2, 1, dims, rows2 // 2, lane_half // 2, 0.0)
        kept = [shrink(x_low(get2, k, n2), quiet) for k in range(n3)]
        kept += [shrink(x_high(get2, k, n2), loud) for k in range(n3)]
        parts = in_pairs(s2, cut(times_wide(jnp.concatenate(kept, axis=0), z2s), rows2))
        parts = [part[:low_rows] for part in parts]
        lows = dict(enumerate(parts[:n3]))
        highs = dict(enumerate(parts[n3:]))
        ghosts = [-3, -2, -1, n2, n2 + 1, n2 + 2]
        for k in range(n2):
            c1[k, :low_rows] += x_synth(k, lows, highs)
        stack = [x_synth(k, lows, highs) for k in ghosts]
        beyond = dict(zip(ghosts, stack))
        zed = times_wide(jnp.concatenate(stack, axis=0), z1)
        for i, plane in enumerate(in_pairs(s1, cut(zed, low_rows))):
            p1[2 * n2 + i] = plane[:out_rows]
        for i in range(0, 2 * n2, 8):
            zed = times_wide(c1[i : i + 8].reshape(8 * rows, nz), z1)
            for j, plane in enumerate(in_pairs(s1, cut(zed, rows))):
                p1[i + j] = plane[:out_rows]
        lows = {k: p1.at[k] for k in range(n2)}
        highs = {k: p1.at[n2 + k] for k in range(n2)}
        for i, k in enumerate(ghosts):
            lows[k] = p1.at[2 * n2 + i]

        def cell(m):
            near = lambda part: {k: ref[...] for k, ref in part.items() if 0 <= m + 3 - 2 * k < 8}
            return x_synth(m, near(lows), near(highs))

        for m in range(-2, n1 + 2):
            approx[m + 2] = cell(m)
        value = lambda part, ks: {k: part[k][...] for k in ks}
        ends = (n2 - 2, n2 - 1)

        def send(message, four, two):
            for i, plane in enumerate(four):
                message[i * own_rows : (i + 1) * own_rows] = plane[:own_rows]
                message[4 * own_rows + 4 * i : 4 * own_rows + 4 * i + 4] = plane[own_rows : own_rows + 4]
            message[4 * own_rows + 16 :] = packed(*two)[spill_at : spill_at + spill_rows]

        up_two = spill_up(value(lows, ends), value(highs, ends), n2)
        send(up, (approx[n1], approx[n1 + 1], *up_two), (beyond[n2], beyond[n2 + 1]))
        down_two = spill_down(value(lows, (0, 1)), value(highs, (0, 1)))
        send(down, (approx[2], approx[3], *down_two), (beyond[-1], beyond[-2]))

    message = 4 * own_rows + 16 + spill_rows
    return whole_call(
        kernel,
        [shape(n1 + 4, out_rows, nz), shape(message, nz), shape(message, nz)],
        [table, index, bands, left, right, halo, h_left, h_right, approx_in, za1, yx0, ya1, zs1, za2, zs2, ya2, ys2, ys1],
        scratch=[pltpu.VMEM((2 * n2, rows, nz), F32), pltpu.VMEM((2 * n2 + 6, out_rows, nz), F32)],
        received=[(3, "gx"), (6, "gy")],
        sent=[(1, "gx")],
        name="coarse",
    )


def received_taps(n1):
    n2, nx = n1 // 2, 2 * n1
    from_approx = np.zeros((nx, n1 + 4))
    for m in range(nx):
        for k in range(-2, n1 + 2):
            from_approx[m, k + 2] = tap(H, m + 3 - 2 * k)
    approx = np.zeros((n1 + 4, 12))
    third = {0: THIRD_UP, 6: THIRD_DOWN}
    for first, cell, second in ((0, lambda i: i, lambda i: i), (6, lambda i: n1 - 1 - i, lambda i: n2 - 1 - i)):
        ghost = (-2, -1) if first == 0 else (n1, n1 + 1)
        for i in range(2):
            approx[ghost[i] + 2, first + i] = 1.0
        for place, source, coef in ((0, 0, 1.0), (1, 1, 1.0), (2, 1, third[first])):
            approx[cell(place) + 2, first + 2 + source] += coef
            for m in range(n1):
                approx[m + 2, first + 4 + source] += coef * tap(H, m + 3 - 2 * second(place))
    return from_approx @ approx


def final(left, right, own, zs1, ys1, z_matrix, y_matrix, rows, spill_rows):
    nx, ny, nz = own.shape
    half_z = nz // 2
    own_rows = ny // 2
    step_rows = 16
    steps = ny // step_rows
    taps = received_taps(nx // 2)

    def kernel(l_ref, r_ref, d_ref, z1, s1, z, y, out, planes, parts, done, sems):
        stack = [p for ref in (l_ref, r_ref) for p in unpacked(ref[4 * own_rows + 16 :])]
        spilled = cut(times(jnp.concatenate(stack, axis=0), z1), spill_rows)
        for side, ref in enumerate((l_ref, r_ref)):
            for i in range(4):
                plane = planes.at[4 * side + i]
                plane[:own_rows] = ref[i * own_rows : (i + 1) * own_rows]
                plane[own_rows:] = jnp.zeros((rows - own_rows, half_z), F32)
                plane[own_rows : own_rows + 4] = ref[4 * own_rows + 4 * i : 4 * own_rows + 4 * i + 4]
        for i, plane in enumerate(cut(times(planes[...].reshape(8 * rows, half_z), z), rows)):
            parts[6 * (i // 4) + i % 4] = left_times(y, plane)
        for i, plane in enumerate(spilled):
            parts[6 * (i // 2) + 4 + i % 2] = left_times(s1, plane)

        def copy(i):
            at = pl.ds(pl.multiple_of(i * step_rows, step_rows), step_rows)
            return pltpu.make_async_copy(done.at[:, at], out.at[:, at], sems.at[i])

        def step(i, carry):
            for t in range(step_rows // 8):
                at = pl.ds(pl.multiple_of(i * step_rows + 8 * t, 8), 8)
                for lane in range(0, nz, 128):
                    lanes = pl.ds(lane, 128)
                    values = [parts[i, at, lanes] for i in range(12)]
                    for m in range(nx):
                        value = d_ref[m, at, lanes]
                        value += added([(float(c), v) for c, v in zip(taps[m], values) if c != 0.0])
                        done[m, at, lanes] = value
            copy(i).start()
            return carry

        lax.fori_loop(0, steps, step, 0)

        def finish(i, carry):
            copy(i).wait()
            return carry

        lax.fori_loop(0, steps, finish, 0)

    return whole_call(
        kernel,
        shape(nx, ny, nz),
        [left, right, own, zs1, ys1, z_matrix, y_matrix],
        scratch=[
            pltpu.VMEM((8, rows, half_z), F32),
            pltpu.VMEM((12, ny, nz), F32),
            pltpu.VMEM((nx, ny, nz), F32),
            pltpu.SemaphoreType.DMA((steps,)),
        ],
        received=[(0, "gx")],
        name="final",
        out_specs=pl.BlockSpec(memory_space=pl.ANY),
    )


def exchange(first, second, axis):
    size = lax.axis_size(axis)
    assert size % 2 == 0
    here = [(i, i ^ 1) for i in range(size)]
    across = [(i, (i + 1) % size if i % 2 else (i - 1) % size) for i in range(size)]
    return lax.ppermute(first, axis, here), lax.ppermute(second, axis, across)


def local(velocity, table, index):
    nx, ny, nz = velocity.shape
    y1, y2, y3 = ny // 2, ny // 4, ny // 8
    ghost, wide = 24, 48
    cells0 = list(range(-8, ny + 8))
    rows0 = up_to(y1 + 4, 8)
    ks0 = fill(list(range(y1)) + [-2, -1, y1, y1 + 1], rows0)
    cells1 = ks0 + list(range(2 - ghost, 2)) + list(range(y1 - 2, y1 + ghost - 2))
    once = [c if cells1.index(c) == i else None for i, c in enumerate(cells1)]
    rows1 = up_to(y2 + 18, 8)
    low1 = fill(list(range(-9, y2 + 9)), rows1)
    high1 = fill(list(range(-3, y2 + 3)), up_to(y2 + 6, 8))
    spill_at, spill_rows = 6, up_to(y2 + 6, 8)
    ks2 = fill(list(range(-3, y3 + 3)), up_to(y3 + 6, 8))
    ya0 = from_left(analysis_rows(cells0, ks0, ks0))
    ys0_matrix = synthesis_rows(list(range(ny)), ks0, ks0)
    ys0 = from_left(ys0_matrix)
    ys0_low = from_left(ys0_matrix[:, :rows0])
    yl0 = from_left(analysis_rows(list(range(ny)), ks0, []))
    yx0 = from_left(analysis_rows(list(range(-wide, ny + wide)), once, []))
    ya1 = from_left(analysis_rows(cells1, low1, high1))
    ys1 = from_left(synthesis_rows(ks0, low1, high1))
    spill_matrix = synthesis_rows(ks0, low1[spill_at : spill_at + spill_rows], [])
    ys_spill = from_left(ys0_matrix[:, :rows0] @ spill_matrix)
    ya2 = from_left(analysis_rows(low1, ks2, ks2))
    ys2 = from_left(synthesis_rows(low1, ks2, ks2))
    z0 = periodic(nz, nz)
    z1 = periodic(nz // 2, nz // 2)
    z2 = periodic(nz // 4, nz // 2)
    za0, zs0, zs0_low = from_right(z0), from_right(z0.T), from_right(z0.T[: nz // 2])
    za1, zs1 = wide_right(z1), wide_right(z1.T)
    za2, zs2 = wide_right(z2), wide_right(z2.T)
    zs_spill = from_right(z1.T @ z0.T[: nz // 2])

    x_up, x_down, y_up, y_down = first_messages(velocity)
    x_left, x_right = exchange(x_up, x_down, "gx")
    y_here, y_across = exchange(y_up, y_down, "gy")
    zed = depth(velocity, za0, 16, "depth_analysis")
    approx, a_up, a_down = own_approx(zed, yl0, y1, rows0, ghost)
    a_left, a_right = exchange(a_up, a_down, "gy")
    zed, a_up = lax.optimization_barrier((zed, a_up))
    bands = y_analysis(zed, y_across, y_here, za0, ya0)
    ends = edge_own(bands)
    x_left, x_right, ends = lax.optimization_barrier((x_left, x_right, ends))
    halo, h_up, h_down = x_halo_messages(x_left, x_right, approx, za0, wide, ghost)
    h_left, h_right = exchange(h_up, h_down, "gy")
    approx, halo = lax.optimization_barrier((approx, halo))
    bands1, b_up, b_down = second_bands(approx, a_left, a_right, za1, ya1, rows1)
    b_left, b_right = exchange(b_up, b_down, "gx")
    h_left, h_right, bands1 = lax.optimization_barrier((h_left, h_right, bands1))
    edge, e_up, e_down = edge_details(nx, ends, halo, h_left, h_right, table, index, ya0, zs0, ys0, wide)
    e_left, e_right = exchange(e_up, e_down, "gx")
    bands1, edge = lax.optimization_barrier((bands1, edge))
    approx1, s_up, s_down = coarse(
        bands1, b_left, b_right, halo, h_left, h_right, approx, table, index,
        za1, yx0, ya1, zs1, za2, zs2, ya2, ys2, ys1, len(cells1), rows1, rows0, y1, spill_at, spill_rows, wide,
    )
    s_left, s_right = exchange(s_up, s_down, "gx")
    bands, approx1 = lax.optimization_barrier((bands, approx1))
    parts = detail_yz(edge, inner_bands(bands, table, index), approx1, zs0, ys0)
    own = own_result(parts, approx1, e_left, e_right, zs0_low, ys0_low)
    return final(s_left, s_right, own, zs_spill, ys_spill, zs0_low, ys0_low, rows0, spill_rows)


def solution(mesh):
    return jax.shard_map(
        local,
        mesh=mesh,
        in_specs=(P("gx", "gy", None), P(), P()),
        out_specs=P("gx", "gy", None),
        check_vma=False,
    )
```

```python
import functools

import jax
import jax.numpy as jnp
import ml_dtypes
import numpy as np
from jax import lax
from jax.experimental import pallas as pl
from jax.experimental.pallas import tpu as pltpu
from jax.sharding import PartitionSpec as P

H = [
    0.23037781330885523,
    0.7148465705525415,
    0.6308807679295904,
    -0.02798376941698385,
    -0.18703481171888114,
    0.030841381835986965,
    0.032883011666982945,
    -0.010597401784997278,
]
G = [(-1.0) ** j * H[7 - j] for j in range(8)]
F32 = jnp.float32
BF16 = jnp.bfloat16
NOTHING = 3.0e38
VMEM_BYTES = 16 * 1024 * 1024


def tap(filt, j):
    return filt[j] if 0 <= j < 8 else 0.0


def analysis_rows(cells, low_ks, high_ks):
    matrix = np.zeros((len(low_ks) + len(high_ks), len(cells)))
    rows = [(H, k) for k in low_ks] + [(G, k) for k in high_ks]
    for row, (filt, k) in enumerate(rows):
        for col, cell in enumerate(cells):
            if k is not None and cell is not None:
                matrix[row, col] = tap(filt, cell - 2 * k + 3)
    return matrix


def synthesis_rows(cells, low_ks, high_ks):
    return analysis_rows(cells, low_ks, high_ks).T


def periodic(length, padded_to):
    matrix = np.zeros((padded_to, padded_to))
    for k in range(length // 2):
        for j in range(8):
            matrix[(2 * k + j - 3) % length, k] += H[j]
            matrix[(2 * k + j - 3) % length, length // 2 + k] += G[j]
    return matrix


def fill(items, length):
    return items + [None] * (length - len(items))


def up_to(count, step):
    return -(-count // step) * step


def pieces(matrix, axis):
    rows, cols = matrix.shape
    matrix = np.pad(matrix, ((0, up_to(rows, 16) - rows), (0, up_to(cols, 16) - cols))).astype(np.float32)
    high = matrix.astype(ml_dtypes.bfloat16)
    low = (matrix - high.astype(np.float32)).astype(ml_dtypes.bfloat16)
    return np.concatenate([high, high, low], axis=axis)


def from_left(matrix):
    return pieces(matrix, 1)


def from_right(matrix):
    return pieces(matrix, 0)


def wide_right(matrix):
    rows, cols = matrix.shape
    both = pieces(matrix, 0)
    high, low = both[:rows], both[2 * rows :]
    return np.block([[high, low], [high, np.zeros_like(low)]])


def tall_left(matrix):
    return np.ascontiguousarray(wide_right(np.ascontiguousarray(padded_to_tiles(matrix).T)).T)


def padded_to_tiles(matrix):
    rows, cols = matrix.shape
    return np.pad(matrix, ((0, up_to(rows, 16) - rows), (0, up_to(cols, 16) - cols)))


def halves(values):
    high = values.astype(BF16)
    return high, (values - high.astype(F32)).astype(BF16)


def times(values, matrix):
    high, low = halves(values)
    return jnp.dot(jnp.concatenate([high, low, high], axis=1), matrix[...], preferred_element_type=F32)


def left_times(matrix, values):
    missing = matrix.shape[1] // 3 - values.shape[0]
    if missing:
        values = jnp.concatenate([values, jnp.zeros((missing, values.shape[1]), F32)], axis=0)
    high, low = halves(values)
    return jnp.dot(matrix[...], jnp.concatenate([high, low, high], axis=0), preferred_element_type=F32)


def times_wide(values, matrix):
    both = jnp.dot(jnp.concatenate(halves(values), axis=1), matrix[...], preferred_element_type=F32)
    return both[:, : both.shape[1] // 2] + both[:, both.shape[1] // 2 :]


def left_times_tall(matrix, values):
    missing = matrix.shape[1] // 2 - values.shape[0]
    if missing:
        values = jnp.concatenate([values, jnp.zeros((missing, values.shape[1]), F32)], axis=0)
    both = jnp.dot(matrix[...], jnp.concatenate(halves(values), axis=0), preferred_element_type=F32)
    return both[: both.shape[0] // 2] + both[both.shape[0] // 2 :]


def added(terms):
    total = None
    for coef, value in terms:
        part = value if coef == 1.0 else coef * value
        total = part if total is None else total + part
    return total


def x_terms(k, n):
    terms = []
    for j in range(8):
        cell = 2 * k + j - 3
        if 0 <= cell < n:
            terms.append((cell, H[j], G[j]))
        elif cell == -1:
            terms.append(("l1", H[j], G[j]))
        elif cell == n:
            terms.append(("r1", H[j], G[j]))
    if k == 0:
        terms.append(("l2", 1.0, G[0] / H[0]))
    if k == n // 2 - 1:
        terms.append(("r2", 1.0, G[6] / H[6]))
    return terms


def lattice():
    low = np.array(H).reshape(4, 2)
    high = np.array(G).reshape(4, 2)
    tangents = []
    for _ in range(3):
        t = (low[0] @ high[0]) / (high[0] @ high[0])
        tangents.append(float(t))
        low, high = (low - t * high)[1:] / (1 + t * t), (high + t * low)[:-1] / (1 + t * t)
    return low[0].tolist(), high[0].tolist(), tangents[::-1]


def x_interior(get, n):
    first, second, tangents = lattice()
    a, b = {}, {}
    for i in range(1, n // 2):
        x, y = get(2 * i - 1), get(2 * i)
        a[i] = first[0] * x + first[1] * y
        b[i] = second[0] * x + second[1] * y
    for t in tangents:
        shared = [i for i in a if i + 1 in a]
        a, b = {i: a[i + 1] + t * b[i] for i in shared}, {i: b[i] - t * a[i + 1] for i in shared}
    return {i + 1: (a[i], b[i]) for i in a}


def x_low(get, k, n):
    return added([(low, get(key)) for key, low, _ in x_terms(k, n)])


def x_high(get, k, n):
    return added([(high, get(key)) for key, _, high in x_terms(k, n)])


def x_synth(m, lows, highs):
    terms = [(H[m + 3 - 2 * k], v) for k, v in lows.items() if 0 <= m + 3 - 2 * k < 8]
    terms += [(G[m + 3 - 2 * k], v) for k, v in highs.items() if 0 <= m + 3 - 2 * k < 8]
    return added(terms)


def x_synth_interior(lows, highs, n):
    first, second, tangents = lattice()
    a = {k - 1: lows[k] for k in range(n)}
    b = {k - 1: highs[k] for k in range(n)}
    for t in reversed(tangents):
        a, b = {i + 1: a[i] - t * b[i] for i in a}, {i: b[i] + t * a[i] for i in b}
        both = [i for i in a if i in b]
        a, b = {i: a[i] for i in both}, {i: b[i] for i in both}
    cells = {}
    for i in a:
        cells[2 * i - 1] = first[0] * a[i] + second[0] * b[i]
        cells[2 * i] = first[1] * a[i] + second[1] * b[i]
    return cells


def spill_up(low, high, n):
    first = added([(H[5], low[n - 1]), (G[5], high[n - 1]), (H[7], low[n - 2]), (G[7], high[n - 2])])
    return first, added([(H[6], low[n - 1]), (G[6], high[n - 1])])


def spill_down(low, high):
    first = added([(H[2], low[0]), (G[2], high[0]), (H[0], low[1]), (G[0], high[1])])
    return first, added([(H[1], low[0]), (G[1], high[0])])


THIRD_UP = H[7] / H[6]
THIRD_DOWN = H[0] / H[1]


def shrink(values, thresh):
    return values - jnp.minimum(jnp.maximum(values, -thresh), thresh)


def paired(kernel, args, outs, scratch, received, sent):
    extra = [pltpu.VMEM((2,) + args[i].shape, F32) for i, _ in received]
    extra += [pltpu.VMEM((2,) + outs[j].shape, F32) for j, _ in sent]

    def wrapped(*refs):
        refs, both = list(refs[: len(refs) - len(extra)]), refs[len(refs) - len(extra) :]
        for (i, axis), pair in zip(received, both):
            parity = lax.rem(lax.axis_index(axis), 2)
            pair[0], pair[1] = refs[i][...], refs[i + 1][...]
            refs[i], refs[i + 1] = pair.at[1 - parity], pair.at[parity]
        carried = []
        for (j, axis), pair in zip(sent, both[len(received) :]):
            parity = lax.rem(lax.axis_index(axis), 2)
            j += len(args)
            carried.append((refs[j], refs[j + 1], pair))
            refs[j], refs[j + 1] = pair.at[parity], pair.at[1 - parity]
        kernel(*refs)
        for first, second, pair in carried:
            first[...], second[...] = pair[0], pair[1]

    return wrapped, list(scratch) + extra


def whole_call(kernel, outs, args, scratch=(), received=(), sent=(), name=None, **changes):
    out_list = outs if isinstance(outs, list) else [outs]
    kernel, scratch = paired(kernel, args, out_list, scratch, received, sent)
    specs = [SMEM if a.ndim == 1 or a.dtype == jnp.int32 else VMEM for a in args]
    return pl.pallas_call(
        kernel,
        in_specs=changes.get("in_specs", specs),
        out_specs=changes.get("out_specs", [VMEM] * len(outs) if outs is out_list else VMEM),
        out_shape=outs,
        scratch_shapes=scratch,
        name=name,
        cost_estimate=pl.CostEstimate(flops=1000, bytes_accessed=1000, transcendentals=0),
        compiler_params=pltpu.CompilerParams(vmem_limit_bytes=changes.get("vmem", VMEM_BYTES)),
    )(*args)


def shape(*dims):
    return jax.ShapeDtypeStruct(dims, F32)


SMEM = pl.BlockSpec(memory_space=pltpu.SMEM)
VMEM = pl.BlockSpec(memory_space=pltpu.VMEM)


def first_messages(v):
    nx, ny, nz = v.shape

    kept = nx - nx // 8

    def kernel(v_ref, up, down, y_up, y_down, last, first, rows_up, rows_down, sems):
        copies = [
            pltpu.make_async_copy(source, target, sems.at[i])
            for i, (source, target) in enumerate(
                (
                    (v_ref.at[pl.ds(nx - 3, 3)], last),
                    (v_ref.at[pl.ds(0, 3)], first),
                    (v_ref.at[:, pl.ds(ny - 8, 8)], rows_up),
                    (v_ref.at[:, pl.ds(0, 8)], rows_down),
                )
            )
        ]
        for copy in copies:
            copy.start()
        for copy in copies:
            copy.wait()
        up[0] = last[2]
        up[1] = H[0] * last[0] + H[1] * last[1]
        down[0] = first[0]
        down[1] = H[6] * first[1] + H[7] * first[2]
        y_up[...] = rows_up[:kept]
        y_down[...] = rows_down[:kept]
        for i in range(kept):
            plane, row = kept + i // 7, i % 7
            y_up[i, 0:1] = rows_up[plane, row + 1 : row + 2]
            y_down[i, 7:8] = rows_down[plane, row : row + 1]

    return whole_call(
        kernel,
        [shape(2, ny, nz)] * 2 + [shape(kept, 8, nz)] * 2,
        [v],
        scratch=[pltpu.VMEM((3, ny, nz), F32)] * 2
        + [pltpu.VMEM((nx, 8, nz), F32)] * 2
        + [pltpu.SemaphoreType.DMA((4,))],
        sent=[(0, "gx"), (2, "gy")],
        name="first_messages",
        in_specs=[pl.BlockSpec(memory_space=pltpu.HBM)],
        vmem=50 * 1024 * 1024,
    )


def over_planes(count, group, body):
    def step(i, carry):
        body(i * group)
        return carry

    lax.fori_loop(0, count // group, step, 0)


def depth(v, z_matrix, group, name):
    nx, rows, nz = v.shape

    def kernel(v_ref, z, out):
        def body(first):
            at = pl.ds(first, group)
            out[at] = times(v_ref[at].reshape(group * rows, nz), z).reshape(group, rows, nz)

        over_planes(nx, group, body)

    return whole_call(kernel, shape(nx, rows, nz), [v, z_matrix], name=name)


def y_analysis(zed, y_across, y_here, z_matrix, y_matrix):
    nx, ny, nz = zed.shape
    rows = y_matrix.shape[0]
    kept = y_here.shape[0]
    group = 8

    def kernel(zed_ref, right, left, z, y, out, left_z, right_z):
        for part, out_z in ((left, left_z), (right, right_z)):
            out_z[:kept] = times(part[...].reshape(8 * kept, nz), z).reshape(kept, 8, nz)
            out_z[kept:] = jnp.zeros((nx - kept, 8, nz), F32)
        for i in range(kept):
            plane, row = kept + i // 7, i % 7
            left_z[plane, row + 1 : row + 2] = left_z[i, 0:1]
            right_z[plane, row : row + 1] = right_z[i, 7:8]

        def body(first):
            for j in range(group):
                i = first + j
                out[i] = left_times(y, jnp.concatenate([left_z[i], zed_ref[i], right_z[i]], axis=0))

        over_planes(nx, group, body)

    return whole_call(
        kernel,
        shape(nx, rows, nz),
        [zed, y_across, y_here, z_matrix, y_matrix],
        scratch=[pltpu.VMEM((nx, 8, nz), F32)] * 2,
        received=[(1, "gy")],
        name="y_analysis",
    )


def own_approx(zed, y_matrix, own, rows, ghost_rows):
    nx, ny, nz = zed.shape
    half_z = nz // 2
    n1 = nx // 2

    def kernel(zed_ref, y, approx, up, down, low):
        def y_body(first):
            planes = [zed_ref[first + i, :, :half_z] for i in range(8)]
            for i, plane in enumerate(in_pairs(y, planes)):
                low[first + i] = plane[:rows]

        over_planes(nx, 8, y_body)

        def tile(t, carry):
            at = pl.ds(pl.multiple_of(t * 8, 8), 8)
            values = {i: low[i, at] for i in range(nx)}
            for k in range(n1):
                approx[k, at] = added([(c, values[i]) for i, c, _ in x_terms(k, nx) if i in values])
            approx[n1, at] = added([(H[5 + i], values[i]) for i in range(3)])
            approx[n1 + 1, at] = H[1] * H[7] * values[0]
            approx[n1 + 2, at] = added([(H[i], values[nx - 3 + i]) for i in range(3)])
            approx[n1 + 3, at] = H[6] * H[0] * values[nx - 1]
            return carry

        lax.fori_loop(0, rows // 8, tile, 0)
        inside = ghost_rows - 2
        up[:, :inside] = approx[:n1, own - inside : own]
        up[:, inside:] = approx[:n1, own + 2 : own + 4]
        down[:, :2] = approx[:n1, own : own + 2]
        down[:, 2:] = approx[:n1, :inside]

    return whole_call(
        kernel,
        [shape(n1 + 4, rows, half_z), shape(n1, ghost_rows, half_z), shape(n1, ghost_rows, half_z)],
        [zed, y_matrix],
        scratch=[pltpu.VMEM((nx, rows, half_z), F32)],
        sent=[(1, "gy")],
        name="own_approx",
    )


def x_halo_messages(x_left, x_right, approx, z_matrix, wide, ghost_rows):
    _, ny, nz = x_left.shape
    half_z = nz // 2
    n1 = approx.shape[0] - 4
    own, inside = ny // 2, ghost_rows - 2
    message = wide + 8 + ghost_rows

    def kernel(xl, xr, a_ref, z, out, up, down):
        planes = jnp.concatenate([xl[0], xl[1], xr[0], xr[1]], axis=0)
        out[...] = times(planes, z).reshape(4, ny, nz)
        up[:, :wide] = out[:, ny - wide :, :half_z]
        up[:, wide : wide + 8] = out[:, ny - 8 :, half_z:]
        down[:, :wide] = out[:, :wide, :half_z]
        down[:, wide : wide + 8] = out[:, :8, half_z:]
        up[:, wide + 8 : wide + 8 + inside] = a_ref[n1:, own - inside : own]
        up[:, wide + 8 + inside :] = a_ref[n1:, own + 2 : own + 4]
        down[:, wide + 8 : wide + 10] = a_ref[n1:, own : own + 2]
        down[:, wide + 10 :] = a_ref[n1:, :inside]

    return whole_call(
        kernel,
        [shape(4, ny, nz), shape(4, message, half_z), shape(4, message, half_z)],
        [x_left, x_right, approx, z_matrix],
        received=[(0, "gx")],
        sent=[(1, "gy")],
        name="x_halo_messages",
    )


def edges_of(n):
    return [0, 1, n - 2, n - 1]


def band_limits(table_ref, index_ref, by, bz):
    band = 2 * by + bz
    quiet = table_ref[index_ref[0, band - 1]] if band else NOTHING
    return quiet, table_ref[index_ref[0, band + 3]]


def over_tiles(rows, nz, body, unroll=3):
    half_z, half_tiles = nz // 2, rows // 16
    for by in range(2):

        def tile(t, carry, by=by):
            at = pl.ds(pl.multiple_of((t + by * half_tiles) * 8, 8), 8)
            for bz in range(2):
                body(at, pl.ds(bz * half_z, half_z), by, bz)
            return carry

        lax.fori_loop(0, half_tiles, tile, 0, unroll=unroll if half_tiles % unroll == 0 else 1)


def inner_bands(bands, table, index):
    nx, rows, nz = bands.shape
    count = nx // 2 - 4

    def kernel(table_ref, index_ref, b_ref, out):
        def body(at, lanes, by, bz):
            quiet, loud = band_limits(table_ref, index_ref, by, bz)
            values = {i: b_ref[i, at, lanes] for i in range(nx)}
            for k, (low, high) in x_interior(values.get, nx).items():
                out[k - 2, at, lanes] = shrink(low, quiet) if by + bz else jnp.zeros_like(low)
                out[count + k - 2, at, lanes] = shrink(high, loud)

        over_tiles(rows, nz, body)

    return whole_call(
        kernel,
        shape(2 * count, rows, nz),
        [table, index, bands],
        name="inner_bands",
    )


def yz_synthesis(planes, z, y, out, zed):
    count, rows, nz = zed.shape
    group = max(g for g in range(1, 17) if count % g == 0)
    for first in range(0, count, group):
        zed[first : first + group] = times(planes(first, group), z).reshape(group, rows, nz)

    def y_body(first):
        for j in range(4):
            out[first + j] = left_times(y, zed[first + j])

    over_planes(count, 4, y_body)


def edge_own(bands):
    nx, rows, nz = bands.shape

    def kernel(b_ref, out):
        def body(at, lanes, by, bz):
            values = {i: b_ref[i, at, lanes] for i in [*range(7), *range(nx - 7, nx)]}
            for i, k in enumerate(edges_of(nx // 2)):
                terms = [t for t in x_terms(k, nx) if t[0] in values]
                out[i, at, lanes] = added([(low, values[key]) for key, low, _ in terms])
                out[4 + i, at, lanes] = added([(high, values[key]) for key, _, high in terms])

        over_tiles(rows, nz, body)

    return whole_call(kernel, shape(8, rows, nz), [bands], name="edge_own")


def edge_details(nx, own, halo, h_left, h_right, table, index, ya_matrix, z_matrix, y_matrix, wide):
    _, rows, nz = own.shape
    ny = y_matrix.shape[0]
    n1 = nx // 2
    half_z = nz // 2
    ends = edges_of(n1)

    def kernel(table_ref, index_ref, b_ref, x_ref, hl, hr, ya, z, y, coeffs, up, down, h_ref, beyond, zed):
        for i in range(4):
            low = jnp.concatenate([hl[i, wide - 8 : wide], x_ref[i, :, :half_z], hr[i, :8]], axis=0)
            high = jnp.concatenate(
                [hl[i, wide : wide + 8], x_ref[i, :, half_z:], hr[i, wide : wide + 8]], axis=0
            )
            h_ref[i] = left_times(ya, jnp.concatenate([low, high], axis=1))
        place = {"l1": 0, "l2": 1, "r1": 2, "r2": 3}

        def body(at, lanes, by, bz):
            quiet, loud = band_limits(table_ref, index_ref, by, bz)
            values = {key: h_ref[i, at, lanes] for key, i in place.items()}
            lows, highs = {}, {}
            for i, k in enumerate(ends):
                terms = [t for t in x_terms(k, nx) if t[0] in values]
                low = b_ref[i, at, lanes] + added([(c, values[key]) for key, c, _ in terms])
                high = b_ref[4 + i, at, lanes] + added([(c, values[key]) for key, _, c in terms])
                lows[k] = shrink(low, quiet) if by + bz else jnp.zeros_like(low)
                highs[k] = shrink(high, loud)
                coeffs[i, at, lanes] = lows[k]
                coeffs[4 + i, at, lanes] = highs[k]
            spilled = spill_up(lows, highs, n1) + spill_down(lows, highs)
            for i, part in enumerate(spilled):
                beyond[i, at, lanes] = part

        over_tiles(rows, nz, body, 9)
        zed[...] = times(beyond[...].reshape(4 * rows, nz), z).reshape(4, rows, nz)
        for i, target in enumerate((up.at[0], up.at[1], down.at[0], down.at[1])):
            target[...] = left_times(y, zed[i])

    return whole_call(
        kernel,
        [shape(8, rows, nz), shape(2, ny, nz), shape(2, ny, nz)],
        [table, index, own, halo, h_left, h_right, ya_matrix, z_matrix, y_matrix],
        scratch=[pltpu.VMEM((4, rows, nz), F32)] * 3,
        received=[(4, "gy")],
        sent=[(1, "gx")],
        name="edge_details",
    )


def detail_yz(edge, inner, approx, z_matrix, y_matrix):
    count, rows, nz = inner.shape
    ny = y_matrix.shape[0]
    _, low_rows, half_z = approx.shape
    n1 = count // 2 + 4
    ends = edges_of(n1)

    def kernel(e_ref, i_ref, a_ref, z, y, out, zed):
        def coeff(k, high):
            if k in ends:
                return e_ref.at[4 * high + ends.index(k)]
            return i_ref.at[(n1 - 4) * high + k - 2]

        def plane(i):
            ref = coeff(i % n1, i // n1)
            if i >= n1:
                return ref[...]
            corner = ref[:low_rows, :half_z] + a_ref[i + 2]
            top = jnp.concatenate([corner, ref[:low_rows, half_z:]], axis=1)
            return jnp.concatenate([top, ref[low_rows:]], axis=0)

        def planes(first, n):
            return jnp.concatenate([plane(i) for i in range(first, first + n)], axis=0)

        yz_synthesis(planes, z, y, out, zed)

    return whole_call(
        kernel,
        shape(2 * n1, ny, nz),
        [edge, inner, approx, z_matrix, y_matrix],
        scratch=[pltpu.VMEM((2 * n1, rows, nz), F32)],
        name="detail_yz",
    )


def own_result(parts, approx, left, right, z_matrix, y_matrix):
    nx, ny, nz = parts.shape
    n1 = nx // 2
    planes, rows, half_z = approx.shape

    def kernel(p_ref, a_ref, el, er, z, y, out, ghosts):
        stack = jnp.concatenate([a_ref[i] for i in (0, 1, n1 + 2, n1 + 3)], axis=0)
        for i, plane in enumerate(cut(times(stack, z), rows)):
            ghosts[i] = left_times(y, plane)

        def tile(t, carry):
            at = pl.ds(pl.multiple_of(t * 8, 8), 8)
            for lane in range(0, nz, 128):
                lanes = pl.ds(lane, 128)
                lows = {k: p_ref[k, at, lanes] for k in range(n1)}
                highs = {k: p_ref[n1 + k, at, lanes] for k in range(n1)}
                for i, k in enumerate((-2, -1, n1, n1 + 1)):
                    lows[k] = ghosts[i, at, lanes]
                cells = x_synth_interior(lows, highs, n1)
                for m in range(nx):
                    value = cells[m] if m in cells else x_synth(m, lows, highs)
                    if m < 3:
                        extra = el[(0, 1, 1)[m], at, lanes]
                        value += extra if m < 2 else THIRD_UP * extra
                    if m >= nx - 3:
                        extra = er[(0, 1, 1)[nx - 1 - m], at, lanes]
                        value += extra if m > nx - 3 else THIRD_DOWN * extra
                    out[m, at, lanes] = value
            return carry

        lax.fori_loop(0, ny // 8, tile, 0)

    return whole_call(
        kernel,
        shape(nx, ny, nz),
        [parts, approx, left, right, z_matrix, y_matrix],
        scratch=[pltpu.VMEM((4, ny, nz), F32)],
        received=[(2, "gx")],
        name="own_result",
    )


def in_pairs(matrix, planes):
    results = []
    for i in range(0, len(planes), 2):
        both = left_times(matrix, jnp.concatenate(planes[i : i + 2], axis=1))
        width = both.shape[1] // 2
        results += [both[:, :width], both[:, width:]]
    return results


def cut(values, rows):
    return [values[i : i + rows] for i in range(0, values.shape[0], rows)]


def packed(first, second):
    half = first.shape[1] // 2
    lane = lax.broadcasted_iota(jnp.int32, first.shape, 1)
    return jnp.where(lane < half, first, pltpu.roll(second, half, 1))


def unpacked(both):
    half = both.shape[1] // 2
    lane = lax.broadcasted_iota(jnp.int32, both.shape, 1)
    return [jnp.where(lane < half, part, 0.0) for part in (both, pltpu.roll(both, half, 1))]


def second_bands(own, left, right, z_matrix, y_matrix, low_rows):
    _, own_rows, nz = own.shape
    n1 = left.shape[0]
    in_rows = own_rows + 2 * left.shape[1]
    rows = y_matrix.shape[0]


    def kernel(o_ref, l_ref, r_ref, z, y, out, up, down):
        for i in range(0, n1, 16):
            stack = [part[j] for j in range(i, min(i + 16, n1)) for part in (o_ref, l_ref, r_ref)]
            zed = times_wide(jnp.concatenate(stack, axis=0), z)
            for j, plane in enumerate(in_pairs(y, cut(zed, in_rows))):
                out[i + j] = plane
        low = lambda c: out[c, :low_rows]
        up[0:rows] = out[n1 - 1]
        up[rows : 2 * rows] = H[0] * out[n1 - 3] + H[1] * out[n1 - 2]
        first = added([(H[j], low(n1 - 5 + j)) for j in range(5)])
        second = added([(H[0] * H[j], low(n1 - 9 + j)) for j in range(8)])
        second += added([(H[1] * H[j], low(n1 - 7 + j)) for j in range(7)])
        up[2 * rows :] = packed(first, second)
        down[0:rows] = out[0]
        down[rows : 2 * rows] = H[6] * out[1] + H[7] * out[2]
        first = added([(H[j], low(j - 3)) for j in range(3, 8)])
        second = added([(H[6] * H[j], low(j - 1)) for j in range(1, 8)])
        second += added([(H[7] * H[j], low(j + 1)) for j in range(8)])
        down[2 * rows :] = packed(first, second)

    message = 2 * rows + low_rows
    return whole_call(
        kernel,
        [shape(n1, rows, nz), shape(message, nz), shape(message, nz)],
        [own, left, right, z_matrix, y_matrix],
        received=[(1, "gy")],
        sent=[(1, "gx")],
        name="second_bands",
    )


def limits_plane(table_ref, index_ref, level, bx, dims, row_split, lane_split, zeroth):
    row_high = lax.broadcasted_iota(jnp.int32, dims, 0) >= row_split
    lane_high = lax.broadcasted_iota(jnp.int32, dims, 1) >= lane_split

    def limit(by, bz):
        band = 4 * bx + 2 * by + bz
        return zeroth if band == 0 else table_ref[index_ref[level, band - 1]]

    low_y = jnp.where(lane_high, limit(0, 1), limit(0, 0))
    return jnp.where(row_high, jnp.where(lane_high, limit(1, 1), limit(1, 0)), low_y)


def coarse(
    bands, left, right, halo, h_left, h_right, approx_in, table, index, za1, yx0, ya1, zs1, za2, zs2, ya2, ys2, ys1,
    in_rows1, low_rows, out_rows, own_rows, spill_at, spill_rows, wide,
):
    n1, rows, nz = bands.shape
    in_rows = in_rows1
    n2, n3 = n1 // 2, n1 // 4
    rows2 = ya2.shape[0]
    lane_half = nz // 2

    def kernel(
        table_ref, index_ref, b_ref, l_ref, r_ref, x_ref, hl, hr, a_ref, z1a, yx, a1, z1, z2a, z2s, a2, s2, s1,
        approx, up, down, c1, p1,
    ):
        halo_planes = [jnp.concatenate([hl[i, :wide], x_ref[i, :, :nz], hr[i, :wide]], axis=0) for i in range(4)]
        halo_planes = [plane[:in_rows] for plane in in_pairs(yx, halo_planes)]
        own_planes = [
            jnp.concatenate([a_ref[n1 + i], hl[i, wide + 8 :], hr[i, wide + 8 :]], axis=0) for i in range(4)
        ]
        both = times_wide(jnp.concatenate(halo_planes + own_planes, axis=0), z1a)
        hl1, hl2, hr1, hr2, xl1, xl2, xr1, xr2 = in_pairs(a1, cut(both, in_rows))
        values = {k: b_ref[k] for k in range(2, n1 - 2)}
        values[0] = b_ref[0] + (hl2 + H[2] * hl1)
        values[1] = b_ref[1] + H[0] * hl1
        values[n1 - 2] = b_ref[n1 - 2] + H[7] * hr1
        values[n1 - 1] = b_ref[n1 - 1] + (hr2 + H[5] * hr1)
        values["l1"] = l_ref[0:rows] + xl1
        values["l2"] = l_ref[rows : 2 * rows] + xl2
        values["r1"] = r_ref[0:rows] + xr1
        values["r2"] = r_ref[rows : 2 * rows] + xr2
        get = values.get
        low_part = lambda c: values[c][:low_rows]
        xl1, xl2, xr1, xr2 = [part[:low_rows] for part in (xl1, xl2, xr1, xr2)]
        dims = (rows, nz)
        quiet = limits_plane(table_ref, index_ref, 1, 0, dims, low_rows, lane_half, NOTHING)
        loud = limits_plane(table_ref, index_ref, 1, 1, dims, low_rows, lane_half, NOTHING)
        planes = []
        for k in range(n2):
            low = x_low(get, k, n1)
            planes.append(low[:low_rows])
            c1[k] = shrink(low, quiet)
            c1[n2 + k] = shrink(x_high(get, k, n1), loud)
        first, second = unpacked(l_ref[2 * rows :])
        own = [(H[5 + i], low_part(i)) for i in range(3)]
        planes.append(first + added([(H[3] / H[1], xl2), (H[4], xl1)] + own))
        own = [((H[0] * H[7] + H[1] * H[5]) / H[1], xl2), (H[1] * H[6], xl1), (H[1] * H[7], low_part(0))]
        planes.append(second + added(own))
        first, second = unpacked(r_ref[2 * rows :])
        own = [(H[i], low_part(n1 - 3 + i)) for i in range(3)]
        planes.append(first + added([(H[3], xr1), (H[4] / H[6], xr2)] + own))
        own = [((H[6] * H[2] + H[7] * H[0]) / H[6], xr2), (H[6] * H[1], xr1), (H[6] * H[0], low_part(n1 - 1))]
        planes.append(second + added(own))
        third = in_pairs(a2, cut(times_wide(jnp.concatenate(planes, axis=0), z2a), low_rows))
        keys = {"l1": n2, "l2": n2 + 1, "r1": n2 + 2, "r2": n2 + 3}
        get2 = lambda key: third[keys.get(key, key)]
        dims = (rows2, nz)
        quiet = limits_plane(table_ref, index_ref, 2, 0, dims, rows2 // 2, lane_half // 2, 0.0)
        loud = limits_plane(table_ref, index_ref, 2, 1, dims, rows2 // 2, lane_half // 2, 0.0)
        kept = [shrink(x_low(get2, k, n2), quiet) for k in range(n3)]
        kept += [shrink(x_high(get2, k, n2), loud) for k in range(n3)]
        parts = in_pairs(s2, cut(times_wide(jnp.concatenate(kept, axis=0), z2s), rows2))
        parts = [part[:low_rows] for part in parts]
        lows = dict(enumerate(parts[:n3]))
        highs = dict(enumerate(parts[n3:]))
        ghosts = [-3, -2, -1, n2, n2 + 1, n2 + 2]
        for k in range(n2):
            c1[k, :low_rows] += x_synth(k, lows, highs)
        stack = [x_synth(k, lows, highs) for k in ghosts]
        beyond = dict(zip(ghosts, stack))
        zed = times_wide(jnp.concatenate(stack, axis=0), z1)
        for i, plane in enumerate(in_pairs(s1, cut(zed, low_rows))):
            p1[2 * n2 + i] = plane[:out_rows]
        for i in range(0, 2 * n2, 16):
            zed = times_wide(c1[i : i + 16].reshape(16 * rows, nz), z1)
            for j, plane in enumerate(in_pairs(s1, cut(zed, rows))):
                p1[i + j] = plane[:out_rows]
        lows = {k: p1.at[k] for k in range(n2)}
        highs = {k: p1.at[n2 + k] for k in range(n2)}
        for i, k in enumerate(ghosts):
            lows[k] = p1.at[2 * n2 + i]

        def cell(m):
            near = lambda part: {k: ref[...] for k, ref in part.items() if 0 <= m + 3 - 2 * k < 8}
            return x_synth(m, near(lows), near(highs))

        for m in range(-2, n1 + 2):
            approx[m + 2] = cell(m)
        value = lambda part, ks: {k: part[k][...] for k in ks}
        ends = (n2 - 2, n2 - 1)

        def send(message, four, two):
            for i, plane in enumerate(four):
                message[i * own_rows : (i + 1) * own_rows] = plane[:own_rows]
                message[4 * own_rows + 4 * i : 4 * own_rows + 4 * i + 4] = plane[own_rows : own_rows + 4]
            message[4 * own_rows + 16 :] = packed(*two)[spill_at : spill_at + spill_rows]

        up_two = spill_up(value(lows, ends), value(highs, ends), n2)
        send(up, (approx[n1], approx[n1 + 1], *up_two), (beyond[n2], beyond[n2 + 1]))
        down_two = spill_down(value(lows, (0, 1)), value(highs, (0, 1)))
        send(down, (approx[2], approx[3], *down_two), (beyond[-1], beyond[-2]))

    message = 4 * own_rows + 16 + spill_rows
    return whole_call(
        kernel,
        [shape(n1 + 4, out_rows, nz), shape(message, nz), shape(message, nz)],
        [table, index, bands, left, right, halo, h_left, h_right, approx_in, za1, yx0, ya1, zs1, za2, zs2, ya2, ys2, ys1],
        scratch=[pltpu.VMEM((2 * n2, rows, nz), F32), pltpu.VMEM((2 * n2 + 6, out_rows, nz), F32)],
        received=[(3, "gx"), (6, "gy")],
        sent=[(1, "gx")],
        name="coarse",
    )


def received_taps(n1):
    n2, nx = n1 // 2, 2 * n1
    from_approx = np.zeros((nx, n1 + 4))
    for m in range(nx):
        for k in range(-2, n1 + 2):
            from_approx[m, k + 2] = tap(H, m + 3 - 2 * k)
    approx = np.zeros((n1 + 4, 12))
    third = {0: THIRD_UP, 6: THIRD_DOWN}
    for first, cell, second in ((0, lambda i: i, lambda i: i), (6, lambda i: n1 - 1 - i, lambda i: n2 - 1 - i)):
        ghost = (-2, -1) if first == 0 else (n1, n1 + 1)
        for i in range(2):
            approx[ghost[i] + 2, first + i] = 1.0
        for place, source, coef in ((0, 0, 1.0), (1, 1, 1.0), (2, 1, third[first])):
            approx[cell(place) + 2, first + 2 + source] += coef
            for m in range(n1):
                approx[m + 2, first + 4 + source] += coef * tap(H, m + 3 - 2 * second(place))
    return from_approx @ approx


def final(left, right, own, zs1, ys1, z_matrix, y_matrix, rows, spill_rows):
    nx, ny, nz = own.shape
    half_z = nz // 2
    own_rows = ny // 2
    step_rows = 16
    steps = ny // step_rows
    taps = received_taps(nx // 2)

    def kernel(l_ref, r_ref, d_ref, z1, s1, z, y, out, planes, parts, done, sems):
        stack = [p for ref in (l_ref, r_ref) for p in unpacked(ref[4 * own_rows + 16 :])]
        spilled = cut(times(jnp.concatenate(stack, axis=0), z1), spill_rows)
        for side, ref in enumerate((l_ref, r_ref)):
            for i in range(4):
                plane = planes.at[4 * side + i]
                plane[:own_rows] = ref[i * own_rows : (i + 1) * own_rows]
                plane[own_rows:] = jnp.zeros((rows - own_rows, half_z), F32)
                plane[own_rows : own_rows + 4] = ref[4 * own_rows + 4 * i : 4 * own_rows + 4 * i + 4]
        for i, plane in enumerate(cut(times(planes[...].reshape(8 * rows, half_z), z), rows)):
            parts[6 * (i // 4) + i % 4] = left_times(y, plane)
        for i, plane in enumerate(spilled):
            parts[6 * (i // 2) + 4 + i % 2] = left_times(s1, plane)

        def copy(i):
            at = pl.ds(pl.multiple_of(i * step_rows, step_rows), step_rows)
            return pltpu.make_async_copy(done.at[:, at], out.at[:, at], sems.at[i])

        def step(i, carry):
            for t in range(step_rows // 8):
                at = pl.ds(pl.multiple_of(i * step_rows + 8 * t, 8), 8)
                for lane in range(0, nz, 128):
                    lanes = pl.ds(lane, 128)
                    values = [parts[i, at, lanes] for i in range(12)]
                    for m in range(nx):
                        value = d_ref[m, at, lanes]
                        value += added([(float(c), v) for c, v in zip(taps[m], values) if c != 0.0])
                        done[m, at, lanes] = value
            copy(i).start()
            return carry

        lax.fori_loop(0, steps, step, 0)

        def finish(i, carry):
            copy(i).wait()
            return carry

        lax.fori_loop(0, steps, finish, 0)

    return whole_call(
        kernel,
        shape(nx, ny, nz),
        [left, right, own, zs1, ys1, z_matrix, y_matrix],
        scratch=[
            pltpu.VMEM((8, rows, half_z), F32),
            pltpu.VMEM((12, ny, nz), F32),
            pltpu.VMEM((nx, ny, nz), F32),
            pltpu.SemaphoreType.DMA((steps,)),
        ],
        received=[(0, "gx")],
        name="final",
        out_specs=pl.BlockSpec(memory_space=pl.ANY),
    )


def exchange(first, second, axis):
    size = lax.axis_size(axis)
    assert size % 2 == 0
    here = [(i, i ^ 1) for i in range(size)]
    across = [(i, (i + 1) % size if i % 2 else (i - 1) % size) for i in range(size)]
    return lax.ppermute(first, axis, here), lax.ppermute(second, axis, across)


def local(velocity, table, index):
    nx, ny, nz = velocity.shape
    y1, y2, y3 = ny // 2, ny // 4, ny // 8
    ghost, wide = 24, 48
    cells0 = list(range(-8, ny + 8))
    rows0 = up_to(y1 + 4, 8)
    ks0 = fill(list(range(y1)) + [-2, -1, y1, y1 + 1], rows0)
    cells1 = ks0 + list(range(2 - ghost, 2)) + list(range(y1 - 2, y1 + ghost - 2))
    once = [c if cells1.index(c) == i else None for i, c in enumerate(cells1)]
    rows1 = up_to(y2 + 18, 8)
    low1 = fill(list(range(-9, y2 + 9)), rows1)
    high1 = fill(list(range(-3, y2 + 3)), up_to(y2 + 6, 8))
    spill_at, spill_rows = 6, up_to(y2 + 6, 8)
    ks2 = fill(list(range(-3, y3 + 3)), up_to(y3 + 6, 8))
    ya0 = from_left(analysis_rows(cells0, ks0, ks0))
    ys0_matrix = synthesis_rows(list(range(ny)), ks0, ks0)
    ys0 = from_left(ys0_matrix)
    ys0_low = from_left(ys0_matrix[:, :rows0])
    yl0 = from_left(analysis_rows(list(range(ny)), ks0, []))
    yx0 = from_left(analysis_rows(list(range(-wide, ny + wide)), once, []))
    ya1 = from_left(analysis_rows(cells1, low1, high1))
    ys1 = from_left(synthesis_rows(ks0, low1, high1))
    spill_matrix = synthesis_rows(ks0, low1[spill_at : spill_at + spill_rows], [])
    ys_spill = from_left(ys0_matrix[:, :rows0] @ spill_matrix)
    ya2 = from_left(analysis_rows(low1, ks2, ks2))
    ys2 = from_left(synthesis_rows(low1, ks2, ks2))
    z0 = periodic(nz, nz)
    z1 = periodic(nz // 2, nz // 2)
    z2 = periodic(nz // 4, nz // 2)
    za0, zs0, zs0_low = from_right(z0), from_right(z0.T), from_right(z0.T[: nz // 2])
    za1, zs1 = wide_right(z1), wide_right(z1.T)
    za2, zs2 = wide_right(z2), wide_right(z2.T)
    zs_spill = from_right(z1.T @ z0.T[: nz // 2])

    x_up, x_down, y_up, y_down = first_messages(velocity)
    x_left, x_right = exchange(x_up, x_down, "gx")
    y_here, y_across = exchange(y_up, y_down, "gy")
    zed = depth(velocity, za0, 16, "depth_analysis")
    approx, a_up, a_down = own_approx(zed, yl0, y1, rows0, ghost)
    a_left, a_right = exchange(a_up, a_down, "gy")
    zed, a_up = lax.optimization_barrier((zed, a_up))
    bands = y_analysis(zed, y_across, y_here, za0, ya0)
    ends = edge_own(bands)
    x_left, x_right, ends = lax.optimization_barrier((x_left, x_right, ends))
    halo, h_up, h_down = x_halo_messages(x_left, x_right, approx, za0, wide, ghost)
    h_left, h_right = exchange(h_up, h_down, "gy")
    approx, halo = lax.optimization_barrier((approx, halo))
    bands1, b_up, b_down = second_bands(approx, a_left, a_right, za1, ya1, rows1)
    b_left, b_right = exchange(b_up, b_down, "gx")
    h_left, h_right, bands1 = lax.optimization_barrier((h_left, h_right, bands1))
    edge, e_up, e_down = edge_details(nx, ends, halo, h_left, h_right, table, index, ya0, zs0, ys0, wide)
    e_left, e_right = exchange(e_up, e_down, "gx")
    bands1, edge = lax.optimization_barrier((bands1, edge))
    approx1, s_up, s_down = coarse(
        bands1, b_left, b_right, halo, h_left, h_right, approx, table, index,
        za1, yx0, ya1, zs1, za2, zs2, ya2, ys2, ys1, len(cells1), rows1, rows0, y1, spill_at, spill_rows, wide,
    )
    s_left, s_right = exchange(s_up, s_down, "gx")
    bands, approx1 = lax.optimization_barrier((bands, approx1))
    parts = detail_yz(edge, inner_bands(bands, table, index), approx1, zs0, ys0)
    own = own_result(parts, approx1, e_left, e_right, zs0_low, ys0_low)
    return final(s_left, s_right, own, zs_spill, ys_spill, zs0_low, ys0_low, rows0, spill_rows)


def solution(mesh):
    return jax.shard_map(
        local,
        mesh=mesh,
        in_specs=(P("gx", "gy", None), P(), P()),
        out_specs=P("gx", "gy", None),
        check_vma=False,
    )
```

```python
import functools

import jax
import jax.numpy as jnp
import ml_dtypes
import numpy as np
from jax import lax
from jax.experimental import pallas as pl
from jax.experimental.pallas import tpu as pltpu
from jax.sharding import PartitionSpec as P

H = [
    0.23037781330885523,
    0.7148465705525415,
    0.6308807679295904,
    -0.02798376941698385,
    -0.18703481171888114,
    0.030841381835986965,
    0.032883011666982945,
    -0.010597401784997278,
]
G = [(-1.0) ** j * H[7 - j] for j in range(8)]
F32 = jnp.float32
BF16 = jnp.bfloat16
NOTHING = 3.0e38
VMEM_BYTES = 16 * 1024 * 1024


def tap(filt, j):
    return filt[j] if 0 <= j < 8 else 0.0


def analysis_rows(cells, low_ks, high_ks):
    matrix = np.zeros((len(low_ks) + len(high_ks), len(cells)))
    rows = [(H, k) for k in low_ks] + [(G, k) for k in high_ks]
    for row, (filt, k) in enumerate(rows):
        for col, cell in enumerate(cells):
            if k is not None and cell is not None:
                matrix[row, col] = tap(filt, cell - 2 * k + 3)
    return matrix


def synthesis_rows(cells, low_ks, high_ks):
    return analysis_rows(cells, low_ks, high_ks).T


def periodic(length, padded_to):
    matrix = np.zeros((padded_to, padded_to))
    for k in range(length // 2):
        for j in range(8):
            matrix[(2 * k + j - 3) % length, k] += H[j]
            matrix[(2 * k + j - 3) % length, length // 2 + k] += G[j]
    return matrix


def fill(items, length):
    return items + [None] * (length - len(items))


def up_to(count, step):
    return -(-count // step) * step


def pieces(matrix, axis):
    rows, cols = matrix.shape
    matrix = np.pad(matrix, ((0, up_to(rows, 16) - rows), (0, up_to(cols, 16) - cols))).astype(np.float32)
    high = matrix.astype(ml_dtypes.bfloat16)
    low = (matrix - high.astype(np.float32)).astype(ml_dtypes.bfloat16)
    return np.concatenate([high, high, low], axis=axis)


def from_left(matrix):
    return pieces(matrix, 1)


def from_right(matrix):
    return pieces(matrix, 0)


def wide_right(matrix):
    rows, cols = matrix.shape
    both = pieces(matrix, 0)
    high, low = both[:rows], both[2 * rows :]
    return np.block([[high, low], [high, np.zeros_like(low)]])


def tall_left(matrix):
    return np.ascontiguousarray(wide_right(np.ascontiguousarray(padded_to_tiles(matrix).T)).T)


def padded_to_tiles(matrix):
    rows, cols = matrix.shape
    return np.pad(matrix, ((0, up_to(rows, 16) - rows), (0, up_to(cols, 16) - cols)))


def halves(values):
    high = values.astype(BF16)
    return high, (values - high.astype(F32)).astype(BF16)


def times(values, matrix):
    high, low = halves(values)
    return jnp.dot(jnp.concatenate([high, low, high], axis=1), matrix[...], preferred_element_type=F32)


def left_times(matrix, values):
    missing = matrix.shape[1] // 3 - values.shape[0]
    if missing:
        values = jnp.concatenate([values, jnp.zeros((missing, values.shape[1]), F32)], axis=0)
    high, low = halves(values)
    return jnp.dot(matrix[...], jnp.concatenate([high, low, high], axis=0), preferred_element_type=F32)


def times_wide(values, matrix):
    both = jnp.dot(jnp.concatenate(halves(values), axis=1), matrix[...], preferred_element_type=F32)
    return both[:, : both.shape[1] // 2] + both[:, both.shape[1] // 2 :]


def left_times_tall(matrix, values):
    missing = matrix.shape[1] // 2 - values.shape[0]
    if missing:
        values = jnp.concatenate([values, jnp.zeros((missing, values.shape[1]), F32)], axis=0)
    both = jnp.dot(matrix[...], jnp.concatenate(halves(values), axis=0), preferred_element_type=F32)
    return both[: both.shape[0] // 2] + both[both.shape[0] // 2 :]


def added(terms):
    total = None
    for coef, value in terms:
        part = value if coef == 1.0 else coef * value
        total = part if total is None else total + part
    return total


def x_terms(k, n):
    terms = []
    for j in range(8):
        cell = 2 * k + j - 3
        if 0 <= cell < n:
            terms.append((cell, H[j], G[j]))
        elif cell == -1:
            terms.append(("l1", H[j], G[j]))
        elif cell == n:
            terms.append(("r1", H[j], G[j]))
    if k == 0:
        terms.append(("l2", 1.0, G[0] / H[0]))
    if k == n // 2 - 1:
        terms.append(("r2", 1.0, G[6] / H[6]))
    return terms


def lattice():
    low = np.array(H).reshape(4, 2)
    high = np.array(G).reshape(4, 2)
    tangents = []
    for _ in range(3):
        t = (low[0] @ high[0]) / (high[0] @ high[0])
        tangents.append(float(t))
        low, high = (low - t * high)[1:] / (1 + t * t), (high + t * low)[:-1] / (1 + t * t)
    return low[0].tolist(), high[0].tolist(), tangents[::-1]


def x_interior(get, n):
    first, second, tangents = lattice()
    a, b = {}, {}
    for i in range(1, n // 2):
        x, y = get(2 * i - 1), get(2 * i)
        a[i] = first[0] * x + first[1] * y
        b[i] = second[0] * x + second[1] * y
    for t in tangents:
        shared = [i for i in a if i + 1 in a]
        a, b = {i: a[i + 1] + t * b[i] for i in shared}, {i: b[i] - t * a[i + 1] for i in shared}
    return {i + 1: (a[i], b[i]) for i in a}


def x_low(get, k, n):
    return added([(low, get(key)) for key, low, _ in x_terms(k, n)])


def x_high(get, k, n):
    return added([(high, get(key)) for key, _, high in x_terms(k, n)])


def x_synth(m, lows, highs):
    terms = [(H[m + 3 - 2 * k], v) for k, v in lows.items() if 0 <= m + 3 - 2 * k < 8]
    terms += [(G[m + 3 - 2 * k], v) for k, v in highs.items() if 0 <= m + 3 - 2 * k < 8]
    return added(terms)


def x_synth_interior(lows, highs, n):
    first, second, tangents = lattice()
    a = {k - 1: lows[k] for k in range(n)}
    b = {k - 1: highs[k] for k in range(n)}
    for t in reversed(tangents):
        a, b = {i + 1: a[i] - t * b[i] for i in a}, {i: b[i] + t * a[i] for i in b}
        both = [i for i in a if i in b]
        a, b = {i: a[i] for i in both}, {i: b[i] for i in both}
    cells = {}
    for i in a:
        cells[2 * i - 1] = first[0] * a[i] + second[0] * b[i]
        cells[2 * i] = first[1] * a[i] + second[1] * b[i]
    return cells


def spill_up(low, high, n):
    first = added([(H[5], low[n - 1]), (G[5], high[n - 1]), (H[7], low[n - 2]), (G[7], high[n - 2])])
    return first, added([(H[6], low[n - 1]), (G[6], high[n - 1])])


def spill_down(low, high):
    first = added([(H[2], low[0]), (G[2], high[0]), (H[0], low[1]), (G[0], high[1])])
    return first, added([(H[1], low[0]), (G[1], high[0])])


THIRD_UP = H[7] / H[6]
THIRD_DOWN = H[0] / H[1]


def shrink(values, thresh):
    return values - jnp.minimum(jnp.maximum(values, -thresh), thresh)


def paired(kernel, args, outs, scratch, received, sent):
    extra = [pltpu.VMEM((2,) + args[i].shape, F32) for i, _ in received]
    extra += [pltpu.VMEM((2,) + outs[j].shape, F32) for j, _ in sent]

    def wrapped(*refs):
        refs, both = list(refs[: len(refs) - len(extra)]), refs[len(refs) - len(extra) :]
        for (i, axis), pair in zip(received, both):
            parity = lax.rem(lax.axis_index(axis), 2)
            pair[0], pair[1] = refs[i][...], refs[i + 1][...]
            refs[i], refs[i + 1] = pair.at[1 - parity], pair.at[parity]
        carried = []
        for (j, axis), pair in zip(sent, both[len(received) :]):
            parity = lax.rem(lax.axis_index(axis), 2)
            j += len(args)
            carried.append((refs[j], refs[j + 1], pair))
            refs[j], refs[j + 1] = pair.at[parity], pair.at[1 - parity]
        kernel(*refs)
        for first, second, pair in carried:
            first[...], second[...] = pair[0], pair[1]

    return wrapped, list(scratch) + extra


def whole_call(kernel, outs, args, scratch=(), received=(), sent=(), name=None, **changes):
    out_list = outs if isinstance(outs, list) else [outs]
    kernel, scratch = paired(kernel, args, out_list, scratch, received, sent)
    specs = [SMEM if a.ndim == 1 or a.dtype == jnp.int32 else VMEM for a in args]
    return pl.pallas_call(
        kernel,
        in_specs=changes.get("in_specs", specs),
        out_specs=changes.get("out_specs", [VMEM] * len(outs) if outs is out_list else VMEM),
        out_shape=outs,
        scratch_shapes=scratch,
        name=name,
        cost_estimate=pl.CostEstimate(flops=1000, bytes_accessed=1000, transcendentals=0),
        compiler_params=pltpu.CompilerParams(vmem_limit_bytes=changes.get("vmem", VMEM_BYTES)),
    )(*args)


def shape(*dims):
    return jax.ShapeDtypeStruct(dims, F32)


SMEM = pl.BlockSpec(memory_space=pltpu.SMEM)
VMEM = pl.BlockSpec(memory_space=pltpu.VMEM)


def first_messages(v):
    nx, ny, nz = v.shape

    kept = nx - nx // 8

    def kernel(v_ref, up, down, y_up, y_down, last, first, rows_up, rows_down, sems):
        copies = [
            pltpu.make_async_copy(source, target, sems.at[i])
            for i, (source, target) in enumerate(
                (
                    (v_ref.at[pl.ds(nx - 3, 3)], last),
                    (v_ref.at[pl.ds(0, 3)], first),
                    (v_ref.at[:, pl.ds(ny - 8, 8)], rows_up),
                    (v_ref.at[:, pl.ds(0, 8)], rows_down),
                )
            )
        ]
        for copy in copies:
            copy.start()
        for copy in copies:
            copy.wait()
        up[0] = last[2]
        up[1] = H[0] * last[0] + H[1] * last[1]
        down[0] = first[0]
        down[1] = H[6] * first[1] + H[7] * first[2]
        y_up[...] = rows_up[:kept]
        y_down[...] = rows_down[:kept]
        for i in range(kept):
            plane, row = kept + i // 7, i % 7
            y_up[i, 0:1] = rows_up[plane, row + 1 : row + 2]
            y_down[i, 7:8] = rows_down[plane, row : row + 1]

    return whole_call(
        kernel,
        [shape(2, ny, nz)] * 2 + [shape(kept, 8, nz)] * 2,
        [v],
        scratch=[pltpu.VMEM((3, ny, nz), F32)] * 2
        + [pltpu.VMEM((nx, 8, nz), F32)] * 2
        + [pltpu.SemaphoreType.DMA((4,))],
        sent=[(0, "gx"), (2, "gy")],
        name="first_messages",
        in_specs=[pl.BlockSpec(memory_space=pltpu.HBM)],
        vmem=50 * 1024 * 1024,
    )


def over_planes(count, group, body):
    def step(i, carry):
        body(i * group)
        return carry

    lax.fori_loop(0, count // group, step, 0)


def depth(v, z_matrix, group, name):
    nx, rows, nz = v.shape

    def kernel(v_ref, z, out):
        def body(first):
            at = pl.ds(first, group)
            out[at] = times(v_ref[at].reshape(group * rows, nz), z).reshape(group, rows, nz)

        over_planes(nx, group, body)

    return whole_call(kernel, shape(nx, rows, nz), [v, z_matrix], name=name)


def y_analysis(zed, y_across, y_here, z_matrix, y_matrix):
    nx, ny, nz = zed.shape
    rows = y_matrix.shape[0]
    kept = y_here.shape[0]
    group = 8

    def kernel(zed_ref, right, left, z, y, out, left_z, right_z):
        for part, out_z in ((left, left_z), (right, right_z)):
            out_z[:kept] = times(part[...].reshape(8 * kept, nz), z).reshape(kept, 8, nz)
            out_z[kept:] = jnp.zeros((nx - kept, 8, nz), F32)
        for i in range(kept):
            plane, row = kept + i // 7, i % 7
            left_z[plane, row + 1 : row + 2] = left_z[i, 0:1]
            right_z[plane, row : row + 1] = right_z[i, 7:8]

        def body(first):
            for j in range(group):
                i = first + j
                out[i] = left_times(y, jnp.concatenate([left_z[i], zed_ref[i], right_z[i]], axis=0))

        over_planes(nx, group, body)

    return whole_call(
        kernel,
        shape(nx, rows, nz),
        [zed, y_across, y_here, z_matrix, y_matrix],
        scratch=[pltpu.VMEM((nx, 8, nz), F32)] * 2,
        received=[(1, "gy")],
        name="y_analysis",
    )


def own_approx(zed, y_matrix, own, rows, ghost_rows):
    nx, ny, nz = zed.shape
    half_z = nz // 2
    n1 = nx // 2

    def kernel(zed_ref, y, approx, up, down, low):
        def y_body(first):
            planes = [zed_ref[first + i, :, :half_z] for i in range(8)]
            for i, plane in enumerate(in_pairs(y, planes)):
                low[first + i] = plane[:rows]

        over_planes(nx, 8, y_body)

        def tile(t, carry):
            at = pl.ds(pl.multiple_of(t * 8, 8), 8)
            values = {i: low[i, at] for i in range(nx)}
            for k in range(n1):
                approx[k, at] = added([(c, values[i]) for i, c, _ in x_terms(k, nx) if i in values])
            approx[n1, at] = added([(H[5 + i], values[i]) for i in range(3)])
            approx[n1 + 1, at] = H[1] * H[7] * values[0]
            approx[n1 + 2, at] = added([(H[i], values[nx - 3 + i]) for i in range(3)])
            approx[n1 + 3, at] = H[6] * H[0] * values[nx - 1]
            return carry

        lax.fori_loop(0, rows // 8, tile, 0)
        inside = ghost_rows - 2
        up[:, :inside] = approx[:n1, own - inside : own]
        up[:, inside:] = approx[:n1, own + 2 : own + 4]
        down[:, :2] = approx[:n1, own : own + 2]
        down[:, 2:] = approx[:n1, :inside]

    return whole_call(
        kernel,
        [shape(n1 + 4, rows, half_z), shape(n1, ghost_rows, half_z), shape(n1, ghost_rows, half_z)],
        [zed, y_matrix],
        scratch=[pltpu.VMEM((nx, rows, half_z), F32)],
        sent=[(1, "gy")],
        name="own_approx",
    )


def x_halo_messages(x_left, x_right, approx, z_matrix, wide, ghost_rows):
    _, ny, nz = x_left.shape
    half_z = nz // 2
    n1 = approx.shape[0] - 4
    own, inside = ny // 2, ghost_rows - 2
    message = wide + 8 + ghost_rows

    def kernel(xl, xr, a_ref, z, out, up, down):
        planes = jnp.concatenate([xl[0], xl[1], xr[0], xr[1]], axis=0)
        out[...] = times(planes, z).reshape(4, ny, nz)
        up[:, :wide] = out[:, ny - wide :, :half_z]
        up[:, wide : wide + 8] = out[:, ny - 8 :, half_z:]
        down[:, :wide] = out[:, :wide, :half_z]
        down[:, wide : wide + 8] = out[:, :8, half_z:]
        up[:, wide + 8 : wide + 8 + inside] = a_ref[n1:, own - inside : own]
        up[:, wide + 8 + inside :] = a_ref[n1:, own + 2 : own + 4]
        down[:, wide + 8 : wide + 10] = a_ref[n1:, own : own + 2]
        down[:, wide + 10 :] = a_ref[n1:, :inside]

    return whole_call(
        kernel,
        [shape(4, ny, nz), shape(4, message, half_z), shape(4, message, half_z)],
        [x_left, x_right, approx, z_matrix],
        received=[(0, "gx")],
        sent=[(1, "gy")],
        name="x_halo_messages",
    )


def edges_of(n):
    return [0, 1, n - 2, n - 1]


def band_limits(table_ref, index_ref, by, bz):
    band = 2 * by + bz
    quiet = table_ref[index_ref[0, band - 1]] if band else NOTHING
    return quiet, table_ref[index_ref[0, band + 3]]


def over_tiles(rows, nz, body, unroll=3):
    half_z, half_tiles = nz // 2, rows // 16
    for by in range(2):

        def tile(t, carry, by=by):
            at = pl.ds(pl.multiple_of((t + by * half_tiles) * 8, 8), 8)
            for bz in range(2):
                body(at, pl.ds(bz * half_z, half_z), by, bz)
            return carry

        lax.fori_loop(0, half_tiles, tile, 0, unroll=unroll if half_tiles % unroll == 0 else 1)


def inner_bands(bands, table, index):
    nx, rows, nz = bands.shape
    count = nx // 2 - 4

    def kernel(table_ref, index_ref, b_ref, out):
        def body(at, lanes, by, bz):
            quiet, loud = band_limits(table_ref, index_ref, by, bz)
            values = {i: b_ref[i, at, lanes] for i in range(nx)}
            for k, (low, high) in x_interior(values.get, nx).items():
                out[k - 2, at, lanes] = shrink(low, quiet) if by + bz else jnp.zeros_like(low)
                out[count + k - 2, at, lanes] = shrink(high, loud)

        over_tiles(rows, nz, body)

    return whole_call(
        kernel,
        shape(2 * count, rows, nz),
        [table, index, bands],
        name="inner_bands",
    )


def yz_synthesis(planes, z, y, out, zed):
    count, rows, nz = zed.shape
    group = max(g for g in range(1, 17) if count % g == 0)
    for first in range(0, count, group):
        zed[first : first + group] = times(planes(first, group), z).reshape(group, rows, nz)

    def y_body(first):
        for j in range(4):
            out[first + j] = left_times(y, zed[first + j])

    over_planes(count, 4, y_body)


def edge_own(bands):
    nx, rows, nz = bands.shape

    def kernel(b_ref, out):
        def body(at, lanes, by, bz):
            values = {i: b_ref[i, at, lanes] for i in [*range(7), *range(nx - 7, nx)]}
            for i, k in enumerate(edges_of(nx // 2)):
                terms = [t for t in x_terms(k, nx) if t[0] in values]
                out[i, at, lanes] = added([(low, values[key]) for key, low, _ in terms])
                out[4 + i, at, lanes] = added([(high, values[key]) for key, _, high in terms])

        over_tiles(rows, nz, body)

    return whole_call(kernel, shape(8, rows, nz), [bands], name="edge_own")


def edge_details(nx, own, halo, h_left, h_right, table, index, ya_matrix, z_matrix, y_matrix, wide):
    _, rows, nz = own.shape
    ny = y_matrix.shape[0]
    n1 = nx // 2
    half_z = nz // 2
    ends = edges_of(n1)

    def kernel(table_ref, index_ref, b_ref, x_ref, hl, hr, ya, z, y, coeffs, up, down, h_ref, beyond, zed):
        for i in range(4):
            low = jnp.concatenate([hl[i, wide - 8 : wide], x_ref[i, :, :half_z], hr[i, :8]], axis=0)
            high = jnp.concatenate(
                [hl[i, wide : wide + 8], x_ref[i, :, half_z:], hr[i, wide : wide + 8]], axis=0
            )
            h_ref[i] = left_times(ya, jnp.concatenate([low, high], axis=1))
        place = {"l1": 0, "l2": 1, "r1": 2, "r2": 3}

        def body(at, lanes, by, bz):
            quiet, loud = band_limits(table_ref, index_ref, by, bz)
            values = {key: h_ref[i, at, lanes] for key, i in place.items()}
            lows, highs = {}, {}
            for i, k in enumerate(ends):
                terms = [t for t in x_terms(k, nx) if t[0] in values]
                low = b_ref[i, at, lanes] + added([(c, values[key]) for key, c, _ in terms])
                high = b_ref[4 + i, at, lanes] + added([(c, values[key]) for key, _, c in terms])
                lows[k] = shrink(low, quiet) if by + bz else jnp.zeros_like(low)
                highs[k] = shrink(high, loud)
                coeffs[i, at, lanes] = lows[k]
                coeffs[4 + i, at, lanes] = highs[k]
            spilled = spill_up(lows, highs, n1) + spill_down(lows, highs)
            for i, part in enumerate(spilled):
                beyond[i, at, lanes] = part

        over_tiles(rows, nz, body, 9)
        zed[...] = times(beyond[...].reshape(4 * rows, nz), z).reshape(4, rows, nz)
        for i, target in enumerate((up.at[0], up.at[1], down.at[0], down.at[1])):
            target[...] = left_times(y, zed[i])

    return whole_call(
        kernel,
        [shape(8, rows, nz), shape(2, ny, nz), shape(2, ny, nz)],
        [table, index, own, halo, h_left, h_right, ya_matrix, z_matrix, y_matrix],
        scratch=[pltpu.VMEM((4, rows, nz), F32)] * 3,
        received=[(4, "gy")],
        sent=[(1, "gx")],
        name="edge_details",
    )


def detail_yz(edge, inner, approx, z_matrix, y_matrix):
    count, rows, nz = inner.shape
    ny = y_matrix.shape[0]
    _, low_rows, half_z = approx.shape
    n1 = count // 2 + 4
    ends = edges_of(n1)

    def kernel(e_ref, i_ref, a_ref, z, y, out, zed):
        def coeff(k, high):
            if k in ends:
                return e_ref.at[4 * high + ends.index(k)]
            return i_ref.at[(n1 - 4) * high + k - 2]

        def plane(i):
            ref = coeff(i % n1, i // n1)
            if i >= n1:
                return ref[...]
            corner = ref[:low_rows, :half_z] + a_ref[i + 2]
            top = jnp.concatenate([corner, ref[:low_rows, half_z:]], axis=1)
            return jnp.concatenate([top, ref[low_rows:]], axis=0)

        def planes(first, n):
            return jnp.concatenate([plane(i) for i in range(first, first + n)], axis=0)

        yz_synthesis(planes, z, y, out, zed)

    return whole_call(
        kernel,
        shape(2 * n1, ny, nz),
        [edge, inner, approx, z_matrix, y_matrix],
        scratch=[pltpu.VMEM((2 * n1, rows, nz), F32)],
        name="detail_yz",
    )


def own_result(parts, approx, z_matrix, y_matrix):
    nx, ny, nz = parts.shape
    n1 = nx // 2
    planes, rows, half_z = approx.shape

    def kernel(p_ref, a_ref, z, y, out, ghosts):
        stack = jnp.concatenate([a_ref[i] for i in (0, 1, n1 + 2, n1 + 3)], axis=0)
        for i, plane in enumerate(cut(times(stack, z), rows)):
            ghosts[i] = left_times(y, plane)

        def tile(t, carry):
            at = pl.ds(pl.multiple_of(t * 8, 8), 8)
            for lane in range(0, nz, 128):
                lanes = pl.ds(lane, 128)
                lows = {k: p_ref[k, at, lanes] for k in range(n1)}
                highs = {k: p_ref[n1 + k, at, lanes] for k in range(n1)}
                for i, k in enumerate((-2, -1, n1, n1 + 1)):
                    lows[k] = ghosts[i, at, lanes]
                cells = x_synth_interior(lows, highs, n1)
                for m in range(nx):
                    out[m, at, lanes] = cells[m] if m in cells else x_synth(m, lows, highs)
            return carry

        lax.fori_loop(0, ny // 8, tile, 0)

    return whole_call(
        kernel,
        shape(nx, ny, nz),
        [parts, approx, z_matrix, y_matrix],
        scratch=[pltpu.VMEM((4, ny, nz), F32)],
        name="own_result",
    )


def in_pairs(matrix, planes):
    results = []
    for i in range(0, len(planes), 2):
        both = left_times(matrix, jnp.concatenate(planes[i : i + 2], axis=1))
        width = both.shape[1] // 2
        results += [both[:, :width], both[:, width:]]
    return results


def cut(values, rows):
    return [values[i : i + rows] for i in range(0, values.shape[0], rows)]


def packed(first, second):
    half = first.shape[1] // 2
    lane = lax.broadcasted_iota(jnp.int32, first.shape, 1)
    return jnp.where(lane < half, first, pltpu.roll(second, half, 1))


def unpacked(both):
    half = both.shape[1] // 2
    lane = lax.broadcasted_iota(jnp.int32, both.shape, 1)
    return [jnp.where(lane < half, part, 0.0) for part in (both, pltpu.roll(both, half, 1))]


def second_bands(own, left, right, z_matrix, y_matrix, low_rows):
    _, own_rows, nz = own.shape
    n1 = left.shape[0]
    in_rows = own_rows + 2 * left.shape[1]
    rows = y_matrix.shape[0]


    def kernel(o_ref, l_ref, r_ref, z, y, out, up, down):
        for i in range(0, n1, 16):
            stack = [part[j] for j in range(i, min(i + 16, n1)) for part in (o_ref, l_ref, r_ref)]
            zed = times_wide(jnp.concatenate(stack, axis=0), z)
            for j, plane in enumerate(in_pairs(y, cut(zed, in_rows))):
                out[i + j] = plane
        low = lambda c: out[c, :low_rows]
        up[0:rows] = out[n1 - 1]
        up[rows : 2 * rows] = H[0] * out[n1 - 3] + H[1] * out[n1 - 2]
        first = added([(H[j], low(n1 - 5 + j)) for j in range(5)])
        second = added([(H[0] * H[j], low(n1 - 9 + j)) for j in range(8)])
        second += added([(H[1] * H[j], low(n1 - 7 + j)) for j in range(7)])
        up[2 * rows :] = packed(first, second)
        down[0:rows] = out[0]
        down[rows : 2 * rows] = H[6] * out[1] + H[7] * out[2]
        first = added([(H[j], low(j - 3)) for j in range(3, 8)])
        second = added([(H[6] * H[j], low(j - 1)) for j in range(1, 8)])
        second += added([(H[7] * H[j], low(j + 1)) for j in range(8)])
        down[2 * rows :] = packed(first, second)

    message = 2 * rows + low_rows
    return whole_call(
        kernel,
        [shape(n1, rows, nz), shape(message, nz), shape(message, nz)],
        [own, left, right, z_matrix, y_matrix],
        received=[(1, "gy")],
        sent=[(1, "gx")],
        name="second_bands",
    )


def limits_plane(table_ref, index_ref, level, bx, dims, row_split, lane_split, zeroth):
    row_high = lax.broadcasted_iota(jnp.int32, dims, 0) >= row_split
    lane_high = lax.broadcasted_iota(jnp.int32, dims, 1) >= lane_split

    def limit(by, bz):
        band = 4 * bx + 2 * by + bz
        return zeroth if band == 0 else table_ref[index_ref[level, band - 1]]

    low_y = jnp.where(lane_high, limit(0, 1), limit(0, 0))
    return jnp.where(row_high, jnp.where(lane_high, limit(1, 1), limit(1, 0)), low_y)


def coarse(
    bands, left, right, halo, h_left, h_right, approx_in, table, index, za1, yx0, ya1, zs1, za2, zs2, ya2, ys2, ys1,
    in_rows1, low_rows, out_rows, own_rows, spill_at, spill_rows, wide,
):
    n1, rows, nz = bands.shape
    in_rows = in_rows1
    n2, n3 = n1 // 2, n1 // 4
    rows2 = ya2.shape[0]
    lane_half = nz // 2

    def kernel(
        table_ref, index_ref, b_ref, l_ref, r_ref, x_ref, hl, hr, a_ref, z1a, yx, a1, z1, z2a, z2s, a2, s2, s1,
        approx, up, down, c1, p1,
    ):
        halo_planes = [jnp.concatenate([hl[i, :wide], x_ref[i, :, :nz], hr[i, :wide]], axis=0) for i in range(4)]
        halo_planes = [plane[:in_rows] for plane in in_pairs(yx, halo_planes)]
        own_planes = [
            jnp.concatenate([a_ref[n1 + i], hl[i, wide + 8 :], hr[i, wide + 8 :]], axis=0) for i in range(4)
        ]
        both = times_wide(jnp.concatenate(halo_planes + own_planes, axis=0), z1a)
        hl1, hl2, hr1, hr2, xl1, xl2, xr1, xr2 = in_pairs(a1, cut(both, in_rows))
        values = {k: b_ref[k] for k in range(2, n1 - 2)}
        values[0] = b_ref[0] + (hl2 + H[2] * hl1)
        values[1] = b_ref[1] + H[0] * hl1
        values[n1 - 2] = b_ref[n1 - 2] + H[7] * hr1
        values[n1 - 1] = b_ref[n1 - 1] + (hr2 + H[5] * hr1)
        values["l1"] = l_ref[0:rows] + xl1
        values["l2"] = l_ref[rows : 2 * rows] + xl2
        values["r1"] = r_ref[0:rows] + xr1
        values["r2"] = r_ref[rows : 2 * rows] + xr2
        get = values.get
        low_part = lambda c: values[c][:low_rows]
        xl1, xl2, xr1, xr2 = [part[:low_rows] for part in (xl1, xl2, xr1, xr2)]
        dims = (rows, nz)
        quiet = limits_plane(table_ref, index_ref, 1, 0, dims, low_rows, lane_half, NOTHING)
        loud = limits_plane(table_ref, index_ref, 1, 1, dims, low_rows, lane_half, NOTHING)
        planes = []
        for k in range(n2):
            low = x_low(get, k, n1)
            planes.append(low[:low_rows])
            c1[k] = shrink(low, quiet)
            c1[n2 + k] = shrink(x_high(get, k, n1), loud)
        first, second = unpacked(l_ref[2 * rows :])
        own = [(H[5 + i], low_part(i)) for i in range(3)]
        planes.append(first + added([(H[3] / H[1], xl2), (H[4], xl1)] + own))
        own = [((H[0] * H[7] + H[1] * H[5]) / H[1], xl2), (H[1] * H[6], xl1), (H[1] * H[7], low_part(0))]
        planes.append(second + added(own))
        first, second = unpacked(r_ref[2 * rows :])
        own = [(H[i], low_part(n1 - 3 + i)) for i in range(3)]
        planes.append(first + added([(H[3], xr1), (H[4] / H[6], xr2)] + own))
        own = [((H[6] * H[2] + H[7] * H[0]) / H[6], xr2), (H[6] * H[1], xr1), (H[6] * H[0], low_part(n1 - 1))]
        planes.append(second + added(own))
        third = in_pairs(a2, cut(times_wide(jnp.concatenate(planes, axis=0), z2a), low_rows))
        keys = {"l1": n2, "l2": n2 + 1, "r1": n2 + 2, "r2": n2 + 3}
        get2 = lambda key: third[keys.get(key, key)]
        dims = (rows2, nz)
        quiet = limits_plane(table_ref, index_ref, 2, 0, dims, rows2 // 2, lane_half // 2, 0.0)
        loud = limits_plane(table_ref, index_ref, 2, 1, dims, rows2 // 2, lane_half // 2, 0.0)
        kept = [shrink(x_low(get2, k, n2), quiet) for k in range(n3)]
        kept += [shrink(x_high(get2, k, n2), loud) for k in range(n3)]
        parts = in_pairs(s2, cut(times_wide(jnp.concatenate(kept, axis=0), z2s), rows2))
        parts = [part[:low_rows] for part in parts]
        lows = dict(enumerate(parts[:n3]))
        highs = dict(enumerate(parts[n3:]))
        ghosts = [-3, -2, -1, n2, n2 + 1, n2 + 2]
        for k in range(n2):
            c1[k, :low_rows] += x_synth(k, lows, highs)
        stack = [x_synth(k, lows, highs) for k in ghosts]
        beyond = dict(zip(ghosts, stack))
        zed = times_wide(jnp.concatenate(stack, axis=0), z1)
        for i, plane in enumerate(in_pairs(s1, cut(zed, low_rows))):
            p1[2 * n2 + i] = plane[:out_rows]
        for i in range(0, 2 * n2, 16):
            zed = times_wide(c1[i : i + 16].reshape(16 * rows, nz), z1)
            for j, plane in enumerate(in_pairs(s1, cut(zed, rows))):
                p1[i + j] = plane[:out_rows]
        lows = {k: p1.at[k] for k in range(n2)}
        highs = {k: p1.at[n2 + k] for k in range(n2)}
        for i, k in enumerate(ghosts):
            lows[k] = p1.at[2 * n2 + i]

        def cell(m):
            near = lambda part: {k: ref[...] for k, ref in part.items() if 0 <= m + 3 - 2 * k < 8}
            return x_synth(m, near(lows), near(highs))

        for m in range(-2, n1 + 2):
            approx[m + 2] = cell(m)
        value = lambda part, ks: {k: part[k][...] for k in ks}
        ends = (n2 - 2, n2 - 1)

        def send(message, four, two):
            for i, plane in enumerate(four):
                message[i * own_rows : (i + 1) * own_rows] = plane[:own_rows]
                message[4 * own_rows + 4 * i : 4 * own_rows + 4 * i + 4] = plane[own_rows : own_rows + 4]
            message[4 * own_rows + 16 :] = packed(*two)[spill_at : spill_at + spill_rows]

        up_two = spill_up(value(lows, ends), value(highs, ends), n2)
        send(up, (approx[n1], approx[n1 + 1], *up_two), (beyond[n2], beyond[n2 + 1]))
        down_two = spill_down(value(lows, (0, 1)), value(highs, (0, 1)))
        send(down, (approx[2], approx[3], *down_two), (beyond[-1], beyond[-2]))

    message = 4 * own_rows + 16 + spill_rows
    return whole_call(
        kernel,
        [shape(n1 + 4, out_rows, nz), shape(message, nz), shape(message, nz)],
        [table, index, bands, left, right, halo, h_left, h_right, approx_in, za1, yx0, ya1, zs1, za2, zs2, ya2, ys2, ys1],
        scratch=[pltpu.VMEM((2 * n2, rows, nz), F32), pltpu.VMEM((2 * n2 + 6, out_rows, nz), F32)],
        received=[(3, "gx"), (6, "gy")],
        sent=[(1, "gx")],
        name="coarse",
    )


def received_taps(n1):
    n2, nx = n1 // 2, 2 * n1
    from_approx = np.zeros((nx, n1 + 4))
    for m in range(nx):
        for k in range(-2, n1 + 2):
            from_approx[m, k + 2] = tap(H, m + 3 - 2 * k)
    approx = np.zeros((n1 + 4, 12))
    third = {0: THIRD_UP, 6: THIRD_DOWN}
    for first, cell, second in ((0, lambda i: i, lambda i: i), (6, lambda i: n1 - 1 - i, lambda i: n2 - 1 - i)):
        ghost = (-2, -1) if first == 0 else (n1, n1 + 1)
        for i in range(2):
            approx[ghost[i] + 2, first + i] = 1.0
        for place, source, coef in ((0, 0, 1.0), (1, 1, 1.0), (2, 1, third[first])):
            approx[cell(place) + 2, first + 2 + source] += coef
            for m in range(n1):
                approx[m + 2, first + 4 + source] += coef * tap(H, m + 3 - 2 * second(place))
    return from_approx @ approx


def final(left, right, own, e_left, e_right, zs1, ys1, z_matrix, y_matrix, rows, spill_rows):
    nx, ny, nz = own.shape
    half_z = nz // 2
    own_rows = ny // 2
    step_rows = 16
    steps = ny // step_rows
    taps = received_taps(nx // 2)

    def kernel(l_ref, r_ref, d_ref, el, er, z1, s1, z, y, out, planes, parts, done, sems):
        stack = [p for ref in (l_ref, r_ref) for p in unpacked(ref[4 * own_rows + 16 :])]
        spilled = cut(times(jnp.concatenate(stack, axis=0), z1), spill_rows)
        for side, ref in enumerate((l_ref, r_ref)):
            for i in range(4):
                plane = planes.at[4 * side + i]
                plane[:own_rows] = ref[i * own_rows : (i + 1) * own_rows]
                plane[own_rows:] = jnp.zeros((rows - own_rows, half_z), F32)
                plane[own_rows : own_rows + 4] = ref[4 * own_rows + 4 * i : 4 * own_rows + 4 * i + 4]
        for i, plane in enumerate(cut(times(planes[...].reshape(8 * rows, half_z), z), rows)):
            parts[6 * (i // 4) + i % 4] = left_times(y, plane)
        for i, plane in enumerate(spilled):
            parts[6 * (i // 2) + 4 + i % 2] = left_times(s1, plane)

        def copy(i):
            at = pl.ds(pl.multiple_of(i * step_rows, step_rows), step_rows)
            return pltpu.make_async_copy(done.at[:, at], out.at[:, at], sems.at[i])

        def step(i, carry):
            for t in range(step_rows // 8):
                at = pl.ds(pl.multiple_of(i * step_rows + 8 * t, 8), 8)
                for lane in range(0, nz, 128):
                    lanes = pl.ds(lane, 128)
                    values = [parts[i, at, lanes] for i in range(12)]
                    for m in range(nx):
                        value = d_ref[m, at, lanes]
                        value += added([(float(c), v) for c, v in zip(taps[m], values) if c != 0.0])
                        if m < 3:
                            extra = el[(0, 1, 1)[m], at, lanes]
                            value += extra if m < 2 else THIRD_UP * extra
                        if m >= nx - 3:
                            extra = er[(0, 1, 1)[nx - 1 - m], at, lanes]
                            value += extra if m > nx - 3 else THIRD_DOWN * extra
                        done[m, at, lanes] = value
            copy(i).start()
            return carry

        lax.fori_loop(0, steps, step, 0)

        def finish(i, carry):
            copy(i).wait()
            return carry

        lax.fori_loop(0, steps, finish, 0)

    return whole_call(
        kernel,
        shape(nx, ny, nz),
        [left, right, own, e_left, e_right, zs1, ys1, z_matrix, y_matrix],
        scratch=[
            pltpu.VMEM((8, rows, half_z), F32),
            pltpu.VMEM((12, ny, nz), F32),
            pltpu.VMEM((nx, ny, nz), F32),
            pltpu.SemaphoreType.DMA((steps,)),
        ],
        received=[(0, "gx"), (3, "gx")],
        name="final",
        out_specs=pl.BlockSpec(memory_space=pl.ANY),
    )


def exchange(first, second, axis):
    size = lax.axis_size(axis)
    assert size % 2 == 0
    here = [(i, i ^ 1) for i in range(size)]
    across = [(i, (i + 1) % size if i % 2 else (i - 1) % size) for i in range(size)]
    return lax.ppermute(first, axis, here), lax.ppermute(second, axis, across)


def local(velocity, table, index):
    nx, ny, nz = velocity.shape
    y1, y2, y3 = ny // 2, ny // 4, ny // 8
    ghost, wide = 24, 48
    cells0 = list(range(-8, ny + 8))
    rows0 = up_to(y1 + 4, 8)
    ks0 = fill(list(range(y1)) + [-2, -1, y1, y1 + 1], rows0)
    cells1 = ks0 + list(range(2 - ghost, 2)) + list(range(y1 - 2, y1 + ghost - 2))
    once = [c if cells1.index(c) == i else None for i, c in enumerate(cells1)]
    rows1 = up_to(y2 + 18, 8)
    low1 = fill(list(range(-9, y2 + 9)), rows1)
    high1 = fill(list(range(-3, y2 + 3)), up_to(y2 + 6, 8))
    spill_at, spill_rows = 6, up_to(y2 + 6, 8)
    ks2 = fill(list(range(-3, y3 + 3)), up_to(y3 + 6, 8))
    ya0 = from_left(analysis_rows(cells0, ks0, ks0))
    ys0_matrix = synthesis_rows(list(range(ny)), ks0, ks0)
    ys0 = from_left(ys0_matrix)
    ys0_low = from_left(ys0_matrix[:, :rows0])
    yl0 = from_left(analysis_rows(list(range(ny)), ks0, []))
    yx0 = from_left(analysis_rows(list(range(-wide, ny + wide)), once, []))
    ya1 = from_left(analysis_rows(cells1, low1, high1))
    ys1 = from_left(synthesis_rows(ks0, low1, high1))
    spill_matrix = synthesis_rows(ks0, low1[spill_at : spill_at + spill_rows], [])
    ys_spill = from_left(ys0_matrix[:, :rows0] @ spill_matrix)
    ya2 = from_left(analysis_rows(low1, ks2, ks2))
    ys2 = from_left(synthesis_rows(low1, ks2, ks2))
    z0 = periodic(nz, nz)
    z1 = periodic(nz // 2, nz // 2)
    z2 = periodic(nz // 4, nz // 2)
    za0, zs0, zs0_low = from_right(z0), from_right(z0.T), from_right(z0.T[: nz // 2])
    za1, zs1 = wide_right(z1), wide_right(z1.T)
    za2, zs2 = wide_right(z2), wide_right(z2.T)
    zs_spill = from_right(z1.T @ z0.T[: nz // 2])

    x_up, x_down, y_up, y_down = first_messages(velocity)
    x_left, x_right = exchange(x_up, x_down, "gx")
    y_here, y_across = exchange(y_up, y_down, "gy")
    zed = depth(velocity, za0, 16, "depth_analysis")
    approx, a_up, a_down = own_approx(zed, yl0, y1, rows0, ghost)
    a_left, a_right = exchange(a_up, a_down, "gy")
    zed, a_up = lax.optimization_barrier((zed, a_up))
    bands = y_analysis(zed, y_across, y_here, za0, ya0)
    ends = edge_own(bands)
    x_left, x_right, ends = lax.optimization_barrier((x_left, x_right, ends))
    halo, h_up, h_down = x_halo_messages(x_left, x_right, approx, za0, wide, ghost)
    h_left, h_right = exchange(h_up, h_down, "gy")
    approx, halo = lax.optimization_barrier((approx, halo))
    bands1, b_up, b_down = second_bands(approx, a_left, a_right, za1, ya1, rows1)
    b_left, b_right = exchange(b_up, b_down, "gx")
    h_left, h_right, bands1 = lax.optimization_barrier((h_left, h_right, bands1))
    edge, e_up, e_down = edge_details(nx, ends, halo, h_left, h_right, table, index, ya0, zs0, ys0, wide)
    e_left, e_right = exchange(e_up, e_down, "gx")
    bands1, edge = lax.optimization_barrier((bands1, edge))
    approx1, s_up, s_down = coarse(
        bands1, b_left, b_right, halo, h_left, h_right, approx, table, index,
        za1, yx0, ya1, zs1, za2, zs2, ya2, ys2, ys1, len(cells1), rows1, rows0, y1, spill_at, spill_rows, wide,
    )
    s_left, s_right = exchange(s_up, s_down, "gx")
    bands, approx1 = lax.optimization_barrier((bands, approx1))
    parts = detail_yz(edge, inner_bands(bands, table, index), approx1, zs0, ys0)
    own = own_result(parts, approx1, zs0_low, ys0_low)
    return final(s_left, s_right, own, e_left, e_right, zs_spill, ys_spill, zs0_low, ys0_low, rows0, spill_rows)


def solution(mesh):
    return jax.shard_map(
        local,
        mesh=mesh,
        in_specs=(P("gx", "gy", None), P(), P()),
        out_specs=P("gx", "gy", None),
        check_vma=False,
    )
```
